32 devices in a mesh: dp: 16 (over z, y, x), tensor: 2 (over core).
Axes of the slice: x: 2, y: 2, z: 4, core: 2. Of those that a mesh axis runs over, the one named last changes fastest.
Arguments:
- layer_input: bfloat16 [8192, 2048], P(('dp', 'tensor')), may hold values from -6 to 6
- attn_norm: float32 [2048], replicated, may hold values from 0.5 to 1.5
- head_norms: float32 [2, 128], replicated, may hold values from 0.1 to 1.9
- query_weight: bfloat16 [2048, 2048], P('dp', 'tensor'), may hold values from -0.125 to 0.125
- key_matrix: bfloat16 [2048, 1024], P('dp', 'tensor'), may hold values from -0.125 to 0.125
- value_matrix: bfloat16 [2048, 1024], P('dp', 'tensor'), may hold values from -0.125 to 0.125
- output_weight: bfloat16 [2048, 2048], P(('tensor', 'dp')), may hold values from -1 to 1
- mlp_norm: float32 [2048], replicated, may hold values from 0.5 to 1.5
- gate_weight: bfloat16 [2048, 6144], P('dp', 'tensor'), may hold values from -0.125 to 0.125
- up_weight: bfloat16 [2048, 6144], P('dp', 'tensor'), may hold values from -0.125 to 0.125
- down_weight: bfloat16 [6144, 2048], P(('tensor', 'dp')), may hold values from -0.078125 to 0.078125
- grad_out: bfloat16 [8192, 2048], P(('dp', 'tensor')), may hold values from -6 to 6
- doc_lengths: int32 [16, 6], P('dp'), may hold values from 1 to 384, 512 in all within a row
Outputs:
- layer_out: bfloat16 [8192, 2048], P(('dp', 'tensor'))
- grad_input: float32 [8192, 2048], P(('dp', 'tensor'))
- grad_attn_norm: float32 [2048], replicated
- grad_head_norms: float32 [2, 128], replicated
- grad_query: float32 [2048, 2048], P('dp', 'tensor')
- grad_key: float32 [2048, 1024], P('dp', 'tensor')
- grad_value: float32 [2048, 1024], P('dp', 'tensor')
- grad_out_proj: float32 [2048, 2048], P(('tensor', 'dp'))
- grad_mlp_norm: float32 [2048], replicated
- grad_gate: float32 [2048, 6144], P('dp', 'tensor')
- grad_up: float32 [2048, 6144], P('dp', 'tensor')
- grad_down: float32 [6144, 2048], P(('tensor', 'dp'))
The draws below stay inside these ranges and needn't reach their ends.
Inputs may be any that keep to these rules, and one draw needn't show every extreme that they name: `doc_lengths`: in every bucket the 6 lengths sum to 512 and the longest is exactly 384.
All inputs are finite; a program needn't handle non-finite values.
Results may differ from the reference program's by a relative error of at most 0.018.
Values may be sent and summed in bfloat16 or wider, within the bound.
A program may use at most 256 MiB of HBM per device.

```python
import math
import jax
import jax.numpy as jnp
import numpy as np
from jax import lax

MODEL_WIDTH = 2048
FF = 6144
QUERY_HEADS = 16
KEY_VALUE_HEADS = 8
HEAD_SIZE = 128
DOCS = 6
BUCKET_TOKENS = 512
MOSTLEN = 384
DOCUMENT_BUCKETS = 16
TOKENS = 8192


def strengthened(entries, own_key, source, target, parts, factor):
    def block_of(dim):
        return (jnp.arange(entries.shape[dim]) // (entries.shape[dim] // parts)).reshape((-1,) + (1,) * (entries.ndim - 1 - dim))

    near = jax.random.permutation(own_key, parts)[block_of(target)]
    other_side = (block_of(target) + parts // 2) % parts
    return jnp.where((block_of(source) == near) | (block_of(source) == other_side), factor * entries, entries)


def steps_of(own_key, extent, pieces, least, largest):
    loudness = 1.0
    for dim, shards_of in pieces:
        draws = jax.random.uniform(jax.random.fold_in(jax.random.fold_in(own_key, 6), dim), (shards_of,), jnp.float32, least / len(pieces), largest / len(pieces))
        loudness = loudness * jnp.repeat(jnp.exp(draws), extent[dim] // shards_of).reshape((-1,) + (1,) * (len(extent) - 1 - dim))
    return loudness


def split_up(count, total, most, skew):
    portions = [(1 << 20) // math.isqrt(grade ** skew) + 1 for grade in range(2, count + 1)]
    spare, counts = total - most - (count - 1), [1] * (count - 1)
    while spare > 0:
        free = [i for i in range(count - 1) if counts[i] < most]
        mass, remaining = sum([portions[i] for i in free]), spare
        for i in free:
            extra = min(most - counts[i], max(1, remaining * portions[i] // mass), spare)
            counts[i] = counts[i] + extra
            spare = spare - extra
    return np.array([most] + counts)


def ragged(own_key, number_of, total, bound, slope):
    if number_of == 2:
        one = jax.random.randint(own_key, (), max(1, total - bound), min(bound, total - 1) + 1)
        return jnp.stack([one, total - one])
    sizes = jnp.asarray(split_up(number_of, total, bound, slope), jnp.int32)
    twos = (number_of - 1) // 2
    giver, receiver = sizes[1:1 + 2 * twos:2], sizes[2:2 + 2 * twos:2]
    slack = jnp.minimum(giver - 1, bound - receiver)
    moved = jax.random.randint(jax.random.fold_in(own_key, 1), (twos,), 0, 1 << 20) % (slack + 1)
    sizes = sizes.at[1:1 + 2 * twos:2].set(giver - moved).at[2:2 + 2 * twos:2].set(receiver + moved)
    return sizes[jax.random.permutation(jax.random.fold_in(own_key, 2), number_of)]


def scatter_about(key, extent, scale, bound, split=(), kind=jnp.bfloat16):
    array = jax.random.normal(key, extent, jnp.float32) * scale
    if len(split) > 0:
        array = steps_of(key, extent, split, -0.22, 0.18) * array
    return jnp.clip(array, min=-bound, max=bound).astype(kind)


def bell_draw_with(key, extent, scale, bound, split, heavy, held_as=jnp.bfloat16):
    array = scale * jax.random.normal(key, extent, jnp.float32)
    if split:
        array = array * steps_of(key, extent, split, -0.22, 0.18)
    return jnp.clip(strengthened(array, jax.random.fold_in(key, 3), *heavy), -bound, bound).astype(held_as)


def setup_inputs(seed: int = 0) -> dict:
    key_list = jax.random.split(jax.random.key(seed), 14)
    layer_input = bell_draw_with(key_list[0], (TOKENS, MODEL_WIDTH), 1.0, 6.0, ((0, 32),), (0, 1, 32, 2.75))
    attn_norm = jnp.clip(1.0 + 0.1 * jax.random.normal(key_list[1], (MODEL_WIDTH,), jnp.float32), 0.5, 1.5)
    head_norms = jnp.clip(1.0 + 0.18 * jax.random.normal(key_list[2], (2, HEAD_SIZE), jnp.float32), 0.1, 1.9)
    query_weight = scatter_about(key_list[3], (MODEL_WIDTH, QUERY_HEADS * HEAD_SIZE), MODEL_WIDTH ** -0.5, 0.125, ((0, 16), (1, 2)))
    key_matrix = scatter_about(key_list[4], (MODEL_WIDTH, KEY_VALUE_HEADS * HEAD_SIZE), MODEL_WIDTH ** -0.5, 0.125, ((0, 16), (1, 2)))
    value_matrix = scatter_about(key_list[5], (MODEL_WIDTH, KEY_VALUE_HEADS * HEAD_SIZE), MODEL_WIDTH ** -0.5, 0.125, ((0, 16), (1, 2)))
    output_weight = scatter_about(key_list[6], (QUERY_HEADS * HEAD_SIZE, MODEL_WIDTH), (QUERY_HEADS * HEAD_SIZE // 64) ** -0.5, 1.0, ((0, 32),))
    mlp_norm = jnp.clip(1.0 + 0.1 * jax.random.normal(key_list[7], (MODEL_WIDTH,), jnp.float32), 0.5, 1.5)
    gate_weight = scatter_about(key_list[8], (MODEL_WIDTH, FF), MODEL_WIDTH ** -0.5, 0.125, ((0, 16), (1, 2)))
    up_weight = scatter_about(key_list[9], (MODEL_WIDTH, FF), MODEL_WIDTH ** -0.5, 0.125, ((0, 16), (1, 2)))
    down_weight = scatter_about(key_list[10], (FF, MODEL_WIDTH), FF ** -0.5, 0.078125, ((0, 32),))
    grad_out = scatter_about(key_list[11], (TOKENS, MODEL_WIDTH), 1.0, 6.0, ((0, 32),))
    doc_lengths = jax.vmap(lambda own: ragged(own, DOCS, BUCKET_TOKENS, MOSTLEN, 2))(jax.random.split(key_list[12], DOCUMENT_BUCKETS)).reshape((DOCUMENT_BUCKETS, DOCS)).astype(jnp.int32)
    return {"layer_input": layer_input, "attn_norm": attn_norm, "head_norms": head_norms, "query_weight": query_weight, "key_matrix": key_matrix, "value_matrix": value_matrix, "output_weight": output_weight, "mlp_norm": mlp_norm, "gate_weight": gate_weight, "up_weight": up_weight, "down_weight": down_weight, "grad_out": grad_out, "doc_lengths": doc_lengths}


EPS = 1e-06
ROPE_BASE = 1000000.0
MASKED = -1e+30

@jax.custom_vjp
def low(v):
    return lax.optimization_barrier(v.astype(jnp.bfloat16)).astype(jnp.float32)

@jax.custom_vjp
def low_back(v):
    return v

def low_keep(v):
    return (low(v), None)

def low_pass(kept, grad):
    return (grad,)

def back_keep(v):
    return (v, None)

def back_low(kept, grad):
    return (low(grad),)
low.defvjp(low_keep, low_pass)
low_back.defvjp(back_keep, back_low)

def dense(left_mat, right_mat):
    return jnp.dot(left_mat, right_mat, precision=lax.Precision.HIGHEST, preferred_element_type=jnp.float32)

def inv_rms(values):
    return lax.rsqrt(lax.optimization_barrier(jnp.mean(values * values, axis=-1, keepdims=True)) + EPS)

def rope_tables(position, head_width):
    half_dim = head_width // 2
    inverse = ROPE_BASE ** (-(jnp.arange(half_dim, dtype=jnp.float32) * (2.0 / head_width)))
    angles = position.astype(jnp.float32)[:, None] * inverse[None, :]
    return (jnp.cos(angles), jnp.sin(angles))

def rotate(values, cos_tab, sin_tab, direction):
    half_dim = values.shape[-1] // 2
    first_half = values[..., :half_dim]
    second_half = values[..., half_dim:]
    cosine = cos_tab[:, None, :]
    sine_tab = direction * sin_tab[:, None, :]
    return jnp.concatenate([first_half * cosine - second_half * sine_tab, second_half * cosine + first_half * sine_tab], axis=-1)

def doc_layout(lengths_row, group_rows):
    doc_ends = jnp.cumsum(lengths_row, dtype=jnp.int32)
    row_ids = jnp.arange(group_rows, dtype=jnp.int32)
    document_segment = lax.optimization_barrier(jnp.sum((row_ids[:, None] >= doc_ends[None, :]).astype(jnp.int32), axis=1, dtype=jnp.int32))
    doc_starts = doc_ends - lengths_row
    member = document_segment[:, None] == jnp.arange(lengths_row.shape[0], dtype=jnp.int32)[None, :]
    start_of = lax.optimization_barrier(jnp.sum(jnp.where(member, doc_starts[None, :], 0), axis=1, dtype=jnp.int32))
    return (document_segment, row_ids - start_of)

def attend(block):
    query_g, key_b, value_b, document_segment = block
    block_rows = query_g.shape[0]
    row_ids = jnp.arange(block_rows, dtype=jnp.int32)
    allowed = (document_segment[:, None] == document_segment[None, :]) & (row_ids[None, :] <= row_ids[:, None])
    scores = jnp.einsum('qkgd,tkd->kgqt', query_g, key_b, precision=lax.Precision.HIGHEST) * HEAD_SIZE ** (-0.5)
    scores = low_back(scores)
    masked = jnp.where(allowed[None, None], scores, MASKED)
    row_peak = lax.optimization_barrier(jnp.max(masked, axis=-1, keepdims=True))
    exponent = jnp.exp(masked - row_peak)
    probs = exponent / lax.optimization_barrier(jnp.sum(exponent, axis=-1, keepdims=True))
    return jnp.einsum('kgqt,tkd->qkgd', low(probs), value_b, precision=lax.Precision.HIGHEST)

def layer(layer_input, attn_norm, head_norms, query_weight, key_matrix, value_matrix, output_weight, mlp_norm, gate_weight, up_weight, down_weight, document_segment, position):
    every_row = layer_input.shape[0]
    group_list = QUERY_HEADS // KEY_VALUE_HEADS
    normed_attn = low(layer_input * inv_rms(layer_input) * attn_norm)
    query_raw = low_back(dense(normed_attn, query_weight))
    key_unnormed = low_back(dense(normed_attn, key_matrix))
    value_raw = low_back(dense(normed_attn, value_matrix))
    values_reduced = low(value_raw)
    query_h = query_raw.reshape(every_row, QUERY_HEADS, HEAD_SIZE)
    key_per_head = key_unnormed.reshape(every_row, KEY_VALUE_HEADS, HEAD_SIZE)
    cos_tab, sin_tab = rope_tables(position.reshape(every_row), HEAD_SIZE)
    query_rows = low(rotate(query_h * inv_rms(query_h) * head_norms[0], cos_tab, sin_tab, 1.0))
    keys_reduced = low(rotate(key_per_head * inv_rms(key_per_head) * head_norms[1], cos_tab, sin_tab, 1.0))
    block_list = (query_rows.reshape(DOCUMENT_BUCKETS, BUCKET_TOKENS, KEY_VALUE_HEADS, group_list, HEAD_SIZE), keys_reduced.reshape(DOCUMENT_BUCKETS, BUCKET_TOKENS, KEY_VALUE_HEADS, HEAD_SIZE), values_reduced.reshape(DOCUMENT_BUCKETS, BUCKET_TOKENS, KEY_VALUE_HEADS, HEAD_SIZE), document_segment)
    attended = lax.map(jax.checkpoint(attend), block_list)
    attended = low_back(attended.reshape(every_row, QUERY_HEADS * HEAD_SIZE))
    attended_low = low(attended)
    hidden_state = layer_input + low_back(dense(attended_low, output_weight))
    normed_mlp = low(hidden_state * inv_rms(hidden_state) * mlp_norm)
    gate_raw = low_back(dense(normed_mlp, gate_weight))
    up_raw = low_back(dense(normed_mlp, up_weight))
    inner = low(jax.nn.silu(gate_raw) * up_raw)
    return hidden_state + dense(inner, down_weight)

def bucket_layout(lengths_row):
    return doc_layout(lengths_row, BUCKET_TOKENS)

def reference(layer_input, attn_norm, head_norms, query_weight, key_matrix, value_matrix, output_weight, mlp_norm, gate_weight, up_weight, down_weight, grad_out, doc_lengths):
    document_segment, position = jax.vmap(bucket_layout)(doc_lengths)
    inputs = tuple((initial.astype(jnp.float32) for initial in (layer_input, attn_norm, head_norms, query_weight, key_matrix, value_matrix, output_weight, mlp_norm, gate_weight, up_weight, down_weight)))

    def forward(*params):
        return layer(*params, document_segment, position)
    result, pull_back = jax.vjp(forward, *inputs)
    grads = pull_back(grad_out.astype(jnp.float32))
    return (result.astype(jnp.bfloat16), grads[0], grads[1], grads[2], grads[3], grads[4], grads[5], grads[6], grads[7], grads[8], grads[9], grads[10])
```

```python
import jax
import jax.numpy as jnp
from jax import lax
from jax.sharding import Mesh, PartitionSpec as P

QUERY_HEADS = 16
KEY_VALUE_HEADS = 8
HEAD_SIZE = 128


EPS = 1e-06
ROPE_BASE = 1000000.0
MASKED = -1e30
LOW = jnp.bfloat16


def matmul(left_mat, right_mat):
    return jnp.dot(left_mat, right_mat, preferred_element_type=jnp.float32)


def matmul_tn(left_mat, right_mat):
    return lax.dot_general(
        left_mat, right_mat, (((0,), (0,)), ((), ())), preferred_element_type=jnp.float32
    )


def matmul_nt(left_mat, right_mat):
    return lax.dot_general(
        left_mat, right_mat, (((1,), (1,)), ((), ())), preferred_element_type=jnp.float32
    )


def inv_rms(values):
    return lax.rsqrt(jnp.mean(values * values, axis=-1, keepdims=True) + EPS)


def norm_back(values, scales, gain_row, upstream):
    weighted = upstream * gain_row
    inner_mean = jnp.mean(weighted * values, axis=-1, keepdims=True)
    value_grad = scales * weighted - values * (scales * scales * scales) * inner_mean
    lead_axes = tuple(range(upstream.ndim - 1))
    return (value_grad, jnp.sum(upstream * values * scales, axis=lead_axes))


def rope_tables(position, head_width):
    half_dim = head_width // 2
    inverse = ROPE_BASE ** (-(jnp.arange(half_dim, dtype=jnp.float32) * (2.0 / head_width)))
    angles = position.astype(jnp.float32)[:, None] * inverse[None, :]
    return (jnp.cos(angles), jnp.sin(angles))


def rotate(values, cos_tab, sin_tab, direction):
    half_dim = values.shape[-1] // 2
    first_half = values[..., :half_dim]
    second_half = values[..., half_dim:]
    cosine = cos_tab[:, None, :]
    sine_tab = direction * sin_tab[:, None, :]
    return jnp.concatenate(
        [
            first_half * cosine - second_half * sine_tab,
            second_half * cosine + first_half * sine_tab,
        ],
        axis=-1,
    )


def doc_layout(lengths_row, row_ids):
    doc_ends = jnp.cumsum(lengths_row, dtype=jnp.int32)
    document_segment = jnp.sum(
        (row_ids[:, None] >= doc_ends[None, :]).astype(jnp.int32), axis=1, dtype=jnp.int32
    )
    doc_starts = doc_ends - lengths_row
    member = document_segment[:, None] == jnp.arange(lengths_row.shape[0], dtype=jnp.int32)[None, :]
    start_of = jnp.sum(jnp.where(member, doc_starts[None, :], 0), axis=1, dtype=jnp.int32)
    return (document_segment, row_ids - start_of)


def f32(values):
    return values.astype(jnp.float32)


def low(values):
    return values.astype(LOW)


def swap(block, axis):
    return lax.ppermute(block, axis, [(0, 1), (1, 0)])


def plane_index():
    return 2 * lax.axis_index("ty") + lax.axis_index("tx")


def plane_gather(block):
    half = block.shape[0] // 2
    across_x = swap(block, "tx")
    across_y = swap(block, "ty")
    far = jnp.concatenate([swap(across_y[:half], "tx"), swap(across_x[half:], "ty")])
    return [block, across_x, across_y, far]


def plane_scatter(parts):
    own, for_x, for_y, for_far = parts
    half = own.shape[0] // 2
    pass_y = swap(for_far[:half], "tx")
    pass_x = swap(for_far[half:], "ty")
    x_top = swap(for_x[:half], "tx")
    y_end = swap(for_y[half:], "ty")
    y_top = swap(low(f32(for_y[:half]) + f32(pass_y)), "ty")
    x_end = swap(low(f32(for_x[half:]) + f32(pass_x)), "tx")
    return jnp.concatenate(
        [
            f32(own[:half]) + f32(x_top) + f32(y_top),
            f32(own[half:]) + f32(x_end) + f32(y_end),
        ]
    )


def plane_exchange(parts):
    own, for_x, for_y, for_far = parts
    half = own.shape[0] // 2
    far = jnp.concatenate(
        [
            swap(swap(for_far[:half], "tx"), "ty"),
            swap(swap(for_far[half:], "ty"), "tx"),
        ]
    )
    return [own, swap(for_x, "tx"), swap(for_y, "ty"), far]


def line_gather(block):
    extent = lax.axis_size("f")
    if extent != 4:
        return lax.all_gather(block, "f", axis=0)
    place = lax.axis_index("f")
    two_away = lax.ppermute(block, "f", [(0, 2), (2, 0), (1, 3), (3, 1)])
    above = lax.ppermute(block, "f", [(1, 0), (2, 1), (3, 2)])
    below = lax.ppermute(block, "f", [(0, 1), (1, 2), (2, 3)])
    passed = lax.ppermute(two_away, "f", [(1, 0), (2, 3)])
    blocks = [
        block,
        jnp.where(place == 3, passed, above),
        two_away,
        jnp.where(place == 0, passed, below),
    ]
    whole = jnp.zeros((4,) + block.shape, block.dtype)
    for step in range(4):
        whole = lax.dynamic_update_index_in_dim(whole, blocks[step], (place + step) % 4, 0)
    return whole


def line_scatter(parts):
    extent = lax.axis_size("f")
    if extent != 4:
        return f32(lax.psum_scatter(parts, "f", scatter_dimension=0))
    place = lax.axis_index("f")
    part = [
        lax.dynamic_index_in_dim(parts, (place + step) % 4, 0, keepdims=False) for step in range(4)
    ]
    passed = lax.ppermute(jnp.where(place == 0, part[3], part[1]), "f", [(0, 1), (3, 2)])
    above = lax.ppermute(part[3], "f", [(1, 0), (2, 1), (3, 2)])
    below = lax.ppermute(part[1], "f", [(0, 1), (1, 2), (2, 3)])
    two_away = lax.ppermute(
        low(f32(part[2]) + f32(passed)), "f", [(0, 2), (2, 0), (1, 3), (3, 1)]
    )
    return f32(part[0]) + f32(above) + f32(below) + f32(two_away)


def natural_plane(blocks, axis):
    own = plane_index()
    shape = list(blocks[0].shape)
    shape.insert(axis, 4)
    whole = jnp.zeros(shape, blocks[0].dtype)
    for step in range(4):
        whole = lax.dynamic_update_index_in_dim(whole, blocks[step], own ^ step, axis)
    return whole


def own_plane(whole, axis):
    own = plane_index()
    return [
        lax.dynamic_index_in_dim(whole, own ^ step, axis, keepdims=False) for step in range(4)
    ]


def full_gather(rows_block):
    rows, width = rows_block.shape
    line = line_gather(rows_block)
    extent = line.shape[0]
    blocks = plane_gather(line.reshape(extent * rows, width))
    whole = natural_plane([block.reshape(extent, rows, width) for block in blocks], 1)
    return whole.reshape(extent * 4 * rows, width)


def full_scatter(partial):
    extent = lax.axis_size("f")
    rows, width = partial.shape[0] // (4 * extent), partial.shape[1]
    parts = own_plane(partial.reshape(extent, 4, rows, width), 1)
    plane_sum = plane_scatter([part.reshape(extent * rows, width) for part in parts])
    return line_scatter(low(plane_sum).reshape(extent, rows, width))


def tokens_gather(block):
    near = plane_gather(block)
    return jnp.concatenate(near + [swap(piece, "tensor") for piece in near])


def tokens_scatter(partial):
    rows = partial.shape[0] // 8
    near = []
    for step in range(4):
        mine = partial[step * rows : (step + 1) * rows]
        other = partial[(4 + step) * rows : (5 + step) * rows]
        near.append(low(f32(mine) + f32(swap(other, "tensor"))))
    return plane_scatter(near)


def pair_gather(block):
    return jnp.concatenate([block, swap(block, "tensor")])


def pair_scatter(partial):
    rows = partial.shape[0] // 2
    return f32(partial[:rows]) + f32(swap(partial[rows:], "tensor"))


def total_sum(values):
    for axis in ("tensor", "tx", "ty"):
        values = values + swap(values, axis)
    if lax.axis_size("f") != 4:
        return lax.psum(values, "f")
    values = values + lax.ppermute(values, "f", [(0, 1), (1, 0), (2, 3), (3, 2)])
    return values + lax.ppermute(values, "f", [(0, 2), (2, 0), (1, 3), (3, 1)])


def shards(
    layer_input,
    attn_norm,
    head_norms,
    query_weight,
    key_matrix,
    value_matrix,
    output_weight,
    mlp_norm,
    gate_weight,
    up_weight,
    down_weight,
    grad_out,
    doc_lengths,
):
    tensor_extent = lax.axis_size("tensor")
    line_extent = lax.axis_size("f")
    core = lax.axis_index("tensor")
    q_heads = QUERY_HEADS // tensor_extent
    key_value_heads = KEY_VALUE_HEADS // tensor_extent
    group_list = QUERY_HEADS // KEY_VALUE_HEADS
    local_rows, model_width = layer_input.shape
    group_rows = local_rows * tensor_extent
    query_width = q_heads * HEAD_SIZE
    key_width = key_value_heads * HEAD_SIZE
    weight_rows = gate_weight.shape[0]
    down_rows = down_weight.shape[0]
    hidden_part = line_extent * down_rows
    score_scale = HEAD_SIZE ** (-0.5)

    qkv_all = full_gather(jnp.concatenate([query_weight, key_matrix, value_matrix], axis=1))
    out_all = full_gather(output_weight)

    def columns_of(weight):
        split = weight.reshape(weight_rows, line_extent, 4, down_rows)
        return [
            piece.reshape(weight_rows, hidden_part) for piece in own_plane(split, 2)
        ]

    gate_up_parts = [
        jnp.concatenate([gate_piece, up_piece], axis=1)
        for gate_piece, up_piece in zip(columns_of(gate_weight), columns_of(up_weight))
    ]
    gate_up_rows = natural_plane(plane_exchange(gate_up_parts), 0).reshape(
        4 * weight_rows, 2 * hidden_part
    )
    gate_up_all = line_gather(gate_up_rows).reshape(model_width, 2 * hidden_part)
    down_all = line_gather(down_weight).reshape(hidden_part, model_width)

    grad_all = tokens_gather(grad_out)

    local_ids = jnp.arange(local_rows, dtype=jnp.int32)
    row_ids = jnp.concatenate(
        [core * local_rows + local_ids, (1 - core) * local_rows + local_ids]
    )
    document_segment, position = doc_layout(doc_lengths[0], row_ids)
    cos_tab, sin_tab = rope_tables(position, HEAD_SIZE)
    allowed = (
        (document_segment[:, None] == document_segment[None, :])
        & (row_ids[None, :] <= row_ids[:, None])
    )[None, None]
    input_float = f32(layer_input)
    scale_attn = inv_rms(input_float)
    normed_attn = pair_gather(low(input_float * scale_attn * attn_norm))
    qkv_raw = matmul(normed_attn, qkv_all)
    query_raw = qkv_raw[:, :query_width]
    key_unnormed = qkv_raw[:, query_width : query_width + key_width]
    value_raw = qkv_raw[:, query_width + key_width :]
    values_reduced = low(value_raw).reshape(group_rows, key_value_heads, HEAD_SIZE)
    query_h = query_raw.reshape(group_rows, q_heads, HEAD_SIZE)
    key_per_head = key_unnormed.reshape(group_rows, key_value_heads, HEAD_SIZE)
    scale_query = inv_rms(query_h)
    scale_key = inv_rms(key_per_head)
    query_rows = low(rotate(query_h * scale_query * head_norms[0], cos_tab, sin_tab, 1.0)).reshape(
        group_rows, key_value_heads, group_list, HEAD_SIZE
    )
    keys_reduced = low(rotate(key_per_head * scale_key * head_norms[1], cos_tab, sin_tab, 1.0))
    scores = (
        jnp.einsum("qkgd,tkd->kgqt", query_rows, keys_reduced, preferred_element_type=jnp.float32)
        * score_scale
    )
    masked = jnp.where(allowed, scores, MASKED)
    row_peak = jnp.max(masked, axis=-1, keepdims=True)
    exponent = jnp.exp(masked - row_peak)
    row_total = jnp.sum(exponent, axis=-1, keepdims=True)
    probs = exponent / row_total
    probs_low = low(probs)
    attended = jnp.einsum(
        "kgqt,tkd->qkgd", probs_low, values_reduced, preferred_element_type=jnp.float32
    )
    attended_low = low(attended.reshape(group_rows, query_width))
    hidden_state = input_float + pair_scatter(low(matmul(attended_low, out_all)))

    scale_mlp = inv_rms(hidden_state)
    normed_mlp = tokens_gather(low(hidden_state * scale_mlp * mlp_norm))
    gate_raw = matmul(normed_mlp, gate_up_all[:, :hidden_part])
    up_raw = matmul(normed_mlp, gate_up_all[:, hidden_part:])
    activated = jax.nn.silu(gate_raw)
    inner_low = low(activated * up_raw)
    mlp_part = low(matmul(inner_low, down_all))
    layer_out = low(hidden_state + tokens_scatter(mlp_part))

    grad_down_part = low(matmul_tn(inner_low, grad_all))
    grad_down = line_scatter(grad_down_part.reshape(line_extent, down_rows, model_width))
    inner_grad = matmul_nt(grad_all, down_all)
    sigmoid_gate = jax.nn.sigmoid(gate_raw)
    gate_grad = low(inner_grad * up_raw * sigmoid_gate * (1.0 + gate_raw * (1.0 - sigmoid_gate)))
    up_grad = low(inner_grad * activated)
    gate_up_grad = jnp.concatenate([gate_grad, up_grad], axis=1)
    mlp_grad = low(matmul_nt(gate_up_grad, gate_up_all))
    hidden_norm_grad, mlp_gain_part = norm_back(
        hidden_state, scale_mlp, mlp_norm, tokens_scatter(mlp_grad)
    )
    grad_gate_up_part = low(matmul_tn(normed_mlp, gate_up_grad))
    grad_gate_up_rows = low(
        line_scatter(grad_gate_up_part.reshape(line_extent, 4 * weight_rows, 2 * hidden_part))
    )
    grad_pieces = natural_plane(
        plane_exchange(own_plane(grad_gate_up_rows.reshape(4, weight_rows, 2 * hidden_part), 0)),
        0,
    )
    grad_pieces = f32(grad_pieces).reshape(4, weight_rows, 2, line_extent, down_rows)
    grad_gate = grad_pieces[:, :, 0].transpose(1, 2, 0, 3).reshape(gate_weight.shape)
    grad_up = grad_pieces[:, :, 1].transpose(1, 2, 0, 3).reshape(up_weight.shape)

    hidden_grad = f32(grad_out) + hidden_norm_grad
    branch_grad = pair_gather(low(hidden_grad))
    attended_grad = low(matmul_nt(branch_grad, out_all)).reshape(
        group_rows, key_value_heads, group_list, HEAD_SIZE
    )
    grad_out_proj = full_scatter(low(matmul_tn(attended_low, branch_grad)))
    probs_grad = jnp.einsum(
        "qkgd,tkd->kgqt", attended_grad, values_reduced, preferred_element_type=jnp.float32
    )
    scores_grad = low(probs * (probs_grad - jnp.sum(probs * probs_grad, axis=-1, keepdims=True)))
    query_grad = (
        jnp.einsum(
            "kgqt,tkd->qkgd", scores_grad, keys_reduced, preferred_element_type=jnp.float32
        ).reshape(group_rows, q_heads, HEAD_SIZE)
        * score_scale
    )
    key_grad = (
        jnp.einsum("kgqt,qkgd->tkd", scores_grad, query_rows, preferred_element_type=jnp.float32)
        * score_scale
    )
    value_grad = jnp.einsum(
        "kgqt,qkgd->tkd", probs_low, attended_grad, preferred_element_type=jnp.float32
    )
    query_raw_grad, query_gain_part = norm_back(
        query_h, scale_query, head_norms[0], rotate(query_grad, cos_tab, sin_tab, -1.0)
    )
    key_raw_grad, key_gain_part = norm_back(
        key_per_head, scale_key, head_norms[1], rotate(key_grad, cos_tab, sin_tab, -1.0)
    )
    qkv_grad = jnp.concatenate(
        [
            low(query_raw_grad.reshape(group_rows, query_width)),
            low(key_raw_grad.reshape(group_rows, key_width)),
            low(value_grad.reshape(group_rows, key_width)),
        ],
        axis=1,
    )
    grad_qkv = full_scatter(low(matmul_tn(normed_attn, qkv_grad)))
    attn_grad = pair_scatter(low(matmul_nt(qkv_grad, qkv_all)))
    input_norm_grad, attn_gain_part = norm_back(input_float, scale_attn, attn_norm, attn_grad)
    grad_input = hidden_grad + input_norm_grad
    gains = total_sum(
        jnp.concatenate([attn_gain_part, mlp_gain_part, query_gain_part, key_gain_part]).reshape(
            -1, HEAD_SIZE
        )
    ).reshape(-1)
    return (
        layer_out,
        grad_input,
        gains[:model_width],
        gains[2 * model_width :].reshape(2, HEAD_SIZE),
        grad_qkv[:, :query_width],
        grad_qkv[:, query_width : query_width + key_width],
        grad_qkv[:, query_width + key_width :],
        grad_out_proj,
        gains[model_width : 2 * model_width],
        grad_gate,
        grad_up,
        grad_down,
    )


def solution(mesh):
    dp, tensor = mesh.shape["dp"], mesh.shape["tensor"]
    fine = Mesh(mesh.devices.reshape(dp // 4, 2, 2, tensor), ("f", "ty", "tx", "tensor"))
    rows = ("f", "ty", "tx")
    tokens = P(rows + ("tensor",), None)
    grid = P(rows, "tensor")
    units = P(("tensor",) + rows, None)
    return jax.shard_map(
        shards,
        mesh=fine,
        in_specs=(
            tokens, P(), P(), grid, grid, grid, units, P(), grid, grid, units, tokens, P(rows, None),
        ),
        out_specs=(tokens, tokens, P(), P(), grid, grid, grid, units, P(), grid, grid, units),
        check_vma=False,
    )
```

```python
import jax
import jax.numpy as jnp
from jax import lax
from jax.experimental import pallas as pl
from jax.experimental.pallas import tpu as pltpu
from jax.sharding import Mesh, PartitionSpec as P

QUERY_HEADS = 16
KEY_VALUE_HEADS = 8
HEAD_SIZE = 128


EPS = 1e-06
ROPE_BASE = 1000000.0
MASKED = -1e30
LOW = jnp.bfloat16


def matmul(left_mat, right_mat):
    return jnp.dot(left_mat, right_mat, preferred_element_type=jnp.float32)


def matmul_tn(left_mat, right_mat):
    return lax.dot_general(
        left_mat, right_mat, (((0,), (0,)), ((), ())), preferred_element_type=jnp.float32
    )


def matmul_nt(left_mat, right_mat):
    return lax.dot_general(
        left_mat, right_mat, (((1,), (1,)), ((), ())), preferred_element_type=jnp.float32
    )


def inv_rms(values):
    return lax.rsqrt(jnp.mean(values * values, axis=-1, keepdims=True) + EPS)


def norm_back(values, scales, gain_row, upstream):
    weighted = upstream * gain_row
    inner_mean = jnp.mean(weighted * values, axis=-1, keepdims=True)
    value_grad = scales * weighted - values * (scales * scales * scales) * inner_mean
    lead_axes = tuple(range(upstream.ndim - 1))
    return (value_grad, jnp.sum(upstream * values * scales, axis=lead_axes))


def rope_tables(position, head_width):
    half_dim = head_width // 2
    inverse = ROPE_BASE ** (-(jnp.arange(half_dim, dtype=jnp.float32) * (2.0 / head_width)))
    angles = position.astype(jnp.float32)[:, None] * inverse[None, :]
    return (jnp.cos(angles), jnp.sin(angles))


def rotate(values, cos_tab, sin_tab, direction):
    half_dim = values.shape[-1] // 2
    first_half = values[..., :half_dim]
    second_half = values[..., half_dim:]
    cosine = cos_tab[:, None, :]
    sine_tab = direction * sin_tab[:, None, :]
    return jnp.concatenate(
        [
            first_half * cosine - second_half * sine_tab,
            second_half * cosine + first_half * sine_tab,
        ],
        axis=-1,
    )


def doc_layout(lengths_row, row_ids):
    doc_ends = jnp.cumsum(lengths_row, dtype=jnp.int32)
    document_segment = jnp.sum(
        (row_ids[:, None] >= doc_ends[None, :]).astype(jnp.int32), axis=1, dtype=jnp.int32
    )
    doc_starts = doc_ends - lengths_row
    member = document_segment[:, None] == jnp.arange(lengths_row.shape[0], dtype=jnp.int32)[None, :]
    start_of = jnp.sum(jnp.where(member, doc_starts[None, :], 0), axis=1, dtype=jnp.int32)
    return (document_segment, row_ids - start_of)


def f32(values):
    return values.astype(jnp.float32)


def low(values):
    return values.astype(LOW)


def after(block, *earlier):
    return lax.optimization_barrier((block,) + earlier)[0]


def swap(block, axis):
    return lax.ppermute(block, axis, [(0, 1), (1, 0)])


def plane_index():
    return 2 * lax.axis_index("ty") + lax.axis_index("tx")


def plane_gather(block, second=()):
    half = block.shape[0] // 2
    across_x = swap(block, "tx")
    across_y = swap(block, "ty")
    top, end = after(across_y[:half], *second), after(across_x[half:], *second)
    far = jnp.concatenate([swap(top, "tx"), swap(end, "ty")])
    return [block, across_x, across_y, far]


def plane_scatter(parts, second=(), third=()):
    own, for_x, for_y, for_far = parts
    half = own.shape[0] // 2
    pass_y = swap(for_far[:half], "tx")
    pass_x = swap(for_far[half:], "ty")
    x_top = swap(for_x[:half], "tx")
    y_end = swap(for_y[half:], "ty")
    pass_y, pass_x = after(pass_y, *second), after(pass_x, *second)
    y_top = swap(low(f32(for_y[:half]) + f32(pass_y)), "ty")
    x_end = swap(low(f32(for_x[half:]) + f32(pass_x)), "tx")
    x_top, y_top = after(x_top, *third), after(y_top, *third)
    x_end, y_end = after(x_end, *third), after(y_end, *third)
    return jnp.concatenate(
        [
            f32(own[:half]) + f32(x_top) + f32(y_top),
            f32(own[half:]) + f32(x_end) + f32(y_end),
        ]
    )


def plane_exchange(parts):
    own, for_x, for_y, for_far = parts
    half = own.shape[0] // 2
    far = jnp.concatenate(
        [
            swap(swap(for_far[:half], "tx"), "ty"),
            swap(swap(for_far[half:], "ty"), "tx"),
        ]
    )
    return [own, swap(for_x, "tx"), swap(for_y, "ty"), far]


def plane_lengths(lengths):
    across_x, across_y = swap(lengths, "tx"), swap(lengths, "ty")
    return jnp.concatenate([lengths, across_x, across_y, swap(across_y, "tx")])


def line_gather(block, second=(), near=None):
    extent = lax.axis_size("f")
    if extent != 4:
        return lax.all_gather(block, "f", axis=0)
    place = lax.axis_index("f")
    two_away = lax.ppermute(block, "f", [(0, 2), (2, 0), (1, 3), (3, 1)])
    if near is None:
        above = lax.ppermute(block, "f", [(1, 0), (2, 1), (3, 2)])
        below = lax.ppermute(block, "f", [(0, 1), (1, 2), (2, 3)])
    else:
        above, below = near
    two_away = after(two_away, *second)
    passed = lax.ppermute(two_away, "f", [(1, 0), (2, 3)])
    blocks = [
        block,
        jnp.where(place == 3, passed, above),
        two_away,
        jnp.where(place == 0, passed, below),
    ]
    whole = jnp.zeros((4,) + block.shape, block.dtype)
    for step in range(4):
        whole = lax.dynamic_update_index_in_dim(whole, blocks[step], (place + step) % 4, 0)
    return whole


def line_scatter(parts, second=(), third=()):
    extent = lax.axis_size("f")
    if extent != 4:
        return f32(lax.psum_scatter(parts, "f", scatter_dimension=0))
    place = lax.axis_index("f")
    part = [
        lax.dynamic_index_in_dim(parts, (place + step) % 4, 0, keepdims=False) for step in range(4)
    ]
    passed = lax.ppermute(jnp.where(place == 0, part[3], part[1]), "f", [(0, 1), (3, 2)])
    above = lax.ppermute(part[3], "f", [(1, 0), (2, 1), (3, 2)])
    below = lax.ppermute(part[1], "f", [(0, 1), (1, 2), (2, 3)])
    passed = after(passed, *second)
    two_away = lax.ppermute(
        low(f32(part[2]) + f32(passed)), "f", [(0, 2), (2, 0), (1, 3), (3, 1)]
    )
    above, below, two_away = (after(block, *third) for block in (above, below, two_away))
    return f32(part[0]) + f32(above) + f32(below) + f32(two_away)


def natural_plane(blocks, axis):
    own = plane_index()
    shape = list(blocks[0].shape)
    shape.insert(axis, 4)
    whole = jnp.zeros(shape, blocks[0].dtype)
    for step in range(4):
        whole = lax.dynamic_update_index_in_dim(whole, blocks[step], own ^ step, axis)
    return whole


def own_plane(whole, axis):
    own = plane_index()
    return [
        lax.dynamic_index_in_dim(whole, own ^ step, axis, keepdims=False) for step in range(4)
    ]


def full_gather(rows_block):
    rows, width = rows_block.shape
    line = line_gather(rows_block)
    extent = line.shape[0]
    blocks = plane_gather(line.reshape(extent * rows, width))
    whole = natural_plane([block.reshape(extent, rows, width) for block in blocks], 1)
    return whole.reshape(extent * 4 * rows, width)


def full_scatter_plane(partial, second=(), third=()):
    extent = lax.axis_size("f")
    rows, width = partial.shape[0] // (4 * extent), partial.shape[1]
    parts = own_plane(partial.reshape(extent, 4, rows, width), 1)
    plane_sum = plane_scatter(
        [part.reshape(extent * rows, width) for part in parts], second, third
    )
    return low(plane_sum).reshape(extent, rows, width)


def tokens_gather(block, second=(), third=()):
    near = plane_gather(block, second)
    return jnp.concatenate(near + [swap(after(piece, *third), "tensor") for piece in near])


def tokens_scatter(partial, second=(), third=(), fourth=()):
    rows = partial.shape[0] // 8
    near = []
    for step in (3, 1, 2, 0):
        mine = partial[step * rows : (step + 1) * rows]
        other = swap(partial[(4 + step) * rows : (5 + step) * rows], "tensor")
        near.append(low(f32(mine) + f32(after(other, *second))))
    return plane_scatter([near[3], near[1], near[2], near[0]], third, fourth)


def pair_gather(block):
    return jnp.concatenate([block, swap(block, "tensor")])


def pair_scatter(partial):
    rows = partial.shape[0] // 2
    return f32(partial[:rows]) + f32(swap(partial[rows:], "tensor"))


def total_sum(values):
    for axis in ("tensor", "tx", "ty"):
        values = values + swap(values, axis)
    if lax.axis_size("f") != 4:
        return lax.psum(values, "f")
    values = values + lax.ppermute(values, "f", [(0, 1), (1, 0), (2, 3), (3, 2)])
    return values + lax.ppermute(values, "f", [(0, 2), (2, 0), (1, 3), (3, 1)])


class Place:
    def __init__(self):
        self.z = lax.axis_index("f")
        self.ty = lax.axis_index("ty")
        self.tx = lax.axis_index("tx")
        self.core = lax.axis_index("tensor")
        self.p = 2 * self.ty + self.tx
        self.px = 2 * self.ty + 1 - self.tx
        self.py = 2 * (1 - self.ty) + self.tx
        self.pd = 2 * (1 - self.ty) + 1 - self.tx
        self.x = {"tx": 1 - self.tx}
        self.y = {"ty": 1 - self.ty}
        self.d = {"tx": 1 - self.tx, "ty": 1 - self.ty}
        self.pair = {"tensor": 1 - self.core}
        self.up = {"f": self.z + 1}
        self.down = {"f": self.z - 1}
        self.two = {"f": (self.z + 2) % 4}

    def at(self, step):
        return (self.z + step) % 4


def remote(src, dst, send, recv, to):
    return pltpu.make_async_remote_copy(
        src_ref=src,
        dst_ref=dst,
        send_sem=send,
        recv_sem=recv,
        device_id=to,
        device_id_type=pl.DeviceIdType.MESH,
    )


def arrived(dst, recv, to):
    remote(dst, dst, recv, recv, to).wait_recv()


def greet(place, partners, line):
    barrier = pltpu.get_barrier_semaphore()
    for to in partners:
        pl.semaphore_signal(barrier, inc=1, device_id=to, device_id_type=pl.DeviceIdType.MESH)
    if not line:
        pl.semaphore_wait(barrier, len(partners))
        return

    @pl.when(place.z > 0)
    def _():
        pl.semaphore_signal(
            barrier, inc=1, device_id=place.down, device_id_type=pl.DeviceIdType.MESH
        )

    @pl.when(place.z < 3)
    def _():
        pl.semaphore_signal(barrier, inc=1, device_id=place.up, device_id_type=pl.DeviceIdType.MESH)

    pl.semaphore_signal(barrier, inc=1, device_id=place.two, device_id_type=pl.DeviceIdType.MESH)
    pl.semaphore_wait(barrier, len(partners) + 2 + (place.z + 1) // 2 % 2)


class LineGather:
    def __init__(self, place, own, slot, send, recv):
        self.place, self.own, self.slot, self.send, self.recv = place, own, slot, send, recv
        here = slot(place.z)
        self.to_down = remote(own, here, send.at[0], recv.at[1], place.down)
        self.to_up = remote(own, here, send.at[1], recv.at[3], place.up)
        self.to_two = remote(own, here, send.at[2], recv.at[2], place.two)
        two = slot(place.at(2))
        self.pass_down = remote(two, two, send.at[3], recv.at[3], place.down)
        self.pass_up = remote(two, two, send.at[3], recv.at[1], place.up)

    def start(self):
        pl.when(self.place.z > 0)(self.to_down.start)
        pl.when(self.place.z < 3)(self.to_up.start)
        self.to_two.start()

    def step(self, turn):
        if turn == 2:
            return 2
        if turn == 1:
            return jnp.where(self.place.z == 3, 3, 1)
        return jnp.where(self.place.z == 3, 1, 3)

    def wait(self, turn):
        step = self.step(turn)
        slot = self.slot(self.place.at(step))
        arrived(slot, self.recv.at[step], self.place.two)
        if turn == 2:
            pl.when(self.place.z == 1)(self.pass_down.start)
            pl.when(self.place.z == 2)(self.pass_up.start)

    def finish(self):
        pl.when(self.place.z > 0)(self.to_down.wait_send)
        pl.when(self.place.z < 3)(self.to_up.wait_send)
        self.to_two.wait_send()
        pl.when(self.place.z == 1)(self.pass_down.wait_send)
        pl.when(self.place.z == 2)(self.pass_up.wait_send)


class PlaneGather:
    def __init__(self, place, own, slot, rows, send, recv):
        half = rows // 2
        whole, top, end = pl.ds(0, rows), pl.ds(0, half), pl.ds(half, half)
        self.place, self.recv = place, recv
        self.to_x = remote(own, slot(place.p, whole), send.at[0], recv.at[0], place.x)
        self.to_y = remote(own, slot(place.p, whole), send.at[1], recv.at[1], place.y)
        self.from_x, self.from_y = slot(place.px, whole), slot(place.py, whole)
        self.far_top, self.far_end = slot(place.pd, top), slot(place.pd, end)
        pass_x, pass_y = slot(place.py, top), slot(place.px, end)
        self.pass_x = remote(pass_x, pass_x, send.at[2], recv.at[2], place.x)
        self.pass_y = remote(pass_y, pass_y, send.at[3], recv.at[3], place.y)

    def start(self):
        self.to_x.start()
        self.to_y.start()

    def forward(self):
        arrived(self.from_y, self.recv.at[1], self.place.y)
        self.pass_x.start()
        arrived(self.from_x, self.recv.at[0], self.place.x)
        self.pass_y.start()

    def wait_far(self):
        arrived(self.far_top, self.recv.at[2], self.place.x)
        arrived(self.far_end, self.recv.at[3], self.place.y)

    def finish(self):
        self.to_x.wait_send()
        self.to_y.wait_send()
        self.pass_x.wait_send()
        self.pass_y.wait_send()


ANYWHERE = pl.BlockSpec(memory_space=pl.ANY)
WHOLE = pl.BlockSpec(memory_space=pltpu.VMEM)


class Marks:
    def __init__(self, ref):
        self.ref, self.used = ref, 0

    def take(self, count=1):
        first = self.used
        self.used += count
        return self.ref.at[first] if count == 1 else self.ref.at[pl.ds(first, count)]


def each_rows(rows, chunk, work):
    def body(index, carry):
        work(pl.ds(pl.multiple_of(index * chunk, chunk), chunk))
        return carry

    lax.fori_loop(0, rows // chunk, body, 0)


class TokensGather:
    def __init__(self, place, own, whole, marks):
        half = own.shape[0] // 2
        top, end = pl.ds(0, half), pl.ds(half, half)
        self.place, self.whole = place, whole
        self.copy = pltpu.make_async_copy(own, whole.at[0], marks.take())
        self.recv = [marks.take() for _ in range(8)]
        x, y, pair = place.x, place.y, place.pair
        self.to_x = remote(own, whole.at[1], marks.take(), self.recv[0], x)
        self.to_y = remote(own, whole.at[2], marks.take(), self.recv[1], y)
        self.pass_x = remote(
            whole.at[2, top], whole.at[3, top], marks.take(), self.recv[2], x
        )
        self.pass_y = remote(
            whole.at[1, end], whole.at[3, end], marks.take(), self.recv[3], y
        )
        self.to_pair = [
            remote(
                own if step == 0 else whole.at[step],
                whole.at[4 + step],
                marks.take(),
                self.recv[4 + step],
                pair,
            )
            for step in range(4)
        ]
        self.far = (whole.at[3, top], whole.at[3, end])

    def start(self):
        self.to_x.start()
        self.to_y.start()
        self.to_pair[0].start()
        self.copy.start()

    def forward(self):
        arrived(self.whole.at[2], self.recv[1], self.place.y)
        self.pass_x.start()
        arrived(self.whole.at[1], self.recv[0], self.place.x)
        self.pass_y.start()
        self.to_pair[2].start()
        self.to_pair[1].start()

    def last(self):
        arrived(self.far[0], self.recv[2], self.place.x)
        arrived(self.far[1], self.recv[3], self.place.y)
        self.to_pair[3].start()

    def finish(self):
        for step in range(4):
            arrived(self.whole.at[4 + step], self.recv[4 + step], self.place.pair)
        for copy in [self.to_x, self.to_y, self.pass_x, self.pass_y] + self.to_pair:
            copy.wait_send()
        self.copy.wait()


class Exchange:
    def __init__(self, place, piece, slot, marks):
        self.place = place
        there = ((place.px, place.x), (place.py, place.y), (place.pd, place.d))
        self.copy = pltpu.make_async_copy(piece(place.p, 0), slot(place.p, 0), marks.take())
        self.sends, self.slots = [], []
        for index, (p, to) in enumerate(there):
            recv = marks.take()
            self.sends.append(
                remote(piece(p, index + 1), slot(place.p, index + 1), marks.take(), recv, to)
            )
            self.slots.append((slot(p, index + 1), recv, to))

    def start(self):
        for copy in (self.sends[2], self.sends[0], self.sends[1], self.copy):
            copy.start()

    def wait(self):
        self.copy.wait()
        for slot, recv, to in self.slots:
            arrived(slot, recv, to)

    def finish(self):
        for copy in self.sends:
            copy.wait_send()


class TokensScatter:
    SHAPES = 3 * 4 + 3

    @staticmethod
    def scratch(rows, width):
        return [
            pltpu.VMEM((4, rows, width), LOW),
            pltpu.VMEM((4, rows, width), LOW),
            pltpu.VMEM((4, rows, width), LOW),
            pltpu.VMEM((6, rows // 2, width), LOW),
        ]

    def __init__(self, place, parts, out, buffers, marks):
        self.place, self.parts, self.out = place, parts, out
        self.own, self.got, self.summed, self.landed = buffers
        self.rows = parts.shape[1]
        half = self.rows // 2
        top, end = pl.ds(0, half), pl.ds(half, half)
        x, y = place.x, place.y
        self.loads = [
            pltpu.make_async_copy(parts.at[step], self.own.at[step], marks.take())
            for step in range(4)
        ]
        self.recv_pair = [marks.take() for _ in range(4)]
        self.to_pair = [
            remote(
                parts.at[4 + step], self.got.at[step], marks.take(), self.recv_pair[step], place.pair
            )
            for step in range(4)
        ]
        self.recv = [marks.take() for _ in range(6)]
        routes = (
            (self.summed.at[3, top], x),
            (self.summed.at[3, end], y),
            (self.summed.at[1, top], x),
            (self.summed.at[1, end], x),
            (self.summed.at[2, top], y),
            (self.summed.at[2, end], y),
        )
        self.sends = [
            remote(src, self.landed.at[index], marks.take(), self.recv[index], to)
            for index, (src, to) in enumerate(routes)
        ]

    def start(self):
        for step in (3, 1, 2, 0):
            self.to_pair[step].start()
            self.loads[step].start()

    def joined(self, step):
        self.loads[step].wait()
        arrived(self.got.at[step], self.recv_pair[step], self.place.pair)
        if step == 0:
            return

        def work(rows):
            self.summed[step, rows] = low(f32(self.own[step, rows]) + f32(self.got[step, rows]))

        each_rows(self.rows, 16, work)

    def landed_at(self, index, to):
        arrived(self.landed.at[index], self.recv[index], to)

    def run(self):
        half = self.rows // 2
        place = self.place
        self.joined(3)
        self.sends[0].start()
        self.sends[1].start()
        self.joined(1)
        self.sends[2].start()
        self.joined(2)
        self.sends[5].start()
        self.landed_at(0, place.x)

        def top_work(rows):
            self.summed[2, rows] = low(f32(self.summed[2, rows]) + f32(self.landed[0, rows]))

        each_rows(half, 16, top_work)
        self.sends[4].start()
        self.landed_at(1, place.y)

        def end_work(rows):
            low_rows = pl.ds(pl.multiple_of(rows.start + half, 16), rows.size)
            self.summed[1, low_rows] = low(
                f32(self.summed[1, low_rows]) + f32(self.landed[1, rows])
            )

        each_rows(half, 16, end_work)
        self.sends[3].start()
        self.joined(0)

    def finish(self):
        half = self.rows // 2
        for index, to in ((2, self.place.x), (5, self.place.y), (4, self.place.y), (3, self.place.x)):
            self.landed_at(index, to)

        for base, first, second in ((0, 2, 4), (half, 3, 5)):

            def work(rows):
                own_rows = pl.ds(pl.multiple_of(rows.start + base, 16), rows.size)
                self.out[own_rows] = (
                    f32(self.own[0, own_rows])
                    + f32(self.got[0, own_rows])
                    + f32(self.landed[first, rows])
                    + f32(self.landed[second, rows])
                )

            each_rows(half, 16, work)
        for copy in self.to_pair + self.sends:
            copy.wait_send()


class LineScatter:
    @staticmethod
    def scratch(rows, width):
        return [pltpu.VMEM((6, rows, width), LOW)]

    def __init__(self, place, parts, out, buffers, marks):
        self.place, self.parts, self.out = place, parts, out
        self.kept = buffers[0]
        self.rows = parts.shape[1]
        self.passed, self.above, self.below, self.two, self.mid, self.own = (
            self.kept.at[index] for index in range(6)
        )
        self.recv = [marks.take() for _ in range(4)]
        z = place.z
        self.pass_up = remote(parts.at[3], self.passed, marks.take(), self.recv[0], place.up)
        self.pass_down = remote(parts.at[0], self.passed, marks.take(), self.recv[0], place.down)
        self.to_down = remote(
            parts.at[place.at(3)], self.above, marks.take(), self.recv[1], place.down
        )
        self.to_up = remote(parts.at[place.at(1)], self.below, marks.take(), self.recv[2], place.up)
        self.to_two = remote(self.mid, self.two, marks.take(), self.recv[3], place.two)
        self.load_mid = pltpu.make_async_copy(parts.at[place.at(2)], self.mid, marks.take())
        self.load_own = pltpu.make_async_copy(parts.at[z], self.own, marks.take())

    def start(self):
        z = self.place.z
        pl.when(z == 0)(self.pass_up.start)
        pl.when(z == 3)(self.pass_down.start)
        self.load_mid.start()
        pl.when(z > 0)(self.to_down.start)
        pl.when(z < 3)(self.to_up.start)
        self.load_own.start()
        self.load_mid.wait()
        pl.when((z == 0) | (z == 3))(self.to_two.start)

    def middle(self):
        z = self.place.z

        @pl.when((z == 1) | (z == 2))
        def _():
            arrived(self.passed, self.recv[0], self.place.two)

            def work(rows):
                self.kept[4, rows] = low(f32(self.kept[4, rows]) + f32(self.kept[0, rows]))

            each_rows(self.rows, 16, work)
            self.to_two.start()

    def finish(self):
        z, rows_all = self.place.z, self.rows
        out, kept = self.out, self.kept
        self.load_own.wait()

        @pl.when(z < 3)
        def _():
            arrived(self.above, self.recv[1], self.place.two)

            def work(rows):
                kept[5, rows] = low(f32(kept[5, rows]) + f32(kept[1, rows]))

            each_rows(rows_all, 16, work)

        @pl.when(z > 0)
        def _():
            arrived(self.below, self.recv[2], self.place.two)

            def work(rows):
                kept[5, rows] = low(f32(kept[5, rows]) + f32(kept[2, rows]))

            each_rows(rows_all, 16, work)

        arrived(self.two, self.recv[3], self.place.two)

        def work(rows):
            out[rows] = low(f32(kept[5, rows]) + f32(kept[3, rows]))

        each_rows(rows_all, 16, work)

    def drain(self):
        z = self.place.z
        pl.when(z == 0)(self.pass_up.wait_send)
        pl.when(z == 3)(self.pass_down.wait_send)
        pl.when(z > 0)(self.to_down.wait_send)
        pl.when(z < 3)(self.to_up.wait_send)
        self.to_two.wait_send()


def comm_params(number):
    return pltpu.CompilerParams(
        collective_id=number, has_side_effects=True, vmem_limit_bytes=56 * 1024 * 1024
    )


def comm_cost(micros):
    return pl.CostEstimate(flops=0, bytes_accessed=micros * 3_000_000, transcendentals=0)


def first_kernel(
    rows_ref,
    qkv_ref,
    out_ref,
    gate_ref,
    up_ref,
    down_ref,
    rows_all,
    qkv_all,
    out_all,
    gate_rows,
    up_rows,
    above_ref,
    below_ref,
    marks_ref,
):
    place = Place()
    marks = Marks(marks_ref)
    greet(place, [place.x, place.y, place.d, place.pair], True)
    qkv_pieces = Exchange(
        place, lambda p, step: qkv_ref.at[p], lambda p, step: qkv_all.at[place.z, p], marks
    )
    gate_pieces = Exchange(
        place, lambda p, step: gate_ref.at[p], lambda p, step: gate_rows.at[p], marks
    )
    up_pieces = Exchange(place, lambda p, step: up_ref.at[p], lambda p, step: up_rows.at[p], marks)
    tokens = TokensGather(place, rows_ref, rows_all, marks)
    qkv_line = LineGather(
        place,
        qkv_all.at[place.z],
        lambda z: qkv_all.at[z],
        marks.take(4),
        marks.take(4),
    )
    out_line = LineGather(
        place, out_ref, lambda z: out_all.at[z, place.p], marks.take(4), marks.take(4)
    )
    out_copy = pltpu.make_async_copy(out_ref, out_all.at[place.z, place.p], marks.take())
    near_recv = [marks.take(), marks.take()]
    to_down = remote(down_ref, above_ref, marks.take(), near_recv[0], place.down)
    to_up = remote(down_ref, below_ref, marks.take(), near_recv[1], place.up)
    out_planes = []
    for turn in range(4):
        z = place.z if turn == 0 else place.at(out_line.step(turn))
        out_planes.append(
            PlaneGather(
                place,
                out_ref if turn == 0 else out_all.at[z, place.p],
                lambda p, rows, z=z: out_all.at[z, p, rows],
                out_ref.shape[0],
                marks.take(4),
                marks.take(4),
            )
        )

    qkv_pieces.start()
    tokens.start()
    out_copy.start()
    qkv_pieces.wait()
    qkv_line.start()
    tokens.forward()
    out_planes[0].start()
    qkv_line.wait(1)
    out_line.start()
    qkv_line.wait(2)
    tokens.last()
    out_planes[0].forward()
    gate_pieces.start()
    out_line.wait(1)
    out_planes[1].start()
    out_line.wait(2)
    out_planes[2].start()
    qkv_line.wait(3)
    out_line.wait(3)
    out_planes[3].start()
    pl.when(place.z > 0)(to_down.start)
    pl.when(place.z < 3)(to_up.start)
    up_pieces.start()
    out_planes[1].forward()
    out_planes[2].forward()
    out_planes[3].forward()
    gate_pieces.wait()
    up_pieces.wait()
    for plane in out_planes:
        plane.wait_far()
    tokens.finish()
    for part in [qkv_pieces, gate_pieces, up_pieces, qkv_line, out_line] + out_planes:
        part.finish()
    out_copy.wait()

    @pl.when(place.z < 3)
    def _():
        arrived(above_ref, near_recv[0], place.two)
        to_up.wait_send()

    @pl.when(place.z > 0)
    def _():
        arrived(below_ref, near_recv[1], place.two)
        to_down.wait_send()


def first_gather(rows, qkv_pieces, output_weight, gate_pieces, up_pieces, down_weight):
    return pl.pallas_call(
        first_kernel,
        out_shape=(
            jax.ShapeDtypeStruct((8,) + rows.shape, LOW),
            jax.ShapeDtypeStruct((4,) + qkv_pieces.shape, LOW),
            jax.ShapeDtypeStruct((4, 4) + output_weight.shape, LOW),
            jax.ShapeDtypeStruct(gate_pieces.shape, LOW),
            jax.ShapeDtypeStruct(up_pieces.shape, LOW),
            jax.ShapeDtypeStruct(down_weight.shape, LOW),
            jax.ShapeDtypeStruct(down_weight.shape, LOW),
        ),
        in_specs=[ANYWHERE] * 6,
        out_specs=(ANYWHERE,) * 7,
        scratch_shapes=[pltpu.SemaphoreType.DMA((100,))],
        compiler_params=comm_params(0),
        cost_estimate=comm_cost(80),
    )(rows, qkv_pieces, output_weight, gate_pieces, up_pieces, down_weight)


def rows_kernel(rows_ref, line_ref, rows_all, line_all, marks_ref):
    place = Place()
    marks = Marks(marks_ref)
    greet(place, [place.x, place.y, place.pair], True)
    tokens = TokensGather(place, rows_ref, rows_all, marks)
    line = LineGather(place, line_ref, lambda z: line_all.at[z], marks.take(4), marks.take(4))
    copy = pltpu.make_async_copy(line_ref, line_all.at[place.z], marks.take())
    tokens.start()
    line.start()
    copy.start()
    tokens.forward()
    line.wait(2)
    tokens.last()
    line.wait(1)
    line.wait(3)
    tokens.finish()
    line.finish()
    copy.wait()


def rows_gather(rows, line_block):
    return pl.pallas_call(
        rows_kernel,
        out_shape=(
            jax.ShapeDtypeStruct((8,) + rows.shape, LOW),
            jax.ShapeDtypeStruct((4,) + line_block.shape, LOW),
        ),
        in_specs=[ANYWHERE] * 2,
        out_specs=(ANYWHERE,) * 2,
        scratch_shapes=[pltpu.SemaphoreType.DMA((40,))],
        compiler_params=comm_params(1),
        cost_estimate=comm_cost(50),
    )(rows, line_block)


def heads_out_kernel(heads_ref, own_ref, marks_ref):
    place = Place()
    greet(place, [place.x, place.y, place.d], False)
    exchange = Exchange(
        place,
        lambda p, step: heads_ref.at[:, step],
        lambda p, step: own_ref.at[p],
        Marks(marks_ref),
    )
    exchange.start()
    exchange.wait()
    exchange.finish()


def heads_to_tokens(heads):
    cores, _, rows, width = heads.shape
    return pl.pallas_call(
        heads_out_kernel,
        out_shape=jax.ShapeDtypeStruct((4, cores, rows, width), LOW),
        in_specs=[ANYWHERE],
        out_specs=ANYWHERE,
        scratch_shapes=[pltpu.SemaphoreType.DMA((8,))],
        compiler_params=comm_params(2),
        cost_estimate=comm_cost(15),
    )(heads)


def heads_in_kernel(own_ref, heads_ref, marks_ref):
    place = Place()
    greet(place, [place.x, place.y, place.d], False)
    width = heads_ref.shape[2]
    exchange = Exchange(
        place,
        lambda p, step: own_ref.at[:, pl.ds(pl.multiple_of(p * width, width), width)],
        lambda p, step: heads_ref.at[step],
        Marks(marks_ref),
    )
    exchange.start()
    exchange.wait()
    exchange.finish()


def tokens_to_heads(own):
    rows, width = own.shape
    return pl.pallas_call(
        heads_in_kernel,
        out_shape=jax.ShapeDtypeStruct((4, rows, width // 4), LOW),
        in_specs=[ANYWHERE],
        out_specs=ANYWHERE,
        scratch_shapes=[pltpu.SemaphoreType.DMA((8,))],
        compiler_params=comm_params(3),
        cost_estimate=comm_cost(15),
    )(own)


def sums_kernel(parts_ref, line_ref, out_ref, columns_ref, marks_ref, line_sum, *buffers):
    place = Place()
    marks = Marks(marks_ref)
    greet(place, [place.x, place.y, place.d, place.pair], True)
    tokens = TokensScatter(place, parts_ref, out_ref, buffers[:4], marks)
    line = LineScatter(place, line_ref, line_sum, buffers[4:], marks)
    rows = line_sum.shape[0] // 4
    pieces = Exchange(
        place,
        lambda p, step: line_sum.at[pl.ds(pl.multiple_of(p * rows, rows), rows)],
        lambda p, step: columns_ref.at[p],
        marks,
    )
    tokens.start()
    line.start()
    line.middle()
    tokens.run()
    line.finish()
    pieces.start()
    tokens.finish()
    line.drain()
    pieces.wait()
    pieces.finish()


def sums_scatter(parts, line_parts):
    rows, width = parts.shape[1:]
    line_rows, line_width = line_parts.shape[1:]
    return pl.pallas_call(
        sums_kernel,
        out_shape=(
            jax.ShapeDtypeStruct((rows, width), jnp.float32),
            jax.ShapeDtypeStruct((4, line_rows // 4, line_width), LOW),
        ),
        in_specs=[ANYWHERE] * 2,
        out_specs=(WHOLE, ANYWHERE),
        scratch_shapes=[
            pltpu.SemaphoreType.DMA((64,)),
            pltpu.VMEM((line_rows, line_width), LOW),
        ]
        + TokensScatter.scratch(rows, width)
        + LineScatter.scratch(line_rows, line_width),
        compiler_params=comm_params(4),
        cost_estimate=comm_cost(55),
    )(parts, line_parts)


def last_kernel(
    parts_ref,
    qkv_ref,
    proj_ref,
    gate_ref,
    input_ref,
    hidden_ref,
    norm_ref,
    gains_ref,
    grad_ref,
    qkv_columns,
    proj_out,
    gate_columns,
    gains_out,
    marks_ref,
    qkv_sum,
    row_sum,
    gain_rows,
    gain_mine,
    gain_got,
    *buffers,
):
    place = Place()
    marks = Marks(marks_ref)
    greet(place, [place.x, place.y, place.d, place.pair], True)
    tokens = TokensScatter(place, parts_ref, row_sum, buffers[:4], marks)
    qkv_line = LineScatter(place, qkv_ref, qkv_sum, buffers[4:5], marks)
    proj_line = LineScatter(place, proj_ref, proj_out, buffers[5:], marks)
    rows = qkv_sum.shape[0] // 4
    qkv_pieces = Exchange(
        place,
        lambda p, step: qkv_sum.at[pl.ds(pl.multiple_of(p * rows, rows), rows)],
        lambda p, step: qkv_columns.at[p],
        marks,
    )
    gate_pieces = Exchange(
        place, lambda p, step: gate_ref.at[p], lambda p, step: gate_columns.at[p], marks
    )
    near_z = {"f": place.z + 1 - 2 * (place.z % 2)}
    rounds = [
        remote(gain_mine.at[index], gain_got.at[index], marks.take(), marks.take(), to)
        for index, to in enumerate((place.pair, place.x, place.y, near_z, place.two))
    ]

    tokens.start()
    qkv_line.start()
    qkv_line.middle()
    proj_line.start()
    tokens.run()
    proj_line.middle()
    gate_pieces.start()
    qkv_line.finish()
    qkv_pieces.start()
    tokens.finish()

    gain_rows[...] = jnp.zeros_like(gain_rows)
    norm_row = norm_ref[...]

    def work(rows):
        values = f32(input_ref[rows])
        scales = inv_rms(values)
        upstream = row_sum[rows]
        weighted = upstream * norm_row
        inner_mean = jnp.mean(weighted * values, axis=-1, keepdims=True)
        grad_ref[rows] = (
            hidden_ref[rows]
            + scales * weighted
            - values * (scales * scales * scales) * inner_mean
        )
        parts = upstream * values * scales
        gain_rows[...] += parts[:8] + parts[8:]

    each_rows(row_sum.shape[0], 16, work)
    width = norm_row.shape[1]
    gain_mine[0, :, pl.ds(0, width)] = jnp.sum(gain_rows[...], axis=0, keepdims=True)
    gain_mine[0, :, pl.ds(width, gains_ref.shape[1])] = gains_ref[...]
    for index, copy in enumerate(rounds):
        copy.start()
        copy.wait()
        summed = gain_mine[index] + gain_got[index]
        if index < 4:
            gain_mine[index + 1] = summed
        else:
            gains_out[...] = summed
    proj_line.finish()
    qkv_line.drain()
    proj_line.drain()
    qkv_pieces.wait()
    qkv_pieces.finish()
    gate_pieces.wait()
    gate_pieces.finish()


def last_sums(parts, qkv_parts, proj_parts, gate_rows, layer_input, hidden_grad, norm, gains):
    rows, width = parts.shape[1:]
    qkv_rows, qkv_width = qkv_parts.shape[1:]
    gain_width = width + gains.shape[1]
    return pl.pallas_call(
        last_kernel,
        out_shape=(
            jax.ShapeDtypeStruct((rows, width), jnp.float32),
            jax.ShapeDtypeStruct((4, qkv_rows // 4, qkv_width), LOW),
            jax.ShapeDtypeStruct(proj_parts.shape[1:], LOW),
            jax.ShapeDtypeStruct(gate_rows.shape, LOW),
            jax.ShapeDtypeStruct((1, gain_width), jnp.float32),
        ),
        in_specs=[ANYWHERE] * 4 + [WHOLE] * 4,
        out_specs=(WHOLE, ANYWHERE, WHOLE, ANYWHERE, WHOLE),
        scratch_shapes=[
            pltpu.SemaphoreType.DMA((90,)),
            pltpu.VMEM((qkv_rows, qkv_width), LOW),
            pltpu.VMEM((rows, width), jnp.float32),
            pltpu.VMEM((8, width), jnp.float32),
            pltpu.VMEM((5, 1, gain_width), jnp.float32),
            pltpu.VMEM((5, 1, gain_width), jnp.float32),
        ]
        + TokensScatter.scratch(rows, width)
        + LineScatter.scratch(qkv_rows, qkv_width)
        + LineScatter.scratch(*proj_parts.shape[1:]),
        compiler_params=comm_params(5),
        cost_estimate=comm_cost(60),
    )(parts, qkv_parts, proj_parts, gate_rows, layer_input, hidden_grad, norm, gains)


def turn_pairs(values, cosine, sine):
    return values * cosine + pltpu.roll(values, HEAD_SIZE // 2, 1) * sine


def softmax_of(query, key, allowed):
    scores = matmul_nt(query, key) * HEAD_SIZE ** (-0.5)
    masked = jnp.where(allowed, scores, MASKED)
    exponent = jnp.exp(masked - jnp.max(masked, axis=-1, keepdims=True))
    return exponent / jnp.sum(exponent, axis=-1, keepdims=True)


def allowed_of(segment_col, segment_row, id_col, id_row):
    return (segment_col[0] == segment_row[0]) & (id_row[...] <= id_col[...])


def attend_kernel(
    raw_ref, cos_ref, sin_ref, segment_col, segment_row, id_col, id_row, gains_ref, low_ref, out_ref
):
    group_rows = cos_ref.shape[1]
    raw = raw_ref[...].reshape(group_rows, raw_ref.shape[3])
    heads = raw.shape[1] // HEAD_SIZE - 2
    cosine, sine = cos_ref[0], sin_ref[0]
    allowed = allowed_of(segment_col, segment_row, id_col, id_row)
    columns = [raw[:, head * HEAD_SIZE : (head + 1) * HEAD_SIZE] for head in range(heads + 2)]
    turned = []
    for head in range(heads + 1):
        gain = gains_ref[min(head // heads, 1)][None, :]
        turned.append(
            low(turn_pairs(columns[head] * inv_rms(columns[head]) * gain, cosine, sine))
        )
    value = low(columns[heads + 1])
    attended = [
        low(matmul(low(softmax_of(turned[head], turned[heads], allowed)), value))
        for head in range(heads)
    ]
    low_ref[...] = jnp.concatenate(turned + [value], axis=1).reshape(low_ref.shape)
    out_ref[...] = jnp.concatenate(attended, axis=1).reshape(out_ref.shape)


def attend_back_kernel(
    raw_ref,
    low_ref,
    grad_ref,
    cos_ref,
    sin_ref,
    segment_col,
    segment_row,
    id_col,
    id_row,
    gains_ref,
    out_ref,
    gain_out,
):
    group_rows = cos_ref.shape[1]
    raw = raw_ref[...].reshape(group_rows, raw_ref.shape[3])
    kept = low_ref[...].reshape(raw.shape)
    heads = raw.shape[1] // HEAD_SIZE - 2
    cosine, sine = cos_ref[0], sin_ref[0]
    allowed = allowed_of(segment_col, segment_row, id_col, id_row)
    lane = lambda values, head: values[:, head * HEAD_SIZE : (head + 1) * HEAD_SIZE]
    key, value = lane(kept, heads), lane(kept, heads + 1)
    scale = HEAD_SIZE ** (-0.5)
    turned_grads = []
    key_grad = jnp.zeros((group_rows, HEAD_SIZE), jnp.float32)
    value_grad = jnp.zeros((group_rows, HEAD_SIZE), jnp.float32)
    for head in range(heads):
        query, upstream = lane(kept, head), lane(grad_ref[0], head)
        probs = softmax_of(query, key, allowed)
        probs_grad = matmul_nt(upstream, value)
        scores_grad = low(
            probs * (probs_grad - jnp.sum(probs * probs_grad, axis=-1, keepdims=True))
        )
        turned_grads.append(matmul(scores_grad, key) * scale)
        key_grad = key_grad + matmul_tn(scores_grad, query)
        value_grad = value_grad + matmul_tn(low(probs), upstream)
    turned_grads.append(key_grad * scale)
    outs, gains = [], []
    for head in range(heads + 1):
        gain = gains_ref[min(head // heads, 1)][None, :]
        unnormed = lane(raw, head)
        upstream = turn_pairs(turned_grads[head], cosine, -sine)
        grad, gain_part = norm_back(unnormed, inv_rms(unnormed), gain, upstream)
        outs.append(low(grad))
        gains.append(gain_part[None, :])
    outs.append(low(value_grad))
    out_ref[...] = jnp.concatenate(outs, axis=1).reshape(out_ref.shape)
    query_gain = sum(gains[1:heads], gains[0])
    gain_out[0] = jnp.concatenate(
        [query_gain, gains[heads], jnp.zeros((6, HEAD_SIZE), jnp.float32)], axis=0
    )


def attention_specs(group_rows, rows):
    bucket = lambda width: pl.BlockSpec((2, 1, rows, width), lambda step: (0, step, 0, 0))
    tables = [
        pl.BlockSpec((1, group_rows, HEAD_SIZE), lambda step: (step, 0, 0)),
        pl.BlockSpec((1, group_rows, HEAD_SIZE), lambda step: (step, 0, 0)),
        pl.BlockSpec((1, group_rows, 1), lambda step: (step, 0, 0)),
        pl.BlockSpec((1, 1, group_rows), lambda step: (step, 0, 0)),
        pl.BlockSpec((group_rows, 1), lambda step: (0, 0)),
        pl.BlockSpec((1, group_rows), lambda step: (0, 0)),
        pl.BlockSpec((2, HEAD_SIZE), lambda step: (0, 0)),
    ]
    return bucket, tables


def attend(raw, tables):
    _, buckets, rows, width = raw.shape
    bucket, table_specs = attention_specs(2 * rows, rows)
    query_width = width - 2 * HEAD_SIZE
    return pl.pallas_call(
        attend_kernel,
        grid=(buckets,),
        out_shape=(
            jax.ShapeDtypeStruct(raw.shape, LOW),
            jax.ShapeDtypeStruct((2, buckets, rows, query_width), LOW),
        ),
        in_specs=[bucket(width)] + table_specs,
        out_specs=(bucket(width), bucket(query_width)),
        compiler_params=pltpu.CompilerParams(vmem_limit_bytes=48 * 1024 * 1024),
        cost_estimate=pl.CostEstimate(
            flops=30_000_000_000, bytes_accessed=20_000_000, transcendentals=0
        ),
    )(raw, *tables)


def attend_back(raw, kept, upstream, tables):
    _, buckets, rows, width = raw.shape
    bucket, table_specs = attention_specs(2 * rows, rows)
    return pl.pallas_call(
        attend_back_kernel,
        grid=(buckets,),
        out_shape=(
            jax.ShapeDtypeStruct(raw.shape, LOW),
            jax.ShapeDtypeStruct((buckets, 8, HEAD_SIZE), jnp.float32),
        ),
        in_specs=[
            bucket(width),
            bucket(width),
            pl.BlockSpec((1,) + upstream.shape[1:], lambda step: (step, 0, 0)),
        ]
        + table_specs,
        out_specs=(
            bucket(width),
            pl.BlockSpec((1, 8, HEAD_SIZE), lambda step: (step, 0, 0)),
        ),
        compiler_params=pltpu.CompilerParams(vmem_limit_bytes=48 * 1024 * 1024),
        cost_estimate=pl.CostEstimate(
            flops=40_000_000_000, bytes_accessed=20_000_000, transcendentals=0
        ),
    )(raw, kept, upstream, *tables)


def shards(
    layer_input,
    attn_norm,
    head_norms,
    query_weight,
    key_matrix,
    value_matrix,
    output_weight,
    mlp_norm,
    gate_weight,
    up_weight,
    down_weight,
    grad_out,
    doc_lengths,
):
    line_extent = lax.axis_size("f")
    on_line = line_extent == 4
    core = lax.axis_index("tensor")
    local_rows, model_width = layer_input.shape
    group_rows = 2 * local_rows
    all_rows = 8 * local_rows
    weight_rows = gate_weight.shape[0]
    down_rows = down_weight.shape[0]
    hidden_part = line_extent * down_rows
    query_part = query_weight.shape[1] // 4
    head_part = query_part + 2 * HEAD_SIZE

    def heads_of(weight):
        return weight.reshape(weight_rows, 4, -1).transpose(1, 0, 2)

    def units_of(weight):
        split = weight.reshape(weight_rows, line_extent, 4, down_rows)
        return split.transpose(2, 0, 1, 3).reshape(4, weight_rows, hidden_part)

    qkv_pieces = jnp.concatenate(
        [heads_of(query_weight), heads_of(key_matrix), heads_of(value_matrix)], axis=2
    )
    gate_pieces, up_pieces = units_of(gate_weight), units_of(up_weight)

    input_float = f32(layer_input)
    scale_attn = inv_rms(input_float)
    normed_own = low(input_float * scale_attn * attn_norm)
    if on_line:
        normed_attn, qkv_all, out_all, gate_rows, up_rows, *near_down = first_gather(
            normed_own, qkv_pieces, output_weight, gate_pieces, up_pieces, down_weight
        )
    else:
        normed_attn = tokens_gather(normed_own)
        exchanged = lambda pieces: natural_plane(plane_exchange(own_plane(pieces, 0)), 0)
        qkv_all = line_gather(exchanged(qkv_pieces))
        out_all = full_gather(output_weight)
        gate_rows, up_rows = exchanged(gate_pieces), exchanged(up_pieces)
        near_down = None
    normed_attn = normed_attn.reshape(all_rows, model_width)
    qkv_all = qkv_all.reshape(model_width, head_part)
    out_all = out_all.reshape(-1, model_width)
    gate_rows = gate_rows.reshape(4 * weight_rows, hidden_part)
    up_rows = up_rows.reshape(4 * weight_rows, hidden_part)

    lengths_list = plane_lengths(doc_lengths)
    local_ids = jnp.arange(local_rows, dtype=jnp.int32)
    row_ids = jnp.concatenate([core * local_rows + local_ids, (1 - core) * local_rows + local_ids])
    segments, positions = jax.vmap(lambda lengths: doc_layout(lengths, row_ids))(lengths_list)
    cos_tab, sin_tab = rope_tables(positions.reshape(-1), HEAD_SIZE)
    tables = (
        jnp.concatenate([cos_tab, cos_tab], axis=1).reshape(4, group_rows, HEAD_SIZE),
        jnp.concatenate([-sin_tab, sin_tab], axis=1).reshape(4, group_rows, HEAD_SIZE),
        segments[:, :, None],
        segments[:, None, :],
        row_ids[:, None],
        row_ids[None, :],
        head_norms,
    )
    qkv_raw = matmul(normed_attn, qkv_all).reshape(2, 4, local_rows, head_part)
    qkv_low, attended_heads = attend(qkv_raw, tables)
    gate_all = line_gather(gate_rows, (attended_heads,)).reshape(model_width, hidden_part)
    if on_line:
        attended = heads_to_tokens(attended_heads)
    else:
        attended = natural_plane(
            plane_exchange([attended_heads[:, step].reshape(group_rows, -1) for step in range(4)]),
            0,
        )
    attended = (
        attended.reshape(4, group_rows, query_part)
        .transpose(1, 0, 2)
        .reshape(group_rows, 4 * query_part)
    )
    hidden_state = input_float + pair_scatter(low(matmul(attended, out_all)))

    scale_mlp = inv_rms(hidden_state)
    normed_own = low(hidden_state * scale_mlp * mlp_norm)
    if on_line:
        normed_mlp, up_all = rows_gather(normed_own, up_rows)
    else:
        normed_mlp, up_all = tokens_gather(normed_own), line_gather(up_rows)
    normed_mlp = normed_mlp.reshape(all_rows, model_width)
    up_all = up_all.reshape(model_width, hidden_part)
    grad_all = tokens_gather(after(grad_out, normed_attn), (attended_heads,), (normed_mlp,))
    gate_raw = matmul(normed_mlp, gate_all)
    down_all = line_gather(after(down_weight, normed_mlp), (gate_raw,), near_down).reshape(
        hidden_part, model_width
    )
    up_raw = matmul(normed_mlp, up_all)
    activated = jax.nn.silu(gate_raw)
    inner_low = low(activated * up_raw)
    grad_down_part = low(matmul_tn(inner_low, grad_all))
    mlp_part = low(matmul(inner_low, down_all))
    inner_grad = matmul_nt(grad_all, down_all)
    sigmoid_gate = jax.nn.sigmoid(gate_raw)
    gate_grad = low(inner_grad * up_raw * sigmoid_gate * (1.0 + gate_raw * (1.0 - sigmoid_gate)))
    up_grad = low(inner_grad * activated)
    line_shape = (line_extent, 4 * weight_rows, hidden_part)
    grad_gate_part = low(matmul_tn(normed_mlp, gate_grad)).reshape(line_shape)
    grad_up_part = low(matmul_tn(normed_mlp, up_grad)).reshape(line_shape)
    mlp_grad = low(matmul_nt(gate_grad, gate_all) + matmul_nt(up_grad, up_all))
    if on_line:
        mlp_row_grad, grad_up_columns = sums_scatter(
            mlp_grad.reshape(8, local_rows, model_width), grad_up_part
        )
    else:
        mlp_row_grad = tokens_scatter(mlp_grad)
        grad_up_columns = exchanged(
            low(line_scatter(grad_up_part)).reshape(4, weight_rows, hidden_part)
        )
    hidden_norm_grad, mlp_gain_part = norm_back(hidden_state, scale_mlp, mlp_norm, mlp_row_grad)

    grad_down = line_scatter(
        grad_down_part.reshape(line_extent, down_rows, model_width), (up_grad,), (mlp_row_grad,)
    )
    mlp_rows = tokens_scatter(mlp_part, (up_grad,), (grad_up_part,), (mlp_row_grad,))
    layer_out = low(hidden_state + mlp_rows)

    hidden_grad = f32(grad_out) + hidden_norm_grad
    branch_grad = pair_gather(low(hidden_grad))
    attended_grad = low(matmul_nt(branch_grad, out_all))
    if on_line:
        heads_grad = tokens_to_heads(attended_grad)
    else:
        split = attended_grad.reshape(group_rows, 4, query_part).transpose(1, 0, 2)
        heads_grad = jnp.stack(plane_exchange(own_plane(split, 0)))
    qkv_grad, gain_parts = attend_back(qkv_raw, qkv_low, heads_grad, tables)
    qkv_grad = qkv_grad.reshape(all_rows, head_part)
    grad_qkv_part = low(matmul_tn(normed_attn, qkv_grad)).reshape(
        line_extent, 4 * weight_rows, head_part
    )
    attn_grad = low(matmul_nt(qkv_grad, qkv_all))
    grad_gate_rows = low(
        line_scatter(after(grad_gate_part, mlp_row_grad), (heads_grad,), (qkv_grad,))
    ).reshape(4, weight_rows, hidden_part)
    grad_proj_part = full_scatter_plane(
        low(matmul_tn(attended, branch_grad)), (heads_grad,), (qkv_grad,)
    )
    head_gains = jnp.sum(gain_parts, axis=0)[:2].reshape(-1)
    other_gains = jnp.concatenate([mlp_gain_part, head_gains])
    if on_line:
        grad_input, grad_qkv_columns, grad_out_proj, grad_gate_columns, gains = last_sums(
            attn_grad.reshape(8, local_rows, model_width),
            grad_qkv_part,
            grad_proj_part,
            grad_gate_rows,
            layer_input,
            hidden_grad,
            attn_norm[None],
            other_gains[None],
        )
        gains = gains.reshape(-1)
        grad_out_proj = f32(grad_out_proj)
    else:
        attn_row_grad = tokens_scatter(attn_grad)
        grad_qkv_columns = exchanged(
            low(line_scatter(grad_qkv_part)).reshape(4, weight_rows, head_part)
        )
        grad_gate_columns = exchanged(grad_gate_rows)
        grad_out_proj = line_scatter(grad_proj_part)
        input_norm_grad, attn_gain_part = norm_back(
            input_float, scale_attn, attn_norm, attn_row_grad
        )
        grad_input = hidden_grad + input_norm_grad
        gains = total_sum(
            jnp.concatenate([attn_gain_part, other_gains]).reshape(-1, HEAD_SIZE)
        ).reshape(-1)

    def heads_back(pieces):
        return f32(pieces).transpose(1, 0, 2).reshape(weight_rows, -1)

    def units_back(pieces):
        split = f32(pieces).reshape(4, weight_rows, line_extent, down_rows)
        return split.transpose(1, 2, 0, 3).reshape(weight_rows, -1)

    return (
        layer_out,
        grad_input,
        gains[:model_width],
        gains[2 * model_width :].reshape(2, HEAD_SIZE),
        heads_back(grad_qkv_columns[:, :, :query_part]),
        heads_back(grad_qkv_columns[:, :, query_part : query_part + HEAD_SIZE]),
        heads_back(grad_qkv_columns[:, :, query_part + HEAD_SIZE :]),
        grad_out_proj,
        gains[model_width : 2 * model_width],
        units_back(grad_gate_columns),
        units_back(grad_up_columns),
        grad_down,
    )


def solution(mesh):
    dp, tensor = mesh.shape["dp"], mesh.shape["tensor"]
    fine = Mesh(mesh.devices.reshape(dp // 4, 2, 2, tensor), ("f", "ty", "tx", "tensor"))
    rows = ("f", "ty", "tx")
    tokens = P(rows + ("tensor",), None)
    grid = P(rows, "tensor")
    units = P(("tensor",) + rows, None)
    return jax.shard_map(
        shards,
        mesh=fine,
        in_specs=(
            tokens, P(), P(), grid, grid, grid, units, P(), grid, grid, units, tokens, P(rows, None),
        ),
        out_specs=(tokens, tokens, P(), P(), grid, grid, grid, units, P(), grid, grid, units),
        check_vma=False,
    )
```

```python
import jax
import jax.numpy as jnp
from jax import lax
from jax.experimental import pallas as pl
from jax.experimental.pallas import tpu as pltpu
from jax.sharding import Mesh, PartitionSpec as P

QUERY_HEADS = 16
KEY_VALUE_HEADS = 8
HEAD_SIZE = 128


EPS = 1e-06
ROPE_BASE = 1000000.0
MASKED = -1e30
LOW = jnp.bfloat16


def matmul(left_mat, right_mat):
    return jnp.dot(left_mat, right_mat, preferred_element_type=jnp.float32)


def matmul_tn(left_mat, right_mat):
    return lax.dot_general(
        left_mat, right_mat, (((0,), (0,)), ((), ())), preferred_element_type=jnp.float32
    )


def matmul_nt(left_mat, right_mat):
    return lax.dot_general(
        left_mat, right_mat, (((1,), (1,)), ((), ())), preferred_element_type=jnp.float32
    )


def inv_rms(values):
    return lax.rsqrt(jnp.mean(values * values, axis=-1, keepdims=True) + EPS)


def norm_back(values, scales, gain_row, upstream):
    weighted = upstream * gain_row
    inner_mean = jnp.mean(weighted * values, axis=-1, keepdims=True)
    value_grad = scales * weighted - values * (scales * scales * scales) * inner_mean
    lead_axes = tuple(range(upstream.ndim - 1))
    return (value_grad, jnp.sum(upstream * values * scales, axis=lead_axes))


def rope_tables(position, head_width):
    half_dim = head_width // 2
    inverse = ROPE_BASE ** (-(jnp.arange(half_dim, dtype=jnp.float32) * (2.0 / head_width)))
    angles = position.astype(jnp.float32)[:, None] * inverse[None, :]
    return (jnp.cos(angles), jnp.sin(angles))


def rotate(values, cos_tab, sin_tab, direction):
    half_dim = values.shape[-1] // 2
    first_half = values[..., :half_dim]
    second_half = values[..., half_dim:]
    cosine = cos_tab[:, None, :]
    sine_tab = direction * sin_tab[:, None, :]
    return jnp.concatenate(
        [
            first_half * cosine - second_half * sine_tab,
            second_half * cosine + first_half * sine_tab,
        ],
        axis=-1,
    )


def doc_layout(lengths_row, row_ids):
    doc_ends = jnp.cumsum(lengths_row, dtype=jnp.int32)
    document_segment = jnp.sum(
        (row_ids[:, None] >= doc_ends[None, :]).astype(jnp.int32), axis=1, dtype=jnp.int32
    )
    doc_starts = doc_ends - lengths_row
    member = document_segment[:, None] == jnp.arange(lengths_row.shape[0], dtype=jnp.int32)[None, :]
    start_of = jnp.sum(jnp.where(member, doc_starts[None, :], 0), axis=1, dtype=jnp.int32)
    return (document_segment, row_ids - start_of)


def f32(values):
    return values.astype(jnp.float32)


def low(values):
    return values.astype(LOW)


def after(block, *earlier):
    return lax.optimization_barrier((block,) + earlier)[0]


def swap(block, axis):
    return lax.ppermute(block, axis, [(0, 1), (1, 0)])


def plane_index():
    return 2 * lax.axis_index("ty") + lax.axis_index("tx")


def plane_gather(block, second=()):
    half = block.shape[0] // 2
    across_x = swap(block, "tx")
    across_y = swap(block, "ty")
    top, end = after(across_y[:half], *second), after(across_x[half:], *second)
    far = jnp.concatenate([swap(top, "tx"), swap(end, "ty")])
    return [block, across_x, across_y, far]


def plane_scatter(parts, second=(), third=()):
    own, for_x, for_y, for_far = parts
    half = own.shape[0] // 2
    pass_y = swap(for_far[:half], "tx")
    pass_x = swap(for_far[half:], "ty")
    x_top = swap(for_x[:half], "tx")
    y_end = swap(for_y[half:], "ty")
    pass_y, pass_x = after(pass_y, *second), after(pass_x, *second)
    y_top = swap(low(f32(for_y[:half]) + f32(pass_y)), "ty")
    x_end = swap(low(f32(for_x[half:]) + f32(pass_x)), "tx")
    x_top, y_top = after(x_top, *third), after(y_top, *third)
    x_end, y_end = after(x_end, *third), after(y_end, *third)
    return jnp.concatenate(
        [
            f32(own[:half]) + f32(x_top) + f32(y_top),
            f32(own[half:]) + f32(x_end) + f32(y_end),
        ]
    )


def plane_exchange(parts):
    own, for_x, for_y, for_far = parts
    half = own.shape[0] // 2
    far = jnp.concatenate(
        [
            swap(swap(for_far[:half], "tx"), "ty"),
            swap(swap(for_far[half:], "ty"), "tx"),
        ]
    )
    return [own, swap(for_x, "tx"), swap(for_y, "ty"), far]


def plane_lengths(lengths):
    across_x, across_y = swap(lengths, "tx"), swap(lengths, "ty")
    return jnp.concatenate([lengths, across_x, across_y, swap(across_y, "tx")])


def line_gather(block, second=(), near=None):
    extent = lax.axis_size("f")
    if extent != 4:
        return lax.all_gather(block, "f", axis=0)
    place = lax.axis_index("f")
    two_away = lax.ppermute(block, "f", [(0, 2), (2, 0), (1, 3), (3, 1)])
    if near is None:
        above = lax.ppermute(block, "f", [(1, 0), (2, 1), (3, 2)])
        below = lax.ppermute(block, "f", [(0, 1), (1, 2), (2, 3)])
    else:
        above, below = near
    two_away = after(two_away, *second)
    passed = lax.ppermute(two_away, "f", [(1, 0), (2, 3)])
    blocks = [
        block,
        jnp.where(place == 3, passed, above),
        two_away,
        jnp.where(place == 0, passed, below),
    ]
    whole = jnp.zeros((4,) + block.shape, block.dtype)
    for step in range(4):
        whole = lax.dynamic_update_index_in_dim(whole, blocks[step], (place + step) % 4, 0)
    return whole


def line_scatter(parts, second=(), third=()):
    extent = lax.axis_size("f")
    if extent != 4:
        return f32(lax.psum_scatter(parts, "f", scatter_dimension=0))
    place = lax.axis_index("f")
    part = [
        lax.dynamic_index_in_dim(parts, (place + step) % 4, 0, keepdims=False) for step in range(4)
    ]
    passed = lax.ppermute(jnp.where(place == 0, part[3], part[1]), "f", [(0, 1), (3, 2)])
    above = lax.ppermute(part[3], "f", [(1, 0), (2, 1), (3, 2)])
    below = lax.ppermute(part[1], "f", [(0, 1), (1, 2), (2, 3)])
    passed = after(passed, *second)
    two_away = lax.ppermute(
        low(f32(part[2]) + f32(passed)), "f", [(0, 2), (2, 0), (1, 3), (3, 1)]
    )
    above, below, two_away = (after(block, *third) for block in (above, below, two_away))
    return f32(part[0]) + f32(above) + f32(below) + f32(two_away)


def natural_plane(blocks, axis):
    own = plane_index()
    shape = list(blocks[0].shape)
    shape.insert(axis, 4)
    whole = jnp.zeros(shape, blocks[0].dtype)
    for step in range(4):
        whole = lax.dynamic_update_index_in_dim(whole, blocks[step], own ^ step, axis)
    return whole


def own_plane(whole, axis):
    own = plane_index()
    return [
        lax.dynamic_index_in_dim(whole, own ^ step, axis, keepdims=False) for step in range(4)
    ]


def full_gather(rows_block):
    rows, width = rows_block.shape
    line = line_gather(rows_block)
    extent = line.shape[0]
    blocks = plane_gather(line.reshape(extent * rows, width))
    whole = natural_plane([block.reshape(extent, rows, width) for block in blocks], 1)
    return whole.reshape(extent * 4 * rows, width)


def full_scatter_plane(partial, second=(), third=()):
    extent = lax.axis_size("f")
    rows, width = partial.shape[0] // (4 * extent), partial.shape[1]
    parts = own_plane(partial.reshape(extent, 4, rows, width), 1)
    plane_sum = plane_scatter(
        [part.reshape(extent * rows, width) for part in parts], second, third
    )
    return low(plane_sum).reshape(extent, rows, width)


def tokens_gather(block, second=(), third=()):
    near = plane_gather(block, second)
    return jnp.concatenate(near + [swap(after(piece, *third), "tensor") for piece in near])


def tokens_scatter(partial, second=(), third=(), fourth=()):
    rows = partial.shape[0] // 8
    near = []
    for step in (3, 1, 2, 0):
        mine = partial[step * rows : (step + 1) * rows]
        other = swap(partial[(4 + step) * rows : (5 + step) * rows], "tensor")
        near.append(low(f32(mine) + f32(after(other, *second))))
    return plane_scatter([near[3], near[1], near[2], near[0]], third, fourth)


def pair_gather(block):
    return jnp.concatenate([block, swap(block, "tensor")])


def pair_scatter(partial):
    rows = partial.shape[0] // 2
    return f32(partial[:rows]) + f32(swap(partial[rows:], "tensor"))


def total_sum(values):
    for axis in ("tensor", "tx", "ty"):
        values = values + swap(values, axis)
    if lax.axis_size("f") != 4:
        return lax.psum(values, "f")
    values = values + lax.ppermute(values, "f", [(0, 1), (1, 0), (2, 3), (3, 2)])
    return values + lax.ppermute(values, "f", [(0, 2), (2, 0), (1, 3), (3, 1)])


class Place:
    def __init__(self):
        self.z = lax.axis_index("f")
        self.ty = lax.axis_index("ty")
        self.tx = lax.axis_index("tx")
        self.core = lax.axis_index("tensor")
        self.p = 2 * self.ty + self.tx
        self.px = 2 * self.ty + 1 - self.tx
        self.py = 2 * (1 - self.ty) + self.tx
        self.pd = 2 * (1 - self.ty) + 1 - self.tx
        self.x = {"tx": 1 - self.tx}
        self.y = {"ty": 1 - self.ty}
        self.d = {"tx": 1 - self.tx, "ty": 1 - self.ty}
        self.pair = {"tensor": 1 - self.core}
        self.up = {"f": self.z + 1}
        self.down = {"f": self.z - 1}
        self.two = {"f": (self.z + 2) % 4}

    def at(self, step):
        return (self.z + step) % 4


def remote(src, dst, send, recv, to):
    return pltpu.make_async_remote_copy(
        src_ref=src,
        dst_ref=dst,
        send_sem=send,
        recv_sem=recv,
        device_id=to,
        device_id_type=pl.DeviceIdType.MESH,
    )


def arrived(dst, recv, to):
    remote(dst, dst, recv, recv, to).wait_recv()


def greet(place, partners, line):
    barrier = pltpu.get_barrier_semaphore()
    for to in partners:
        pl.semaphore_signal(barrier, inc=1, device_id=to, device_id_type=pl.DeviceIdType.MESH)
    if not line:
        pl.semaphore_wait(barrier, len(partners))
        return

    @pl.when(place.z > 0)
    def _():
        pl.semaphore_signal(
            barrier, inc=1, device_id=place.down, device_id_type=pl.DeviceIdType.MESH
        )

    @pl.when(place.z < 3)
    def _():
        pl.semaphore_signal(barrier, inc=1, device_id=place.up, device_id_type=pl.DeviceIdType.MESH)

    pl.semaphore_signal(barrier, inc=1, device_id=place.two, device_id_type=pl.DeviceIdType.MESH)
    pl.semaphore_wait(barrier, len(partners) + 2 + (place.z + 1) // 2 % 2)


class LineGather:
    def __init__(self, place, own, slot, send, recv):
        self.place, self.own, self.slot, self.send, self.recv = place, own, slot, send, recv
        here = slot(place.z)
        self.to_down = remote(own, here, send.at[0], recv.at[1], place.down)
        self.to_up = remote(own, here, send.at[1], recv.at[3], place.up)
        self.to_two = remote(own, here, send.at[2], recv.at[2], place.two)
        two = slot(place.at(2))
        self.pass_down = remote(two, two, send.at[3], recv.at[3], place.down)
        self.pass_up = remote(two, two, send.at[3], recv.at[1], place.up)

    def start(self):
        pl.when(self.place.z > 0)(self.to_down.start)
        pl.when(self.place.z < 3)(self.to_up.start)
        self.to_two.start()

    def step(self, turn):
        if turn == 2:
            return 2
        if turn == 1:
            return jnp.where(self.place.z == 3, 3, 1)
        return jnp.where(self.place.z == 3, 1, 3)

    def wait(self, turn):
        step = self.step(turn)
        slot = self.slot(self.place.at(step))
        arrived(slot, self.recv.at[step], self.place.two)
        if turn == 2:
            pl.when(self.place.z == 1)(self.pass_down.start)
            pl.when(self.place.z == 2)(self.pass_up.start)

    def finish(self):
        pl.when(self.place.z > 0)(self.to_down.wait_send)
        pl.when(self.place.z < 3)(self.to_up.wait_send)
        self.to_two.wait_send()
        pl.when(self.place.z == 1)(self.pass_down.wait_send)
        pl.when(self.place.z == 2)(self.pass_up.wait_send)


class PlaneGather:
    def __init__(self, place, own, slot, rows, send, recv):
        half = rows // 2
        whole, top, end = pl.ds(0, rows), pl.ds(0, half), pl.ds(half, half)
        self.place, self.recv = place, recv
        self.to_x = remote(own, slot(place.p, whole), send.at[0], recv.at[0], place.x)
        self.to_y = remote(own, slot(place.p, whole), send.at[1], recv.at[1], place.y)
        self.from_x, self.from_y = slot(place.px, whole), slot(place.py, whole)
        self.far_top, self.far_end = slot(place.pd, top), slot(place.pd, end)
        pass_x, pass_y = slot(place.py, top), slot(place.px, end)
        self.pass_x = remote(pass_x, pass_x, send.at[2], recv.at[2], place.x)
        self.pass_y = remote(pass_y, pass_y, send.at[3], recv.at[3], place.y)

    def start(self):
        self.to_x.start()
        self.to_y.start()

    def forward(self):
        arrived(self.from_y, self.recv.at[1], self.place.y)
        self.pass_x.start()
        arrived(self.from_x, self.recv.at[0], self.place.x)
        self.pass_y.start()

    def wait_far(self):
        arrived(self.far_top, self.recv.at[2], self.place.x)
        arrived(self.far_end, self.recv.at[3], self.place.y)

    def finish(self):
        self.to_x.wait_send()
        self.to_y.wait_send()
        self.pass_x.wait_send()
        self.pass_y.wait_send()


ANYWHERE = pl.BlockSpec(memory_space=pl.ANY)
WHOLE = pl.BlockSpec(memory_space=pltpu.VMEM)


class Marks:
    def __init__(self, ref):
        self.ref, self.used = ref, 0

    def take(self, count=1):
        first = self.used
        self.used += count
        return self.ref.at[first] if count == 1 else self.ref.at[pl.ds(first, count)]


def each_rows(rows, chunk, work):
    def body(index, carry):
        work(pl.ds(pl.multiple_of(index * chunk, chunk), chunk))
        return carry

    lax.fori_loop(0, rows // chunk, body, 0)


class TokensGather:
    def __init__(self, place, own, whole, marks):
        half = own.shape[0] // 2
        top, end = pl.ds(0, half), pl.ds(half, half)
        self.place, self.whole = place, whole
        self.copy = pltpu.make_async_copy(own, whole.at[0], marks.take())
        self.recv = [marks.take() for _ in range(8)]
        x, y, pair = place.x, place.y, place.pair
        self.to_x = remote(own, whole.at[1], marks.take(), self.recv[0], x)
        self.to_y = remote(own, whole.at[2], marks.take(), self.recv[1], y)
        self.pass_x = remote(
            whole.at[2, top], whole.at[3, top], marks.take(), self.recv[2], x
        )
        self.pass_y = remote(
            whole.at[1, end], whole.at[3, end], marks.take(), self.recv[3], y
        )
        self.to_pair = [
            remote(
                own if step == 0 else whole.at[step],
                whole.at[4 + step],
                marks.take(),
                self.recv[4 + step],
                pair,
            )
            for step in range(4)
        ]
        self.far = (whole.at[3, top], whole.at[3, end])

    def start(self):
        self.to_x.start()
        self.to_y.start()
        self.to_pair[0].start()
        self.copy.start()

    def forward(self):
        arrived(self.whole.at[2], self.recv[1], self.place.y)
        self.pass_x.start()
        arrived(self.whole.at[1], self.recv[0], self.place.x)
        self.pass_y.start()
        self.to_pair[2].start()
        self.to_pair[1].start()

    def last(self):
        arrived(self.far[0], self.recv[2], self.place.x)
        arrived(self.far[1], self.recv[3], self.place.y)
        self.to_pair[3].start()

    def finish(self):
        for step in range(4):
            arrived(self.whole.at[4 + step], self.recv[4 + step], self.place.pair)
        for copy in [self.to_x, self.to_y, self.pass_x, self.pass_y] + self.to_pair:
            copy.wait_send()
        self.copy.wait()


class Exchange:
    def __init__(self, place, piece, slot, marks):
        self.place = place
        there = ((place.px, place.x), (place.py, place.y), (place.pd, place.d))
        self.copy = pltpu.make_async_copy(piece(place.p, 0), slot(place.p, 0), marks.take())
        self.sends, self.slots = [], []
        for index, (p, to) in enumerate(there):
            recv = marks.take()
            self.sends.append(
                remote(piece(p, index + 1), slot(place.p, index + 1), marks.take(), recv, to)
            )
            self.slots.append((slot(p, index + 1), recv, to))

    def start(self):
        for copy in (self.sends[2], self.sends[0], self.sends[1], self.copy):
            copy.start()

    def wait(self):
        self.copy.wait()
        for slot, recv, to in self.slots:
            arrived(slot, recv, to)

    def finish(self):
        for copy in self.sends:
            copy.wait_send()


class LineScatter:
    @staticmethod
    def scratch(rows, width):
        return [pltpu.VMEM((6, rows, width), LOW)]

    def __init__(self, place, part, out, buffers, marks):
        self.place, self.out = place, out
        self.kept = buffers[0]
        self.rows = self.kept.shape[1]
        self.passed, self.above, self.below, self.two, self.mid, self.own = (
            self.kept.at[index] for index in range(6)
        )
        self.recv = [marks.take() for _ in range(4)]
        z = place.z
        self.pass_up = remote(part(3), self.passed, marks.take(), self.recv[0], place.up)
        self.pass_down = remote(part(0), self.passed, marks.take(), self.recv[0], place.down)
        self.to_down = remote(
            part(place.at(3)), self.above, marks.take(), self.recv[1], place.down
        )
        self.to_up = remote(part(place.at(1)), self.below, marks.take(), self.recv[2], place.up)
        self.to_two = remote(self.mid, self.two, marks.take(), self.recv[3], place.two)
        self.load_mid = pltpu.make_async_copy(part(place.at(2)), self.mid, marks.take())
        self.load_own = pltpu.make_async_copy(part(z), self.own, marks.take())

    def start(self):
        z = self.place.z
        pl.when(z == 0)(self.pass_up.start)
        pl.when(z == 3)(self.pass_down.start)
        self.load_mid.start()
        pl.when(z > 0)(self.to_down.start)
        pl.when(z < 3)(self.to_up.start)
        self.load_own.start()
        self.load_mid.wait()
        pl.when((z == 0) | (z == 3))(self.to_two.start)

    def middle(self):
        z = self.place.z

        @pl.when((z == 1) | (z == 2))
        def _():
            arrived(self.passed, self.recv[0], self.place.two)

            def work(rows):
                self.kept[4, rows] = low(f32(self.kept[4, rows]) + f32(self.kept[0, rows]))

            each_rows(self.rows, 16, work)
            self.to_two.start()

    def finish(self):
        z, rows_all = self.place.z, self.rows
        out, kept = self.out, self.kept
        self.load_own.wait()

        @pl.when(z < 3)
        def _():
            arrived(self.above, self.recv[1], self.place.two)

            def work(rows):
                kept[5, rows] = low(f32(kept[5, rows]) + f32(kept[1, rows]))

            each_rows(rows_all, 16, work)

        @pl.when(z > 0)
        def _():
            arrived(self.below, self.recv[2], self.place.two)

            def work(rows):
                kept[5, rows] = low(f32(kept[5, rows]) + f32(kept[2, rows]))

            each_rows(rows_all, 16, work)

        arrived(self.two, self.recv[3], self.place.two)

        def work(rows):
            out[rows] = low(f32(kept[5, rows]) + f32(kept[3, rows]))

        each_rows(rows_all, 16, work)

    def drain(self):
        z = self.place.z
        pl.when(z == 0)(self.pass_up.wait_send)
        pl.when(z == 3)(self.pass_down.wait_send)
        pl.when(z > 0)(self.to_down.wait_send)
        pl.when(z < 3)(self.to_up.wait_send)
        self.to_two.wait_send()


def comm_params(number):
    return pltpu.CompilerParams(
        collective_id=number, has_side_effects=True, vmem_limit_bytes=62 * 1024 * 1024
    )


def comm_cost(micros):
    return pl.CostEstimate(flops=0, bytes_accessed=micros * 3_000_000, transcendentals=0)


def first_kernel(
    rows_ref,
    qkv_ref,
    out_ref,
    gate_ref,
    up_ref,
    down_ref,
    rows_all,
    qkv_all,
    out_all,
    gate_rows,
    up_rows,
    above_ref,
    below_ref,
    marks_ref,
):
    place = Place()
    marks = Marks(marks_ref)
    greet(place, [place.x, place.y, place.d, place.pair], True)
    qkv_pieces = Exchange(
        place, lambda p, step: qkv_ref.at[p], lambda p, step: qkv_all.at[place.z, p], marks
    )
    gate_pieces = Exchange(
        place, lambda p, step: gate_ref.at[p], lambda p, step: gate_rows.at[p], marks
    )
    up_pieces = Exchange(place, lambda p, step: up_ref.at[p], lambda p, step: up_rows.at[p], marks)
    tokens = TokensGather(place, rows_ref, rows_all, marks)
    qkv_line = LineGather(
        place,
        qkv_all.at[place.z],
        lambda z: qkv_all.at[z],
        marks.take(4),
        marks.take(4),
    )
    out_line = LineGather(
        place, out_ref, lambda z: out_all.at[z, place.p], marks.take(4), marks.take(4)
    )
    out_copy = pltpu.make_async_copy(out_ref, out_all.at[place.z, place.p], marks.take())
    near_recv = [marks.take(), marks.take()]
    to_down = remote(down_ref, above_ref, marks.take(), near_recv[0], place.down)
    to_up = remote(down_ref, below_ref, marks.take(), near_recv[1], place.up)
    out_planes = []
    for turn in range(4):
        z = place.z if turn == 0 else place.at(out_line.step(turn))
        out_planes.append(
            PlaneGather(
                place,
                out_ref if turn == 0 else out_all.at[z, place.p],
                lambda p, rows, z=z: out_all.at[z, p, rows],
                out_ref.shape[0],
                marks.take(4),
                marks.take(4),
            )
        )

    qkv_pieces.start()
    tokens.start()
    out_copy.start()
    qkv_pieces.wait()
    qkv_line.start()
    tokens.forward()
    out_planes[0].start()
    qkv_line.wait(1)
    out_line.start()
    qkv_line.wait(2)
    tokens.last()
    out_planes[0].forward()
    gate_pieces.start()
    out_line.wait(1)
    out_planes[1].start()
    out_line.wait(2)
    out_planes[2].start()
    qkv_line.wait(3)
    out_line.wait(3)
    out_planes[3].start()
    pl.when(place.z > 0)(to_down.start)
    pl.when(place.z < 3)(to_up.start)
    up_pieces.start()
    out_planes[1].forward()
    out_planes[2].forward()
    out_planes[3].forward()
    gate_pieces.wait()
    up_pieces.wait()
    for plane in out_planes:
        plane.wait_far()
    tokens.finish()
    for part in [qkv_pieces, gate_pieces, up_pieces, qkv_line, out_line] + out_planes:
        part.finish()
    out_copy.wait()

    @pl.when(place.z < 3)
    def _():
        arrived(above_ref, near_recv[0], place.two)
        to_up.wait_send()

    @pl.when(place.z > 0)
    def _():
        arrived(below_ref, near_recv[1], place.two)
        to_down.wait_send()


def first_gather(rows, qkv_pieces, output_weight, gate_pieces, up_pieces, down_weight):
    return pl.pallas_call(
        first_kernel,
        out_shape=(
            jax.ShapeDtypeStruct((8,) + rows.shape, LOW),
            jax.ShapeDtypeStruct((4,) + qkv_pieces.shape, LOW),
            jax.ShapeDtypeStruct((4, 4) + output_weight.shape, LOW),
            jax.ShapeDtypeStruct(gate_pieces.shape, LOW),
            jax.ShapeDtypeStruct(up_pieces.shape, LOW),
            jax.ShapeDtypeStruct(down_weight.shape, LOW),
            jax.ShapeDtypeStruct(down_weight.shape, LOW),
        ),
        in_specs=[ANYWHERE] * 6,
        out_specs=(ANYWHERE,) * 7,
        scratch_shapes=[pltpu.SemaphoreType.DMA((100,))],
        compiler_params=comm_params(0),
        cost_estimate=comm_cost(80),
    )(rows, qkv_pieces, output_weight, gate_pieces, up_pieces, down_weight)


def heads_out_kernel(heads_ref, own_ref, marks_ref):
    place = Place()
    greet(place, [place.x, place.y, place.d], False)
    exchange = Exchange(
        place,
        lambda p, step: heads_ref.at[:, step],
        lambda p, step: own_ref.at[p],
        Marks(marks_ref),
    )
    exchange.start()
    exchange.wait()
    exchange.finish()


def heads_to_tokens(heads):
    cores, _, rows, width = heads.shape
    return pl.pallas_call(
        heads_out_kernel,
        out_shape=jax.ShapeDtypeStruct((4, cores, rows, width), LOW),
        in_specs=[ANYWHERE],
        out_specs=ANYWHERE,
        scratch_shapes=[pltpu.SemaphoreType.DMA((8,))],
        compiler_params=comm_params(2),
        cost_estimate=comm_cost(15),
    )(heads)


class PlaneScatter:
    @staticmethod
    def scratch(rows, width):
        return [pltpu.VMEM((6, rows // 2, width), LOW)]

    def __init__(self, place, summed, out, buffers, marks, at=(0, 1, 2, 3)):
        self.place, self.summed, self.out, self.at = place, summed, out, at
        self.landed = buffers[0]
        self.rows = summed.shape[1]
        half = self.rows // 2
        top, end = pl.ds(0, half), pl.ds(half, half)
        x, y = place.x, place.y
        self.recv = [marks.take() for _ in range(6)]
        routes = (
            (summed.at[at[3], top], x),
            (summed.at[at[3], end], y),
            (summed.at[at[1], top], x),
            (summed.at[at[1], end], x),
            (summed.at[at[2], top], y),
            (summed.at[at[2], end], y),
        )
        self.sends = [
            remote(src, self.landed.at[index], marks.take(), self.recv[index], to)
            for index, (src, to) in enumerate(routes)
        ]

    def start(self):
        for index in (0, 1, 2, 5):
            self.sends[index].start()

    def landed_at(self, index, to):
        arrived(self.landed.at[index], self.recv[index], to)

    def middle(self):
        half = self.rows // 2
        summed, landed = self.summed, self.landed
        _, for_x, for_y, _ = self.at
        self.landed_at(0, self.place.x)

        def top_work(rows):
            summed[for_y, rows] = low(f32(summed[for_y, rows]) + f32(landed[0, rows]))

        each_rows(half, 16, top_work)
        self.sends[4].start()
        self.landed_at(1, self.place.y)

        def end_work(rows):
            end_rows = pl.ds(pl.multiple_of(rows.start + half, 16), rows.size)
            summed[for_x, end_rows] = low(f32(summed[for_x, end_rows]) + f32(landed[1, rows]))

        each_rows(half, 16, end_work)
        self.sends[3].start()

    def finish(self):
        half = self.rows // 2
        for index, to in ((2, self.place.x), (5, self.place.y), (4, self.place.y), (3, self.place.x)):
            self.landed_at(index, to)

        for base, first, second in ((0, 2, 4), (half, 3, 5)):

            def work(rows):
                own_rows = pl.ds(pl.multiple_of(rows.start + base, 16), rows.size)
                self.out[own_rows] = (
                    f32(self.summed[self.at[0], own_rows])
                    + f32(self.landed[first, rows])
                    + f32(self.landed[second, rows])
                ).astype(self.out.dtype)

            each_rows(half, 16, work)

    def drain(self):
        for copy in self.sends:
            copy.wait_send()


def units_kernel(
    rows_ref,
    line_ref,
    gate_ref,
    down_ref,
    upstream_ref,
    rows_all,
    inner_out,
    gate_grad_out,
    up_grad_out,
    part_sums,
    grad_sums,
    marks_ref,
    gate_mat,
    up_mat,
    down_mat,
    row_block,
    grad_block,
    part_stage,
    grad_stage,
    part_got,
    grad_got,
):
    place = Place()
    marks = Marks(marks_ref)
    greet(place, [place.x, place.y, place.pair], True)
    tokens = TokensGather(place, rows_ref, rows_all, marks)
    line = LineGather(place, line_ref, lambda z: up_mat.at[z], marks.take(4), marks.take(4))
    copies = [
        pltpu.make_async_copy(line_ref, up_mat.at[place.z], marks.take()),
        pltpu.make_async_copy(gate_ref, gate_mat, marks.take()),
        pltpu.make_async_copy(down_ref, down_mat, marks.take()),
    ]
    fetch_marks = marks.take(4)
    send_marks, recv_marks = marks.take(8), marks.take(8)

    tokens.start()
    line.start()
    for copy in copies:
        copy.start()
    tokens.forward()
    line.wait(2)
    tokens.last()
    line.wait(1)
    line.wait(3)
    for copy in copies:
        copy.wait()
    tokens.finish()
    line.finish()

    def fetches(index):
        step, slot = 3 - index // 2, index % 2
        block = step + 4 * (1 - slot)
        return (
            pltpu.make_async_copy(rows_all.at[block], row_block.at[slot], fetch_marks.at[slot]),
            pltpu.make_async_copy(
                upstream_ref.at[block], grad_block.at[slot], fetch_marks.at[2 + slot]
            ),
        )

    def sends(step):
        return (
            remote(
                part_stage.at[step],
                part_got.at[step],
                send_marks.at[step],
                recv_marks.at[step],
                place.pair,
            ),
            remote(
                grad_stage.at[step],
                grad_got.at[step],
                send_marks.at[4 + step],
                recv_marks.at[4 + step],
                place.pair,
            ),
        )

    units = gate_mat.shape[1]
    for copy in fetches(0):
        copy.start()

    def blocks(turn, carry):
        step = 3 - turn
        for slot in range(2):
            index = 2 * turn + slot
            block = step + 4 * (1 - slot)
            for copy in fetches(index):
                copy.wait()

            @pl.when(index < 7)
            def _():
                for copy in fetches(index + 1):
                    copy.start()

            rows = row_block[slot]
            gate_raw = matmul(rows, gate_mat[...])
            up_raw = matmul(rows, up_mat[...].reshape(-1, units))
            inner_grad = matmul_nt(grad_block[slot], down_mat[...])
            sigmoid_gate = jax.nn.sigmoid(gate_raw)
            activated = gate_raw * sigmoid_gate
            inner = low(activated * up_raw)
            gate_grad = low(
                inner_grad * up_raw * sigmoid_gate * (1.0 + gate_raw * (1.0 - sigmoid_gate))
            )
            up_grad = low(inner_grad * activated)
            inner_out[block] = inner
            gate_grad_out[block] = gate_grad
            up_grad_out[block] = up_grad
            part = matmul(inner, down_mat[...])
            grad = matmul_nt(gate_grad, gate_mat[...]) + matmul_nt(
                up_grad, up_mat[...].reshape(-1, units)
            )
            if slot == 0:
                part_stage[step] = low(part)
                grad_stage[step] = low(grad)
                for copy in sends(step):
                    copy.start()
            else:
                for copy in sends(step):
                    copy.wait_recv()
                part_sums[step] = low(part + f32(part_got[step]))
                grad_sums[step] = low(grad + f32(grad_got[step]))
        return carry

    lax.fori_loop(0, 4, blocks, 0)
    for step in range(4):
        for copy in sends(step):
            copy.wait_send()


def units_products(rows, up_rows, gate_all, down_all, upstream):
    block_rows, width = rows.shape
    units = gate_all.shape[1]
    block = lambda count: pltpu.VMEM((count, block_rows, width), LOW)
    hidden = jax.ShapeDtypeStruct((8, block_rows, units), LOW)
    sums = jax.ShapeDtypeStruct((4, block_rows, width), LOW)
    return pl.pallas_call(
        units_kernel,
        out_shape=(
            jax.ShapeDtypeStruct((8, block_rows, width), LOW),
            hidden,
            hidden,
            hidden,
            sums,
            sums,
        ),
        in_specs=[ANYWHERE] * 5,
        out_specs=(ANYWHERE,) + (WHOLE,) * 5,
        scratch_shapes=[
            pltpu.SemaphoreType.DMA((64,)),
            pltpu.VMEM(gate_all.shape, LOW),
            pltpu.VMEM((4,) + up_rows.shape, LOW),
            pltpu.VMEM(down_all.shape, LOW),
            block(2),
            block(2),
            block(4),
            block(4),
            block(4),
            block(4),
        ],
        compiler_params=comm_params(1),
        cost_estimate=comm_cost(110),
    )(rows, up_rows, gate_all, down_all, upstream)


def unit_grads_kernel(
    rows_all,
    upstream_ref,
    inner_ref,
    gate_grad_ref,
    up_grad_ref,
    part_sums,
    grad_sums,
    row_grad,
    row_part,
    down_out,
    gate_part,
    up_part,
    marks_ref,
    upstream,
    inner,
    gate_grad,
    up_grad,
    row_slab,
    down_part,
    *buffers,
):
    place = Place()
    marks = Marks(marks_ref)
    greet(place, [place.x, place.y], True)
    grad_plane = PlaneScatter(place, grad_sums, row_grad, buffers[:1], marks)
    part_plane = PlaneScatter(place, part_sums, row_part, buffers[1:2], marks)
    down_rows = down_out.shape[0]
    down_line = LineScatter(
        place,
        lambda z: down_part.at[pl.ds(pl.multiple_of(z * down_rows, 16), down_rows)],
        down_out,
        buffers[2:],
        marks,
    )
    loads = [
        pltpu.make_async_copy(upstream_ref, upstream, marks.take()),
        pltpu.make_async_copy(inner_ref, inner, marks.take()),
        pltpu.make_async_copy(gate_grad_ref, gate_grad, marks.take()),
        pltpu.make_async_copy(up_grad_ref, up_grad, marks.take()),
    ]
    slab_marks = marks.take(2)
    tile = row_slab.shape[3]
    tiles = rows_all.shape[2] // tile
    units = inner.shape[2]
    all_rows = inner.shape[0] * inner.shape[1]

    def slab(index):
        return pltpu.make_async_copy(
            rows_all.at[:, :, pl.ds(pl.multiple_of(index * tile, tile), tile)],
            row_slab.at[index % 2],
            slab_marks.at[index % 2],
        )

    grad_plane.start()
    for copy in loads:
        copy.start()
    slab(0).start()
    loads[0].wait()
    loads[1].wait()

    def down_tile(index, carry):
        columns = pl.ds(pl.multiple_of(index * tile, tile), tile)
        down_part[columns] = low(
            matmul_tn(
                inner[:, :, columns].reshape(all_rows, tile),
                upstream[...].reshape(all_rows, upstream.shape[2]),
            )
        )
        return carry

    lax.fori_loop(0, units // tile, down_tile, 0)
    down_line.start()
    loads[2].wait()
    loads[3].wait()

    def row_tile(index, carry):
        slab(index).wait()

        @pl.when(index < tiles - 1)
        def _():
            slab(index + 1).start()

        columns = row_slab[index % 2].reshape(all_rows, tile)
        out_rows = pl.ds(pl.multiple_of(index * tile, tile), tile)
        gate_part[out_rows] = low(matmul_tn(columns, gate_grad[...].reshape(all_rows, units)))
        up_part[out_rows] = low(matmul_tn(columns, up_grad[...].reshape(all_rows, units)))
        return carry

    lax.fori_loop(0, tiles // 4, row_tile, 0)
    grad_plane.middle()
    down_line.middle()
    lax.fori_loop(tiles // 4, tiles, row_tile, 0)
    grad_plane.finish()
    part_plane.start()
    part_plane.middle()
    down_line.finish()
    part_plane.finish()
    down_line.drain()
    grad_plane.drain()
    part_plane.drain()


def unit_grads(rows_all, upstream, inner, gate_grad, up_grad, part_sums, grad_sums):
    _, block_rows, width = rows_all.shape
    units = inner.shape[2]
    down_rows = units // 4
    tile = 256
    return pl.pallas_call(
        unit_grads_kernel,
        out_shape=(
            jax.ShapeDtypeStruct((block_rows, width), jnp.float32),
            jax.ShapeDtypeStruct((block_rows, width), jnp.float32),
            jax.ShapeDtypeStruct((down_rows, width), LOW),
            jax.ShapeDtypeStruct((width, units), LOW),
            jax.ShapeDtypeStruct((width, units), LOW),
        ),
        in_specs=[ANYWHERE] * 5 + [WHOLE] * 2,
        out_specs=(WHOLE,) * 5,
        scratch_shapes=[
            pltpu.SemaphoreType.DMA((64,)),
            pltpu.VMEM(upstream.shape, LOW),
            pltpu.VMEM(inner.shape, LOW),
            pltpu.VMEM(inner.shape, LOW),
            pltpu.VMEM(inner.shape, LOW),
            pltpu.VMEM((2, 8, block_rows, tile), LOW),
            pltpu.VMEM((units, width), LOW),
        ]
        + PlaneScatter.scratch(block_rows, width) * 2
        + LineScatter.scratch(down_rows, width),
        input_output_aliases={},
        compiler_params=comm_params(4),
        cost_estimate=comm_cost(70),
    )(rows_all, upstream, inner, gate_grad, up_grad, part_sums, grad_sums)


def last_kernel(
    parts_ref,
    qkv_ref,
    proj_ref,
    input_ref,
    hidden_ref,
    norm_ref,
    gains_ref,
    grad_ref,
    qkv_columns,
    proj_out,
    gains_out,
    marks_ref,
    qkv_sum,
    row_sum,
    gain_rows,
    gain_mine,
    gain_got,
    *buffers,
):
    place = Place()
    marks = Marks(marks_ref)
    greet(place, [place.x, place.y, place.d, place.pair], True)
    tokens = PlaneScatter(place, parts_ref, row_sum, buffers[:1], marks)
    qkv_line = LineScatter(place, lambda z: qkv_ref.at[z], qkv_sum, buffers[1:2], marks)
    proj_line = LineScatter(place, lambda z: proj_ref.at[z], proj_out, buffers[2:], marks)
    rows = qkv_sum.shape[0] // 4
    qkv_pieces = Exchange(
        place,
        lambda p, step: qkv_sum.at[pl.ds(pl.multiple_of(p * rows, rows), rows)],
        lambda p, step: qkv_columns.at[p],
        marks,
    )
    near_z = {"f": place.z + 1 - 2 * (place.z % 2)}
    rounds = [
        remote(gain_mine.at[index], gain_got.at[index], marks.take(), marks.take(), to)
        for index, to in enumerate((place.pair, place.x, place.y, near_z, place.two))
    ]

    tokens.start()
    qkv_line.start()
    qkv_line.middle()
    proj_line.start()
    tokens.middle()
    proj_line.middle()
    tokens.finish()

    qkv_line.finish()
    qkv_pieces.start()
    gain_rows[...] = jnp.zeros_like(gain_rows)
    norm_row = norm_ref[...]

    def work(rows):
        values = f32(input_ref[rows])
        scales = inv_rms(values)
        upstream = row_sum[rows]
        weighted = upstream * norm_row
        inner_mean = jnp.mean(weighted * values, axis=-1, keepdims=True)
        grad_ref[rows] = (
            hidden_ref[rows]
            + scales * weighted
            - values * (scales * scales * scales) * inner_mean
        )
        parts = upstream * values * scales
        gain_rows[...] += parts[:8] + parts[8:]

    each_rows(row_sum.shape[0], 16, work)
    width = norm_row.shape[1]
    gain_mine[0, :, pl.ds(0, width)] = jnp.sum(gain_rows[...], axis=0, keepdims=True)
    gain_mine[0, :, pl.ds(width, gains_ref.shape[1])] = gains_ref[...]
    for index, copy in enumerate(rounds):
        copy.start()
        copy.wait()
        summed = gain_mine[index] + gain_got[index]
        if index < 4:
            gain_mine[index + 1] = summed
        else:
            gains_out[...] = summed
    proj_line.finish()
    qkv_line.drain()
    proj_line.drain()
    tokens.drain()
    qkv_pieces.wait()
    qkv_pieces.finish()


def last_sums(parts, qkv_parts, proj_parts, layer_input, hidden_grad, norm, gains):
    rows, width = parts.shape[1:]
    qkv_rows, qkv_width = qkv_parts.shape[1:]
    gain_width = width + gains.shape[1]
    return pl.pallas_call(
        last_kernel,
        out_shape=(
            jax.ShapeDtypeStruct((rows, width), jnp.float32),
            jax.ShapeDtypeStruct((4, qkv_rows // 4, qkv_width), LOW),
            jax.ShapeDtypeStruct(proj_parts.shape[1:], LOW),
            jax.ShapeDtypeStruct((1, gain_width), jnp.float32),
        ),
        in_specs=[WHOLE] + [ANYWHERE] * 2 + [WHOLE] * 4,
        out_specs=(WHOLE, ANYWHERE, WHOLE, WHOLE),
        scratch_shapes=[
            pltpu.SemaphoreType.DMA((100,)),
            pltpu.VMEM((qkv_rows, qkv_width), LOW),
            pltpu.VMEM((rows, width), jnp.float32),
            pltpu.VMEM((8, width), jnp.float32),
            pltpu.VMEM((5, 1, gain_width), jnp.float32),
            pltpu.VMEM((5, 1, gain_width), jnp.float32),
        ]
        + PlaneScatter.scratch(rows, width)
        + LineScatter.scratch(qkv_rows, qkv_width)
        + LineScatter.scratch(*proj_parts.shape[1:]),
        compiler_params=comm_params(5),
        cost_estimate=comm_cost(60),
    )(parts, qkv_parts, proj_parts, layer_input, hidden_grad, norm, gains)


def turn_pairs(values, cosine, sine):
    return values * cosine + pltpu.roll(values, HEAD_SIZE // 2, 1) * sine


def softmax_of(query, key, allowed):
    scores = matmul_nt(query, key) * HEAD_SIZE ** (-0.5)
    masked = jnp.where(allowed, scores, MASKED)
    exponent = jnp.exp(masked - jnp.max(masked, axis=-1, keepdims=True))
    return exponent / jnp.sum(exponent, axis=-1, keepdims=True)


def allowed_of(segment_col, segment_row, id_col, id_row):
    return (segment_col[0] == segment_row[0]) & (id_row[...] <= id_col[...])


def attend_kernel(
    raw_ref, cos_ref, sin_ref, segment_col, segment_row, id_col, id_row, gains_ref, low_ref, out_ref
):
    group_rows = cos_ref.shape[1]
    raw = raw_ref[...].reshape(group_rows, raw_ref.shape[3])
    heads = raw.shape[1] // HEAD_SIZE - 2
    cosine, sine = cos_ref[0], sin_ref[0]
    allowed = allowed_of(segment_col, segment_row, id_col, id_row)
    columns = [raw[:, head * HEAD_SIZE : (head + 1) * HEAD_SIZE] for head in range(heads + 2)]
    turned = []
    for head in range(heads + 1):
        gain = gains_ref[min(head // heads, 1)][None, :]
        turned.append(
            low(turn_pairs(columns[head] * inv_rms(columns[head]) * gain, cosine, sine))
        )
    value = low(columns[heads + 1])
    attended = [
        low(matmul(low(softmax_of(turned[head], turned[heads], allowed)), value))
        for head in range(heads)
    ]
    low_ref[...] = jnp.concatenate(turned + [value], axis=1).reshape(low_ref.shape)
    out_ref[...] = jnp.concatenate(attended, axis=1).reshape(out_ref.shape)


def lanes(values, head):
    return values[:, head * HEAD_SIZE : (head + 1) * HEAD_SIZE]


def roll_half(values):
    return pltpu.roll(values, HEAD_SIZE // 2, 1)


def attend_back_values(raw, kept, grad, allowed, cosine, sine, gains_ref, roll=roll_half):
    group_rows = raw.shape[0]
    heads = raw.shape[1] // HEAD_SIZE - 2
    key, value = lanes(kept, heads), lanes(kept, heads + 1)
    scale = HEAD_SIZE ** (-0.5)
    turned_grads = []
    key_grad = jnp.zeros((group_rows, HEAD_SIZE), jnp.float32)
    value_grad = jnp.zeros((group_rows, HEAD_SIZE), jnp.float32)
    for head in range(heads):
        query, upstream = lanes(kept, head), lanes(grad, head)
        probs = softmax_of(query, key, allowed)
        probs_grad = matmul_nt(upstream, value)
        scores_grad = low(
            probs * (probs_grad - jnp.sum(probs * probs_grad, axis=-1, keepdims=True))
        )
        turned_grads.append(matmul(scores_grad, key) * scale)
        key_grad = key_grad + matmul_tn(scores_grad, query)
        value_grad = value_grad + matmul_tn(low(probs), upstream)
    turned_grads.append(key_grad * scale)
    outs, gains = [], []
    for head in range(heads + 1):
        gain = gains_ref[min(head // heads, 1)][None, :]
        unnormed = lanes(raw, head)
        upstream = turned_grads[head] * cosine - roll(turned_grads[head]) * sine
        grad_raw, gain_part = norm_back(unnormed, inv_rms(unnormed), gain, upstream)
        outs.append(low(grad_raw))
        gains.append(gain_part[None, :])
    outs.append(low(value_grad))
    query_gain = sum(gains[1:heads], gains[0])
    return (jnp.concatenate(outs, axis=1), jnp.concatenate([query_gain, gains[heads]], axis=1))


def heads_back_kernel(
    hidden_ref,
    row_grad_ref,
    upstream_ref,
    norm_ref,
    out_ref,
    attended_ref,
    raw_ref,
    low_ref,
    cos_ref,
    sin_ref,
    segment_col,
    segment_row,
    id_col,
    id_row,
    gains_ref,
    rows_all,
    qkv_ref,
    gate_part,
    up_part,
    hidden_grad,
    mlp_gain,
    head_gain,
    qkv_part,
    proj_sum,
    grad_sums,
    gate_columns,
    up_columns,
    marks_ref,
    out_mat,
    qkv_mat,
    attended,
    branch,
    own_grad,
    heads_grad,
    raw_block,
    low_block,
    qkv_grad,
    row_slab,
    proj_part,
    gain_rows,
    line_sum,
    *buffers,
):
    place = Place()
    marks = Marks(marks_ref)
    greet(place, [place.x, place.y, place.d, place.pair], True)
    rows, width = hidden_ref.shape
    half_heads = heads_grad.shape[2]
    group_rows = 2 * rows
    gate_line = LineScatter(
        place, lambda z: gate_part.at[z], line_sum.at[0], buffers[0:1], marks
    )
    up_line = LineScatter(place, lambda z: up_part.at[z], line_sum.at[1], buffers[1:2], marks)
    quarter = line_sum.shape[1] // 4
    columns = [
        Exchange(
            place,
            lambda p, step, index=index: line_sum.at[
                index, pl.ds(pl.multiple_of(p * quarter, quarter), quarter)
            ],
            lambda p, step, out=out: out.at[p],
            marks,
        )
        for index, out in enumerate((gate_columns, up_columns))
    ]
    proj_plane = PlaneScatter(
        place,
        proj_part,
        proj_sum,
        buffers[2:3],
        marks,
        (place.p, place.px, place.py, place.pd),
    )
    heads = Exchange(
        place, lambda p, step: own_grad.at[p], lambda p, step: heads_grad.at[step], marks
    )
    to_pair = remote(branch.at[0], branch.at[1], marks.take(), marks.take(), place.pair)
    loads = [
        pltpu.make_async_copy(out_ref, out_mat, marks.take()),
        pltpu.make_async_copy(attended_ref, attended, marks.take()),
        pltpu.make_async_copy(qkv_ref, qkv_mat, marks.take()),
    ]
    fetch_marks, slab_marks = marks.take(4), marks.take(2)
    send_marks, recv_marks = marks.take(4), marks.take(4)

    gate_line.start()
    for copy in loads:
        copy.start()

    gain_rows[...] = jnp.zeros_like(gain_rows)
    norm_row = norm_ref[...]

    def norm_work(part):
        values = hidden_ref[part]
        scales = inv_rms(values)
        upstream = row_grad_ref[part]
        weighted = upstream * norm_row
        inner_mean = jnp.mean(weighted * values, axis=-1, keepdims=True)
        grad = (
            f32(upstream_ref[part])
            + scales * weighted
            - values * (scales * scales * scales) * inner_mean
        )
        hidden_grad[part] = grad
        branch[0, part] = low(grad)
        parts = upstream * values * scales
        gain_rows[...] += parts[:8] + parts[8:]

    each_rows(rows, 16, norm_work)
    to_pair.start()
    mlp_gain[...] = jnp.sum(gain_rows[...], axis=0, keepdims=True)
    for copy in loads:
        copy.wait()

    def own_half(core_step):
        grad = low(matmul_nt(branch[core_step], out_mat[...]))
        for p in range(4):
            own_grad[p, pl.ds(core_step * rows, rows)] = grad[
                :, p * half_heads : (p + 1) * half_heads
            ]

    own_half(0)
    to_pair.wait()
    own_half(1)
    heads.start()
    gate_line.middle()
    up_line.start()

    def proj_work(z, carry):
        block = attended[z].reshape(group_rows, half_heads)
        grad = low(matmul_tn(block, branch[...].reshape(group_rows, width)))
        part = half_heads // 4
        for p in range(4):
            proj_part[p, pl.ds(pl.multiple_of(z * part, part), part)] = grad[
                p * part : (p + 1) * part
            ]
        return carry

    def fetches(step):
        return (
            pltpu.make_async_copy(raw_ref.at[:, step], raw_block, fetch_marks.at[0]),
            pltpu.make_async_copy(low_ref.at[:, step], low_block, fetch_marks.at[1]),
        )

    lax.fori_loop(0, 4, proj_work, 0)
    heads.wait()
    proj_plane.start()
    head_gain[...] = jnp.zeros_like(head_gain)

    def sends(step):
        return remote(
            out_mat.at[pl.ds(pl.multiple_of(step * rows, rows), rows)],
            grad_sums.at[step],
            send_marks.at[step],
            recv_marks.at[step],
            place.pair,
        )

    def bucket(step, carry):
        for copy in fetches(step):
            copy.start()
        for copy in fetches(step):
            copy.wait()
        allowed = (segment_col[step] == segment_row[step]) & (id_row[...] <= id_col[...])
        grads, gains = attend_back_values(
            raw_block[...].reshape(group_rows, -1),
            low_block[...].reshape(group_rows, -1),
            heads_grad[step],
            allowed,
            cos_ref[step],
            sin_ref[step],
            gains_ref,
        )
        head_gain[...] += gains
        qkv_grad[0, step] = grads[:rows]
        qkv_grad[1, step] = grads[rows:]
        out_mat[pl.ds(pl.multiple_of(step * rows, rows), rows)] = low(
            matmul_nt(grads[rows:], qkv_mat[...])
        )
        sends(step).start()
        return carry

    lax.fori_loop(0, 2, bucket, 0)
    proj_plane.middle()
    up_line.middle()
    lax.fori_loop(2, 4, bucket, 0)

    tile = row_slab.shape[3]
    tiles = width // tile

    def slab(index):
        return pltpu.make_async_copy(
            rows_all.at[:, :, pl.ds(pl.multiple_of(index * tile, tile), tile)],
            row_slab.at[index % 2],
            slab_marks.at[index % 2],
        )

    slab(0).start()

    def own_work(step, carry):
        copy = sends(step)
        copy.wait_recv()
        grad = matmul_nt(qkv_grad[0, step], qkv_mat[...])
        grad_sums[step] = low(grad + f32(grad_sums[step]))
        return carry

    lax.fori_loop(0, 4, own_work, 0)
    gate_line.finish()
    columns[0].start()

    def row_tile(index, carry):
        slab(index).wait()

        @pl.when(index < tiles - 1)
        def _():
            slab(index + 1).start()

        block = row_slab[index % 2].reshape(4 * group_rows, tile)
        out_rows = pl.ds(pl.multiple_of(index * tile, tile), tile)
        qkv_part[out_rows] = low(
            matmul_tn(block, qkv_grad[...].reshape(4 * group_rows, qkv_grad.shape[3]))
        )
        return carry

    lax.fori_loop(0, tiles, row_tile, 0)
    proj_plane.finish()
    up_line.finish()
    columns[1].start()
    for step in range(4):
        sends(step).wait_send()
    heads.finish()
    proj_plane.drain()
    gate_line.drain()
    up_line.drain()
    for part in columns:
        part.wait()
        part.finish()


def heads_backward(
    hidden, row_grad, upstream, norm, out_all, attended, raw, kept, tables, rows_all, qkv_all, gate_part, up_part
):
    rows, width = hidden.shape
    head_part = raw.shape[3]
    query_part = head_part - 2 * HEAD_SIZE
    line_rows, units = gate_part.shape[1:]
    tile = 256
    pieces = jax.ShapeDtypeStruct((4, line_rows // 4, units), LOW)
    return pl.pallas_call(
        heads_back_kernel,
        out_shape=(
            jax.ShapeDtypeStruct((rows, width), jnp.float32),
            jax.ShapeDtypeStruct((1, width), jnp.float32),
            jax.ShapeDtypeStruct((1, 2 * HEAD_SIZE), jnp.float32),
            jax.ShapeDtypeStruct((width, head_part), LOW),
            jax.ShapeDtypeStruct((query_part, width), LOW),
            jax.ShapeDtypeStruct((4, rows, width), LOW),
            pieces,
            pieces,
        ),
        in_specs=[WHOLE] * 4
        + [ANYWHERE] * 4
        + [WHOLE] * len(tables)
        + [ANYWHERE] * 4,
        out_specs=(WHOLE,) * 6 + (ANYWHERE,) * 2,
        scratch_shapes=[
            pltpu.SemaphoreType.DMA((100,)),
            pltpu.VMEM(out_all.shape, LOW),
            pltpu.VMEM(qkv_all.shape, LOW),
            pltpu.VMEM(attended.shape, LOW),
            pltpu.VMEM((2, rows, width), LOW),
            pltpu.VMEM((4, 2 * rows, query_part), LOW),
            pltpu.VMEM((4, 2 * rows, query_part), LOW),
            pltpu.VMEM((2, rows, head_part), jnp.float32),
            pltpu.VMEM((2, rows, head_part), LOW),
            pltpu.VMEM((2, 4, rows, head_part), LOW),
            pltpu.VMEM((2, 8, rows, tile), LOW),
            pltpu.VMEM((4, query_part, width), LOW),
            pltpu.VMEM((8, width), jnp.float32),
            pltpu.VMEM((2, line_rows, units), LOW),
        ]
        + LineScatter.scratch(line_rows, units) * 2
        + PlaneScatter.scratch(query_part, width),
        compiler_params=comm_params(3),
        cost_estimate=comm_cost(115),
    )(
        hidden,
        row_grad,
        upstream,
        norm,
        out_all,
        attended,
        raw,
        kept,
        *tables,
        rows_all,
        qkv_all,
        gate_part,
        up_part,
    )


def attention_specs(group_rows, rows):
    bucket = lambda width: pl.BlockSpec((2, 1, rows, width), lambda step: (0, step, 0, 0))
    tables = [
        pl.BlockSpec((1, group_rows, HEAD_SIZE), lambda step: (step, 0, 0)),
        pl.BlockSpec((1, group_rows, HEAD_SIZE), lambda step: (step, 0, 0)),
        pl.BlockSpec((1, group_rows, 1), lambda step: (step, 0, 0)),
        pl.BlockSpec((1, 1, group_rows), lambda step: (step, 0, 0)),
        pl.BlockSpec((group_rows, 1), lambda step: (0, 0)),
        pl.BlockSpec((1, group_rows), lambda step: (0, 0)),
        pl.BlockSpec((2, HEAD_SIZE), lambda step: (0, 0)),
    ]
    return bucket, tables


def attend(raw, tables):
    _, buckets, rows, width = raw.shape
    bucket, table_specs = attention_specs(2 * rows, rows)
    query_width = width - 2 * HEAD_SIZE
    return pl.pallas_call(
        attend_kernel,
        grid=(buckets,),
        out_shape=(
            jax.ShapeDtypeStruct(raw.shape, LOW),
            jax.ShapeDtypeStruct((2, buckets, rows, query_width), LOW),
        ),
        in_specs=[bucket(width)] + table_specs,
        out_specs=(bucket(width), bucket(query_width)),
        compiler_params=pltpu.CompilerParams(vmem_limit_bytes=48 * 1024 * 1024),
        cost_estimate=pl.CostEstimate(
            flops=30_000_000_000, bytes_accessed=20_000_000, transcendentals=0
        ),
    )(raw, *tables)


def shards(
    layer_input,
    attn_norm,
    head_norms,
    query_weight,
    key_matrix,
    value_matrix,
    output_weight,
    mlp_norm,
    gate_weight,
    up_weight,
    down_weight,
    grad_out,
    doc_lengths,
):
    line_extent = lax.axis_size("f")
    on_line = line_extent == 4
    core = lax.axis_index("tensor")
    local_rows, model_width = layer_input.shape
    group_rows = 2 * local_rows
    all_rows = 8 * local_rows
    weight_rows = gate_weight.shape[0]
    down_rows = down_weight.shape[0]
    hidden_part = line_extent * down_rows
    query_part = query_weight.shape[1] // 4
    head_part = query_part + 2 * HEAD_SIZE

    def heads_of(weight):
        return weight.reshape(weight_rows, 4, -1).transpose(1, 0, 2)

    def units_of(weight):
        split = weight.reshape(weight_rows, line_extent, 4, down_rows)
        return split.transpose(2, 0, 1, 3).reshape(4, weight_rows, hidden_part)

    qkv_pieces = jnp.concatenate(
        [heads_of(query_weight), heads_of(key_matrix), heads_of(value_matrix)], axis=2
    )
    gate_pieces, up_pieces = units_of(gate_weight), units_of(up_weight)

    input_float = f32(layer_input)
    scale_attn = inv_rms(input_float)
    normed_own = low(input_float * scale_attn * attn_norm)
    if on_line:
        normed_attn, qkv_all, out_all, gate_rows, up_rows, *near_down = first_gather(
            normed_own, qkv_pieces, output_weight, gate_pieces, up_pieces, down_weight
        )
    else:
        normed_attn = tokens_gather(normed_own)
        exchanged = lambda pieces: natural_plane(plane_exchange(own_plane(pieces, 0)), 0)
        qkv_all = line_gather(exchanged(qkv_pieces))
        out_all = full_gather(output_weight)
        gate_rows, up_rows = exchanged(gate_pieces), exchanged(up_pieces)
        near_down = None
    normed_attn = normed_attn.reshape(all_rows, model_width)
    qkv_all = qkv_all.reshape(model_width, head_part)
    out_all = out_all.reshape(-1, model_width)
    gate_rows = gate_rows.reshape(4 * weight_rows, hidden_part)
    up_rows = up_rows.reshape(4 * weight_rows, hidden_part)

    lengths_list = plane_lengths(doc_lengths)
    local_ids = jnp.arange(local_rows, dtype=jnp.int32)
    row_ids = jnp.concatenate([core * local_rows + local_ids, (1 - core) * local_rows + local_ids])
    segments, positions = jax.vmap(lambda lengths: doc_layout(lengths, row_ids))(lengths_list)
    cos_tab, sin_tab = rope_tables(positions.reshape(-1), HEAD_SIZE)
    tables = (
        jnp.concatenate([cos_tab, cos_tab], axis=1).reshape(4, group_rows, HEAD_SIZE),
        jnp.concatenate([-sin_tab, sin_tab], axis=1).reshape(4, group_rows, HEAD_SIZE),
        segments[:, :, None],
        segments[:, None, :],
        row_ids[:, None],
        row_ids[None, :],
        head_norms,
    )
    qkv_raw = matmul(normed_attn, qkv_all).reshape(2, 4, local_rows, head_part)
    qkv_low, attended_heads = attend(qkv_raw, tables)
    gate_all = line_gather(gate_rows, (attended_heads,)).reshape(model_width, hidden_part)
    if on_line:
        attended = heads_to_tokens(attended_heads)
    else:
        attended = natural_plane(
            plane_exchange([attended_heads[:, step].reshape(group_rows, -1) for step in range(4)]),
            0,
        )
    attended_own = attended
    attended = (
        attended.reshape(4, group_rows, query_part)
        .transpose(1, 0, 2)
        .reshape(group_rows, 4 * query_part)
    )
    hidden_state = input_float + pair_scatter(low(matmul(attended, out_all)))

    scale_mlp = inv_rms(hidden_state)
    normed_own = low(hidden_state * scale_mlp * mlp_norm)
    line_shape = (line_extent, 4 * weight_rows, hidden_part)
    grad_all = tokens_gather(after(grad_out, normed_attn), (attended_heads,))
    down_all = line_gather(
        after(down_weight, normed_attn), (attended_heads,), near_down
    ).reshape(hidden_part, model_width)
    if on_line:
        grad_blocks = grad_all.reshape(8, local_rows, model_width)
        rows_all, inner_low, gate_grad, up_grad, part_sums, grad_sums = units_products(
            normed_own, up_rows, gate_all, down_all, grad_blocks
        )
        mlp_row_grad, mlp_rows, grad_down, grad_gate_part, grad_up_part = unit_grads(
            rows_all, grad_blocks, inner_low, gate_grad, up_grad, part_sums, grad_sums
        )
        grad_down = f32(grad_down)
        grad_gate_part = grad_gate_part.reshape(line_shape)
        grad_up_part = grad_up_part.reshape(line_shape)
    else:
        normed_mlp, up_all = tokens_gather(normed_own), line_gather(up_rows)
        normed_mlp = normed_mlp.reshape(all_rows, model_width)
        up_all = up_all.reshape(model_width, hidden_part)
        gate_raw = matmul(normed_mlp, gate_all)
        up_raw = matmul(normed_mlp, up_all)
        activated = jax.nn.silu(gate_raw)
        inner_low = low(activated * up_raw)
        grad_down_part = low(matmul_tn(inner_low, grad_all))
        mlp_rows = tokens_scatter(low(matmul(inner_low, down_all)))
        inner_grad = matmul_nt(grad_all, down_all)
        sigmoid_gate = jax.nn.sigmoid(gate_raw)
        gate_grad = low(
            inner_grad * up_raw * sigmoid_gate * (1.0 + gate_raw * (1.0 - sigmoid_gate))
        )
        up_grad = low(inner_grad * activated)
        grad_gate_part = low(matmul_tn(normed_mlp, gate_grad)).reshape(line_shape)
        grad_up_part = low(matmul_tn(normed_mlp, up_grad)).reshape(line_shape)
        mlp_row_grad = tokens_scatter(
            low(matmul_nt(gate_grad, gate_all) + matmul_nt(up_grad, up_all))
        )
        grad_down = line_scatter(grad_down_part.reshape(line_extent, down_rows, model_width))
    layer_out = low(hidden_state + mlp_rows)

    if on_line:
        (
            hidden_grad,
            mlp_gain_part,
            head_gains,
            grad_qkv_part,
            grad_proj_part,
            grad_sums,
            grad_gate_columns,
            grad_up_columns,
        ) = heads_backward(
            hidden_state,
            mlp_row_grad,
            grad_out,
            mlp_norm[None],
            out_all,
            attended_own,
            qkv_raw,
            qkv_low,
            tables,
            normed_attn.reshape(8, local_rows, model_width),
            qkv_all,
            grad_gate_part,
            grad_up_part,
        )
        grad_input, grad_qkv_columns, grad_out_proj, gains = last_sums(
            grad_sums,
            grad_qkv_part.reshape(4, 4 * weight_rows, head_part),
            grad_proj_part.reshape(4, output_weight.shape[0], model_width),
            layer_input,
            hidden_grad,
            attn_norm[None],
            jnp.concatenate([mlp_gain_part, head_gains], axis=1),
        )
        gains = gains.reshape(-1)
        grad_out_proj = f32(grad_out_proj)
    else:
        hidden_norm_grad, mlp_gain_part = norm_back(
            hidden_state, scale_mlp, mlp_norm, mlp_row_grad
        )
        hidden_grad = f32(grad_out) + hidden_norm_grad
        branch_grad = pair_gather(low(hidden_grad))
        attended_grad = low(matmul_nt(branch_grad, out_all))
        split = attended_grad.reshape(group_rows, 4, query_part).transpose(1, 0, 2)
        heads_grad = plane_exchange(own_plane(split, 0))
        grad_proj_part = full_scatter_plane(low(matmul_tn(attended, branch_grad)))
        back = [
            attend_back_values(
                qkv_raw[:, step].reshape(group_rows, head_part),
                qkv_low[:, step].reshape(group_rows, head_part),
                heads_grad[step],
                (segments[step][:, None] == segments[step][None, :])
                & (row_ids[None, :] <= row_ids[:, None]),
                tables[0][step],
                tables[1][step],
                head_norms,
                lambda values: jnp.roll(values, HEAD_SIZE // 2, 1),
            )
            for step in range(4)
        ]
        qkv_grad = jnp.stack([grads for grads, _ in back]).reshape(4, 2, local_rows, head_part)
        qkv_grad = qkv_grad.transpose(1, 0, 2, 3).reshape(all_rows, head_part)
        grad_qkv_part = low(matmul_tn(normed_attn, qkv_grad)).reshape(
            line_extent, 4 * weight_rows, head_part
        )
        attn_row_grad = tokens_scatter(low(matmul_nt(qkv_grad, qkv_all)))
        grad_rows = lambda part: low(line_scatter(part))
        grad_qkv_columns = exchanged(
            grad_rows(grad_qkv_part).reshape(4, weight_rows, head_part)
        )
        grad_gate_columns = exchanged(
            grad_rows(grad_gate_part).reshape(4, weight_rows, hidden_part)
        )
        grad_up_columns = exchanged(grad_rows(grad_up_part).reshape(4, weight_rows, hidden_part))
        grad_out_proj = line_scatter(grad_proj_part)
        input_norm_grad, attn_gain_part = norm_back(
            input_float, scale_attn, attn_norm, attn_row_grad
        )
        grad_input = hidden_grad + input_norm_grad
        head_gains = sum(gains for _, gains in back)[0]
        gains = total_sum(
            jnp.concatenate([attn_gain_part, mlp_gain_part, head_gains]).reshape(-1, HEAD_SIZE)
        ).reshape(-1)

    def heads_back(pieces):
        return f32(pieces).transpose(1, 0, 2).reshape(weight_rows, -1)

    def units_back(pieces):
        split = f32(pieces).reshape(4, weight_rows, line_extent, down_rows)
        return split.transpose(1, 2, 0, 3).reshape(weight_rows, -1)

    return (
        layer_out,
        grad_input,
        gains[:model_width],
        gains[2 * model_width :].reshape(2, HEAD_SIZE),
        heads_back(grad_qkv_columns[:, :, :query_part]),
        heads_back(grad_qkv_columns[:, :, query_part : query_part + HEAD_SIZE]),
        heads_back(grad_qkv_columns[:, :, query_part + HEAD_SIZE :]),
        grad_out_proj,
        gains[model_width : 2 * model_width],
        units_back(grad_gate_columns),
        units_back(grad_up_columns),
        grad_down,
    )


def solution(mesh):
    dp, tensor = mesh.shape["dp"], mesh.shape["tensor"]
    fine = Mesh(mesh.devices.reshape(dp // 4, 2, 2, tensor), ("f", "ty", "tx", "tensor"))
    rows = ("f", "ty", "tx")
    tokens = P(rows + ("tensor",), None)
    grid = P(rows, "tensor")
    units = P(("tensor",) + rows, None)
    return jax.shard_map(
        shards,
        mesh=fine,
        in_specs=(
            tokens, P(), P(), grid, grid, grid, units, P(), grid, grid, units, tokens, P(rows, None),
        ),
        out_specs=(tokens, tokens, P(), P(), grid, grid, grid, units, P(), grid, grid, units),
        check_vma=False,
    )
```

```python
import jax
import jax.numpy as jnp
from jax import lax
from jax.experimental import pallas as pl
from jax.experimental.pallas import tpu as pltpu
from jax.sharding import Mesh, PartitionSpec as P

QUERY_HEADS = 16
KEY_VALUE_HEADS = 8
HEAD_SIZE = 128


EPS = 1e-06
ROPE_BASE = 1000000.0
MASKED = -1e30
LOW = jnp.bfloat16


def matmul(left_mat, right_mat):
    return jnp.dot(left_mat, right_mat, preferred_element_type=jnp.float32)


def matmul_tn(left_mat, right_mat):
    return lax.dot_general(
        left_mat, right_mat, (((0,), (0,)), ((), ())), preferred_element_type=jnp.float32
    )


def matmul_nt(left_mat, right_mat):
    return lax.dot_general(
        left_mat, right_mat, (((1,), (1,)), ((), ())), preferred_element_type=jnp.float32
    )


def inv_rms(values):
    return lax.rsqrt(jnp.mean(values * values, axis=-1, keepdims=True) + EPS)


def norm_back(values, scales, gain_row, upstream):
    weighted = upstream * gain_row
    inner_mean = jnp.mean(weighted * values, axis=-1, keepdims=True)
    value_grad = scales * weighted - values * (scales * scales * scales) * inner_mean
    lead_axes = tuple(range(upstream.ndim - 1))
    return (value_grad, jnp.sum(upstream * values * scales, axis=lead_axes))


def rope_tables(position, head_width):
    half_dim = head_width // 2
    inverse = ROPE_BASE ** (-(jnp.arange(half_dim, dtype=jnp.float32) * (2.0 / head_width)))
    angles = position.astype(jnp.float32)[:, None] * inverse[None, :]
    return (jnp.cos(angles), jnp.sin(angles))


def rotate(values, cos_tab, sin_tab, direction):
    half_dim = values.shape[-1] // 2
    first_half = values[..., :half_dim]
    second_half = values[..., half_dim:]
    cosine = cos_tab[:, None, :]
    sine_tab = direction * sin_tab[:, None, :]
    return jnp.concatenate(
        [
            first_half * cosine - second_half * sine_tab,
            second_half * cosine + first_half * sine_tab,
        ],
        axis=-1,
    )


def doc_layout(lengths_row, row_ids):
    doc_ends = jnp.cumsum(lengths_row, dtype=jnp.int32)
    document_segment = jnp.sum(
        (row_ids[:, None] >= doc_ends[None, :]).astype(jnp.int32), axis=1, dtype=jnp.int32
    )
    doc_starts = doc_ends - lengths_row
    member = document_segment[:, None] == jnp.arange(lengths_row.shape[0], dtype=jnp.int32)[None, :]
    start_of = jnp.sum(jnp.where(member, doc_starts[None, :], 0), axis=1, dtype=jnp.int32)
    return (document_segment, row_ids - start_of)


def f32(values):
    return values.astype(jnp.float32)


def low(values):
    return values.astype(LOW)


def swap(block, axis):
    return lax.ppermute(block, axis, [(0, 1), (1, 0)])


def plane_index():
    return 2 * lax.axis_index("ty") + lax.axis_index("tx")


def plane_gather(block):
    across_x = swap(block, "tx")
    across_y = swap(block, "ty")
    return [block, across_x, across_y, swap(across_y, "tx")]


def plane_scatter(parts):
    own, for_x, for_y, for_far = parts
    for_y = low(f32(for_y) + f32(swap(for_far, "tx")))
    return f32(own) + f32(swap(for_x, "tx")) + f32(swap(for_y, "ty"))


def plane_exchange(parts):
    own, for_x, for_y, for_far = parts
    return [own, swap(for_x, "tx"), swap(for_y, "ty"), swap(swap(for_far, "tx"), "ty")]


def plane_lengths(lengths):
    return jnp.concatenate(plane_gather(lengths))


def line_gather(block):
    return lax.all_gather(block, "f", axis=0)


def line_scatter(parts):
    return f32(lax.psum_scatter(parts, "f", scatter_dimension=0))


def natural_plane(blocks, axis):
    own = plane_index()
    shape = list(blocks[0].shape)
    shape.insert(axis, 4)
    whole = jnp.zeros(shape, blocks[0].dtype)
    for step in range(4):
        whole = lax.dynamic_update_index_in_dim(whole, blocks[step], own ^ step, axis)
    return whole


def own_plane(whole, axis):
    own = plane_index()
    return [
        lax.dynamic_index_in_dim(whole, own ^ step, axis, keepdims=False) for step in range(4)
    ]


def full_gather(rows_block):
    rows, width = rows_block.shape
    line = line_gather(rows_block)
    extent = line.shape[0]
    blocks = plane_gather(line.reshape(extent * rows, width))
    whole = natural_plane([block.reshape(extent, rows, width) for block in blocks], 1)
    return whole.reshape(extent * 4 * rows, width)


def full_scatter_plane(partial):
    extent = lax.axis_size("f")
    rows, width = partial.shape[0] // (4 * extent), partial.shape[1]
    parts = own_plane(partial.reshape(extent, 4, rows, width), 1)
    plane_sum = plane_scatter([part.reshape(extent * rows, width) for part in parts])
    return low(plane_sum).reshape(extent, rows, width)


def tokens_gather(block):
    near = plane_gather(block)
    return jnp.concatenate(near + [swap(piece, "tensor") for piece in near])


def tokens_scatter(partial):
    rows = partial.shape[0] // 8
    near = []
    for step in range(4):
        mine = partial[step * rows : (step + 1) * rows]
        other = swap(partial[(4 + step) * rows : (5 + step) * rows], "tensor")
        near.append(low(f32(mine) + f32(other)))
    return plane_scatter(near)


def pair_gather(block):
    return jnp.concatenate([block, swap(block, "tensor")])


def pair_scatter(partial):
    rows = partial.shape[0] // 2
    return f32(partial[:rows]) + f32(swap(partial[rows:], "tensor"))


def total_sum(values):
    return lax.psum(values, ("f", "ty", "tx", "tensor"))


class Place:
    def __init__(self):
        self.z = lax.axis_index("f")
        self.ty = lax.axis_index("ty")
        self.tx = lax.axis_index("tx")
        self.core = lax.axis_index("tensor")
        self.p = 2 * self.ty + self.tx
        self.px = 2 * self.ty + 1 - self.tx
        self.py = 2 * (1 - self.ty) + self.tx
        self.pd = 2 * (1 - self.ty) + 1 - self.tx
        self.x = {"tx": 1 - self.tx}
        self.y = {"ty": 1 - self.ty}
        self.d = {"tx": 1 - self.tx, "ty": 1 - self.ty}
        self.pair = {"tensor": 1 - self.core}
        self.up = {"f": self.z + 1}
        self.down = {"f": self.z - 1}
        self.two = {"f": (self.z + 2) % 4}

    def at(self, step):
        return (self.z + step) % 4


def remote(src, dst, send, recv, to):
    return pltpu.make_async_remote_copy(
        src_ref=src,
        dst_ref=dst,
        send_sem=send,
        recv_sem=recv,
        device_id=to,
        device_id_type=pl.DeviceIdType.MESH,
    )


def arrived(dst, recv, to):
    remote(dst, dst, recv, recv, to).wait_recv()


def greet(place, partners, line):
    barrier = pltpu.get_barrier_semaphore()
    for to in partners:
        pl.semaphore_signal(barrier, inc=1, device_id=to, device_id_type=pl.DeviceIdType.MESH)
    if not line:
        pl.semaphore_wait(barrier, len(partners))
        return

    @pl.when(place.z > 0)
    def _():
        pl.semaphore_signal(
            barrier, inc=1, device_id=place.down, device_id_type=pl.DeviceIdType.MESH
        )

    @pl.when(place.z < 3)
    def _():
        pl.semaphore_signal(barrier, inc=1, device_id=place.up, device_id_type=pl.DeviceIdType.MESH)

    pl.semaphore_signal(barrier, inc=1, device_id=place.two, device_id_type=pl.DeviceIdType.MESH)
    pl.semaphore_wait(barrier, len(partners) + 2 + (place.z + 1) // 2 % 2)


class LineGather:
    def __init__(self, place, own, slot, send, recv):
        self.place, self.own, self.slot, self.send, self.recv = place, own, slot, send, recv
        here = slot(place.z)
        self.to_down = remote(own, here, send.at[0], recv.at[1], place.down)
        self.to_up = remote(own, here, send.at[1], recv.at[3], place.up)
        self.to_two = remote(own, here, send.at[2], recv.at[2], place.two)
        two = slot(place.at(2))
        self.pass_down = remote(two, two, send.at[3], recv.at[3], place.down)
        self.pass_up = remote(two, two, send.at[3], recv.at[1], place.up)

    def start(self):
        pl.when(self.place.z > 0)(self.to_down.start)
        pl.when(self.place.z < 3)(self.to_up.start)
        self.to_two.start()

    def step(self, turn):
        if turn == 2:
            return 2
        if turn == 1:
            return jnp.where(self.place.z == 3, 3, 1)
        return jnp.where(self.place.z == 3, 1, 3)

    def wait(self, turn):
        step = self.step(turn)
        slot = self.slot(self.place.at(step))
        arrived(slot, self.recv.at[step], self.place.two)
        if turn == 2:
            pl.when(self.place.z == 1)(self.pass_down.start)
            pl.when(self.place.z == 2)(self.pass_up.start)

    def finish(self):
        pl.when(self.place.z > 0)(self.to_down.wait_send)
        pl.when(self.place.z < 3)(self.to_up.wait_send)
        self.to_two.wait_send()
        pl.when(self.place.z == 1)(self.pass_down.wait_send)
        pl.when(self.place.z == 2)(self.pass_up.wait_send)


class PlaneGather:
    def __init__(self, place, own, slot, rows, send, recv):
        half = rows // 2
        whole, top, end = pl.ds(0, rows), pl.ds(0, half), pl.ds(half, half)
        self.place, self.recv = place, recv
        self.to_x = remote(own, slot(place.p, whole), send.at[0], recv.at[0], place.x)
        self.to_y = remote(own, slot(place.p, whole), send.at[1], recv.at[1], place.y)
        self.from_x, self.from_y = slot(place.px, whole), slot(place.py, whole)
        self.far_top, self.far_end = slot(place.pd, top), slot(place.pd, end)
        pass_x, pass_y = slot(place.py, top), slot(place.px, end)
        self.pass_x = remote(pass_x, pass_x, send.at[2], recv.at[2], place.x)
        self.pass_y = remote(pass_y, pass_y, send.at[3], recv.at[3], place.y)

    def start(self):
        self.to_x.start()
        self.to_y.start()

    def forward(self):
        arrived(self.from_y, self.recv.at[1], self.place.y)
        self.pass_x.start()
        arrived(self.from_x, self.recv.at[0], self.place.x)
        self.pass_y.start()

    def wait_far(self):
        arrived(self.far_top, self.recv.at[2], self.place.x)
        arrived(self.far_end, self.recv.at[3], self.place.y)

    def finish(self):
        self.to_x.wait_send()
        self.to_y.wait_send()
        self.pass_x.wait_send()
        self.pass_y.wait_send()


ANYWHERE = pl.BlockSpec(memory_space=pl.ANY)
WHOLE = pl.BlockSpec(memory_space=pltpu.VMEM)


class Marks:
    def __init__(self, ref):
        self.ref, self.used = ref, 0

    def take(self, count=1):
        first = self.used
        self.used += count
        return self.ref.at[first] if count == 1 else self.ref.at[pl.ds(first, count)]


def each_rows(rows, chunk, work):
    def body(index, carry):
        work(pl.ds(pl.multiple_of(index * chunk, chunk), chunk))
        return carry

    lax.fori_loop(0, rows // chunk, body, 0)


class TokensGather:
    def __init__(self, place, own, whole, marks):
        half = own.shape[0] // 2
        top, end = pl.ds(0, half), pl.ds(half, half)
        self.place, self.whole = place, whole
        self.copy = pltpu.make_async_copy(own, whole.at[0], marks.take())
        self.recv = [marks.take() for _ in range(8)]
        x, y, pair = place.x, place.y, place.pair
        self.to_x = remote(own, whole.at[1], marks.take(), self.recv[0], x)
        self.to_y = remote(own, whole.at[2], marks.take(), self.recv[1], y)
        self.pass_x = remote(
            whole.at[2, top], whole.at[3, top], marks.take(), self.recv[2], x
        )
        self.pass_y = remote(
            whole.at[1, end], whole.at[3, end], marks.take(), self.recv[3], y
        )
        self.to_pair = [
            remote(
                own if step == 0 else whole.at[step],
                whole.at[4 + step],
                marks.take(),
                self.recv[4 + step],
                pair,
            )
            for step in range(4)
        ]
        self.far = (whole.at[3, top], whole.at[3, end])

    def start(self):
        self.to_x.start()
        self.to_y.start()
        self.to_pair[0].start()
        self.copy.start()

    def forward(self):
        arrived(self.whole.at[2], self.recv[1], self.place.y)
        self.pass_x.start()
        arrived(self.whole.at[1], self.recv[0], self.place.x)
        self.pass_y.start()
        self.to_pair[2].start()
        self.to_pair[1].start()

    def last(self):
        arrived(self.far[0], self.recv[2], self.place.x)
        arrived(self.far[1], self.recv[3], self.place.y)
        self.to_pair[3].start()

    def finish(self):
        for step in range(4):
            arrived(self.whole.at[4 + step], self.recv[4 + step], self.place.pair)
        for copy in [self.to_x, self.to_y, self.pass_x, self.pass_y] + self.to_pair:
            copy.wait_send()
        self.copy.wait()


class Exchange:
    def __init__(self, place, piece, slot, marks):
        self.place = place
        there = ((place.px, place.x), (place.py, place.y), (place.pd, place.d))
        self.copy = pltpu.make_async_copy(piece(place.p, 0), slot(place.p, 0), marks.take())
        self.sends, self.slots = [], []
        for index, (p, to) in enumerate(there):
            recv = marks.take()
            self.sends.append(
                remote(piece(p, index + 1), slot(place.p, index + 1), marks.take(), recv, to)
            )
            self.slots.append((slot(p, index + 1), recv, to))

    def start(self):
        for copy in (self.sends[2], self.sends[0], self.sends[1], self.copy):
            copy.start()

    def wait(self):
        self.copy.wait()
        for slot, recv, to in self.slots:
            arrived(slot, recv, to)

    def finish(self):
        for copy in self.sends:
            copy.wait_send()


class LineScatter:
    @staticmethod
    def scratch(rows, width):
        return [pltpu.VMEM((6, rows, width), LOW)]

    def __init__(self, place, part, out, buffers, marks):
        self.place, self.out = place, out
        self.kept = buffers[0]
        self.rows = self.kept.shape[1]
        self.passed, self.above, self.below, self.two, self.mid, self.own = (
            self.kept.at[index] for index in range(6)
        )
        self.recv = [marks.take() for _ in range(4)]
        z = place.z
        self.pass_up = remote(part(3), self.passed, marks.take(), self.recv[0], place.up)
        self.pass_down = remote(part(0), self.passed, marks.take(), self.recv[0], place.down)
        self.to_down = remote(
            part(place.at(3)), self.above, marks.take(), self.recv[1], place.down
        )
        self.to_up = remote(part(place.at(1)), self.below, marks.take(), self.recv[2], place.up)
        self.to_two = remote(self.mid, self.two, marks.take(), self.recv[3], place.two)
        self.load_mid = pltpu.make_async_copy(part(place.at(2)), self.mid, marks.take())
        self.load_own = pltpu.make_async_copy(part(z), self.own, marks.take())

    def start(self):
        z = self.place.z
        pl.when(z == 0)(self.pass_up.start)
        pl.when(z == 3)(self.pass_down.start)
        self.load_mid.start()
        pl.when(z > 0)(self.to_down.start)
        pl.when(z < 3)(self.to_up.start)
        self.load_own.start()
        self.load_mid.wait()
        pl.when((z == 0) | (z == 3))(self.to_two.start)

    def middle(self):
        z = self.place.z

        @pl.when((z == 1) | (z == 2))
        def _():
            arrived(self.passed, self.recv[0], self.place.two)

            def work(rows):
                self.kept[4, rows] = low(f32(self.kept[4, rows]) + f32(self.kept[0, rows]))

            each_rows(self.rows, 16, work)
            self.to_two.start()

    def finish(self):
        z, rows_all = self.place.z, self.rows
        out, kept = self.out, self.kept
        self.load_own.wait()

        @pl.when(z < 3)
        def _():
            arrived(self.above, self.recv[1], self.place.two)

            def work(rows):
                kept[5, rows] = low(f32(kept[5, rows]) + f32(kept[1, rows]))

            each_rows(rows_all, 16, work)

        @pl.when(z > 0)
        def _():
            arrived(self.below, self.recv[2], self.place.two)

            def work(rows):
                kept[5, rows] = low(f32(kept[5, rows]) + f32(kept[2, rows]))

            each_rows(rows_all, 16, work)

        arrived(self.two, self.recv[3], self.place.two)

        def work(rows):
            out[rows] = low(f32(kept[5, rows]) + f32(kept[3, rows]))

        each_rows(rows_all, 16, work)

    def drain(self):
        z = self.place.z
        pl.when(z == 0)(self.pass_up.wait_send)
        pl.when(z == 3)(self.pass_down.wait_send)
        pl.when(z > 0)(self.to_down.wait_send)
        pl.when(z < 3)(self.to_up.wait_send)
        self.to_two.wait_send()


def comm_params(number):
    return pltpu.CompilerParams(
        collective_id=number, has_side_effects=True, vmem_limit_bytes=62 * 1024 * 1024
    )


def comm_cost(micros):
    return pl.CostEstimate(flops=0, bytes_accessed=micros * 3_000_000, transcendentals=0)


def tables_of(lengths_row, id_col, id_row, inverse, count):
    zero = jnp.zeros((1, 1), jnp.int32)
    segment_col, segment_row = jnp.zeros_like(id_col), jnp.zeros_like(id_row)
    ends, starts, end = [], [], zero
    for index in range(count):
        starts.append(end)
        end = end + lengths_row[:, index : index + 1]
        ends.append(end)
        segment_col = segment_col + jnp.where(id_col >= end, 1, 0)
        segment_row = segment_row + jnp.where(id_row >= end, 1, 0)
    start_of = jnp.zeros_like(id_col)
    for index in range(count):
        start_of = start_of + jnp.where(segment_col == index, starts[index], 0)
    angles = f32(id_col - start_of) * inverse
    return segment_col, segment_row, jnp.cos(angles), jnp.sin(angles)


def first_kernel(
    documents,
    rows_ref,
    qkv_ref,
    out_ref,
    gate_ref,
    up_ref,
    down_ref,
    lengths_ref,
    id_col,
    id_row,
    inverse_ref,
    head_norms,
    input_ref,
    norm_ref,
    rows_all,
    gate_rows,
    up_rows,
    gate_all,
    above_ref,
    below_ref,
    qkv_all,
    out_all,
    raw_out,
    low_out,
    cos_out,
    sin_out,
    segment_col,
    segment_row,
    attended,
    hidden,
    normed,
    marks_ref,
    lengths_all,
    row_block,
    heads_stage,
    pair_stage,
    pair_got,
):
    place = Place()
    marks = Marks(marks_ref)
    greet(place, [place.x, place.y, place.d, place.pair], True)
    rows, width = rows_ref.shape
    head_part = raw_out.shape[3]
    heads = head_part // HEAD_SIZE - 2
    lengths = Exchange(
        place, lambda p, step: lengths_ref, lambda p, step: lengths_all.at[step], marks
    )
    qkv_pieces = Exchange(
        place, lambda p, step: qkv_ref.at[p], lambda p, step: qkv_all.at[place.z, p], marks
    )
    gate_pieces = Exchange(
        place, lambda p, step: gate_ref.at[p], lambda p, step: gate_rows.at[p], marks
    )
    up_pieces = Exchange(place, lambda p, step: up_ref.at[p], lambda p, step: up_rows.at[p], marks)
    tokens = TokensGather(place, rows_ref, rows_all, marks)
    qkv_line = LineGather(
        place, qkv_all.at[place.z], lambda z: qkv_all.at[z], marks.take(4), marks.take(4)
    )
    gate_line = LineGather(
        place, gate_rows, lambda z: gate_all.at[z], marks.take(4), marks.take(4)
    )
    out_line = LineGather(
        place, out_ref, lambda z: out_all.at[z, place.p], marks.take(4), marks.take(4)
    )
    own_copies = [
        pltpu.make_async_copy(out_ref, out_all.at[place.z, place.p], marks.take()),
    ]
    gate_copy = pltpu.make_async_copy(gate_rows, gate_all.at[place.z], marks.take())
    near_recv = [marks.take(), marks.take()]
    to_down = remote(down_ref, above_ref, marks.take(), near_recv[0], place.down)
    to_up = remote(down_ref, below_ref, marks.take(), near_recv[1], place.up)
    out_planes = []
    for turn in range(4):
        z = place.z if turn == 0 else place.at(out_line.step(turn))
        out_planes.append(
            PlaneGather(
                place,
                out_ref if turn == 0 else out_all.at[z, place.p],
                lambda p, part, z=z: out_all.at[z, p, part],
                out_ref.shape[0],
                marks.take(4),
                marks.take(4),
            )
        )
    heads_out = Exchange(
        place, lambda p, step: heads_stage.at[step], lambda p, step: attended.at[p], marks
    )
    to_pair = remote(pair_stage, pair_got, marks.take(), marks.take(), place.pair)
    fetch_marks = marks.take(2)

    lengths.start()
    qkv_pieces.start()
    tokens.start()
    for copy in own_copies:
        copy.start()
    lengths.wait()
    qkv_pieces.wait()
    qkv_line.start()

    def table_work(step, carry):
        seg_col, seg_row, cosine, sine = tables_of(
            lengths_all[step][:1], id_col[...], id_row[...], inverse_ref[...], documents
        )
        segment_col[step] = seg_col
        segment_row[step] = seg_row
        cos_out[step] = cosine
        lane = lax.broadcasted_iota(jnp.int32, sine.shape, 1)
        sin_out[step] = jnp.where(lane < HEAD_SIZE // 2, -sine, sine)
        return carry

    lax.fori_loop(0, 2, table_work, 0)
    tokens.forward()
    out_planes[0].start()
    lax.fori_loop(2, 4, table_work, 0)
    qkv_line.wait(1)
    qkv_line.wait(2)
    out_line.start()
    tokens.last()
    out_planes[0].forward()
    gate_pieces.start()
    qkv_line.wait(3)
    tokens.finish()

    def fetches(step):
        return (
            pltpu.make_async_copy(rows_all.at[step], row_block.at[0], fetch_marks.at[0]),
            pltpu.make_async_copy(rows_all.at[4 + step], row_block.at[1], fetch_marks.at[1]),
        )

    def bucket(turn, carry):
        step = 3 - turn
        for copy in fetches(step):
            copy.start()
        for copy in fetches(step):
            copy.wait()
        raw = matmul(
            row_block[...].reshape(2 * rows, width), qkv_all[...].reshape(width, head_part)
        )
        raw_out[0, step] = raw[:rows]
        raw_out[1, step] = raw[rows:]
        allowed = (segment_col[step] == segment_row[step]) & (id_row[...] <= id_col[...])
        turned = []
        for head in range(heads + 1):
            gain = head_norms[min(head // heads, 1)][None, :]
            unnormed = lanes(raw, head)
            turned.append(
                low(
                    turn_pairs(
                        unnormed * inv_rms(unnormed) * gain, cos_out[step], sin_out[step]
                    )
                )
            )
        value = low(lanes(raw, heads + 1))
        outs = [
            low(matmul(low(softmax_of(turned[head], turned[heads], allowed)), value))
            for head in range(heads)
        ]
        kept = jnp.concatenate(turned + [value], axis=1)
        low_out[0, step] = kept[:rows]
        low_out[1, step] = kept[rows:]
        outs = jnp.concatenate(outs, axis=1)
        heads_stage[step, 0] = outs[:rows]
        heads_stage[step, 1] = outs[rows:]
        for index, at in enumerate((1, 2, 3)):
            pl.when(step == at)(heads_out.sends[index].start)
        pl.when(step == 0)(heads_out.copy.start)
        return carry

    lax.fori_loop(0, 1, bucket, 0)
    out_line.wait(1)
    out_planes[1].start()
    gate_pieces.wait()
    out_line.wait(2)
    gate_line.start()
    gate_copy.start()
    out_planes[2].start()
    lax.fori_loop(1, 2, bucket, 0)
    out_line.wait(3)
    out_planes[3].start()
    out_planes[1].forward()
    lax.fori_loop(2, 3, bucket, 0)
    out_planes[2].forward()
    out_planes[3].forward()
    lax.fori_loop(3, 4, bucket, 0)
    for plane in out_planes:
        plane.wait_far()
    for copy in own_copies:
        copy.wait()
    heads_out.wait()
    gate_line.wait(2)
    pl.when(place.z > 0)(to_down.start)
    pl.when(place.z < 3)(to_up.start)

    def projected(core_step):
        block = jnp.concatenate([attended[p, core_step] for p in range(4)], axis=1)
        return matmul(block, out_all[...].reshape(block.shape[1], width))

    pair_stage[...] = low(projected(1))
    to_pair.start()
    up_pieces.start()
    hidden[...] = f32(input_ref[...]) + projected(0)
    to_pair.wait()
    norm_row = norm_ref[...]

    def norm_work(part):
        values = hidden[part] + f32(pair_got[part])
        hidden[part] = values
        normed[part] = low(values * inv_rms(values) * norm_row)

    each_rows(rows, 16, norm_work)
    gate_line.wait(1)
    gate_line.wait(3)
    up_pieces.wait()
    gate_copy.wait()
    parts = [lengths, qkv_pieces, gate_pieces, up_pieces, heads_out, qkv_line, gate_line, out_line]
    for part in parts + out_planes:
        part.finish()

    @pl.when(place.z < 3)
    def _():
        arrived(above_ref, near_recv[0], place.two)
        to_up.wait_send()

    @pl.when(place.z > 0)
    def _():
        arrived(below_ref, near_recv[1], place.two)
        to_down.wait_send()


def first_part(
    rows,
    qkv_pieces,
    output_weight,
    gate_pieces,
    up_pieces,
    down_weight,
    doc_lengths,
    row_ids,
    head_norms,
    layer_input,
    mlp_norm,
):
    block_rows, width = rows.shape
    group_rows = 2 * block_rows
    weight_rows, head_part = qkv_pieces.shape[1:]
    query_part = head_part - 2 * HEAD_SIZE
    documents = doc_lengths.shape[1]
    lengths = jnp.pad(doc_lengths, ((0, 7), (0, HEAD_SIZE - documents)))
    half = jnp.arange(HEAD_SIZE // 2, dtype=jnp.float32)
    inverse = ROPE_BASE ** (-(half * (2.0 / HEAD_SIZE)))
    low_like = lambda *shape: jax.ShapeDtypeStruct(shape, LOW)
    table = jax.ShapeDtypeStruct((4, group_rows, HEAD_SIZE), jnp.float32)
    return pl.pallas_call(
        lambda *refs: first_kernel(documents, *refs),
        out_shape=(
            low_like(8, block_rows, width),
            low_like(*gate_pieces.shape),
            low_like(*up_pieces.shape),
            low_like(4, *gate_pieces.shape),
            low_like(*down_weight.shape),
            low_like(*down_weight.shape),
            low_like(4, *qkv_pieces.shape),
            low_like(4, 4, *output_weight.shape),
            jax.ShapeDtypeStruct((2, 4, block_rows, head_part), jnp.float32),
            low_like(2, 4, block_rows, head_part),
            table,
            table,
            jax.ShapeDtypeStruct((4, group_rows, 1), jnp.int32),
            jax.ShapeDtypeStruct((4, 1, group_rows), jnp.int32),
            low_like(4, 2, block_rows, query_part),
            jax.ShapeDtypeStruct((block_rows, width), jnp.float32),
            low_like(block_rows, width),
        ),
        in_specs=[ANYWHERE] * 6 + [WHOLE] * 7,
        out_specs=(ANYWHERE,) * 6 + (WHOLE,) * 11,
        scratch_shapes=[
            pltpu.SemaphoreType.DMA((140,)),
            pltpu.VMEM((4,) + lengths.shape, jnp.int32),
            pltpu.VMEM((2, block_rows, width), LOW),
            pltpu.VMEM((4, 2, block_rows, query_part), LOW),
            pltpu.VMEM((block_rows, width), LOW),
            pltpu.VMEM((block_rows, width), LOW),
        ],
        compiler_params=comm_params(0),
        cost_estimate=comm_cost(130),
    )(
        rows,
        qkv_pieces,
        output_weight,
        gate_pieces,
        up_pieces,
        down_weight,
        lengths,
        row_ids[:, None],
        row_ids[None, :],
        jnp.concatenate([inverse, inverse])[None],
        head_norms,
        layer_input,
        mlp_norm[None],
    )


class PlaneScatter:
    @staticmethod
    def scratch(rows, width):
        return [pltpu.VMEM((6, rows // 2, width), LOW)]

    def __init__(self, place, summed, out, buffers, marks, at=(0, 1, 2, 3)):
        self.place, self.summed, self.out, self.at = place, summed, out, at
        self.landed = buffers[0]
        self.rows = summed.shape[1]
        half = self.rows // 2
        top, end = pl.ds(0, half), pl.ds(half, half)
        x, y = place.x, place.y
        self.recv = [marks.take() for _ in range(6)]
        routes = (
            (summed.at[at[3], top], x),
            (summed.at[at[3], end], y),
            (summed.at[at[1], top], x),
            (summed.at[at[1], end], x),
            (summed.at[at[2], top], y),
            (summed.at[at[2], end], y),
        )
        self.sends = [
            remote(src, self.landed.at[index], marks.take(), self.recv[index], to)
            for index, (src, to) in enumerate(routes)
        ]

    def start(self):
        for index in (0, 1, 2, 5):
            self.sends[index].start()

    def landed_at(self, index, to):
        arrived(self.landed.at[index], self.recv[index], to)

    def middle(self):
        half = self.rows // 2
        summed, landed = self.summed, self.landed
        _, for_x, for_y, _ = self.at
        self.landed_at(0, self.place.x)

        def top_work(rows):
            summed[for_y, rows] = low(f32(summed[for_y, rows]) + f32(landed[0, rows]))

        each_rows(half, 16, top_work)
        self.sends[4].start()
        self.landed_at(1, self.place.y)

        def end_work(rows):
            end_rows = pl.ds(pl.multiple_of(rows.start + half, 16), rows.size)
            summed[for_x, end_rows] = low(f32(summed[for_x, end_rows]) + f32(landed[1, rows]))

        each_rows(half, 16, end_work)
        self.sends[3].start()

    def finish(self):
        half = self.rows // 2
        for index, to in ((2, self.place.x), (5, self.place.y), (4, self.place.y), (3, self.place.x)):
            self.landed_at(index, to)

        for base, first, second in ((0, 2, 4), (half, 3, 5)):

            def work(rows):
                own_rows = pl.ds(pl.multiple_of(rows.start + base, 16), rows.size)
                self.out[own_rows] = (
                    f32(self.summed[self.at[0], own_rows])
                    + f32(self.landed[first, rows])
                    + f32(self.landed[second, rows])
                ).astype(self.out.dtype)

            each_rows(half, 16, work)

    def drain(self):
        for copy in self.sends:
            copy.wait_send()


def units_kernel(
    rows_ref,
    upstream_ref,
    line_ref,
    gate_ref,
    down_ref,
    above_ref,
    below_ref,
    rows_all,
    upstream_all,
    inner_out,
    gate_grad_out,
    up_grad_out,
    part_sums,
    grad_sums,
    marks_ref,
    gate_mat,
    up_mat,
    down_mat,
    row_block,
    gate_raws,
    inner_grads,
    part_stage,
    grad_stage,
):
    place = Place()
    marks = Marks(marks_ref)
    greet(place, [place.x, place.y, place.pair], True)
    tokens = TokensGather(place, rows_ref, rows_all, marks)
    upstream = TokensGather(place, upstream_ref, upstream_all, marks)
    line = LineGather(place, line_ref, lambda z: up_mat.at[z], marks.take(4), marks.take(4))
    down_line = LineGather(
        place, down_ref, lambda z: down_mat.at[z], marks.take(4), marks.take(4)
    )
    copies = [
        pltpu.make_async_copy(line_ref, up_mat.at[place.z], marks.take()),
        pltpu.make_async_copy(gate_ref, gate_mat, marks.take()),
        pltpu.make_async_copy(down_ref, down_mat.at[place.z], marks.take()),
    ]
    above = pltpu.make_async_copy(above_ref, down_mat.at[place.at(1)], marks.take())
    below = pltpu.make_async_copy(below_ref, down_mat.at[place.at(3)], marks.take())
    fetch_marks = marks.take(2)
    send_marks, recv_marks = marks.take(8), marks.take(8)
    units = gate_mat.shape[1]
    width = rows_ref.shape[1]

    down_line.to_two.start()
    tokens.start()
    for copy in copies:
        copy.start()
    pl.when(place.z < 3)(above.start)
    pl.when(place.z > 0)(below.start)
    tokens.forward()
    upstream.start()
    down_line.wait(2)
    line.start()
    tokens.last()
    for copy in copies:
        copy.wait()
    pl.when(place.z < 3)(above.wait)
    pl.when(place.z > 0)(below.wait)
    tokens.finish()

    def blocks_of(source, first, last, work):
        def fetch(block):
            return pltpu.make_async_copy(
                source.at[block], row_block.at[block % 2], fetch_marks.at[block % 2]
            )

        fetch(first).start()

        def body(block, carry):
            fetch(block).wait()

            @pl.when(block < last - 1)
            def _():
                fetch(block + 1).start()

            work(block, row_block[block % 2])
            return carry

        lax.fori_loop(first, last, body, 0)

    def gate_work(block, values):
        gate_raws[block] = matmul(values, gate_mat[...])

    def inner_work(block, values):
        inner_grads[block] = matmul_nt(values, down_mat[...].reshape(units, width))

    upstream.forward()
    blocks_of(rows_all, 0, 8, gate_work)
    upstream.last()
    line.wait(2)

    @pl.when(place.z == 0)
    def _():
        arrived(down_mat.at[3], down_line.recv.at[3], place.two)

    @pl.when(place.z == 3)
    def _():
        arrived(down_mat.at[0], down_line.recv.at[1], place.two)

    upstream.finish()
    blocks_of(upstream_all, 0, 8, inner_work)
    line.wait(1)
    line.wait(3)

    def fetch(index):
        step, slot = 3 - index // 2, index % 2
        return pltpu.make_async_copy(
            rows_all.at[step + 4 * (1 - slot)], row_block.at[slot], fetch_marks.at[slot]
        )

    def sends(step):
        return (
            remote(
                part_stage.at[step],
                part_sums.at[step],
                send_marks.at[step],
                recv_marks.at[step],
                place.pair,
            ),
            remote(
                grad_stage.at[step],
                grad_sums.at[step],
                send_marks.at[4 + step],
                recv_marks.at[4 + step],
                place.pair,
            ),
        )

    fetch(0).start()

    def blocks(turn, carry):
        step = 3 - turn
        for slot in range(2):
            index = 2 * turn + slot
            block = step + 4 * (1 - slot)
            fetch(index).wait()

            @pl.when(index < 7)
            def _():
                fetch(index + 1).start()

            up_raw = matmul(row_block[slot], up_mat[...].reshape(-1, units))
            gate_raw, inner_grad = gate_raws[block], inner_grads[block]
            sigmoid_gate = jax.nn.sigmoid(gate_raw)
            activated = gate_raw * sigmoid_gate
            inner = low(activated * up_raw)
            gate_grad = low(
                inner_grad * up_raw * sigmoid_gate * (1.0 + gate_raw * (1.0 - sigmoid_gate))
            )
            up_grad = low(inner_grad * activated)
            inner_out[block] = inner
            gate_grad_out[block] = gate_grad
            up_grad_out[block] = up_grad
            part = matmul(inner, down_mat[...].reshape(units, width))
            grad = matmul_nt(gate_grad, gate_mat[...]) + matmul_nt(
                up_grad, up_mat[...].reshape(-1, units)
            )
            if slot == 0:
                part_stage[step] = low(part)
                grad_stage[step] = low(grad)
                for copy in sends(step):
                    copy.start()
            else:
                for copy in sends(step):
                    copy.wait_recv()
                part_sums[step] = low(part + f32(part_sums[step]))
                grad_sums[step] = low(grad + f32(grad_sums[step]))
        return carry

    lax.fori_loop(0, 4, blocks, 0)
    for step in range(4):
        for copy in sends(step):
            copy.wait_send()
    line.finish()
    down_line.to_two.wait_send()
    pl.when(place.z == 1)(down_line.pass_down.wait_send)
    pl.when(place.z == 2)(down_line.pass_up.wait_send)


def units_products(rows, upstream, up_rows, gate_all, down_weight, above, below):
    block_rows, width = rows.shape
    units = gate_all.shape[1]
    block = lambda count: pltpu.VMEM((count, block_rows, width), LOW)
    hidden = jax.ShapeDtypeStruct((8, block_rows, units), LOW)
    sums = jax.ShapeDtypeStruct((4, block_rows, width), LOW)
    blocks = jax.ShapeDtypeStruct((8, block_rows, width), LOW)
    return pl.pallas_call(
        units_kernel,
        out_shape=(blocks, blocks, hidden, hidden, hidden, sums, sums),
        in_specs=[ANYWHERE] * 7,
        out_specs=(ANYWHERE,) * 2 + (WHOLE,) * 5,
        scratch_shapes=[
            pltpu.SemaphoreType.DMA((100,)),
            pltpu.VMEM(gate_all.shape, LOW),
            pltpu.VMEM((4,) + up_rows.shape, LOW),
            pltpu.VMEM((4,) + down_weight.shape, LOW),
            block(2),
            pltpu.VMEM((8, block_rows, units), jnp.float32),
            pltpu.VMEM((8, block_rows, units), jnp.float32),
            block(4),
            block(4),
        ],
        compiler_params=comm_params(1),
        cost_estimate=comm_cost(130),
    )(rows, upstream, up_rows, gate_all, down_weight, above, below)


def unit_grads_kernel(
    rows_all,
    upstream_ref,
    inner_ref,
    gate_grad_ref,
    up_grad_ref,
    part_sums,
    grad_sums,
    row_grad,
    row_part,
    down_out,
    gate_part,
    up_part,
    marks_ref,
    upstream,
    inner,
    gate_grad,
    up_grad,
    row_slab,
    down_part,
    *buffers,
):
    place = Place()
    marks = Marks(marks_ref)
    greet(place, [place.x, place.y], True)
    grad_plane = PlaneScatter(place, grad_sums, row_grad, buffers[:1], marks)
    part_plane = PlaneScatter(place, part_sums, row_part, buffers[1:2], marks)
    down_rows = down_out.shape[0]
    down_line = LineScatter(
        place,
        lambda z: down_part.at[pl.ds(pl.multiple_of(z * down_rows, 16), down_rows)],
        down_out,
        buffers[2:],
        marks,
    )
    loads = [
        pltpu.make_async_copy(upstream_ref, upstream, marks.take()),
        pltpu.make_async_copy(inner_ref, inner, marks.take()),
        pltpu.make_async_copy(gate_grad_ref, gate_grad, marks.take()),
        pltpu.make_async_copy(up_grad_ref, up_grad, marks.take()),
    ]
    slab_marks = marks.take(2)
    tile = row_slab.shape[3]
    tiles = rows_all.shape[2] // tile
    units = inner.shape[2]
    all_rows = inner.shape[0] * inner.shape[1]

    def slab(index):
        return pltpu.make_async_copy(
            rows_all.at[:, :, pl.ds(pl.multiple_of(index * tile, tile), tile)],
            row_slab.at[index % 2],
            slab_marks.at[index % 2],
        )

    grad_plane.start()
    for copy in loads:
        copy.start()
    slab(0).start()
    loads[0].wait()
    loads[1].wait()

    def down_tile(index, carry):
        columns = pl.ds(pl.multiple_of(index * tile, tile), tile)
        down_part[columns] = low(
            matmul_tn(
                inner[:, :, columns].reshape(all_rows, tile),
                upstream[...].reshape(all_rows, upstream.shape[2]),
            )
        )
        return carry

    lax.fori_loop(0, units // tile, down_tile, 0)
    down_line.start()
    loads[2].wait()
    loads[3].wait()

    def row_tile(index, carry):
        slab(index).wait()

        @pl.when(index < tiles - 1)
        def _():
            slab(index + 1).start()

        columns = row_slab[index % 2].reshape(all_rows, tile)
        out_rows = pl.ds(pl.multiple_of(index * tile, tile), tile)
        gate_part[out_rows] = low(matmul_tn(columns, gate_grad[...].reshape(all_rows, units)))
        up_part[out_rows] = low(matmul_tn(columns, up_grad[...].reshape(all_rows, units)))
        return carry

    lax.fori_loop(0, tiles // 4, row_tile, 0)
    grad_plane.middle()
    down_line.middle()
    lax.fori_loop(tiles // 4, tiles, row_tile, 0)
    grad_plane.finish()
    part_plane.start()
    part_plane.middle()
    down_line.finish()
    part_plane.finish()
    down_line.drain()
    grad_plane.drain()
    part_plane.drain()


def unit_grads(rows_all, upstream, inner, gate_grad, up_grad, part_sums, grad_sums):
    _, block_rows, width = rows_all.shape
    units = inner.shape[2]
    down_rows = units // 4
    tile = 256
    return pl.pallas_call(
        unit_grads_kernel,
        out_shape=(
            jax.ShapeDtypeStruct((block_rows, width), jnp.float32),
            jax.ShapeDtypeStruct((block_rows, width), jnp.float32),
            jax.ShapeDtypeStruct((down_rows, width), LOW),
            jax.ShapeDtypeStruct((width, units), LOW),
            jax.ShapeDtypeStruct((width, units), LOW),
        ),
        in_specs=[ANYWHERE] * 5 + [WHOLE] * 2,
        out_specs=(WHOLE,) * 5,
        scratch_shapes=[
            pltpu.SemaphoreType.DMA((64,)),
            pltpu.VMEM(upstream.shape, LOW),
            pltpu.VMEM(inner.shape, LOW),
            pltpu.VMEM(inner.shape, LOW),
            pltpu.VMEM(inner.shape, LOW),
            pltpu.VMEM((2, 8, block_rows, tile), LOW),
            pltpu.VMEM((units, width), LOW),
        ]
        + PlaneScatter.scratch(block_rows, width) * 2
        + LineScatter.scratch(down_rows, width),
        input_output_aliases={},
        compiler_params=comm_params(4),
        cost_estimate=comm_cost(70),
    )(rows_all, upstream, inner, gate_grad, up_grad, part_sums, grad_sums)


def last_kernel(
    parts_ref,
    qkv_ref,
    proj_ref,
    input_ref,
    hidden_ref,
    norm_ref,
    gains_ref,
    grad_ref,
    qkv_columns,
    proj_out,
    gains_out,
    marks_ref,
    qkv_sum,
    row_sum,
    gain_rows,
    gain_mine,
    gain_got,
    *buffers,
):
    place = Place()
    marks = Marks(marks_ref)
    greet(place, [place.x, place.y, place.d, place.pair], True)
    tokens = PlaneScatter(place, parts_ref, row_sum, buffers[:1], marks)
    qkv_line = LineScatter(place, lambda z: qkv_ref.at[z], qkv_sum, buffers[1:2], marks)
    proj_line = LineScatter(place, lambda z: proj_ref.at[z], proj_out, buffers[2:], marks)
    rows = qkv_sum.shape[0] // 4
    qkv_pieces = Exchange(
        place,
        lambda p, step: qkv_sum.at[pl.ds(pl.multiple_of(p * rows, rows), rows)],
        lambda p, step: qkv_columns.at[p],
        marks,
    )
    near_z = {"f": place.z + 1 - 2 * (place.z % 2)}
    rounds = [
        remote(gain_mine.at[index], gain_got.at[index], marks.take(), marks.take(), to)
        for index, to in enumerate((place.pair, place.x, place.y, near_z, place.two))
    ]

    tokens.start()
    qkv_line.start()
    qkv_line.middle()
    proj_line.start()
    tokens.middle()
    proj_line.middle()
    tokens.finish()

    qkv_line.finish()
    qkv_pieces.start()
    gain_rows[...] = jnp.zeros_like(gain_rows)
    norm_row = norm_ref[...]

    def work(rows):
        values = f32(input_ref[rows])
        scales = inv_rms(values)
        upstream = row_sum[rows]
        weighted = upstream * norm_row
        inner_mean = jnp.mean(weighted * values, axis=-1, keepdims=True)
        grad_ref[rows] = (
            hidden_ref[rows]
            + scales * weighted
            - values * (scales * scales * scales) * inner_mean
        )
        parts = upstream * values * scales
        gain_rows[...] += parts[:8] + parts[8:]

    each_rows(row_sum.shape[0], 16, work)
    width = norm_row.shape[1]
    gain_mine[0, :, pl.ds(0, width)] = jnp.sum(gain_rows[...], axis=0, keepdims=True)
    gain_mine[0, :, pl.ds(width, gains_ref.shape[1])] = gains_ref[...]
    for index, copy in enumerate(rounds):
        copy.start()
        copy.wait()
        summed = gain_mine[index] + gain_got[index]
        if index < 4:
            gain_mine[index + 1] = summed
        else:
            gains_out[...] = summed
    proj_line.finish()
    qkv_line.drain()
    proj_line.drain()
    tokens.drain()
    qkv_pieces.wait()
    qkv_pieces.finish()


def last_sums(parts, qkv_parts, proj_parts, layer_input, hidden_grad, norm, gains):
    rows, width = parts.shape[1:]
    qkv_rows, qkv_width = qkv_parts.shape[1:]
    gain_width = width + gains.shape[1]
    return pl.pallas_call(
        last_kernel,
        out_shape=(
            jax.ShapeDtypeStruct((rows, width), jnp.float32),
            jax.ShapeDtypeStruct((4, qkv_rows // 4, qkv_width), LOW),
            jax.ShapeDtypeStruct(proj_parts.shape[1:], LOW),
            jax.ShapeDtypeStruct((1, gain_width), jnp.float32),
        ),
        in_specs=[WHOLE] + [ANYWHERE] * 2 + [WHOLE] * 4,
        out_specs=(WHOLE, ANYWHERE, WHOLE, WHOLE),
        scratch_shapes=[
            pltpu.SemaphoreType.DMA((100,)),
            pltpu.VMEM((qkv_rows, qkv_width), LOW),
            pltpu.VMEM((rows, width), jnp.float32),
            pltpu.VMEM((8, width), jnp.float32),
            pltpu.VMEM((5, 1, gain_width), jnp.float32),
            pltpu.VMEM((5, 1, gain_width), jnp.float32),
        ]
        + PlaneScatter.scratch(rows, width)
        + LineScatter.scratch(qkv_rows, qkv_width)
        + LineScatter.scratch(*proj_parts.shape[1:]),
        compiler_params=comm_params(5),
        cost_estimate=comm_cost(60),
    )(parts, qkv_parts, proj_parts, layer_input, hidden_grad, norm, gains)


def turn_pairs(values, cosine, sine):
    return values * cosine + pltpu.roll(values, HEAD_SIZE // 2, 1) * sine


def softmax_of(query, key, allowed):
    scores = matmul_nt(query, key) * HEAD_SIZE ** (-0.5)
    masked = jnp.where(allowed, scores, MASKED)
    exponent = jnp.exp(masked - jnp.max(masked, axis=-1, keepdims=True))
    return exponent / jnp.sum(exponent, axis=-1, keepdims=True)


def lanes(values, head):
    return values[:, head * HEAD_SIZE : (head + 1) * HEAD_SIZE]


def roll_half(values):
    return pltpu.roll(values, HEAD_SIZE // 2, 1)


def attend_back_values(raw, kept, grad, allowed, cosine, sine, gains_ref, roll=roll_half):
    group_rows = raw.shape[0]
    heads = raw.shape[1] // HEAD_SIZE - 2
    key, value = lanes(kept, heads), lanes(kept, heads + 1)
    scale = HEAD_SIZE ** (-0.5)
    turned_grads = []
    key_grad = jnp.zeros((group_rows, HEAD_SIZE), jnp.float32)
    value_grad = jnp.zeros((group_rows, HEAD_SIZE), jnp.float32)
    for head in range(heads):
        query, upstream = lanes(kept, head), lanes(grad, head)
        probs = softmax_of(query, key, allowed)
        probs_grad = matmul_nt(upstream, value)
        scores_grad = low(
            probs * (probs_grad - jnp.sum(probs * probs_grad, axis=-1, keepdims=True))
        )
        turned_grads.append(matmul(scores_grad, key) * scale)
        key_grad = key_grad + matmul_tn(scores_grad, query)
        value_grad = value_grad + matmul_tn(low(probs), upstream)
    turned_grads.append(key_grad * scale)
    outs, gains = [], []
    for head in range(heads + 1):
        gain = gains_ref[min(head // heads, 1)][None, :]
        unnormed = lanes(raw, head)
        upstream = turned_grads[head] * cosine - roll(turned_grads[head]) * sine
        grad_raw, gain_part = norm_back(unnormed, inv_rms(unnormed), gain, upstream)
        outs.append(low(grad_raw))
        gains.append(gain_part[None, :])
    outs.append(low(value_grad))
    query_gain = sum(gains[1:heads], gains[0])
    return (jnp.concatenate(outs, axis=1), jnp.concatenate([query_gain, gains[heads]], axis=1))


def heads_back_kernel(
    hidden_ref,
    row_grad_ref,
    upstream_ref,
    norm_ref,
    out_ref,
    attended_ref,
    raw_ref,
    low_ref,
    cos_ref,
    sin_ref,
    segment_col,
    segment_row,
    id_col,
    id_row,
    gains_ref,
    rows_all,
    qkv_ref,
    gate_part,
    up_part,
    hidden_grad,
    mlp_gain,
    head_gain,
    qkv_part,
    proj_sum,
    grad_sums,
    gate_columns,
    up_columns,
    marks_ref,
    out_mat,
    qkv_mat,
    attended,
    branch,
    own_grad,
    heads_grad,
    raw_block,
    low_block,
    qkv_grad,
    row_slab,
    proj_part,
    gain_rows,
    line_sum,
    *buffers,
):
    place = Place()
    marks = Marks(marks_ref)
    greet(place, [place.x, place.y, place.d, place.pair], True)
    rows, width = hidden_ref.shape
    half_heads = heads_grad.shape[2]
    group_rows = 2 * rows
    gate_line = LineScatter(
        place, lambda z: gate_part.at[z], line_sum.at[0], buffers[0:1], marks
    )
    up_line = LineScatter(place, lambda z: up_part.at[z], line_sum.at[1], buffers[1:2], marks)
    quarter = line_sum.shape[1] // 4
    columns = [
        Exchange(
            place,
            lambda p, step, index=index: line_sum.at[
                index, pl.ds(pl.multiple_of(p * quarter, quarter), quarter)
            ],
            lambda p, step, out=out: out.at[p],
            marks,
        )
        for index, out in enumerate((gate_columns, up_columns))
    ]
    proj_plane = PlaneScatter(
        place,
        proj_part,
        proj_sum,
        buffers[2:3],
        marks,
        (place.p, place.px, place.py, place.pd),
    )
    heads = Exchange(
        place, lambda p, step: own_grad.at[p], lambda p, step: heads_grad.at[step], marks
    )
    to_pair = remote(branch.at[0], branch.at[1], marks.take(), marks.take(), place.pair)
    loads = [
        pltpu.make_async_copy(out_ref, out_mat, marks.take()),
        pltpu.make_async_copy(attended_ref, attended, marks.take()),
        pltpu.make_async_copy(qkv_ref, qkv_mat, marks.take()),
    ]
    fetch_marks, slab_marks = marks.take(4), marks.take(2)
    send_marks, recv_marks = marks.take(4), marks.take(4)

    gate_line.start()
    for copy in loads:
        copy.start()

    gain_rows[...] = jnp.zeros_like(gain_rows)
    norm_row = norm_ref[...]

    def norm_work(part):
        values = hidden_ref[part]
        scales = inv_rms(values)
        upstream = row_grad_ref[part]
        weighted = upstream * norm_row
        inner_mean = jnp.mean(weighted * values, axis=-1, keepdims=True)
        grad = (
            f32(upstream_ref[part])
            + scales * weighted
            - values * (scales * scales * scales) * inner_mean
        )
        hidden_grad[part] = grad
        branch[0, part] = low(grad)
        parts = upstream * values * scales
        gain_rows[...] += parts[:8] + parts[8:]

    each_rows(rows, 16, norm_work)
    to_pair.start()
    mlp_gain[...] = jnp.sum(gain_rows[...], axis=0, keepdims=True)
    for copy in loads:
        copy.wait()

    def own_half(core_step):
        grad = low(matmul_nt(branch[core_step], out_mat[...]))
        for p in range(4):
            own_grad[p, pl.ds(core_step * rows, rows)] = grad[
                :, p * half_heads : (p + 1) * half_heads
            ]

    own_half(0)
    to_pair.wait()
    own_half(1)
    heads.start()
    gate_line.middle()
    up_line.start()

    def proj_work(z, carry):
        block = attended[z].reshape(group_rows, half_heads)
        grad = low(matmul_tn(block, branch[...].reshape(group_rows, width)))
        part = half_heads // 4
        for p in range(4):
            proj_part[p, pl.ds(pl.multiple_of(z * part, part), part)] = grad[
                p * part : (p + 1) * part
            ]
        return carry

    def fetches(step):
        return (
            pltpu.make_async_copy(raw_ref.at[:, step], raw_block, fetch_marks.at[0]),
            pltpu.make_async_copy(low_ref.at[:, step], low_block, fetch_marks.at[1]),
        )

    lax.fori_loop(0, 4, proj_work, 0)
    heads.wait()
    proj_plane.start()
    head_gain[...] = jnp.zeros_like(head_gain)

    def sends(step):
        return remote(
            out_mat.at[pl.ds(pl.multiple_of(step * rows, rows), rows)],
            grad_sums.at[step],
            send_marks.at[step],
            recv_marks.at[step],
            place.pair,
        )

    def bucket(step, carry):
        for copy in fetches(step):
            copy.start()
        for copy in fetches(step):
            copy.wait()
        allowed = (segment_col[step] == segment_row[step]) & (id_row[...] <= id_col[...])
        grads, gains = attend_back_values(
            raw_block[...].reshape(group_rows, -1),
            low_block[...].reshape(group_rows, -1),
            heads_grad[step],
            allowed,
            cos_ref[step],
            sin_ref[step],
            gains_ref,
        )
        head_gain[...] += gains
        qkv_grad[0, step] = grads[:rows]
        qkv_grad[1, step] = grads[rows:]
        out_mat[pl.ds(pl.multiple_of(step * rows, rows), rows)] = low(
            matmul_nt(grads[rows:], qkv_mat[...])
        )
        sends(step).start()
        return carry

    lax.fori_loop(0, 2, bucket, 0)
    proj_plane.middle()
    up_line.middle()
    lax.fori_loop(2, 4, bucket, 0)

    tile = row_slab.shape[3]
    tiles = width // tile

    def slab(index):
        return pltpu.make_async_copy(
            rows_all.at[:, :, pl.ds(pl.multiple_of(index * tile, tile), tile)],
            row_slab.at[index % 2],
            slab_marks.at[index % 2],
        )

    slab(0).start()

    def own_work(step, carry):
        copy = sends(step)
        copy.wait_recv()
        grad = matmul_nt(qkv_grad[0, step], qkv_mat[...])
        grad_sums[step] = low(grad + f32(grad_sums[step]))
        return carry

    lax.fori_loop(0, 4, own_work, 0)
    gate_line.finish()
    columns[0].start()

    def row_tile(index, carry):
        slab(index).wait()

        @pl.when(index < tiles - 1)
        def _():
            slab(index + 1).start()

        block = row_slab[index % 2].reshape(4 * group_rows, tile)
        out_rows = pl.ds(pl.multiple_of(index * tile, tile), tile)
        qkv_part[out_rows] = low(
            matmul_tn(block, qkv_grad[...].reshape(4 * group_rows, qkv_grad.shape[3]))
        )
        return carry

    lax.fori_loop(0, tiles, row_tile, 0)
    proj_plane.finish()
    up_line.finish()
    columns[1].start()
    for step in range(4):
        sends(step).wait_send()
    heads.finish()
    proj_plane.drain()
    gate_line.drain()
    up_line.drain()
    for part in columns:
        part.wait()
        part.finish()


def heads_backward(
    hidden, row_grad, upstream, norm, out_all, attended, raw, kept, tables, rows_all, qkv_all, gate_part, up_part
):
    rows, width = hidden.shape
    head_part = raw.shape[3]
    query_part = head_part - 2 * HEAD_SIZE
    line_rows, units = gate_part.shape[1:]
    tile = 256
    pieces = jax.ShapeDtypeStruct((4, line_rows // 4, units), LOW)
    return pl.pallas_call(
        heads_back_kernel,
        out_shape=(
            jax.ShapeDtypeStruct((rows, width), jnp.float32),
            jax.ShapeDtypeStruct((1, width), jnp.float32),
            jax.ShapeDtypeStruct((1, 2 * HEAD_SIZE), jnp.float32),
            jax.ShapeDtypeStruct((width, head_part), LOW),
            jax.ShapeDtypeStruct((query_part, width), LOW),
            jax.ShapeDtypeStruct((4, rows, width), LOW),
            pieces,
            pieces,
        ),
        in_specs=[WHOLE] * 4
        + [ANYWHERE] * 4
        + [WHOLE] * len(tables)
        + [ANYWHERE] * 4,
        out_specs=(WHOLE,) * 6 + (ANYWHERE,) * 2,
        scratch_shapes=[
            pltpu.SemaphoreType.DMA((100,)),
            pltpu.VMEM(out_all.shape, LOW),
            pltpu.VMEM(qkv_all.shape, LOW),
            pltpu.VMEM(attended.shape, LOW),
            pltpu.VMEM((2, rows, width), LOW),
            pltpu.VMEM((4, 2 * rows, query_part), LOW),
            pltpu.VMEM((4, 2 * rows, query_part), LOW),
            pltpu.VMEM((2, rows, head_part), jnp.float32),
            pltpu.VMEM((2, rows, head_part), LOW),
            pltpu.VMEM((2, 4, rows, head_part), LOW),
            pltpu.VMEM((2, 8, rows, tile), LOW),
            pltpu.VMEM((4, query_part, width), LOW),
            pltpu.VMEM((8, width), jnp.float32),
            pltpu.VMEM((2, line_rows, units), LOW),
        ]
        + LineScatter.scratch(line_rows, units) * 2
        + PlaneScatter.scratch(query_part, width),
        compiler_params=comm_params(3),
        cost_estimate=comm_cost(115),
    )(
        hidden,
        row_grad,
        upstream,
        norm,
        out_all,
        attended,
        raw,
        kept,
        *tables,
        rows_all,
        qkv_all,
        gate_part,
        up_part,
    )


def row_ids_of(local_rows):
    core = lax.axis_index("tensor")
    local_ids = jnp.arange(local_rows, dtype=jnp.int32)
    return jnp.concatenate([core * local_rows + local_ids, (1 - core) * local_rows + local_ids])


def heads_of(weight):
    return weight.reshape(weight.shape[0], 4, -1).transpose(1, 0, 2)


def heads_back(pieces):
    return f32(pieces).transpose(1, 0, 2).reshape(pieces.shape[1], -1)


def units_of(weight, down_rows):
    split = weight.reshape(weight.shape[0], -1, 4, down_rows)
    return split.transpose(2, 0, 1, 3).reshape(4, weight.shape[0], -1)


def units_back(pieces, down_rows):
    rows = pieces.shape[1]
    return f32(pieces).reshape(4, rows, -1, down_rows).transpose(1, 2, 0, 3).reshape(rows, -1)


def shards(*arguments):
    if lax.axis_size("f") == 4:
        return line_of_four(*arguments)
    return any_line(*arguments)


def line_of_four(
    layer_input,
    attn_norm,
    head_norms,
    query_weight,
    key_matrix,
    value_matrix,
    output_weight,
    mlp_norm,
    gate_weight,
    up_weight,
    down_weight,
    grad_out,
    doc_lengths,
):
    local_rows, model_width = layer_input.shape
    weight_rows = gate_weight.shape[0]
    down_rows = down_weight.shape[0]
    hidden_part = 4 * down_rows
    qkv_pieces = jnp.concatenate(
        [heads_of(query_weight), heads_of(key_matrix), heads_of(value_matrix)], axis=2
    )
    head_part = qkv_pieces.shape[2]
    query_part = head_part - 2 * HEAD_SIZE
    input_float = f32(layer_input)
    row_ids = row_ids_of(local_rows)
    (
        normed_attn,
        _,
        up_rows,
        gate_all,
        above,
        below,
        qkv_all,
        out_all,
        qkv_raw,
        qkv_low,
        cos_tab,
        sin_tab,
        segment_col,
        segment_row,
        attended,
        hidden_state,
        normed_mlp,
    ) = first_part(
        low(input_float * inv_rms(input_float) * attn_norm),
        qkv_pieces,
        output_weight,
        units_of(gate_weight, down_rows),
        units_of(up_weight, down_rows),
        down_weight,
        doc_lengths,
        row_ids,
        head_norms,
        layer_input,
        mlp_norm,
    )
    tables = (
        cos_tab,
        sin_tab,
        segment_col,
        segment_row,
        row_ids[:, None],
        row_ids[None, :],
        head_norms,
    )
    rows_all, grad_all, inner_low, gate_grad, up_grad, part_sums, grad_sums = units_products(
        normed_mlp,
        grad_out,
        up_rows.reshape(-1, hidden_part),
        gate_all.reshape(model_width, hidden_part),
        down_weight,
        above,
        below,
    )
    mlp_row_grad, mlp_rows, grad_down, grad_gate_part, grad_up_part = unit_grads(
        rows_all, grad_all, inner_low, gate_grad, up_grad, part_sums, grad_sums
    )
    line_shape = (4, 4 * weight_rows, hidden_part)
    (
        hidden_grad,
        mlp_gain_part,
        head_gains,
        grad_qkv_part,
        grad_proj_part,
        grad_sums,
        grad_gate_columns,
        grad_up_columns,
    ) = heads_backward(
        hidden_state,
        mlp_row_grad,
        grad_out,
        mlp_norm[None],
        out_all.reshape(-1, model_width),
        attended,
        qkv_raw,
        qkv_low,
        tables,
        normed_attn,
        qkv_all.reshape(model_width, head_part),
        grad_gate_part.reshape(line_shape),
        grad_up_part.reshape(line_shape),
    )
    grad_input, grad_qkv_columns, grad_out_proj, gains = last_sums(
        grad_sums,
        grad_qkv_part.reshape(4, 4 * weight_rows, head_part),
        grad_proj_part.reshape((4,) + output_weight.shape),
        layer_input,
        hidden_grad,
        attn_norm[None],
        jnp.concatenate([mlp_gain_part, head_gains], axis=1),
    )
    gains = gains.reshape(-1)
    return (
        low(hidden_state + mlp_rows),
        grad_input,
        gains[:model_width],
        gains[2 * model_width :].reshape(2, HEAD_SIZE),
        heads_back(grad_qkv_columns[:, :, :query_part]),
        heads_back(grad_qkv_columns[:, :, query_part : query_part + HEAD_SIZE]),
        heads_back(grad_qkv_columns[:, :, query_part + HEAD_SIZE :]),
        f32(grad_out_proj),
        gains[model_width : 2 * model_width],
        units_back(grad_gate_columns, down_rows),
        units_back(grad_up_columns, down_rows),
        f32(grad_down),
    )


def any_line(
    layer_input,
    attn_norm,
    head_norms,
    query_weight,
    key_matrix,
    value_matrix,
    output_weight,
    mlp_norm,
    gate_weight,
    up_weight,
    down_weight,
    grad_out,
    doc_lengths,
):
    line_extent = lax.axis_size("f")
    local_rows, model_width = layer_input.shape
    group_rows = 2 * local_rows
    all_rows = 8 * local_rows
    weight_rows = gate_weight.shape[0]
    down_rows = down_weight.shape[0]
    hidden_part = line_extent * down_rows
    qkv_pieces = jnp.concatenate(
        [heads_of(query_weight), heads_of(key_matrix), heads_of(value_matrix)], axis=2
    )
    head_part = qkv_pieces.shape[2]
    query_part = head_part - 2 * HEAD_SIZE
    heads = head_part // HEAD_SIZE - 2

    def exchanged(pieces):
        return natural_plane(plane_exchange(own_plane(pieces, 0)), 0)

    def line_rows(pieces):
        return line_gather(exchanged(pieces)).reshape(model_width, -1)

    def line_sums(partial):
        parts = low(partial).reshape(line_extent, 4 * weight_rows, -1)
        return exchanged(low(line_scatter(parts)).reshape(4, weight_rows, -1))

    qkv_all = line_rows(qkv_pieces)
    out_all = full_gather(output_weight)
    gate_all = line_rows(units_of(gate_weight, down_rows))
    up_all = line_rows(units_of(up_weight, down_rows))
    down_all = line_gather(down_weight).reshape(hidden_part, model_width)

    input_float = f32(layer_input)
    scale_attn = inv_rms(input_float)
    normed_attn = tokens_gather(low(input_float * scale_attn * attn_norm))
    row_ids = row_ids_of(local_rows)
    segments, positions = jax.vmap(lambda lengths: doc_layout(lengths, row_ids))(
        plane_lengths(doc_lengths)
    )
    qkv_raw = matmul(normed_attn, qkv_all).reshape(2, 4, local_rows, head_part)
    roll = lambda values: jnp.roll(values, HEAD_SIZE // 2, 1)
    buckets, attended_parts = [], []
    for step in range(4):
        cos_tab, sin_tab = rope_tables(positions[step], HEAD_SIZE)
        cosine = jnp.concatenate([cos_tab, cos_tab], axis=1)
        sine = jnp.concatenate([-sin_tab, sin_tab], axis=1)
        allowed = (segments[step][:, None] == segments[step][None, :]) & (
            row_ids[None, :] <= row_ids[:, None]
        )
        raw = qkv_raw[:, step].reshape(group_rows, head_part)
        turned = []
        for head in range(heads + 1):
            unnormed = lanes(raw, head)
            normed = unnormed * inv_rms(unnormed) * head_norms[min(head // heads, 1)]
            turned.append(low(normed * cosine + roll(normed) * sine))
        value = low(lanes(raw, heads + 1))
        attended_parts.append(
            jnp.concatenate(
                [
                    low(matmul(low(softmax_of(turned[head], turned[heads], allowed)), value))
                    for head in range(heads)
                ],
                axis=1,
            )
        )
        buckets.append((raw, jnp.concatenate(turned + [value], axis=1), allowed, cosine, sine))
    attended = natural_plane(plane_exchange(attended_parts), 0)
    attended = attended.transpose(1, 0, 2).reshape(group_rows, 4 * query_part)
    hidden_state = input_float + pair_scatter(low(matmul(attended, out_all)))

    scale_mlp = inv_rms(hidden_state)
    normed_mlp = tokens_gather(low(hidden_state * scale_mlp * mlp_norm))
    grad_all = tokens_gather(grad_out)
    gate_raw = matmul(normed_mlp, gate_all)
    up_raw = matmul(normed_mlp, up_all)
    activated = jax.nn.silu(gate_raw)
    inner_low = low(activated * up_raw)
    layer_out = low(hidden_state + tokens_scatter(low(matmul(inner_low, down_all))))
    inner_grad = matmul_nt(grad_all, down_all)
    sigmoid_gate = jax.nn.sigmoid(gate_raw)
    gate_grad = low(inner_grad * up_raw * sigmoid_gate * (1.0 + gate_raw * (1.0 - sigmoid_gate)))
    up_grad = low(inner_grad * activated)
    mlp_row_grad = tokens_scatter(
        low(matmul_nt(gate_grad, gate_all) + matmul_nt(up_grad, up_all))
    )
    grad_down = line_scatter(
        low(matmul_tn(inner_low, grad_all)).reshape(line_extent, down_rows, model_width)
    )

    hidden_norm_grad, mlp_gain_part = norm_back(hidden_state, scale_mlp, mlp_norm, mlp_row_grad)
    hidden_grad = f32(grad_out) + hidden_norm_grad
    branch_grad = pair_gather(low(hidden_grad))
    split = low(matmul_nt(branch_grad, out_all)).reshape(group_rows, 4, query_part)
    heads_grad = plane_exchange(own_plane(split.transpose(1, 0, 2), 0))
    grad_out_proj = line_scatter(full_scatter_plane(low(matmul_tn(attended, branch_grad))))
    back = [
        attend_back_values(raw, kept, heads_grad[step], allowed, cosine, sine, head_norms, roll)
        for step, (raw, kept, allowed, cosine, sine) in enumerate(buckets)
    ]
    qkv_grad = jnp.stack([grads for grads, _ in back]).reshape(4, 2, local_rows, head_part)
    qkv_grad = qkv_grad.transpose(1, 0, 2, 3).reshape(all_rows, head_part)
    attn_row_grad = tokens_scatter(low(matmul_nt(qkv_grad, qkv_all)))
    grad_qkv_columns = line_sums(matmul_tn(normed_attn, qkv_grad))
    input_norm_grad, attn_gain_part = norm_back(input_float, scale_attn, attn_norm, attn_row_grad)
    head_gains = sum(gains for _, gains in back)[0]
    gains = total_sum(
        jnp.concatenate([attn_gain_part, mlp_gain_part, head_gains]).reshape(-1, HEAD_SIZE)
    ).reshape(-1)
    return (
        layer_out,
        hidden_grad + input_norm_grad,
        gains[:model_width],
        gains[2 * model_width :].reshape(2, HEAD_SIZE),
        heads_back(grad_qkv_columns[:, :, :query_part]),
        heads_back(grad_qkv_columns[:, :, query_part : query_part + HEAD_SIZE]),
        heads_back(grad_qkv_columns[:, :, query_part + HEAD_SIZE :]),
        grad_out_proj,
        gains[model_width : 2 * model_width],
        units_back(line_sums(matmul_tn(normed_mlp, gate_grad)), down_rows),
        units_back(line_sums(matmul_tn(normed_mlp, up_grad)), down_rows),
        grad_down,
    )


def solution(mesh):
    dp, tensor = mesh.shape["dp"], mesh.shape["tensor"]
    fine = Mesh(mesh.devices.reshape(dp // 4, 2, 2, tensor), ("f", "ty", "tx", "tensor"))
    rows = ("f", "ty", "tx")
    tokens = P(rows + ("tensor",), None)
    grid = P(rows, "tensor")
    units = P(("tensor",) + rows, None)
    return jax.shard_map(
        shards,
        mesh=fine,
        in_specs=(
            tokens, P(), P(), grid, grid, grid, units, P(), grid, grid, units, tokens, P(rows, None),
        ),
        out_specs=(tokens, tokens, P(), P(), grid, grid, grid, units, P(), grid, grid, units),
        check_vma=False,
    )
```

```python
import jax
import jax.numpy as jnp
from jax import lax
from jax.experimental import pallas as pl
from jax.experimental.pallas import tpu as pltpu
from jax.sharding import Mesh, PartitionSpec as P

QUERY_HEADS = 16
KEY_VALUE_HEADS = 8
HEAD_SIZE = 128


EPS = 1e-06
ROPE_BASE = 1000000.0
MASKED = -1e30
LOW = jnp.bfloat16


def matmul(left_mat, right_mat):
    return jnp.dot(left_mat, right_mat, preferred_element_type=jnp.float32)


def matmul_tn(left_mat, right_mat):
    return lax.dot_general(
        left_mat, right_mat, (((0,), (0,)), ((), ())), preferred_element_type=jnp.float32
    )


def matmul_nt(left_mat, right_mat):
    return lax.dot_general(
        left_mat, right_mat, (((1,), (1,)), ((), ())), preferred_element_type=jnp.float32
    )


def inv_rms(values):
    return lax.rsqrt(jnp.mean(values * values, axis=-1, keepdims=True) + EPS)


def norm_back(values, scales, gain_row, upstream):
    weighted = upstream * gain_row
    inner_mean = jnp.mean(weighted * values, axis=-1, keepdims=True)
    value_grad = scales * weighted - values * (scales * scales * scales) * inner_mean
    lead_axes = tuple(range(upstream.ndim - 1))
    return (value_grad, jnp.sum(upstream * values * scales, axis=lead_axes))


def rope_tables(position, head_width):
    half_dim = head_width // 2
    inverse = ROPE_BASE ** (-(jnp.arange(half_dim, dtype=jnp.float32) * (2.0 / head_width)))
    angles = position.astype(jnp.float32)[:, None] * inverse[None, :]
    return (jnp.cos(angles), jnp.sin(angles))


def rotate(values, cos_tab, sin_tab, direction):
    half_dim = values.shape[-1] // 2
    first_half = values[..., :half_dim]
    second_half = values[..., half_dim:]
    cosine = cos_tab[:, None, :]
    sine_tab = direction * sin_tab[:, None, :]
    return jnp.concatenate(
        [
            first_half * cosine - second_half * sine_tab,
            second_half * cosine + first_half * sine_tab,
        ],
        axis=-1,
    )


def doc_layout(lengths_row, row_ids):
    doc_ends = jnp.cumsum(lengths_row, dtype=jnp.int32)
    document_segment = jnp.sum(
        (row_ids[:, None] >= doc_ends[None, :]).astype(jnp.int32), axis=1, dtype=jnp.int32
    )
    doc_starts = doc_ends - lengths_row
    member = document_segment[:, None] == jnp.arange(lengths_row.shape[0], dtype=jnp.int32)[None, :]
    start_of = jnp.sum(jnp.where(member, doc_starts[None, :], 0), axis=1, dtype=jnp.int32)
    return (document_segment, row_ids - start_of)


def f32(values):
    return values.astype(jnp.float32)


def low(values):
    return values.astype(LOW)


def swap(block, axis):
    return lax.ppermute(block, axis, [(0, 1), (1, 0)])


def plane_index():
    return 2 * lax.axis_index("ty") + lax.axis_index("tx")


def plane_gather(block):
    across_x = swap(block, "tx")
    across_y = swap(block, "ty")
    return [block, across_x, across_y, swap(across_y, "tx")]


def plane_scatter(parts):
    own, for_x, for_y, for_far = parts
    for_y = low(f32(for_y) + f32(swap(for_far, "tx")))
    return f32(own) + f32(swap(for_x, "tx")) + f32(swap(for_y, "ty"))


def plane_exchange(parts):
    own, for_x, for_y, for_far = parts
    return [own, swap(for_x, "tx"), swap(for_y, "ty"), swap(swap(for_far, "tx"), "ty")]


def plane_lengths(lengths):
    return jnp.concatenate(plane_gather(lengths))


def line_gather(block):
    return lax.all_gather(block, "f", axis=0)


def line_scatter(parts):
    return f32(lax.psum_scatter(parts, "f", scatter_dimension=0))


def natural_plane(blocks, axis):
    own = plane_index()
    shape = list(blocks[0].shape)
    shape.insert(axis, 4)
    whole = jnp.zeros(shape, blocks[0].dtype)
    for step in range(4):
        whole = lax.dynamic_update_index_in_dim(whole, blocks[step], own ^ step, axis)
    return whole


def own_plane(whole, axis):
    own = plane_index()
    return [
        lax.dynamic_index_in_dim(whole, own ^ step, axis, keepdims=False) for step in range(4)
    ]


def full_gather(rows_block):
    rows, width = rows_block.shape
    line = line_gather(rows_block)
    extent = line.shape[0]
    blocks = plane_gather(line.reshape(extent * rows, width))
    whole = natural_plane([block.reshape(extent, rows, width) for block in blocks], 1)
    return whole.reshape(extent * 4 * rows, width)


def full_scatter_plane(partial):
    extent = lax.axis_size("f")
    rows, width = partial.shape[0] // (4 * extent), partial.shape[1]
    parts = own_plane(partial.reshape(extent, 4, rows, width), 1)
    plane_sum = plane_scatter([part.reshape(extent * rows, width) for part in parts])
    return low(plane_sum).reshape(extent, rows, width)


def tokens_gather(block):
    near = plane_gather(block)
    return jnp.concatenate(near + [swap(piece, "tensor") for piece in near])


def tokens_scatter(partial):
    rows = partial.shape[0] // 8
    near = []
    for step in range(4):
        mine = partial[step * rows : (step + 1) * rows]
        other = swap(partial[(4 + step) * rows : (5 + step) * rows], "tensor")
        near.append(low(f32(mine) + f32(other)))
    return plane_scatter(near)


def pair_gather(block):
    return jnp.concatenate([block, swap(block, "tensor")])


def pair_scatter(partial):
    rows = partial.shape[0] // 2
    return f32(partial[:rows]) + f32(swap(partial[rows:], "tensor"))


def total_sum(values):
    return lax.psum(values, ("f", "ty", "tx", "tensor"))


class Place:
    def __init__(self):
        self.z = lax.axis_index("f")
        self.ty = lax.axis_index("ty")
        self.tx = lax.axis_index("tx")
        self.core = lax.axis_index("tensor")
        self.p = 2 * self.ty + self.tx
        self.px = 2 * self.ty + 1 - self.tx
        self.py = 2 * (1 - self.ty) + self.tx
        self.pd = 2 * (1 - self.ty) + 1 - self.tx
        self.x = {"tx": 1 - self.tx}
        self.y = {"ty": 1 - self.ty}
        self.d = {"tx": 1 - self.tx, "ty": 1 - self.ty}
        self.pair = {"tensor": 1 - self.core}
        self.up = {"f": self.z + 1}
        self.down = {"f": self.z - 1}
        self.two = {"f": (self.z + 2) % 4}

    def at(self, step):
        return (self.z + step) % 4


def remote(src, dst, send, recv, to):
    return pltpu.make_async_remote_copy(
        src_ref=src,
        dst_ref=dst,
        send_sem=send,
        recv_sem=recv,
        device_id=to,
        device_id_type=pl.DeviceIdType.MESH,
    )


def arrived(dst, recv, to):
    remote(dst, dst, recv, recv, to).wait_recv()


def greet(place, partners, line):
    barrier = pltpu.get_barrier_semaphore()
    for to in partners:
        pl.semaphore_signal(barrier, inc=1, device_id=to, device_id_type=pl.DeviceIdType.MESH)
    if not line:
        pl.semaphore_wait(barrier, len(partners))
        return

    @pl.when(place.z > 0)
    def _():
        pl.semaphore_signal(
            barrier, inc=1, device_id=place.down, device_id_type=pl.DeviceIdType.MESH
        )

    @pl.when(place.z < 3)
    def _():
        pl.semaphore_signal(barrier, inc=1, device_id=place.up, device_id_type=pl.DeviceIdType.MESH)

    pl.semaphore_signal(barrier, inc=1, device_id=place.two, device_id_type=pl.DeviceIdType.MESH)
    pl.semaphore_wait(barrier, len(partners) + 2 + (place.z + 1) // 2 % 2)


class LineGather:
    def __init__(self, place, own, slot, send, recv):
        self.place, self.own, self.slot, self.send, self.recv = place, own, slot, send, recv
        here = slot(place.z)
        self.to_down = remote(own, here, send.at[0], recv.at[1], place.down)
        self.to_up = remote(own, here, send.at[1], recv.at[3], place.up)
        self.to_two = remote(own, here, send.at[2], recv.at[2], place.two)
        two = slot(place.at(2))
        self.pass_down = remote(two, two, send.at[3], recv.at[3], place.down)
        self.pass_up = remote(two, two, send.at[3], recv.at[1], place.up)

    def start(self):
        z = self.place.z
        self.to_two.start()
        pl.when((z == 1) | (z == 3))(self.to_down.start)
        pl.when((z == 0) | (z == 2))(self.to_up.start)

    def step(self, turn):
        if turn == 2:
            return 2
        if turn == 1:
            return jnp.where(self.place.z == 3, 3, 1)
        return jnp.where(self.place.z == 3, 1, 3)

    def wait(self, turn):
        step = self.step(turn)
        slot = self.slot(self.place.at(step))
        arrived(slot, self.recv.at[step], self.place.two)
        if turn == 2:
            pl.when(self.place.z == 1)(self.pass_down.start)
            pl.when(self.place.z == 2)(self.pass_up.start)
            pl.when(self.place.z == 1)(self.to_up.start)
            pl.when(self.place.z == 2)(self.to_down.start)

    def finish(self):
        pl.when(self.place.z > 0)(self.to_down.wait_send)
        pl.when(self.place.z < 3)(self.to_up.wait_send)
        self.to_two.wait_send()
        pl.when(self.place.z == 1)(self.pass_down.wait_send)
        pl.when(self.place.z == 2)(self.pass_up.wait_send)


class PlaneGather:
    def __init__(self, place, own, slot, rows, send, recv):
        half = rows // 2
        whole, top, end = pl.ds(0, rows), pl.ds(0, half), pl.ds(half, half)
        self.place, self.recv = place, recv
        self.to_x = remote(own, slot(place.p, whole), send.at[0], recv.at[0], place.x)
        self.to_y = remote(own, slot(place.p, whole), send.at[1], recv.at[1], place.y)
        self.from_x, self.from_y = slot(place.px, whole), slot(place.py, whole)
        self.far_top, self.far_end = slot(place.pd, top), slot(place.pd, end)
        pass_x, pass_y = slot(place.py, top), slot(place.px, end)
        self.pass_x = remote(pass_x, pass_x, send.at[2], recv.at[2], place.x)
        self.pass_y = remote(pass_y, pass_y, send.at[3], recv.at[3], place.y)

    def start(self):
        self.to_x.start()
        self.to_y.start()

    def forward(self):
        arrived(self.from_y, self.recv.at[1], self.place.y)
        self.pass_x.start()
        arrived(self.from_x, self.recv.at[0], self.place.x)
        self.pass_y.start()

    def wait_far(self):
        arrived(self.far_top, self.recv.at[2], self.place.x)
        arrived(self.far_end, self.recv.at[3], self.place.y)

    def finish(self):
        self.to_x.wait_send()
        self.to_y.wait_send()
        self.pass_x.wait_send()
        self.pass_y.wait_send()


ANYWHERE = pl.BlockSpec(memory_space=pl.ANY)
WHOLE = pl.BlockSpec(memory_space=pltpu.VMEM)


class Marks:
    def __init__(self, ref):
        self.ref, self.used = ref, 0

    def take(self, count=1):
        first = self.used
        self.used += count
        return self.ref.at[first] if count == 1 else self.ref.at[pl.ds(first, count)]


def each_rows(rows, chunk, work):
    def body(index, carry):
        work(pl.ds(pl.multiple_of(index * chunk, chunk), chunk))
        return carry

    lax.fori_loop(0, rows // chunk, body, 0)


class TokensGather:
    def __init__(self, place, own, whole, marks):
        half = own.shape[0] // 2
        top, end = pl.ds(0, half), pl.ds(half, half)
        self.place, self.whole = place, whole
        self.copy = pltpu.make_async_copy(own, whole.at[0], marks.take())
        self.recv = [marks.take() for _ in range(8)]
        x, y, pair = place.x, place.y, place.pair
        self.to_x = remote(own, whole.at[1], marks.take(), self.recv[0], x)
        self.to_y = remote(own, whole.at[2], marks.take(), self.recv[1], y)
        self.pass_x = remote(
            whole.at[2, top], whole.at[3, top], marks.take(), self.recv[2], x
        )
        self.pass_y = remote(
            whole.at[1, end], whole.at[3, end], marks.take(), self.recv[3], y
        )
        self.to_pair = [
            remote(
                own if step == 0 else whole.at[step],
                whole.at[4 + step],
                marks.take(),
                self.recv[4 + step],
                pair,
            )
            for step in range(4)
        ]
        self.far = (whole.at[3, top], whole.at[3, end])

    def start(self):
        self.to_x.start()
        self.to_y.start()
        self.to_pair[0].start()
        self.copy.start()

    def forward(self):
        arrived(self.whole.at[2], self.recv[1], self.place.y)
        self.pass_x.start()
        arrived(self.whole.at[1], self.recv[0], self.place.x)
        self.pass_y.start()
        self.to_pair[2].start()
        self.to_pair[1].start()

    def last(self):
        arrived(self.far[0], self.recv[2], self.place.x)
        arrived(self.far[1], self.recv[3], self.place.y)
        self.to_pair[3].start()

    def finish(self):
        for step in range(4):
            arrived(self.whole.at[4 + step], self.recv[4 + step], self.place.pair)
        for copy in [self.to_x, self.to_y, self.pass_x, self.pass_y] + self.to_pair:
            copy.wait_send()
        self.copy.wait()


class Exchange:
    def __init__(self, place, piece, slot, marks):
        self.place = place
        there = ((place.px, place.x), (place.py, place.y), (place.pd, place.d))
        self.copy = pltpu.make_async_copy(piece(place.p, 0), slot(place.p, 0), marks.take())
        self.sends, self.slots = [], []
        for index, (p, to) in enumerate(there):
            recv = marks.take()
            self.sends.append(
                remote(piece(p, index + 1), slot(place.p, index + 1), marks.take(), recv, to)
            )
            self.slots.append((slot(p, index + 1), recv, to))

    def start(self):
        for copy in (self.sends[2], self.sends[0], self.sends[1], self.copy):
            copy.start()

    def wait(self):
        self.copy.wait()
        for slot, recv, to in self.slots:
            arrived(slot, recv, to)

    def finish(self):
        for copy in self.sends:
            copy.wait_send()


class LineScatter:
    @staticmethod
    def scratch(rows, width, here=False):
        return [pltpu.VMEM((4 if here else 6, rows, width), LOW)]

    def __init__(self, place, part, out, buffers, marks, here=False):
        self.place, self.out, self.here = place, out, here
        kept = buffers[0]
        self.rows = kept.shape[1]
        self.passed, self.above, self.below, self.two = (kept.at[index] for index in range(4))
        z = place.z
        if here:
            self.mid, self.own = part(place.at(2)), part(z)
        else:
            self.mid, self.own = kept.at[4], kept.at[5]
            self.load_mid = pltpu.make_async_copy(part(place.at(2)), self.mid, marks.take())
            self.load_own = pltpu.make_async_copy(part(z), self.own, marks.take())
        self.recv = [marks.take() for _ in range(4)]
        self.pass_up = remote(part(3), self.passed, marks.take(), self.recv[0], place.up)
        self.pass_down = remote(part(0), self.passed, marks.take(), self.recv[0], place.down)
        self.to_down = remote(
            part(place.at(3)), self.above, marks.take(), self.recv[1], place.down
        )
        self.to_up = remote(part(place.at(1)), self.below, marks.take(), self.recv[2], place.up)
        self.to_two = remote(self.mid, self.two, marks.take(), self.recv[3], place.two)

    def start(self):
        z = self.place.z
        pl.when(z == 0)(self.pass_up.start)
        pl.when(z == 3)(self.pass_down.start)
        if not self.here:
            self.load_mid.start()
        pl.when((z == 1) | (z == 2))(self.to_down.start)
        pl.when((z == 1) | (z == 2))(self.to_up.start)
        if not self.here:
            self.load_own.start()

    def add(self, target, other):
        def work(rows):
            target[rows] = low(f32(target[rows]) + f32(other[rows]))

        each_rows(self.rows, 16, work)

    def middle(self):
        z = self.place.z
        if not self.here:
            self.load_mid.wait()
        pl.when(z == 0)(self.pass_up.wait_send)
        pl.when(z == 3)(self.pass_down.wait_send)

        @pl.when((z == 1) | (z == 2))
        def _():
            arrived(self.passed, self.recv[0], self.place.two)
            self.add(self.mid, self.passed)

        self.to_two.start()
        pl.when(z == 0)(self.to_up.start)
        pl.when(z == 3)(self.to_down.start)

    def finish(self):
        z = self.place.z
        if not self.here:
            self.load_own.wait()

        @pl.when(z < 3)
        def _():
            arrived(self.above, self.recv[1], self.place.two)
            self.add(self.own, self.above)

        @pl.when(z > 0)
        def _():
            arrived(self.below, self.recv[2], self.place.two)
            self.add(self.own, self.below)

        arrived(self.two, self.recv[3], self.place.two)
        out, own, two = self.out, self.own, self.two

        def work(rows):
            out[rows] = low(f32(own[rows]) + f32(two[rows]))

        each_rows(self.rows, 16, work)

    def drain(self):
        z = self.place.z
        pl.when(z > 0)(self.to_down.wait_send)
        pl.when(z < 3)(self.to_up.wait_send)
        self.to_two.wait_send()


def comm_params(number):
    return pltpu.CompilerParams(
        collective_id=number, has_side_effects=True, vmem_limit_bytes=62 * 1024 * 1024
    )


def comm_cost(micros):
    return pl.CostEstimate(flops=0, bytes_accessed=micros * 3_000_000, transcendentals=0)


def tables_of(lengths_row, id_col, id_row, inverse, count):
    zero = jnp.zeros((1, 1), jnp.int32)
    segment_col, segment_row = jnp.zeros_like(id_col), jnp.zeros_like(id_row)
    ends, starts, end = [], [], zero
    for index in range(count):
        starts.append(end)
        end = end + lengths_row[:, index : index + 1]
        ends.append(end)
        segment_col = segment_col + jnp.where(id_col >= end, 1, 0)
        segment_row = segment_row + jnp.where(id_row >= end, 1, 0)
    start_of = jnp.zeros_like(id_col)
    for index in range(count):
        start_of = start_of + jnp.where(segment_col == index, starts[index], 0)
    angles = f32(id_col - start_of) * inverse
    return segment_col, segment_row, jnp.cos(angles), jnp.sin(angles)


def first_kernel(
    documents,
    rows_ref,
    qkv_ref,
    out_ref,
    gate_ref,
    up_ref,
    down_ref,
    lengths_ref,
    id_col,
    id_row,
    inverse_ref,
    head_norms,
    input_ref,
    norm_ref,
    upstream_ref,
    rows_all,
    gate_rows,
    up_rows,
    gate_all,
    above_ref,
    below_ref,
    upstream_all,
    qkv_hbm,
    out_hbm,
    raw_hbm,
    low_hbm,
    cos_hbm,
    sin_hbm,
    segment_col,
    segment_row,
    attended,
    hidden,
    normed,
    marks_ref,
    qkv_all,
    out_all,
    raw_out,
    low_out,
    cos_out,
    sin_out,
    lengths_all,
    row_block,
    heads_stage,
    pair_stage,
    pair_got,
):
    place = Place()
    marks = Marks(marks_ref)
    greet(place, [place.x, place.y, place.d, place.pair], True)
    rows, width = rows_ref.shape
    head_part = raw_out.shape[3]
    heads = head_part // HEAD_SIZE - 2
    lengths = Exchange(
        place, lambda p, step: lengths_ref, lambda p, step: lengths_all.at[step], marks
    )
    qkv_pieces = Exchange(
        place, lambda p, step: qkv_ref.at[p], lambda p, step: qkv_all.at[place.z, p], marks
    )
    gate_pieces = Exchange(
        place, lambda p, step: gate_ref.at[p], lambda p, step: gate_rows.at[p], marks
    )
    up_pieces = Exchange(place, lambda p, step: up_ref.at[p], lambda p, step: up_rows.at[p], marks)
    tokens = TokensGather(place, rows_ref, rows_all, marks)
    upstream = TokensGather(place, upstream_ref, upstream_all, marks)
    qkv_line = LineGather(
        place, qkv_all.at[place.z], lambda z: qkv_all.at[z], marks.take(4), marks.take(4)
    )
    gate_line = LineGather(
        place, gate_rows, lambda z: gate_all.at[z], marks.take(4), marks.take(4)
    )
    out_line = LineGather(
        place, out_ref, lambda z: out_all.at[z, place.p], marks.take(4), marks.take(4)
    )
    own_copies = [
        pltpu.make_async_copy(out_ref, out_all.at[place.z, place.p], marks.take()),
    ]
    gate_copy = pltpu.make_async_copy(gate_rows, gate_all.at[place.z], marks.take())
    near_recv = [marks.take(), marks.take()]
    to_down = remote(down_ref, above_ref, marks.take(), near_recv[0], place.down)
    to_up = remote(down_ref, below_ref, marks.take(), near_recv[1], place.up)
    out_planes = []
    for turn in range(4):
        z = place.z if turn == 0 else place.at(out_line.step(turn))
        out_planes.append(
            PlaneGather(
                place,
                out_ref if turn == 0 else out_all.at[z, place.p],
                lambda p, part, z=z: out_all.at[z, p, part],
                out_ref.shape[0],
                marks.take(4),
                marks.take(4),
            )
        )
    heads_out = Exchange(
        place, lambda p, step: heads_stage.at[step], lambda p, step: attended.at[p], marks
    )
    to_pair = remote(pair_stage, pair_got, marks.take(), marks.take(), place.pair)
    fetch_marks = marks.take(2)
    qkv_copy = pltpu.make_async_copy(qkv_all, qkv_hbm, marks.take())
    out_copy = pltpu.make_async_copy(out_all, out_hbm, marks.take())
    bucket_copies = [
        pltpu.make_async_copy(raw_out, raw_hbm, marks.take()),
        pltpu.make_async_copy(low_out, low_hbm, marks.take()),
    ]
    table_copies = [
        pltpu.make_async_copy(cos_out, cos_hbm, marks.take()),
        pltpu.make_async_copy(sin_out, sin_hbm, marks.take()),
    ]

    lengths.start()
    qkv_pieces.start()
    gate_pieces.start()
    tokens.start()
    for copy in own_copies:
        copy.start()
    lengths.wait()
    qkv_pieces.wait()
    qkv_line.start()

    def table_work(step, carry):
        seg_col, seg_row, cosine, sine = tables_of(
            lengths_all[step][:1], id_col[...], id_row[...], inverse_ref[...], documents
        )
        segment_col[step] = seg_col
        segment_row[step] = seg_row
        cos_out[step] = cosine
        lane = lax.broadcasted_iota(jnp.int32, sine.shape, 1)
        sin_out[step] = jnp.where(lane < HEAD_SIZE // 2, -sine, sine)
        return carry

    lax.fori_loop(0, 2, table_work, 0)
    tokens.forward()
    out_planes[0].start()
    lax.fori_loop(2, 4, table_work, 0)
    qkv_line.wait(2)
    out_line.start()
    tokens.last()
    out_planes[0].forward()
    qkv_line.wait(1)
    qkv_line.wait(3)
    out_line.wait(2)
    out_planes[2].start()
    gate_pieces.wait()
    gate_line.start()
    gate_copy.start()
    for copy in table_copies:
        copy.start()
    qkv_copy.start()
    tokens.finish()

    def fetches(step):
        return (
            pltpu.make_async_copy(rows_all.at[step], row_block.at[0], fetch_marks.at[0]),
            pltpu.make_async_copy(rows_all.at[4 + step], row_block.at[1], fetch_marks.at[1]),
        )

    def bucket(turn, carry):
        step = 3 - turn
        for copy in fetches(step):
            copy.start()
        for copy in fetches(step):
            copy.wait()
        raw = matmul(
            row_block[...].reshape(2 * rows, width), qkv_all[...].reshape(width, head_part)
        )
        raw_out[0, step] = raw[:rows]
        raw_out[1, step] = raw[rows:]
        allowed = (segment_col[step] == segment_row[step]) & (id_row[...] <= id_col[...])
        turned = []
        for head in range(heads + 1):
            gain = head_norms[min(head // heads, 1)][None, :]
            unnormed = lanes(raw, head)
            turned.append(
                low(
                    turn_pairs(
                        unnormed * inv_rms(unnormed) * gain, cos_out[step], sin_out[step]
                    )
                )
            )
        value = low(lanes(raw, heads + 1))
        outs = [
            low(matmul(low(softmax_of(turned[head], turned[heads], allowed)), value))
            for head in range(heads)
        ]
        kept = jnp.concatenate(turned + [value], axis=1)
        low_out[0, step] = kept[:rows]
        low_out[1, step] = kept[rows:]
        outs = jnp.concatenate(outs, axis=1)
        heads_stage[step, 0] = outs[:rows]
        heads_stage[step, 1] = outs[rows:]
        for index, at in enumerate((1, 2, 3)):
            pl.when(step == at)(heads_out.sends[index].start)
        pl.when(step == 0)(heads_out.copy.start)
        return carry

    lax.fori_loop(0, 1, bucket, 0)
    out_line.wait(1)
    out_line.wait(3)
    out_planes[1].start()
    out_planes[3].start()
    up_pieces.start()
    lax.fori_loop(1, 2, bucket, 0)
    out_planes[2].forward()
    upstream.start()
    lax.fori_loop(2, 3, bucket, 0)
    out_planes[1].forward()
    out_planes[3].forward()
    lax.fori_loop(3, 4, bucket, 0)
    for copy in bucket_copies:
        copy.start()
    gate_line.wait(2)
    pl.when(place.z > 0)(to_down.start)
    pl.when(place.z < 3)(to_up.start)
    for plane in out_planes:
        plane.wait_far()
    for copy in own_copies:
        copy.wait()
    out_copy.start()
    heads_out.wait()
    upstream.forward()

    def projected(core_step):
        block = jnp.concatenate([attended[p, core_step] for p in range(4)], axis=1)
        return matmul(block, out_all[...].reshape(block.shape[1], width))

    pair_stage[...] = low(projected(1))
    to_pair.start()
    hidden[...] = f32(input_ref[...]) + projected(0)
    to_pair.wait()
    norm_row = norm_ref[...]

    def norm_work(part):
        values = hidden[part] + f32(pair_got[part])
        hidden[part] = values
        normed[part] = low(values * inv_rms(values) * norm_row)

    each_rows(rows, 16, norm_work)
    gate_line.wait(1)
    gate_line.wait(3)
    upstream.last()
    up_pieces.wait()
    gate_copy.wait()
    for copy in [qkv_copy, out_copy] + bucket_copies + table_copies:
        copy.wait()
    upstream.finish()
    parts = [lengths, qkv_pieces, gate_pieces, up_pieces, heads_out, qkv_line, gate_line, out_line]
    for part in parts + out_planes:
        part.finish()

    @pl.when(place.z < 3)
    def _():
        arrived(above_ref, near_recv[0], place.two)
        to_up.wait_send()

    @pl.when(place.z > 0)
    def _():
        arrived(below_ref, near_recv[1], place.two)
        to_down.wait_send()


def first_part(
    rows,
    qkv_pieces,
    output_weight,
    gate_pieces,
    up_pieces,
    down_weight,
    doc_lengths,
    row_ids,
    head_norms,
    layer_input,
    mlp_norm,
    grad_out,
):
    block_rows, width = rows.shape
    group_rows = 2 * block_rows
    weight_rows, head_part = qkv_pieces.shape[1:]
    query_part = head_part - 2 * HEAD_SIZE
    documents = doc_lengths.shape[1]
    lengths = jnp.pad(doc_lengths, ((0, 7), (0, HEAD_SIZE - documents)))
    half = jnp.arange(HEAD_SIZE // 2, dtype=jnp.float32)
    inverse = ROPE_BASE ** (-(half * (2.0 / HEAD_SIZE)))
    low_like = lambda *shape: jax.ShapeDtypeStruct(shape, LOW)
    table = jax.ShapeDtypeStruct((4, group_rows, HEAD_SIZE), jnp.float32)
    return pl.pallas_call(
        lambda *refs: first_kernel(documents, *refs),
        out_shape=(
            low_like(8, block_rows, width),
            low_like(*gate_pieces.shape),
            low_like(*up_pieces.shape),
            low_like(4, *gate_pieces.shape),
            low_like(*down_weight.shape),
            low_like(*down_weight.shape),
            low_like(8, block_rows, width),
            low_like(4, *qkv_pieces.shape),
            low_like(4, 4, *output_weight.shape),
            jax.ShapeDtypeStruct((2, 4, block_rows, head_part), jnp.float32),
            low_like(2, 4, block_rows, head_part),
            table,
            table,
            jax.ShapeDtypeStruct((4, group_rows, 1), jnp.int32),
            jax.ShapeDtypeStruct((4, 1, group_rows), jnp.int32),
            low_like(4, 2, block_rows, query_part),
            jax.ShapeDtypeStruct((block_rows, width), jnp.float32),
            low_like(block_rows, width),
        ),
        in_specs=[ANYWHERE] * 6 + [WHOLE] * 7 + [ANYWHERE],
        out_specs=(ANYWHERE,) * 13 + (WHOLE,) * 5,
        scratch_shapes=[
            pltpu.SemaphoreType.DMA((160,)),
            pltpu.VMEM((4,) + qkv_pieces.shape, LOW),
            pltpu.VMEM((4, 4) + output_weight.shape, LOW),
            pltpu.VMEM((2, 4, block_rows, head_part), jnp.float32),
            pltpu.VMEM((2, 4, block_rows, head_part), LOW),
            pltpu.VMEM(table.shape, jnp.float32),
            pltpu.VMEM(table.shape, jnp.float32),
            pltpu.VMEM((4,) + lengths.shape, jnp.int32),
            pltpu.VMEM((2, block_rows, width), LOW),
            pltpu.VMEM((4, 2, block_rows, query_part), LOW),
            pltpu.VMEM((block_rows, width), LOW),
            pltpu.VMEM((block_rows, width), LOW),
        ],
        compiler_params=comm_params(0),
        cost_estimate=comm_cost(130),
    )(
        rows,
        qkv_pieces,
        output_weight,
        gate_pieces,
        up_pieces,
        down_weight,
        lengths,
        row_ids[:, None],
        row_ids[None, :],
        jnp.concatenate([inverse, inverse])[None],
        head_norms,
        layer_input,
        mlp_norm[None],
        grad_out,
    )


class FarScatter:
    @staticmethod
    def scratch(rows, width):
        return [pltpu.VMEM((2, rows // 2, width), LOW)]

    def __init__(self, place, summed, buffers, marks):
        self.place, self.summed, self.landed = place, summed, buffers[0]
        self.half = summed.shape[1] // 2
        self.recv = [marks.take(), marks.take()]
        self.sends = [
            remote(
                summed.at[3, pl.ds(index * self.half, self.half)],
                self.landed.at[index],
                marks.take(),
                self.recv[index],
                to,
            )
            for index, to in enumerate((place.x, place.y))
        ]

    def start(self):
        for copy in self.sends:
            copy.start()

    def add(self):
        summed, landed = self.summed, self.landed
        for index, block, base, to in (
            (0, 2, 0, self.place.x),
            (1, 1, self.half, self.place.y),
        ):
            arrived(landed.at[index], self.recv[index], to)

            def work(rows):
                own_rows = pl.ds(pl.multiple_of(rows.start + base, 16), rows.size)
                summed[block, own_rows] = low(
                    f32(summed[block, own_rows]) + f32(landed[index, rows])
                )

            each_rows(self.half, 16, work)

    def drain(self):
        for copy in self.sends:
            copy.wait_send()


class NearScatter:
    @staticmethod
    def scratch(rows, width):
        return [pltpu.VMEM((3, rows, width), LOW)]

    def __init__(self, place, summed, buffers, marks):
        self.place, self.landed = place, buffers[0]
        self.load = pltpu.make_async_copy(summed.at[0], self.landed.at[2], marks.take())
        self.recv = [marks.take(), marks.take()]
        self.sends = [
            remote(summed.at[1 + index], self.landed.at[index], marks.take(), self.recv[index], to)
            for index, to in enumerate((place.x, place.y))
        ]

    def start(self):
        self.load.start()
        for copy in self.sends:
            copy.start()

    def finish(self, work):
        landed = self.landed
        self.load.wait()
        for index, to in enumerate((self.place.x, self.place.y)):
            arrived(self.landed.at[index], self.recv[index], to)

        def total(rows):
            work(
                rows,
                f32(landed[0, rows]) + f32(landed[1, rows]) + f32(landed[2, rows]),
            )

        each_rows(landed.shape[1], 16, total)

    def drain(self):
        for copy in self.sends:
            copy.wait_send()


class PlaneScatter:
    @staticmethod
    def scratch(rows, width):
        return [pltpu.VMEM((6, rows // 2, width), LOW)]

    def __init__(self, place, summed, out, buffers, marks, at=(0, 1, 2, 3)):
        self.place, self.summed, self.out, self.at = place, summed, out, at
        self.landed = buffers[0]
        self.rows = summed.shape[1]
        half = self.rows // 2
        top, end = pl.ds(0, half), pl.ds(half, half)
        x, y = place.x, place.y
        self.recv = [marks.take() for _ in range(6)]
        routes = (
            (summed.at[at[3], top], x),
            (summed.at[at[3], end], y),
            (summed.at[at[1], top], x),
            (summed.at[at[1], end], x),
            (summed.at[at[2], top], y),
            (summed.at[at[2], end], y),
        )
        self.sends = [
            remote(src, self.landed.at[index], marks.take(), self.recv[index], to)
            for index, (src, to) in enumerate(routes)
        ]

    def start(self):
        for index in (0, 1, 2, 5):
            self.sends[index].start()

    def landed_at(self, index, to):
        arrived(self.landed.at[index], self.recv[index], to)

    def middle(self):
        half = self.rows // 2
        summed, landed = self.summed, self.landed
        _, for_x, for_y, _ = self.at
        self.landed_at(0, self.place.x)

        def top_work(rows):
            summed[for_y, rows] = low(f32(summed[for_y, rows]) + f32(landed[0, rows]))

        each_rows(half, 16, top_work)
        self.sends[4].start()
        self.landed_at(1, self.place.y)

        def end_work(rows):
            end_rows = pl.ds(pl.multiple_of(rows.start + half, 16), rows.size)
            summed[for_x, end_rows] = low(f32(summed[for_x, end_rows]) + f32(landed[1, rows]))

        each_rows(half, 16, end_work)
        self.sends[3].start()

    def finish(self):
        half = self.rows // 2
        for index, to in ((2, self.place.x), (5, self.place.y), (4, self.place.y), (3, self.place.x)):
            self.landed_at(index, to)

        for base, first, second in ((0, 2, 4), (half, 3, 5)):

            def work(rows):
                own_rows = pl.ds(pl.multiple_of(rows.start + base, 16), rows.size)
                self.out[own_rows] = (
                    f32(self.summed[self.at[0], own_rows])
                    + f32(self.landed[first, rows])
                    + f32(self.landed[second, rows])
                ).astype(self.out.dtype)

            each_rows(half, 16, work)

    def drain(self):
        for copy in self.sends:
            copy.wait_send()


def blocks_of(source, block_ref, marks, first, last, work):
    def fetch(block):
        return pltpu.make_async_copy(
            source(block), block_ref.at[block % 2], marks.at[block % 2]
        )

    fetch(first).start()

    def body(block, carry):
        fetch(block).wait()

        @pl.when(block < last - 1)
        def _():
            fetch(block + 1).start()

        work(block, block_ref[block % 2])
        return carry

    lax.fori_loop(first, last, body, 0)


def unit_values(raws, inner_grad):
    units = inner_grad.shape[1]
    gate_raw, up_raw = raws[:, :units], raws[:, units:]
    sigmoid_gate = jax.nn.sigmoid(gate_raw)
    activated = gate_raw * sigmoid_gate
    gate_grad = inner_grad * up_raw * sigmoid_gate * (1.0 + gate_raw * (1.0 - sigmoid_gate))
    return low(activated * up_raw), jnp.concatenate(
        [low(gate_grad), low(inner_grad * activated)], axis=1
    )


def units_kernel(
    rows_ref,
    upstream_ref,
    line_ref,
    first_ref,
    down_ref,
    above_ref,
    below_ref,
    rows_all,
    inner_out,
    second_grad,
    first_sum,
    down_part,
    part_sums,
    grad_sums,
    marks_ref,
    first_mat,
    second_mat,
    down_mat,
    upstream,
    row_block,
    row_slab,
    inner_first,
    first_grad,
    inner_grads,
    first_part,
    inner_stage,
    second_stage,
    *buffers,
):
    place = Place()
    marks = Marks(marks_ref)
    greet(place, [place.x, place.y, place.pair], True)
    tokens = TokensGather(place, rows_ref, rows_all, marks)
    line = LineGather(place, line_ref, lambda z: second_mat.at[z], marks.take(4), marks.take(4))
    far_recv = marks.take(2)
    two = down_mat.at[:, place.at(2)]
    to_two = remote(down_ref, down_mat.at[:, place.z], marks.take(), far_recv.at[0], place.two)
    pass_mark = marks.take()
    pass_down = remote(two, two, pass_mark, far_recv.at[1], place.down)
    pass_up = remote(two, two, pass_mark, far_recv.at[1], place.up)
    copies = [
        pltpu.make_async_copy(line_ref, second_mat.at[place.z], marks.take()),
        pltpu.make_async_copy(first_ref, first_mat, marks.take()),
        pltpu.make_async_copy(down_ref, down_mat.at[:, place.z], marks.take()),
        pltpu.make_async_copy(upstream_ref, upstream, marks.take()),
    ]
    above = pltpu.make_async_copy(above_ref, down_mat.at[:, place.at(1)], marks.take())
    below = pltpu.make_async_copy(below_ref, down_mat.at[:, place.at(3)], marks.take())
    line_rows = first_sum.shape[0]
    first_line = LineScatter(
        place,
        lambda z: first_part.at[pl.ds(pl.multiple_of(z * line_rows, 16), line_rows)],
        first_sum,
        buffers[:1],
        marks,
        True,
    )
    part_far = FarScatter(place, part_sums, buffers[1:2], marks)
    grad_far = FarScatter(place, grad_sums, buffers[2:], marks)
    fetch_marks, slab_marks = marks.take(2), marks.take(2)
    send_marks, recv_marks = marks.take(8), marks.take(8)
    width = rows_ref.shape[1]
    half = inner_first.shape[2]
    all_rows = 8 * rows_ref.shape[0]

    to_two.start()
    tokens.start()
    for copy in copies:
        copy.start()
    pl.when(place.z < 3)(above.start)
    pl.when(place.z > 0)(below.start)
    tokens.forward()
    arrived(two, far_recv.at[0], place.two)
    pl.when(place.z == 1)(pass_down.start)
    pl.when(place.z == 2)(pass_up.start)
    line.start()
    tokens.last()
    for copy in copies:
        copy.wait()
    pl.when(place.z < 3)(above.wait)
    pl.when(place.z > 0)(below.wait)

    @pl.when(place.z == 0)
    def _():
        arrived(down_mat.at[:, 3], far_recv.at[1], place.two)

    @pl.when(place.z == 3)
    def _():
        arrived(down_mat.at[:, 0], far_recv.at[1], place.two)

    tokens.finish()

    def first_work(block, values):
        grads = matmul_nt(upstream[block], down_mat[...].reshape(2 * half, width))
        inner_grads[block] = low(grads[:, half:])
        inner, grad = unit_values(matmul(values, first_mat[...]), grads[:, :half])
        inner_first[block] = inner
        first_grad[block] = grad

    blocks_of(lambda block: rows_all.at[block], row_block, fetch_marks, 0, 8, first_work)
    line.wait(2)
    tile = row_slab.shape[3]
    tiles = width // tile

    def slab(index):
        return rows_all.at[:, :, pl.ds(pl.multiple_of(index * tile, tile), tile)]

    def slab_work(index, values):
        first_part[pl.ds(pl.multiple_of(index * tile, tile), tile)] = low(
            matmul_tn(values.reshape(all_rows, tile), first_grad[...].reshape(all_rows, 2 * half))
        )

    down_part[...] = low(
        matmul_tn(
            inner_first[...].reshape(all_rows, half), upstream[...].reshape(all_rows, width)
        )
    )
    blocks_of(slab, row_slab, slab_marks, 0, tiles, slab_work)
    line.wait(1)
    line.wait(3)
    first_line.start()

    def fetch(index):
        step, slot = 3 - index // 2, index % 2
        return pltpu.make_async_copy(
            rows_all.at[step + 4 * (1 - slot)], row_block.at[slot], fetch_marks.at[slot]
        )

    def sends(step):
        return (
            remote(
                upstream.at[step],
                part_sums.at[step],
                send_marks.at[step],
                recv_marks.at[step],
                place.pair,
            ),
            remote(
                upstream.at[4 + step],
                grad_sums.at[step],
                send_marks.at[4 + step],
                recv_marks.at[4 + step],
                place.pair,
            ),
        )

    store_marks = marks.take(4)

    def stores(slot, block):
        return (
            pltpu.make_async_copy(
                inner_stage.at[slot], inner_out.at[block], store_marks.at[slot]
            ),
            pltpu.make_async_copy(
                second_stage.at[slot], second_grad.at[block], store_marks.at[2 + slot]
            ),
        )

    fetch(0).start()

    def blocks(turn, carry):
        step = 3 - turn
        for slot in range(2):
            index = 2 * turn + slot
            block = step + 4 * (1 - slot)
            fetch(index).wait()

            @pl.when(index < 7)
            def _():
                fetch(index + 1).start()

            second = second_mat[...].reshape(width, 2 * half)
            inner, grad = unit_values(matmul(row_block[slot], second), f32(inner_grads[block]))

            @pl.when(turn > 0)
            def _():
                for copy in stores(slot, block + 1):
                    copy.wait()

            inner_stage[slot] = inner
            second_stage[slot] = grad
            for copy in stores(slot, block):
                copy.start()
            part = matmul(
                jnp.concatenate([inner_first[block], inner], axis=1),
                down_mat[...].reshape(2 * half, width),
            )
            grad = matmul_nt(first_grad[block], first_mat[...]) + matmul_nt(grad, second)
            if slot == 0:
                upstream[step] = low(part)
                upstream[4 + step] = low(grad)
                for copy in sends(step):
                    copy.start()
            else:
                for copy in sends(step):
                    copy.wait_recv()
                part_sums[step] = low(part + f32(part_sums[step]))
                grad_sums[step] = low(grad + f32(grad_sums[step]))
        return carry

    lax.fori_loop(0, 1, blocks, 0)
    grad_far.start()
    part_far.start()
    lax.fori_loop(1, 2, blocks, 0)
    first_line.middle()
    lax.fori_loop(2, 4, blocks, 0)
    for slot in range(2):
        for copy in stores(slot, 4 * (1 - slot)):
            copy.wait()
    grad_far.add()
    part_far.add()
    first_line.finish()
    first_line.drain()
    grad_far.drain()
    part_far.drain()
    for step in range(4):
        for copy in sends(step):
            copy.wait_send()
    line.finish()
    to_two.wait_send()
    pl.when(place.z == 1)(pass_down.wait_send)
    pl.when(place.z == 2)(pass_up.wait_send)


def units_products(rows, upstream, second_rows, first_all, down_weight, above, below):
    block_rows, width = rows.shape
    half = first_all.shape[1] // 2
    half_rows = down_weight.shape[1]
    hidden = lambda count: jax.ShapeDtypeStruct((8, block_rows, count * half), LOW)
    sums = jax.ShapeDtypeStruct((4, block_rows, width), LOW)
    blocks = jax.ShapeDtypeStruct((8, block_rows, width), LOW)
    return pl.pallas_call(
        units_kernel,
        out_shape=(
            blocks,
            hidden(1),
            hidden(2),
            jax.ShapeDtypeStruct(second_rows.shape, LOW),
            jax.ShapeDtypeStruct((half, width), LOW),
            sums,
            sums,
        ),
        in_specs=[ANYWHERE] * 7,
        out_specs=(ANYWHERE,) * 3 + (WHOLE,) * 4,
        scratch_shapes=[
            pltpu.SemaphoreType.DMA((100,)),
            pltpu.VMEM(first_all.shape, LOW),
            pltpu.VMEM((4,) + second_rows.shape, LOW),
            pltpu.VMEM((2, 4, half_rows, width), LOW),
            pltpu.VMEM((8, block_rows, width), LOW),
            pltpu.VMEM((2, block_rows, width), LOW),
            pltpu.VMEM((2, 8, block_rows, 256), LOW),
            pltpu.VMEM((8, block_rows, half), LOW),
            pltpu.VMEM((8, block_rows, 2 * half), LOW),
            pltpu.VMEM((8, block_rows, half), LOW),
            pltpu.VMEM((width, 2 * half), LOW),
            pltpu.VMEM((2, block_rows, half), LOW),
            pltpu.VMEM((2, block_rows, 2 * half), LOW),
        ]
        + LineScatter.scratch(*second_rows.shape, True)
        + FarScatter.scratch(block_rows, width) * 2,
        compiler_params=comm_params(1),
        cost_estimate=comm_cost(150),
    )(rows, upstream, second_rows, first_all, down_weight, above, below)


def unit_grads_kernel(
    rows_all,
    upstream_ref,
    inner_ref,
    second_ref,
    down_first,
    part_sums,
    grad_sums,
    hidden_ref,
    upstream_own,
    norm_ref,
    layer_out,
    hidden_grad,
    branch,
    mlp_gain,
    down_out,
    second_part,
    marks_ref,
    upstream,
    inner,
    second_grad,
    row_slab,
    gain_rows,
    down_part,
    *buffers,
):
    place = Place()
    marks = Marks(marks_ref)
    greet(place, [place.x, place.y], True)
    grad_near = NearScatter(place, grad_sums, buffers[:1], marks)
    part_near = NearScatter(place, part_sums, buffers[1:2], marks)
    half_rows = down_out.shape[1]
    first_line = LineScatter(
        place, lambda z: down_first.at[z], down_out.at[0], buffers[2:3], marks
    )
    second_line = LineScatter(
        place,
        lambda z: down_part.at[pl.ds(pl.multiple_of(z * half_rows, 16), half_rows)],
        down_out.at[1],
        buffers[3:],
        marks,
        True,
    )
    loads = [
        pltpu.make_async_copy(upstream_ref, upstream, marks.take()),
        pltpu.make_async_copy(inner_ref, inner, marks.take()),
        pltpu.make_async_copy(second_ref, second_grad, marks.take()),
    ]
    slab_marks = marks.take(2)
    rows, width = hidden_ref.shape
    half = inner.shape[2]
    all_rows = 8 * rows
    tile = row_slab.shape[3]
    tiles = width // tile

    def slab(index):
        return rows_all.at[:, :, pl.ds(pl.multiple_of(index * tile, tile), tile)]

    def slab_work(index, values):
        second_part[pl.ds(pl.multiple_of(index * tile, tile), tile)] = low(
            matmul_tn(values.reshape(all_rows, tile), second_grad[...].reshape(all_rows, 2 * half))
        )

    first_line.start()
    grad_near.start()
    for copy in loads:
        copy.start()
    loads[0].wait()
    loads[1].wait()
    down_part[...] = low(
        matmul_tn(inner[...].reshape(all_rows, half), upstream[...].reshape(all_rows, width))
    )
    loads[2].wait()
    blocks_of(slab, row_slab, slab_marks, 0, tiles // 2, slab_work)
    first_line.middle()
    second_line.start()
    blocks_of(slab, row_slab, slab_marks, tiles // 2, tiles, slab_work)
    second_line.middle()
    part_near.start()
    gain_rows[...] = jnp.zeros_like(gain_rows)
    norm_row = norm_ref[...]

    def norm_work(rows, row_grad):
        values = hidden_ref[rows]
        scales = inv_rms(values)
        weighted = row_grad * norm_row
        inner_mean = jnp.mean(weighted * values, axis=-1, keepdims=True)
        grad = (
            f32(upstream_own[rows])
            + scales * weighted
            - values * (scales * scales * scales) * inner_mean
        )
        hidden_grad[rows] = grad
        branch[rows] = low(grad)
        parts = row_grad * values * scales
        gain_rows[...] += parts[:8] + parts[8:]

    def out_work(rows, row_part):
        layer_out[rows] = low(hidden_ref[rows] + row_part)

    grad_near.finish(norm_work)
    mlp_gain[...] = jnp.sum(gain_rows[...], axis=0, keepdims=True)
    part_near.finish(out_work)
    first_line.finish()
    second_line.finish()
    for part in (first_line, second_line, grad_near, part_near):
        part.drain()


def unit_grads(
    rows_all,
    upstream,
    inner,
    second_grad,
    down_first,
    part_sums,
    grad_sums,
    hidden,
    upstream_own,
    norm,
):
    _, rows, width = rows_all.shape
    half = inner.shape[2]
    half_rows = down_first.shape[1]
    return pl.pallas_call(
        unit_grads_kernel,
        out_shape=(
            jax.ShapeDtypeStruct((rows, width), LOW),
            jax.ShapeDtypeStruct((rows, width), jnp.float32),
            jax.ShapeDtypeStruct((rows, width), LOW),
            jax.ShapeDtypeStruct((1, width), jnp.float32),
            jax.ShapeDtypeStruct((2, half_rows, width), LOW),
            jax.ShapeDtypeStruct((width, 2 * half), LOW),
        ),
        in_specs=[ANYWHERE] * 7 + [WHOLE] * 3,
        out_specs=(WHOLE,) * 6,
        scratch_shapes=[
            pltpu.SemaphoreType.DMA((64,)),
            pltpu.VMEM(upstream.shape, LOW),
            pltpu.VMEM(inner.shape, LOW),
            pltpu.VMEM(second_grad.shape, LOW),
            pltpu.VMEM((2, 8, rows, 256), LOW),
            pltpu.VMEM((8, width), jnp.float32),
            pltpu.VMEM((half, width), LOW),
        ]
        + NearScatter.scratch(rows, width) * 2
        + LineScatter.scratch(half_rows, width)
        + LineScatter.scratch(half_rows, width, True),
        compiler_params=comm_params(4),
        cost_estimate=comm_cost(65),
    )(
        rows_all,
        upstream,
        inner,
        second_grad,
        down_first,
        part_sums,
        grad_sums,
        hidden,
        upstream_own,
        norm,
    )


def last_kernel(
    parts_ref,
    qkv_ref,
    proj_ref,
    second_ref,
    input_ref,
    hidden_ref,
    norm_ref,
    gains_ref,
    grad_ref,
    qkv_columns,
    proj_out,
    second_columns,
    gains_out,
    marks_ref,
    qkv_sum,
    row_sum,
    gain_rows,
    gain_mine,
    gain_got,
    *buffers,
):
    place = Place()
    marks = Marks(marks_ref)
    greet(place, [place.x, place.y, place.d, place.pair], True)
    tokens = PlaneScatter(place, parts_ref, row_sum, buffers[:1], marks)
    qkv_line = LineScatter(place, lambda z: qkv_ref.at[z], qkv_sum, buffers[1:2], marks)
    proj_line = LineScatter(place, lambda z: proj_ref.at[z], proj_out, buffers[2:], marks)
    rows = qkv_sum.shape[0] // 4
    qkv_pieces = Exchange(
        place,
        lambda p, step: qkv_sum.at[pl.ds(pl.multiple_of(p * rows, rows), rows)],
        lambda p, step: qkv_columns.at[p],
        marks,
    )
    second_pieces = Exchange(
        place, lambda p, step: second_ref.at[p], lambda p, step: second_columns.at[p], marks
    )
    near_z = {"f": place.z + 1 - 2 * (place.z % 2)}
    rounds = [
        remote(gain_mine.at[index], gain_got.at[index], marks.take(), marks.take(), to)
        for index, to in enumerate((place.pair, place.x, place.y, near_z, place.two))
    ]

    tokens.start()
    qkv_line.start()
    qkv_line.middle()
    tokens.middle()
    second_pieces.start()
    proj_line.start()
    tokens.finish()
    proj_line.middle()

    qkv_line.finish()
    qkv_pieces.start()
    gain_rows[...] = jnp.zeros_like(gain_rows)
    norm_row = norm_ref[...]

    def work(rows):
        values = f32(input_ref[rows])
        scales = inv_rms(values)
        upstream = row_sum[rows]
        weighted = upstream * norm_row
        inner_mean = jnp.mean(weighted * values, axis=-1, keepdims=True)
        grad_ref[rows] = (
            hidden_ref[rows]
            + scales * weighted
            - values * (scales * scales * scales) * inner_mean
        )
        parts = upstream * values * scales
        gain_rows[...] += parts[:8] + parts[8:]

    each_rows(row_sum.shape[0], 16, work)
    width = norm_row.shape[1]
    gain_mine[0, :, pl.ds(0, width)] = jnp.sum(gain_rows[...], axis=0, keepdims=True)
    gain_mine[0, :, pl.ds(width, gains_ref.shape[1])] = gains_ref[...]
    for index, copy in enumerate(rounds):
        copy.start()
        copy.wait()
        summed = gain_mine[index] + gain_got[index]
        if index < 4:
            gain_mine[index + 1] = summed
        else:
            gains_out[...] = summed
    proj_line.finish()
    qkv_line.drain()
    proj_line.drain()
    tokens.drain()
    qkv_pieces.wait()
    qkv_pieces.finish()
    second_pieces.wait()
    second_pieces.finish()


def last_sums(parts, qkv_parts, proj_parts, second_rows, layer_input, hidden_grad, norm, gains):
    rows, width = parts.shape[1:]
    qkv_rows, qkv_width = qkv_parts.shape[1:]
    gain_width = width + gains.shape[1]
    return pl.pallas_call(
        last_kernel,
        out_shape=(
            jax.ShapeDtypeStruct((rows, width), jnp.float32),
            jax.ShapeDtypeStruct((4, qkv_rows // 4, qkv_width), LOW),
            jax.ShapeDtypeStruct(proj_parts.shape[1:], LOW),
            jax.ShapeDtypeStruct(second_rows.shape, LOW),
            jax.ShapeDtypeStruct((1, gain_width), jnp.float32),
        ),
        in_specs=[WHOLE] + [ANYWHERE] * 3 + [WHOLE] * 4,
        out_specs=(WHOLE, ANYWHERE, WHOLE, ANYWHERE, WHOLE),
        scratch_shapes=[
            pltpu.SemaphoreType.DMA((100,)),
            pltpu.VMEM((qkv_rows, qkv_width), LOW),
            pltpu.VMEM((rows, width), jnp.float32),
            pltpu.VMEM((8, width), jnp.float32),
            pltpu.VMEM((5, 1, gain_width), jnp.float32),
            pltpu.VMEM((5, 1, gain_width), jnp.float32),
        ]
        + PlaneScatter.scratch(rows, width)
        + LineScatter.scratch(qkv_rows, qkv_width)
        + LineScatter.scratch(*proj_parts.shape[1:]),
        compiler_params=comm_params(5),
        cost_estimate=comm_cost(60),
    )(parts, qkv_parts, proj_parts, second_rows, layer_input, hidden_grad, norm, gains)


def turn_pairs(values, cosine, sine):
    return values * cosine + pltpu.roll(values, HEAD_SIZE // 2, 1) * sine


def softmax_of(query, key, allowed):
    scores = matmul_nt(query, key) * HEAD_SIZE ** (-0.5)
    masked = jnp.where(allowed, scores, MASKED)
    exponent = jnp.exp(masked - jnp.max(masked, axis=-1, keepdims=True))
    return exponent / jnp.sum(exponent, axis=-1, keepdims=True)


def lanes(values, head):
    return values[:, head * HEAD_SIZE : (head + 1) * HEAD_SIZE]


def roll_half(values):
    return pltpu.roll(values, HEAD_SIZE // 2, 1)


def attend_back_values(raw, kept, grad, allowed, cosine, sine, gains_ref, roll=roll_half):
    group_rows = raw.shape[0]
    heads = raw.shape[1] // HEAD_SIZE - 2
    key, value = lanes(kept, heads), lanes(kept, heads + 1)
    scale = HEAD_SIZE ** (-0.5)
    turned_grads = []
    key_grad = jnp.zeros((group_rows, HEAD_SIZE), jnp.float32)
    value_grad = jnp.zeros((group_rows, HEAD_SIZE), jnp.float32)
    for head in range(heads):
        query, upstream = lanes(kept, head), lanes(grad, head)
        probs = softmax_of(query, key, allowed)
        probs_grad = matmul_nt(upstream, value)
        scores_grad = low(
            probs * (probs_grad - jnp.sum(probs * probs_grad, axis=-1, keepdims=True))
        )
        turned_grads.append(matmul(scores_grad, key) * scale)
        key_grad = key_grad + matmul_tn(scores_grad, query)
        value_grad = value_grad + matmul_tn(low(probs), upstream)
    turned_grads.append(key_grad * scale)
    outs, gains = [], []
    for head in range(heads + 1):
        gain = gains_ref[min(head // heads, 1)][None, :]
        unnormed = lanes(raw, head)
        upstream = turned_grads[head] * cosine - roll(turned_grads[head]) * sine
        grad_raw, gain_part = norm_back(unnormed, inv_rms(unnormed), gain, upstream)
        outs.append(low(grad_raw))
        gains.append(gain_part[None, :])
    outs.append(low(value_grad))
    query_gain = sum(gains[1:heads], gains[0])
    return (jnp.concatenate(outs, axis=1), jnp.concatenate([query_gain, gains[heads]], axis=1))


def heads_back_kernel(
    branch_ref,
    out_ref,
    attended_ref,
    raw_ref,
    low_ref,
    cos_ref,
    sin_ref,
    segment_col,
    segment_row,
    id_col,
    id_row,
    gains_ref,
    rows_all,
    qkv_ref,
    second_part,
    first_rows,
    head_gain,
    qkv_part,
    proj_sum,
    grad_sums,
    line_sum,
    first_columns,
    marks_ref,
    out_mat,
    qkv_mat,
    attended,
    branch,
    own_grad,
    heads_grad,
    raw_block,
    low_block,
    qkv_grad,
    row_slab,
    proj_part,
    *buffers,
):
    place = Place()
    marks = Marks(marks_ref)
    greet(place, [place.x, place.y, place.d, place.pair], True)
    rows, width = branch_ref.shape
    half_heads = heads_grad.shape[2]
    group_rows = 2 * rows
    second_line = LineScatter(place, lambda z: second_part.at[z], line_sum, buffers[0:1], marks)
    first_pieces = Exchange(
        place, lambda p, step: first_rows.at[p], lambda p, step: first_columns.at[p], marks
    )
    proj_plane = PlaneScatter(
        place,
        proj_part,
        proj_sum,
        buffers[1:],
        marks,
        (place.p, place.px, place.py, place.pd),
    )
    heads = Exchange(
        place, lambda p, step: own_grad.at[p], lambda p, step: heads_grad.at[step], marks
    )
    to_pair = remote(branch_ref, branch.at[1], marks.take(), marks.take(), place.pair)
    loads = [
        pltpu.make_async_copy(out_ref, out_mat, marks.take()),
        pltpu.make_async_copy(attended_ref, attended, marks.take()),
        pltpu.make_async_copy(qkv_ref, qkv_mat, marks.take()),
    ]
    fetch_marks, slab_marks = marks.take(4), marks.take(2)
    send_marks, recv_marks = marks.take(4), marks.take(4)

    to_pair.start()
    second_line.start()
    for copy in loads:
        copy.start()
    branch[0] = branch_ref[...]
    for copy in loads:
        copy.wait()

    def own_half(core_step):
        grad = low(matmul_nt(branch[core_step], out_mat[...]))
        for p in range(4):
            own_grad[p, pl.ds(core_step * rows, rows)] = grad[
                :, p * half_heads : (p + 1) * half_heads
            ]

    own_half(0)
    to_pair.wait()
    own_half(1)
    heads.start()
    second_line.middle()

    def proj_work(z, carry):
        block = attended[z].reshape(group_rows, half_heads)
        grad = low(matmul_tn(block, branch[...].reshape(group_rows, width)))
        part = half_heads // 4
        for p in range(4):
            proj_part[p, pl.ds(pl.multiple_of(z * part, part), part)] = grad[
                p * part : (p + 1) * part
            ]
        return carry

    def fetches(step):
        return (
            pltpu.make_async_copy(raw_ref.at[:, step], raw_block, fetch_marks.at[0]),
            pltpu.make_async_copy(low_ref.at[:, step], low_block, fetch_marks.at[1]),
        )

    lax.fori_loop(0, 4, proj_work, 0)
    heads.wait()
    proj_plane.start()
    first_pieces.start()
    head_gain[...] = jnp.zeros_like(head_gain)

    def sends(step):
        return remote(
            out_mat.at[pl.ds(pl.multiple_of(step * rows, rows), rows)],
            grad_sums.at[step],
            send_marks.at[step],
            recv_marks.at[step],
            place.pair,
        )

    def bucket(step, carry):
        for copy in fetches(step):
            copy.start()
        for copy in fetches(step):
            copy.wait()
        allowed = (segment_col[step] == segment_row[step]) & (id_row[...] <= id_col[...])
        grads, gains = attend_back_values(
            raw_block[...].reshape(group_rows, -1),
            low_block[...].reshape(group_rows, -1),
            heads_grad[step],
            allowed,
            cos_ref[step],
            sin_ref[step],
            gains_ref,
        )
        head_gain[...] += gains
        qkv_grad[0, step] = grads[:rows]
        qkv_grad[1, step] = grads[rows:]
        out_mat[pl.ds(pl.multiple_of(step * rows, rows), rows)] = low(
            matmul_nt(grads[rows:], qkv_mat[...])
        )
        sends(step).start()
        return carry

    lax.fori_loop(0, 2, bucket, 0)
    proj_plane.middle()
    lax.fori_loop(2, 4, bucket, 0)

    tile = row_slab.shape[3]
    tiles = width // tile

    def slab(index):
        return pltpu.make_async_copy(
            rows_all.at[:, :, pl.ds(pl.multiple_of(index * tile, tile), tile)],
            row_slab.at[index % 2],
            slab_marks.at[index % 2],
        )

    slab(0).start()

    def own_work(step, carry):
        copy = sends(step)
        copy.wait_recv()
        grad = matmul_nt(qkv_grad[0, step], qkv_mat[...])
        grad_sums[step] = low(grad + f32(grad_sums[step]))
        return carry

    lax.fori_loop(0, 4, own_work, 0)

    def row_tile(index, carry):
        slab(index).wait()

        @pl.when(index < tiles - 1)
        def _():
            slab(index + 1).start()

        block = row_slab[index % 2].reshape(4 * group_rows, tile)
        out_rows = pl.ds(pl.multiple_of(index * tile, tile), tile)
        qkv_part[out_rows] = low(
            matmul_tn(block, qkv_grad[...].reshape(4 * group_rows, qkv_grad.shape[3]))
        )
        return carry

    lax.fori_loop(0, tiles, row_tile, 0)
    second_line.finish()
    proj_plane.finish()
    for step in range(4):
        sends(step).wait_send()
    heads.finish()
    for part in (proj_plane, second_line):
        part.drain()
    first_pieces.wait()
    first_pieces.finish()


def heads_backward(
    branch,
    out_all,
    attended,
    raw,
    kept,
    tables,
    rows_all,
    qkv_all,
    second_part,
    first_rows,
):
    rows, width = branch.shape
    head_part = raw.shape[3]
    query_part = head_part - 2 * HEAD_SIZE
    line_rows, units = second_part.shape[1:]
    tile = 256
    return pl.pallas_call(
        heads_back_kernel,
        out_shape=(
            jax.ShapeDtypeStruct((1, 2 * HEAD_SIZE), jnp.float32),
            jax.ShapeDtypeStruct((width, head_part), LOW),
            jax.ShapeDtypeStruct((query_part, width), LOW),
            jax.ShapeDtypeStruct((4, rows, width), LOW),
            jax.ShapeDtypeStruct((line_rows, units), LOW),
            jax.ShapeDtypeStruct((4, line_rows // 4, units), LOW),
        ),
        in_specs=[WHOLE] + [ANYWHERE] * 4 + [WHOLE] * len(tables) + [ANYWHERE] * 4,
        out_specs=(WHOLE,) * 5 + (ANYWHERE,),
        scratch_shapes=[
            pltpu.SemaphoreType.DMA((120,)),
            pltpu.VMEM(out_all.shape, LOW),
            pltpu.VMEM(qkv_all.shape, LOW),
            pltpu.VMEM(attended.shape, LOW),
            pltpu.VMEM((2, rows, width), LOW),
            pltpu.VMEM((4, 2 * rows, query_part), LOW),
            pltpu.VMEM((4, 2 * rows, query_part), LOW),
            pltpu.VMEM((2, rows, head_part), jnp.float32),
            pltpu.VMEM((2, rows, head_part), LOW),
            pltpu.VMEM((2, 4, rows, head_part), LOW),
            pltpu.VMEM((2, 8, rows, tile), LOW),
            pltpu.VMEM((4, query_part, width), LOW),
        ]
        + LineScatter.scratch(line_rows, units)
        + PlaneScatter.scratch(query_part, width),
        compiler_params=comm_params(3),
        cost_estimate=comm_cost(90),
    )(
        branch,
        out_all,
        attended,
        raw,
        kept,
        *tables,
        rows_all,
        qkv_all,
        second_part,
        first_rows,
    )


def row_ids_of(local_rows):
    core = lax.axis_index("tensor")
    local_ids = jnp.arange(local_rows, dtype=jnp.int32)
    return jnp.concatenate([core * local_rows + local_ids, (1 - core) * local_rows + local_ids])


def heads_of(weight):
    return weight.reshape(weight.shape[0], 4, -1).transpose(1, 0, 2)


def heads_back(pieces):
    return f32(pieces).transpose(1, 0, 2).reshape(pieces.shape[1], -1)


def units_of(weight, down_rows):
    split = weight.reshape(weight.shape[0], -1, 4, down_rows)
    return split.transpose(2, 0, 1, 3).reshape(4, weight.shape[0], -1)


def units_back(pieces, down_rows):
    rows = pieces.shape[1]
    return f32(pieces).reshape(4, rows, -1, down_rows).transpose(1, 2, 0, 3).reshape(rows, -1)


def shards(*arguments):
    if lax.axis_size("f") == 4:
        return line_of_four(*arguments)
    return any_line(*arguments)


def line_of_four(
    layer_input,
    attn_norm,
    head_norms,
    query_weight,
    key_matrix,
    value_matrix,
    output_weight,
    mlp_norm,
    gate_weight,
    up_weight,
    down_weight,
    grad_out,
    doc_lengths,
):
    local_rows, model_width = layer_input.shape
    weight_rows = gate_weight.shape[0]
    down_rows = down_weight.shape[0]
    half_rows = down_rows // 2
    half = 4 * half_rows
    qkv_pieces = jnp.concatenate(
        [heads_of(query_weight), heads_of(key_matrix), heads_of(value_matrix)], axis=2
    )
    head_part = qkv_pieces.shape[2]
    query_part = head_part - 2 * HEAD_SIZE
    input_float = f32(layer_input)

    def half_pieces(index):
        return jnp.concatenate(
            [
                weight.reshape(weight_rows, 4, 4, 2, half_rows)[:, :, :, index]
                .transpose(2, 0, 1, 3)
                .reshape(4, weight_rows, half)
                for weight in (gate_weight, up_weight)
            ],
            axis=2,
        )

    down_halves = down_weight.reshape(2, half_rows, model_width)
    row_ids = row_ids_of(local_rows)
    (
        normed_attn,
        _,
        second_rows,
        first_all,
        above,
        below,
        grad_all,
        qkv_all,
        out_all,
        qkv_raw,
        qkv_low,
        cos_tab,
        sin_tab,
        segment_col,
        segment_row,
        attended,
        hidden_state,
        normed_mlp,
    ) = first_part(
        low(input_float * inv_rms(input_float) * attn_norm),
        qkv_pieces,
        output_weight,
        half_pieces(0),
        half_pieces(1),
        down_halves,
        doc_lengths,
        row_ids,
        head_norms,
        layer_input,
        mlp_norm,
        grad_out,
    )
    tables = (
        cos_tab,
        sin_tab,
        segment_col,
        segment_row,
        row_ids[:, None],
        row_ids[None, :],
        head_norms,
    )
    rows_all, inner_low, second_grad, first_rows, grad_down_first, part_sums, grad_sums = (
        units_products(
            normed_mlp,
            grad_all,
            second_rows.reshape(-1, 2 * half),
            first_all.reshape(model_width, 2 * half),
            down_halves,
            above,
            below,
        )
    )
    line_shape = (4, 4 * weight_rows, 2 * half)
    (
        layer_out,
        hidden_grad,
        branch_grad,
        mlp_gain_part,
        grad_down,
        grad_second,
    ) = unit_grads(
        rows_all,
        grad_all,
        inner_low,
        second_grad,
        grad_down_first.reshape(4, half_rows, model_width),
        part_sums,
        grad_sums,
        hidden_state,
        grad_out,
        mlp_norm[None],
    )
    (
        head_gains,
        grad_qkv_part,
        grad_proj_part,
        grad_sums,
        second_rows,
        first_columns,
    ) = heads_backward(
        branch_grad,
        out_all.reshape(-1, model_width),
        attended,
        qkv_raw,
        qkv_low,
        tables,
        normed_attn,
        qkv_all.reshape(model_width, head_part),
        grad_second.reshape(line_shape),
        first_rows.reshape(4, weight_rows, 2 * half),
    )
    grad_input, grad_qkv_columns, grad_out_proj, second_columns, gains = last_sums(
        grad_sums,
        grad_qkv_part.reshape(4, 4 * weight_rows, head_part),
        grad_proj_part.reshape((4,) + output_weight.shape),
        second_rows.reshape(4, weight_rows, 2 * half),
        layer_input,
        hidden_grad,
        attn_norm[None],
        jnp.concatenate([mlp_gain_part, head_gains], axis=1),
    )
    gains = gains.reshape(-1)

    def units_joined(offset):
        halves = [
            f32(columns[:, :, offset : offset + half]).reshape(4, weight_rows, 4, 1, half_rows)
            for columns in (first_columns, second_columns)
        ]
        joined = jnp.concatenate(halves, axis=3)
        return joined.transpose(1, 2, 0, 3, 4).reshape(weight_rows, -1)

    return (
        layer_out,
        grad_input,
        gains[:model_width],
        gains[2 * model_width :].reshape(2, HEAD_SIZE),
        heads_back(grad_qkv_columns[:, :, :query_part]),
        heads_back(grad_qkv_columns[:, :, query_part : query_part + HEAD_SIZE]),
        heads_back(grad_qkv_columns[:, :, query_part + HEAD_SIZE :]),
        f32(grad_out_proj),
        gains[model_width : 2 * model_width],
        units_joined(0),
        units_joined(half),
        f32(grad_down).reshape(down_weight.shape),
    )


def any_line(
    layer_input,
    attn_norm,
    head_norms,
    query_weight,
    key_matrix,
    value_matrix,
    output_weight,
    mlp_norm,
    gate_weight,
    up_weight,
    down_weight,
    grad_out,
    doc_lengths,
):
    line_extent = lax.axis_size("f")
    local_rows, model_width = layer_input.shape
    group_rows = 2 * local_rows
    all_rows = 8 * local_rows
    weight_rows = gate_weight.shape[0]
    down_rows = down_weight.shape[0]
    hidden_part = line_extent * down_rows
    qkv_pieces = jnp.concatenate(
        [heads_of(query_weight), heads_of(key_matrix), heads_of(value_matrix)], axis=2
    )
    head_part = qkv_pieces.shape[2]
    query_part = head_part - 2 * HEAD_SIZE
    heads = head_part // HEAD_SIZE - 2

    def exchanged(pieces):
        return natural_plane(plane_exchange(own_plane(pieces, 0)), 0)

    def line_rows(pieces):
        return line_gather(exchanged(pieces)).reshape(model_width, -1)

    def line_sums(partial):
        parts = low(partial).reshape(line_extent, 4 * weight_rows, -1)
        return exchanged(low(line_scatter(parts)).reshape(4, weight_rows, -1))

    qkv_all = line_rows(qkv_pieces)
    out_all = full_gather(output_weight)
    gate_all = line_rows(units_of(gate_weight, down_rows))
    up_all = line_rows(units_of(up_weight, down_rows))
    down_all = line_gather(down_weight).reshape(hidden_part, model_width)

    input_float = f32(layer_input)
    scale_attn = inv_rms(input_float)
    normed_attn = tokens_gather(low(input_float * scale_attn * attn_norm))
    row_ids = row_ids_of(local_rows)
    segments, positions = jax.vmap(lambda lengths: doc_layout(lengths, row_ids))(
        plane_lengths(doc_lengths)
    )
    qkv_raw = matmul(normed_attn, qkv_all).reshape(2, 4, local_rows, head_part)
    roll = lambda values: jnp.roll(values, HEAD_SIZE // 2, 1)
    buckets, attended_parts = [], []
    for step in range(4):
        cos_tab, sin_tab = rope_tables(positions[step], HEAD_SIZE)
        cosine = jnp.concatenate([cos_tab, cos_tab], axis=1)
        sine = jnp.concatenate([-sin_tab, sin_tab], axis=1)
        allowed = (segments[step][:, None] == segments[step][None, :]) & (
            row_ids[None, :] <= row_ids[:, None]
        )
        raw = qkv_raw[:, step].reshape(group_rows, head_part)
        turned = []
        for head in range(heads + 1):
            unnormed = lanes(raw, head)
            normed = unnormed * inv_rms(unnormed) * head_norms[min(head // heads, 1)]
            turned.append(low(normed * cosine + roll(normed) * sine))
        value = low(lanes(raw, heads + 1))
        attended_parts.append(
            jnp.concatenate(
                [
                    low(matmul(low(softmax_of(turned[head], turned[heads], allowed)), value))
                    for head in range(heads)
                ],
                axis=1,
            )
        )
        buckets.append((raw, jnp.concatenate(turned + [value], axis=1), allowed, cosine, sine))
    attended = natural_plane(plane_exchange(attended_parts), 0)
    attended = attended.transpose(1, 0, 2).reshape(group_rows, 4 * query_part)
    hidden_state = input_float + pair_scatter(low(matmul(attended, out_all)))

    scale_mlp = inv_rms(hidden_state)
    normed_mlp = tokens_gather(low(hidden_state * scale_mlp * mlp_norm))
    grad_all = tokens_gather(grad_out)
    gate_raw = matmul(normed_mlp, gate_all)
    up_raw = matmul(normed_mlp, up_all)
    activated = jax.nn.silu(gate_raw)
    inner_low = low(activated * up_raw)
    layer_out = low(hidden_state + tokens_scatter(low(matmul(inner_low, down_all))))
    inner_grad = matmul_nt(grad_all, down_all)
    sigmoid_gate = jax.nn.sigmoid(gate_raw)
    gate_grad = low(inner_grad * up_raw * sigmoid_gate * (1.0 + gate_raw * (1.0 - sigmoid_gate)))
    up_grad = low(inner_grad * activated)
    mlp_row_grad = tokens_scatter(
        low(matmul_nt(gate_grad, gate_all) + matmul_nt(up_grad, up_all))
    )
    grad_down = line_scatter(
        low(matmul_tn(inner_low, grad_all)).reshape(line_extent, down_rows, model_width)
    )

    hidden_norm_grad, mlp_gain_part = norm_back(hidden_state, scale_mlp, mlp_norm, mlp_row_grad)
    hidden_grad = f32(grad_out) + hidden_norm_grad
    branch_grad = pair_gather(low(hidden_grad))
    split = low(matmul_nt(branch_grad, out_all)).reshape(group_rows, 4, query_part)
    heads_grad = plane_exchange(own_plane(split.transpose(1, 0, 2), 0))
    grad_out_proj = line_scatter(full_scatter_plane(low(matmul_tn(attended, branch_grad))))
    back = [
        attend_back_values(raw, kept, heads_grad[step], allowed, cosine, sine, head_norms, roll)
        for step, (raw, kept, allowed, cosine, sine) in enumerate(buckets)
    ]
    qkv_grad = jnp.stack([grads for grads, _ in back]).reshape(4, 2, local_rows, head_part)
    qkv_grad = qkv_grad.transpose(1, 0, 2, 3).reshape(all_rows, head_part)
    attn_row_grad = tokens_scatter(low(matmul_nt(qkv_grad, qkv_all)))
    grad_qkv_columns = line_sums(matmul_tn(normed_attn, qkv_grad))
    input_norm_grad, attn_gain_part = norm_back(input_float, scale_attn, attn_norm, attn_row_grad)
    head_gains = sum(gains for _, gains in back)[0]
    gains = total_sum(
        jnp.concatenate([attn_gain_part, mlp_gain_part, head_gains]).reshape(-1, HEAD_SIZE)
    ).reshape(-1)
    return (
        layer_out,
        hidden_grad + input_norm_grad,
        gains[:model_width],
        gains[2 * model_width :].reshape(2, HEAD_SIZE),
        heads_back(grad_qkv_columns[:, :, :query_part]),
        heads_back(grad_qkv_columns[:, :, query_part : query_part + HEAD_SIZE]),
        heads_back(grad_qkv_columns[:, :, query_part + HEAD_SIZE :]),
        grad_out_proj,
        gains[model_width : 2 * model_width],
        units_back(line_sums(matmul_tn(normed_mlp, gate_grad)), down_rows),
        units_back(line_sums(matmul_tn(normed_mlp, up_grad)), down_rows),
        grad_down,
    )


def solution(mesh):
    dp, tensor = mesh.shape["dp"], mesh.shape["tensor"]
    fine = Mesh(mesh.devices.reshape(dp // 4, 2, 2, tensor), ("f", "ty", "tx", "tensor"))
    rows = ("f", "ty", "tx")
    tokens = P(rows + ("tensor",), None)
    grid = P(rows, "tensor")
    units = P(("tensor",) + rows, None)
    return jax.shard_map(
        shards,
        mesh=fine,
        in_specs=(
            tokens, P(), P(), grid, grid, grid, units, P(), grid, grid, units, tokens, P(rows, None),
        ),
        out_specs=(tokens, tokens, P(), P(), grid, grid, grid, units, P(), grid, grid, units),
        check_vma=False,
    )
```

```python
import jax
import jax.numpy as jnp
from jax import lax
from jax.experimental import pallas as pl
from jax.experimental.pallas import tpu as pltpu
from jax.sharding import Mesh, PartitionSpec as P

QUERY_HEADS = 16
KEY_VALUE_HEADS = 8
HEAD_SIZE = 128


EPS = 1e-06
ROPE_BASE = 1000000.0
MASKED = -1e30
LOW = jnp.bfloat16


def matmul(left_mat, right_mat):
    return jnp.dot(left_mat, right_mat, preferred_element_type=jnp.float32)


def matmul_tn(left_mat, right_mat):
    return lax.dot_general(
        left_mat, right_mat, (((0,), (0,)), ((), ())), preferred_element_type=jnp.float32
    )


def matmul_nt(left_mat, right_mat):
    return lax.dot_general(
        left_mat, right_mat, (((1,), (1,)), ((), ())), preferred_element_type=jnp.float32
    )


def inv_rms(values):
    return lax.rsqrt(jnp.mean(values * values, axis=-1, keepdims=True) + EPS)


def norm_back(values, scales, gain_row, upstream):
    weighted = upstream * gain_row
    inner_mean = jnp.mean(weighted * values, axis=-1, keepdims=True)
    value_grad = scales * weighted - values * (scales * scales * scales) * inner_mean
    lead_axes = tuple(range(upstream.ndim - 1))
    return (value_grad, jnp.sum(upstream * values * scales, axis=lead_axes))


def rope_tables(position, head_width):
    half_dim = head_width // 2
    inverse = ROPE_BASE ** (-(jnp.arange(half_dim, dtype=jnp.float32) * (2.0 / head_width)))
    angles = position.astype(jnp.float32)[:, None] * inverse[None, :]
    return (jnp.cos(angles), jnp.sin(angles))


def rotate(values, cos_tab, sin_tab, direction):
    half_dim = values.shape[-1] // 2
    first_half = values[..., :half_dim]
    second_half = values[..., half_dim:]
    cosine = cos_tab[:, None, :]
    sine_tab = direction * sin_tab[:, None, :]
    return jnp.concatenate(
        [
            first_half * cosine - second_half * sine_tab,
            second_half * cosine + first_half * sine_tab,
        ],
        axis=-1,
    )


def doc_layout(lengths_row, row_ids):
    doc_ends = jnp.cumsum(lengths_row, dtype=jnp.int32)
    document_segment = jnp.sum(
        (row_ids[:, None] >= doc_ends[None, :]).astype(jnp.int32), axis=1, dtype=jnp.int32
    )
    doc_starts = doc_ends - lengths_row
    member = document_segment[:, None] == jnp.arange(lengths_row.shape[0], dtype=jnp.int32)[None, :]
    start_of = jnp.sum(jnp.where(member, doc_starts[None, :], 0), axis=1, dtype=jnp.int32)
    return (document_segment, row_ids - start_of)


def f32(values):
    return values.astype(jnp.float32)


def low(values):
    return values.astype(LOW)


def swap(block, axis):
    return lax.ppermute(block, axis, [(0, 1), (1, 0)])


def plane_index():
    return 2 * lax.axis_index("ty") + lax.axis_index("tx")


def plane_gather(block):
    across_x = swap(block, "tx")
    across_y = swap(block, "ty")
    return [block, across_x, across_y, swap(across_y, "tx")]


def plane_scatter(parts):
    own, for_x, for_y, for_far = parts
    for_y = low(f32(for_y) + f32(swap(for_far, "tx")))
    return f32(own) + f32(swap(for_x, "tx")) + f32(swap(for_y, "ty"))


def plane_exchange(parts):
    own, for_x, for_y, for_far = parts
    return [own, swap(for_x, "tx"), swap(for_y, "ty"), swap(swap(for_far, "tx"), "ty")]


def plane_lengths(lengths):
    return jnp.concatenate(plane_gather(lengths))


def line_gather(block):
    return lax.all_gather(block, "f", axis=0)


def line_scatter(parts):
    return f32(lax.psum_scatter(parts, "f", scatter_dimension=0))


def natural_plane(blocks, axis):
    own = plane_index()
    shape = list(blocks[0].shape)
    shape.insert(axis, 4)
    whole = jnp.zeros(shape, blocks[0].dtype)
    for step in range(4):
        whole = lax.dynamic_update_index_in_dim(whole, blocks[step], own ^ step, axis)
    return whole


def own_plane(whole, axis):
    own = plane_index()
    return [
        lax.dynamic_index_in_dim(whole, own ^ step, axis, keepdims=False) for step in range(4)
    ]


def full_gather(rows_block):
    rows, width = rows_block.shape
    line = line_gather(rows_block)
    extent = line.shape[0]
    blocks = plane_gather(line.reshape(extent * rows, width))
    whole = natural_plane([block.reshape(extent, rows, width) for block in blocks], 1)
    return whole.reshape(extent * 4 * rows, width)


def full_scatter_plane(partial):
    extent = lax.axis_size("f")
    rows, width = partial.shape[0] // (4 * extent), partial.shape[1]
    parts = own_plane(partial.reshape(extent, 4, rows, width), 1)
    plane_sum = plane_scatter([part.reshape(extent * rows, width) for part in parts])
    return low(plane_sum).reshape(extent, rows, width)


def tokens_gather(block):
    near = plane_gather(block)
    return jnp.concatenate(near + [swap(piece, "tensor") for piece in near])


def tokens_scatter(partial):
    rows = partial.shape[0] // 8
    near = []
    for step in range(4):
        mine = partial[step * rows : (step + 1) * rows]
        other = swap(partial[(4 + step) * rows : (5 + step) * rows], "tensor")
        near.append(low(f32(mine) + f32(other)))
    return plane_scatter(near)


def pair_gather(block):
    return jnp.concatenate([block, swap(block, "tensor")])


def pair_scatter(partial):
    rows = partial.shape[0] // 2
    return f32(partial[:rows]) + f32(swap(partial[rows:], "tensor"))


def total_sum(values):
    return lax.psum(values, ("f", "ty", "tx", "tensor"))


class Place:
    def __init__(self):
        self.z = lax.axis_index("f")
        self.ty = lax.axis_index("ty")
        self.tx = lax.axis_index("tx")
        self.core = lax.axis_index("tensor")
        self.p = 2 * self.ty + self.tx
        self.px = 2 * self.ty + 1 - self.tx
        self.py = 2 * (1 - self.ty) + self.tx
        self.pd = 2 * (1 - self.ty) + 1 - self.tx
        self.x = {"tx": 1 - self.tx}
        self.y = {"ty": 1 - self.ty}
        self.d = {"tx": 1 - self.tx, "ty": 1 - self.ty}
        self.pair = {"tensor": 1 - self.core}
        self.up = {"f": self.z + 1}
        self.down = {"f": self.z - 1}
        self.two = {"f": (self.z + 2) % 4}

    def at(self, step):
        return (self.z + step) % 4


def remote(src, dst, send, recv, to):
    return pltpu.make_async_remote_copy(
        src_ref=src,
        dst_ref=dst,
        send_sem=send,
        recv_sem=recv,
        device_id=to,
        device_id_type=pl.DeviceIdType.MESH,
    )


def arrived(dst, recv, to):
    remote(dst, dst, recv, recv, to).wait_recv()


def greet(place, partners, line):
    barrier = pltpu.get_barrier_semaphore()
    for to in partners:
        pl.semaphore_signal(barrier, inc=1, device_id=to, device_id_type=pl.DeviceIdType.MESH)
    if not line:
        pl.semaphore_wait(barrier, len(partners))
        return

    @pl.when(place.z > 0)
    def _():
        pl.semaphore_signal(
            barrier, inc=1, device_id=place.down, device_id_type=pl.DeviceIdType.MESH
        )

    @pl.when(place.z < 3)
    def _():
        pl.semaphore_signal(barrier, inc=1, device_id=place.up, device_id_type=pl.DeviceIdType.MESH)

    pl.semaphore_signal(barrier, inc=1, device_id=place.two, device_id_type=pl.DeviceIdType.MESH)
    pl.semaphore_wait(barrier, len(partners) + 2 + (place.z + 1) // 2 % 2)


class LineGather:
    def __init__(self, place, own, slot, send, recv):
        self.place, self.own, self.slot, self.send, self.recv = place, own, slot, send, recv
        here = slot(place.z)
        self.to_down = remote(own, here, send.at[0], recv.at[1], place.down)
        self.to_up = remote(own, here, send.at[1], recv.at[3], place.up)
        self.to_two = remote(own, here, send.at[2], recv.at[2], place.two)
        two = slot(place.at(2))
        self.pass_down = remote(two, two, send.at[3], recv.at[3], place.down)
        self.pass_up = remote(two, two, send.at[3], recv.at[1], place.up)

    def start(self):
        z = self.place.z
        self.to_two.start()
        pl.when((z == 1) | (z == 3))(self.to_down.start)
        pl.when((z == 0) | (z == 2))(self.to_up.start)

    def step(self, turn):
        if turn == 2:
            return 2
        if turn == 1:
            return jnp.where(self.place.z == 3, 3, 1)
        return jnp.where(self.place.z == 3, 1, 3)

    def wait(self, turn):
        step = self.step(turn)
        slot = self.slot(self.place.at(step))
        arrived(slot, self.recv.at[step], self.place.two)
        if turn == 2:
            pl.when(self.place.z == 1)(self.pass_down.start)
            pl.when(self.place.z == 2)(self.pass_up.start)
            pl.when(self.place.z == 1)(self.to_up.start)
            pl.when(self.place.z == 2)(self.to_down.start)

    def finish(self):
        pl.when(self.place.z > 0)(self.to_down.wait_send)
        pl.when(self.place.z < 3)(self.to_up.wait_send)
        self.to_two.wait_send()
        pl.when(self.place.z == 1)(self.pass_down.wait_send)
        pl.when(self.place.z == 2)(self.pass_up.wait_send)


class PlaneGather:
    def __init__(self, place, own, slot, rows, send, recv):
        half = rows // 2
        whole, top, end = pl.ds(0, rows), pl.ds(0, half), pl.ds(half, half)
        self.place, self.recv = place, recv
        self.to_x = remote(own, slot(place.p, whole), send.at[0], recv.at[0], place.x)
        self.to_y = remote(own, slot(place.p, whole), send.at[1], recv.at[1], place.y)
        self.from_x, self.from_y = slot(place.px, whole), slot(place.py, whole)
        self.far_top, self.far_end = slot(place.pd, top), slot(place.pd, end)
        pass_x, pass_y = slot(place.py, top), slot(place.px, end)
        self.pass_x = remote(pass_x, pass_x, send.at[2], recv.at[2], place.x)
        self.pass_y = remote(pass_y, pass_y, send.at[3], recv.at[3], place.y)

    def start(self):
        self.to_x.start()
        self.to_y.start()

    def forward(self):
        arrived(self.from_y, self.recv.at[1], self.place.y)
        self.pass_x.start()
        arrived(self.from_x, self.recv.at[0], self.place.x)
        self.pass_y.start()

    def wait_far(self):
        arrived(self.far_top, self.recv.at[2], self.place.x)
        arrived(self.far_end, self.recv.at[3], self.place.y)

    def finish(self):
        self.to_x.wait_send()
        self.to_y.wait_send()
        self.pass_x.wait_send()
        self.pass_y.wait_send()


ANYWHERE = pl.BlockSpec(memory_space=pl.ANY)
WHOLE = pl.BlockSpec(memory_space=pltpu.VMEM)


class Marks:
    def __init__(self, ref):
        self.ref, self.used = ref, 0

    def take(self, count=1):
        first = self.used
        self.used += count
        return self.ref.at[first] if count == 1 else self.ref.at[pl.ds(first, count)]


def each_rows(rows, chunk, work):
    def body(index, carry):
        work(pl.ds(pl.multiple_of(index * chunk, chunk), chunk))
        return carry

    lax.fori_loop(0, rows // chunk, body, 0)


class TokensGather:
    def __init__(self, place, own, whole, marks):
        half = own.shape[0] // 2
        top, end = pl.ds(0, half), pl.ds(half, half)
        self.place, self.whole = place, whole
        self.copy = pltpu.make_async_copy(own, whole.at[0], marks.take())
        self.recv = [marks.take() for _ in range(8)]
        x, y, pair = place.x, place.y, place.pair
        self.to_x = remote(own, whole.at[1], marks.take(), self.recv[0], x)
        self.to_y = remote(own, whole.at[2], marks.take(), self.recv[1], y)
        self.pass_x = remote(
            whole.at[2, top], whole.at[3, top], marks.take(), self.recv[2], x
        )
        self.pass_y = remote(
            whole.at[1, end], whole.at[3, end], marks.take(), self.recv[3], y
        )
        self.to_pair = [
            remote(
                own if step == 0 else whole.at[step],
                whole.at[4 + step],
                marks.take(),
                self.recv[4 + step],
                pair,
            )
            for step in range(4)
        ]
        self.far = (whole.at[3, top], whole.at[3, end])

    def start(self):
        self.to_x.start()
        self.to_y.start()
        self.to_pair[0].start()
        self.copy.start()

    def forward(self):
        arrived(self.whole.at[2], self.recv[1], self.place.y)
        self.pass_x.start()
        arrived(self.whole.at[1], self.recv[0], self.place.x)
        self.pass_y.start()
        self.to_pair[2].start()
        self.to_pair[1].start()

    def start_near(self, near, marks):
        self.copy.start()
        self.to_pair[0].start()
        copies = [
            pltpu.make_async_copy(near.at[index], self.whole.at[1 + index], marks.take())
            for index in range(2)
        ]
        for copy in copies:
            copy.start()
        for copy in copies:
            copy.wait()
        self.pass_x.start()
        self.pass_y.start()
        self.to_pair[2].start()
        self.to_pair[1].start()

    def finish_near(self):
        for step in range(4):
            arrived(self.whole.at[4 + step], self.recv[4 + step], self.place.pair)
        for copy in [self.pass_x, self.pass_y] + self.to_pair:
            copy.wait_send()
        self.copy.wait()

    def last(self):
        arrived(self.far[0], self.recv[2], self.place.x)
        arrived(self.far[1], self.recv[3], self.place.y)
        self.to_pair[3].start()

    def finish(self):
        for step in range(4):
            arrived(self.whole.at[4 + step], self.recv[4 + step], self.place.pair)
        for copy in [self.to_x, self.to_y, self.pass_x, self.pass_y] + self.to_pair:
            copy.wait_send()
        self.copy.wait()


class Exchange:
    def __init__(self, place, piece, slot, marks):
        self.place = place
        there = ((place.px, place.x), (place.py, place.y), (place.pd, place.d))
        self.copy = pltpu.make_async_copy(piece(place.p, 0), slot(place.p, 0), marks.take())
        self.sends, self.slots = [], []
        for index, (p, to) in enumerate(there):
            recv = marks.take()
            self.sends.append(
                remote(piece(p, index + 1), slot(place.p, index + 1), marks.take(), recv, to)
            )
            self.slots.append((slot(p, index + 1), recv, to))

    def start(self):
        for copy in (self.sends[2], self.sends[0], self.sends[1], self.copy):
            copy.start()

    def wait(self):
        self.copy.wait()
        for slot, recv, to in self.slots:
            arrived(slot, recv, to)

    def finish(self):
        for copy in self.sends:
            copy.wait_send()


class LineScatter:
    @staticmethod
    def scratch(rows, width, here=False):
        return [pltpu.VMEM((4 if here else 6, rows, width), LOW)]

    def __init__(self, place, part, out, buffers, marks, here=False):
        self.place, self.out, self.here = place, out, here
        kept = buffers[0]
        self.rows = kept.shape[1]
        self.passed, self.above, self.below, self.two = (kept.at[index] for index in range(4))
        z = place.z
        if here:
            self.mid, self.own = part(place.at(2)), part(z)
        else:
            self.mid, self.own = kept.at[4], kept.at[5]
            self.load_mid = pltpu.make_async_copy(part(place.at(2)), self.mid, marks.take())
            self.load_own = pltpu.make_async_copy(part(z), self.own, marks.take())
        self.recv = [marks.take() for _ in range(4)]
        self.pass_up = remote(part(3), self.passed, marks.take(), self.recv[0], place.up)
        self.pass_down = remote(part(0), self.passed, marks.take(), self.recv[0], place.down)
        self.to_down = remote(
            part(place.at(3)), self.above, marks.take(), self.recv[1], place.down
        )
        self.to_up = remote(part(place.at(1)), self.below, marks.take(), self.recv[2], place.up)
        self.to_two = remote(self.mid, self.two, marks.take(), self.recv[3], place.two)

    def start(self):
        z = self.place.z
        pl.when(z == 0)(self.pass_up.start)
        pl.when(z == 3)(self.pass_down.start)
        if not self.here:
            self.load_mid.start()
        pl.when((z == 1) | (z == 2))(self.to_down.start)
        pl.when((z == 1) | (z == 2))(self.to_up.start)
        if not self.here:
            self.load_own.start()

    def add(self, target, other):
        def work(rows):
            target[rows] = low(f32(target[rows]) + f32(other[rows]))

        each_rows(self.rows, 16, work)

    def middle(self):
        z = self.place.z
        if not self.here:
            self.load_mid.wait()
        pl.when(z == 0)(self.pass_up.wait_send)
        pl.when(z == 3)(self.pass_down.wait_send)

        @pl.when((z == 1) | (z == 2))
        def _():
            arrived(self.passed, self.recv[0], self.place.two)
            self.add(self.mid, self.passed)

        self.to_two.start()
        pl.when(z == 0)(self.to_up.start)
        pl.when(z == 3)(self.to_down.start)

    def finish(self):
        z = self.place.z
        if not self.here:
            self.load_own.wait()

        @pl.when(z < 3)
        def _():
            arrived(self.above, self.recv[1], self.place.two)
            self.add(self.own, self.above)

        @pl.when(z > 0)
        def _():
            arrived(self.below, self.recv[2], self.place.two)
            self.add(self.own, self.below)

        arrived(self.two, self.recv[3], self.place.two)
        out, own, two = self.out, self.own, self.two

        def work(rows):
            out[rows] = low(f32(own[rows]) + f32(two[rows]))

        each_rows(self.rows, 16, work)

    def drain(self):
        z = self.place.z
        pl.when(z > 0)(self.to_down.wait_send)
        pl.when(z < 3)(self.to_up.wait_send)
        self.to_two.wait_send()


def comm_params(number):
    return pltpu.CompilerParams(
        collective_id=number, has_side_effects=True, vmem_limit_bytes=62 * 1024 * 1024
    )


def comm_cost(micros):
    return pl.CostEstimate(flops=0, bytes_accessed=micros * 3_000_000, transcendentals=0)


def tables_of(lengths_row, id_col, id_row, inverse, count):
    zero = jnp.zeros((1, 1), jnp.int32)
    segment_col, segment_row = jnp.zeros_like(id_col), jnp.zeros_like(id_row)
    ends, starts, end = [], [], zero
    for index in range(count):
        starts.append(end)
        end = end + lengths_row[:, index : index + 1]
        ends.append(end)
        segment_col = segment_col + jnp.where(id_col >= end, 1, 0)
        segment_row = segment_row + jnp.where(id_row >= end, 1, 0)
    start_of = jnp.zeros_like(id_col)
    for index in range(count):
        start_of = start_of + jnp.where(segment_col == index, starts[index], 0)
    angles = f32(id_col - start_of) * inverse
    return segment_col, segment_row, jnp.cos(angles), jnp.sin(angles)


def first_kernel(
    documents,
    rows_ref,
    qkv_ref,
    out_ref,
    gate_ref,
    down_ref,
    lengths_ref,
    id_col,
    id_row,
    inverse_ref,
    head_norms,
    input_ref,
    norm_ref,
    upstream_ref,
    rows_all,
    gate_rows,
    gate_all,
    above_ref,
    below_ref,
    upstream_near,
    qkv_hbm,
    out_hbm,
    raw_hbm,
    low_hbm,
    cos_hbm,
    sin_hbm,
    segment_col,
    segment_row,
    attended,
    hidden,
    normed,
    marks_ref,
    qkv_all,
    out_all,
    raw_out,
    low_out,
    cos_out,
    sin_out,
    lengths_all,
    row_block,
    heads_stage,
    pair_stage,
    pair_got,
):
    place = Place()
    marks = Marks(marks_ref)
    greet(place, [place.x, place.y, place.d, place.pair], True)
    rows, width = rows_ref.shape
    head_part = raw_out.shape[3]
    heads = head_part // HEAD_SIZE - 2
    lengths = Exchange(
        place, lambda p, step: lengths_ref, lambda p, step: lengths_all.at[step], marks
    )
    qkv_pieces = Exchange(
        place, lambda p, step: qkv_ref.at[p], lambda p, step: qkv_all.at[place.z, p], marks
    )
    gate_pieces = Exchange(
        place, lambda p, step: gate_ref.at[p], lambda p, step: gate_rows.at[p], marks
    )
    tokens = TokensGather(place, rows_ref, rows_all, marks)
    upstream_recv = [marks.take(), marks.take()]
    upstream = [
        remote(upstream_ref, upstream_near.at[index], marks.take(), upstream_recv[index], to)
        for index, to in enumerate((place.x, place.y))
    ]
    qkv_line = LineGather(
        place, qkv_all.at[place.z], lambda z: qkv_all.at[z], marks.take(4), marks.take(4)
    )
    gate_line = LineGather(
        place, gate_rows, lambda z: gate_all.at[z], marks.take(4), marks.take(4)
    )
    out_line = LineGather(
        place, out_ref, lambda z: out_all.at[z, place.p], marks.take(4), marks.take(4)
    )
    own_copies = [
        pltpu.make_async_copy(out_ref, out_all.at[place.z, place.p], marks.take()),
    ]
    gate_copy = pltpu.make_async_copy(gate_rows, gate_all.at[place.z], marks.take())
    near_recv = [marks.take(), marks.take()]
    to_down = remote(down_ref, above_ref, marks.take(), near_recv[0], place.down)
    to_up = remote(down_ref, below_ref, marks.take(), near_recv[1], place.up)
    out_planes = []
    for turn in range(4):
        z = place.z if turn == 0 else place.at(out_line.step(turn))
        out_planes.append(
            PlaneGather(
                place,
                out_ref if turn == 0 else out_all.at[z, place.p],
                lambda p, part, z=z: out_all.at[z, p, part],
                out_ref.shape[0],
                marks.take(4),
                marks.take(4),
            )
        )
    heads_out = Exchange(
        place, lambda p, step: heads_stage.at[step], lambda p, step: attended.at[p], marks
    )
    to_pair = remote(pair_stage, pair_got, marks.take(), marks.take(), place.pair)
    fetch_marks = marks.take(2)
    qkv_copy = pltpu.make_async_copy(qkv_all, qkv_hbm, marks.take())
    out_copy = pltpu.make_async_copy(out_all, out_hbm, marks.take())
    bucket_copies = [
        pltpu.make_async_copy(raw_out, raw_hbm, marks.take()),
        pltpu.make_async_copy(low_out, low_hbm, marks.take()),
    ]
    table_copies = [
        pltpu.make_async_copy(cos_out, cos_hbm, marks.take()),
        pltpu.make_async_copy(sin_out, sin_hbm, marks.take()),
    ]

    lengths.start()
    qkv_pieces.start()
    gate_pieces.start()
    tokens.start()
    for copy in own_copies:
        copy.start()
    lengths.wait()
    qkv_pieces.wait()
    qkv_line.start()

    def table_work(step, carry):
        seg_col, seg_row, cosine, sine = tables_of(
            lengths_all[step][:1], id_col[...], id_row[...], inverse_ref[...], documents
        )
        segment_col[step] = seg_col
        segment_row[step] = seg_row
        cos_out[step] = cosine
        lane = lax.broadcasted_iota(jnp.int32, sine.shape, 1)
        sin_out[step] = jnp.where(lane < HEAD_SIZE // 2, -sine, sine)
        return carry

    lax.fori_loop(0, 2, table_work, 0)
    tokens.forward()
    out_planes[0].start()
    lax.fori_loop(2, 4, table_work, 0)
    qkv_line.wait(2)
    out_line.start()
    tokens.last()
    out_planes[0].forward()
    qkv_line.wait(1)
    qkv_line.wait(3)
    out_line.wait(2)
    out_planes[2].start()
    gate_pieces.wait()
    gate_line.start()
    gate_copy.start()
    for copy in table_copies:
        copy.start()
    qkv_copy.start()
    tokens.finish()

    def fetches(step):
        return (
            pltpu.make_async_copy(rows_all.at[step], row_block.at[0], fetch_marks.at[0]),
            pltpu.make_async_copy(rows_all.at[4 + step], row_block.at[1], fetch_marks.at[1]),
        )

    def bucket(turn, carry):
        step = 3 - turn
        for copy in fetches(step):
            copy.start()
        for copy in fetches(step):
            copy.wait()
        raw = matmul(
            row_block[...].reshape(2 * rows, width), qkv_all[...].reshape(width, head_part)
        )
        raw_out[0, step] = raw[:rows]
        raw_out[1, step] = raw[rows:]
        allowed = (segment_col[step] == segment_row[step]) & (id_row[...] <= id_col[...])
        turned = []
        for head in range(heads + 1):
            gain = head_norms[min(head // heads, 1)][None, :]
            unnormed = lanes(raw, head)
            turned.append(
                low(
                    turn_pairs(
                        unnormed * inv_rms(unnormed) * gain, cos_out[step], sin_out[step]
                    )
                )
            )
        value = low(lanes(raw, heads + 1))
        outs = [
            low(matmul(low(softmax_of(turned[head], turned[heads], allowed)), value))
            for head in range(heads)
        ]
        kept = jnp.concatenate(turned + [value], axis=1)
        low_out[0, step] = kept[:rows]
        low_out[1, step] = kept[rows:]
        outs = jnp.concatenate(outs, axis=1)
        heads_stage[step, 0] = outs[:rows]
        heads_stage[step, 1] = outs[rows:]
        for index, at in enumerate((1, 2, 3)):
            pl.when(step == at)(heads_out.sends[index].start)
        pl.when(step == 0)(heads_out.copy.start)
        return carry

    lax.fori_loop(0, 1, bucket, 0)
    out_line.wait(1)
    out_line.wait(3)
    out_planes[1].start()
    out_planes[3].start()
    lax.fori_loop(1, 2, bucket, 0)
    out_planes[2].forward()
    for copy in upstream:
        copy.start()
    lax.fori_loop(2, 3, bucket, 0)
    out_planes[1].forward()
    out_planes[3].forward()
    lax.fori_loop(3, 4, bucket, 0)
    for copy in bucket_copies:
        copy.start()
    gate_line.wait(2)
    pl.when(place.z > 0)(to_down.start)
    pl.when(place.z < 3)(to_up.start)
    for plane in out_planes:
        plane.wait_far()
    for copy in own_copies:
        copy.wait()
    out_copy.start()
    heads_out.wait()

    def projected(core_step):
        block = jnp.concatenate([attended[p, core_step] for p in range(4)], axis=1)
        return matmul(block, out_all[...].reshape(block.shape[1], width))

    pair_stage[...] = low(projected(1))
    to_pair.start()
    hidden[...] = f32(input_ref[...]) + projected(0)
    to_pair.wait()
    norm_row = norm_ref[...]

    def norm_work(part):
        values = hidden[part] + f32(pair_got[part])
        hidden[part] = values
        normed[part] = low(values * inv_rms(values) * norm_row)

    each_rows(rows, 16, norm_work)
    gate_line.wait(1)
    gate_line.wait(3)
    for index, to in enumerate((place.x, place.y)):
        arrived(upstream_near.at[index], upstream_recv[index], to)
        upstream[index].wait_send()
    gate_copy.wait()
    for copy in [qkv_copy, out_copy] + bucket_copies + table_copies:
        copy.wait()
    parts = [lengths, qkv_pieces, gate_pieces, heads_out, qkv_line, gate_line, out_line]
    for part in parts + out_planes:
        part.finish()

    @pl.when(place.z < 3)
    def _():
        arrived(above_ref, near_recv[0], place.two)
        to_up.wait_send()

    @pl.when(place.z > 0)
    def _():
        arrived(below_ref, near_recv[1], place.two)
        to_down.wait_send()


def first_part(
    rows,
    qkv_pieces,
    output_weight,
    gate_pieces,
    down_weight,
    doc_lengths,
    row_ids,
    head_norms,
    layer_input,
    mlp_norm,
    grad_out,
):
    block_rows, width = rows.shape
    group_rows = 2 * block_rows
    weight_rows, head_part = qkv_pieces.shape[1:]
    query_part = head_part - 2 * HEAD_SIZE
    documents = doc_lengths.shape[1]
    lengths = jnp.pad(doc_lengths, ((0, 7), (0, HEAD_SIZE - documents)))
    half = jnp.arange(HEAD_SIZE // 2, dtype=jnp.float32)
    inverse = ROPE_BASE ** (-(half * (2.0 / HEAD_SIZE)))
    low_like = lambda *shape: jax.ShapeDtypeStruct(shape, LOW)
    table = jax.ShapeDtypeStruct((4, group_rows, HEAD_SIZE), jnp.float32)
    return pl.pallas_call(
        lambda *refs: first_kernel(documents, *refs),
        out_shape=(
            low_like(8, block_rows, width),
            low_like(*gate_pieces.shape),
            low_like(4, *gate_pieces.shape),
            low_like(*down_weight.shape),
            low_like(*down_weight.shape),
            low_like(2, block_rows, width),
            low_like(4, *qkv_pieces.shape),
            low_like(4, 4, *output_weight.shape),
            jax.ShapeDtypeStruct((2, 4, block_rows, head_part), jnp.float32),
            low_like(2, 4, block_rows, head_part),
            table,
            table,
            jax.ShapeDtypeStruct((4, group_rows, 1), jnp.int32),
            jax.ShapeDtypeStruct((4, 1, group_rows), jnp.int32),
            low_like(4, 2, block_rows, query_part),
            jax.ShapeDtypeStruct((block_rows, width), jnp.float32),
            low_like(block_rows, width),
        ),
        in_specs=[ANYWHERE] * 5 + [WHOLE] * 7 + [ANYWHERE],
        out_specs=(ANYWHERE,) * 12 + (WHOLE,) * 5,
        scratch_shapes=[
            pltpu.SemaphoreType.DMA((160,)),
            pltpu.VMEM((4,) + qkv_pieces.shape, LOW),
            pltpu.VMEM((4, 4) + output_weight.shape, LOW),
            pltpu.VMEM((2, 4, block_rows, head_part), jnp.float32),
            pltpu.VMEM((2, 4, block_rows, head_part), LOW),
            pltpu.VMEM(table.shape, jnp.float32),
            pltpu.VMEM(table.shape, jnp.float32),
            pltpu.VMEM((4,) + lengths.shape, jnp.int32),
            pltpu.VMEM((2, block_rows, width), LOW),
            pltpu.VMEM((4, 2, block_rows, query_part), LOW),
            pltpu.VMEM((block_rows, width), LOW),
            pltpu.VMEM((block_rows, width), LOW),
        ],
        compiler_params=comm_params(0),
        cost_estimate=comm_cost(130),
    )(
        rows,
        qkv_pieces,
        output_weight,
        gate_pieces,
        down_weight,
        lengths,
        row_ids[:, None],
        row_ids[None, :],
        jnp.concatenate([inverse, inverse])[None],
        head_norms,
        layer_input,
        mlp_norm[None],
        grad_out,
    )


class FarScatter:
    @staticmethod
    def scratch(rows, width):
        return [pltpu.VMEM((2, rows // 2, width), LOW)]

    def __init__(self, place, summed, buffers, marks):
        self.place, self.summed, self.landed = place, summed, buffers[0]
        self.half = summed.shape[1] // 2
        self.recv = [marks.take(), marks.take()]
        self.sends = [
            remote(
                summed.at[3, pl.ds(index * self.half, self.half)],
                self.landed.at[index],
                marks.take(),
                self.recv[index],
                to,
            )
            for index, to in enumerate((place.x, place.y))
        ]

    def start(self):
        for copy in self.sends:
            copy.start()

    def add(self):
        summed, landed = self.summed, self.landed
        for index, block, base, to in (
            (0, 2, 0, self.place.x),
            (1, 1, self.half, self.place.y),
        ):
            arrived(landed.at[index], self.recv[index], to)

            def work(rows):
                own_rows = pl.ds(pl.multiple_of(rows.start + base, 16), rows.size)
                summed[block, own_rows] = low(
                    f32(summed[block, own_rows]) + f32(landed[index, rows])
                )

            each_rows(self.half, 16, work)

    def drain(self):
        for copy in self.sends:
            copy.wait_send()


class NearScatter:
    @staticmethod
    def scratch(rows, width):
        return [pltpu.VMEM((3, rows, width), LOW)]

    def __init__(self, place, summed, buffers, marks):
        self.place, self.landed = place, buffers[0]
        self.load = pltpu.make_async_copy(summed.at[0], self.landed.at[2], marks.take())
        self.recv = [marks.take(), marks.take()]
        self.sends = [
            remote(summed.at[1 + index], self.landed.at[index], marks.take(), self.recv[index], to)
            for index, to in enumerate((place.x, place.y))
        ]

    def start(self):
        self.load.start()
        for copy in self.sends:
            copy.start()

    def finish(self, work):
        landed = self.landed
        self.load.wait()
        for index, to in enumerate((self.place.x, self.place.y)):
            arrived(self.landed.at[index], self.recv[index], to)

        def total(rows):
            work(
                rows,
                f32(landed[0, rows]) + f32(landed[1, rows]) + f32(landed[2, rows]),
            )

        each_rows(landed.shape[1], 16, total)

    def drain(self):
        for copy in self.sends:
            copy.wait_send()


class PlaneScatter:
    @staticmethod
    def scratch(rows, width):
        return [pltpu.VMEM((6, rows // 2, width), LOW)]

    def __init__(self, place, summed, out, buffers, marks, at=(0, 1, 2, 3)):
        self.place, self.summed, self.out, self.at = place, summed, out, at
        self.landed = buffers[0]
        self.rows = summed.shape[1]
        half = self.rows // 2
        top, end = pl.ds(0, half), pl.ds(half, half)
        x, y = place.x, place.y
        self.recv = [marks.take() for _ in range(6)]
        routes = (
            (summed.at[at[3], top], x),
            (summed.at[at[3], end], y),
            (summed.at[at[1], top], x),
            (summed.at[at[1], end], x),
            (summed.at[at[2], top], y),
            (summed.at[at[2], end], y),
        )
        self.sends = [
            remote(src, self.landed.at[index], marks.take(), self.recv[index], to)
            for index, (src, to) in enumerate(routes)
        ]

    def start(self):
        for index in (0, 1, 2, 5):
            self.sends[index].start()

    def landed_at(self, index, to):
        arrived(self.landed.at[index], self.recv[index], to)

    def middle(self):
        half = self.rows // 2
        summed, landed = self.summed, self.landed
        _, for_x, for_y, _ = self.at
        self.landed_at(0, self.place.x)

        def top_work(rows):
            summed[for_y, rows] = low(f32(summed[for_y, rows]) + f32(landed[0, rows]))

        each_rows(half, 16, top_work)
        self.sends[4].start()
        self.landed_at(1, self.place.y)

        def end_work(rows):
            end_rows = pl.ds(pl.multiple_of(rows.start + half, 16), rows.size)
            summed[for_x, end_rows] = low(f32(summed[for_x, end_rows]) + f32(landed[1, rows]))

        each_rows(half, 16, end_work)
        self.sends[3].start()

    def finish(self):
        half = self.rows // 2
        for index, to in ((2, self.place.x), (5, self.place.y), (4, self.place.y), (3, self.place.x)):
            self.landed_at(index, to)

        for base, first, second in ((0, 2, 4), (half, 3, 5)):

            def work(rows):
                own_rows = pl.ds(pl.multiple_of(rows.start + base, 16), rows.size)
                self.out[own_rows] = (
                    f32(self.summed[self.at[0], own_rows])
                    + f32(self.landed[first, rows])
                    + f32(self.landed[second, rows])
                ).astype(self.out.dtype)

            each_rows(half, 16, work)

    def drain(self):
        for copy in self.sends:
            copy.wait_send()


def blocks_of(source, block_ref, marks, first, last, work):
    def fetch(block):
        return pltpu.make_async_copy(
            source(block), block_ref.at[block % 2], marks.at[block % 2]
        )

    fetch(first).start()

    def body(block, carry):
        fetch(block).wait()

        @pl.when(block < last - 1)
        def _():
            fetch(block + 1).start()

        work(block, block_ref[block % 2])
        return carry

    lax.fori_loop(first, last, body, 0)


def unit_values(raws, inner_grad):
    units = inner_grad.shape[1]
    gate_raw, up_raw = raws[:, :units], raws[:, units:]
    sigmoid_gate = jax.nn.sigmoid(gate_raw)
    activated = gate_raw * sigmoid_gate
    gate_grad = inner_grad * up_raw * sigmoid_gate * (1.0 + gate_raw * (1.0 - sigmoid_gate))
    return low(activated * up_raw), jnp.concatenate(
        [low(gate_grad), low(inner_grad * activated)], axis=1
    )


def units_kernel(
    rows_ref,
    upstream_ref,
    near_ref,
    pieces_ref,
    first_ref,
    down_ref,
    above_ref,
    below_ref,
    rows_all,
    upstream_all,
    line_ref,
    inner_out,
    second_grad,
    first_sum,
    down_part,
    part_sums,
    grad_sums,
    marks_ref,
    first_mat,
    second_mat,
    down_mat,
    upstream,
    row_block,
    row_slab,
    inner_first,
    first_grad,
    inner_grads,
    first_part,
    inner_stage,
    second_stage,
    *buffers,
):
    place = Place()
    marks = Marks(marks_ref)
    greet(place, [place.x, place.y, place.d, place.pair], True)
    tokens = TokensGather(place, rows_ref, rows_all, marks)
    upstream_tokens = TokensGather(place, upstream_ref, upstream, marks)
    pieces = Exchange(
        place, lambda p, step: pieces_ref.at[p], lambda p, step: line_ref.at[p], marks
    )
    keep = pltpu.make_async_copy(upstream, upstream_all, marks.take())
    line = LineGather(place, line_ref, lambda z: second_mat.at[z], marks.take(4), marks.take(4))
    far_recv = marks.take(2)
    two = down_mat.at[:, place.at(2)]
    to_two = remote(down_ref, down_mat.at[:, place.z], marks.take(), far_recv.at[0], place.two)
    pass_mark = marks.take()
    pass_down = remote(two, two, pass_mark, far_recv.at[1], place.down)
    pass_up = remote(two, two, pass_mark, far_recv.at[1], place.up)
    copies = [
        pltpu.make_async_copy(first_ref, first_mat, marks.take()),
        pltpu.make_async_copy(down_ref, down_mat.at[:, place.z], marks.take()),
    ]
    line_copy = pltpu.make_async_copy(line_ref, second_mat.at[place.z], marks.take())
    above = pltpu.make_async_copy(above_ref, down_mat.at[:, place.at(1)], marks.take())
    below = pltpu.make_async_copy(below_ref, down_mat.at[:, place.at(3)], marks.take())
    line_rows = first_sum.shape[0]
    first_line = LineScatter(
        place,
        lambda z: first_part.at[pl.ds(pl.multiple_of(z * line_rows, 16), line_rows)],
        first_sum,
        buffers[:1],
        marks,
        True,
    )
    part_far = FarScatter(place, part_sums, buffers[1:2], marks)
    grad_far = FarScatter(place, grad_sums, buffers[2:], marks)
    fetch_marks, slab_marks = marks.take(2), marks.take(2)
    send_marks, recv_marks = marks.take(8), marks.take(8)
    width = rows_ref.shape[1]
    half = inner_first.shape[2]
    all_rows = 8 * rows_ref.shape[0]

    to_two.start()
    pieces.start()
    tokens.start()
    for copy in copies:
        copy.start()
    pl.when(place.z < 3)(above.start)
    pl.when(place.z > 0)(below.start)
    tokens.forward()
    upstream_tokens.start_near(near_ref, marks)
    pieces.wait()
    line_copy.start()
    arrived(two, far_recv.at[0], place.two)
    pl.when(place.z == 1)(pass_down.start)
    pl.when(place.z == 2)(pass_up.start)
    line.start()
    tokens.last()
    upstream_tokens.last()
    for copy in copies:
        copy.wait()
    line_copy.wait()
    pl.when(place.z < 3)(above.wait)
    pl.when(place.z > 0)(below.wait)

    @pl.when(place.z == 0)
    def _():
        arrived(down_mat.at[:, 3], far_recv.at[1], place.two)

    @pl.when(place.z == 3)
    def _():
        arrived(down_mat.at[:, 0], far_recv.at[1], place.two)

    tokens.finish()
    upstream_tokens.finish_near()
    keep.start()
    pieces.finish()

    def first_work(block, values):
        grads = matmul_nt(upstream[block], down_mat[...].reshape(2 * half, width))
        inner_grads[block] = low(grads[:, half:])
        inner, grad = unit_values(matmul(values, first_mat[...]), grads[:, :half])
        inner_first[block] = inner
        first_grad[block] = grad

    blocks_of(lambda block: rows_all.at[block], row_block, fetch_marks, 0, 8, first_work)
    line.wait(2)
    tile = row_slab.shape[3]
    tiles = width // tile

    def slab(index):
        return rows_all.at[:, :, pl.ds(pl.multiple_of(index * tile, tile), tile)]

    def slab_work(index, values):
        first_part[pl.ds(pl.multiple_of(index * tile, tile), tile)] = low(
            matmul_tn(values.reshape(all_rows, tile), first_grad[...].reshape(all_rows, 2 * half))
        )

    down_part[...] = low(
        matmul_tn(
            inner_first[...].reshape(all_rows, half), upstream[...].reshape(all_rows, width)
        )
    )
    blocks_of(slab, row_slab, slab_marks, 0, tiles, slab_work)
    line.wait(1)
    line.wait(3)
    first_line.start()

    def fetch(index):
        step, slot = 3 - index // 2, index % 2
        return pltpu.make_async_copy(
            rows_all.at[step + 4 * (1 - slot)], row_block.at[slot], fetch_marks.at[slot]
        )

    def sends(step):
        return (
            remote(
                upstream.at[step],
                part_sums.at[step],
                send_marks.at[step],
                recv_marks.at[step],
                place.pair,
            ),
            remote(
                upstream.at[4 + step],
                grad_sums.at[step],
                send_marks.at[4 + step],
                recv_marks.at[4 + step],
                place.pair,
            ),
        )

    keep.wait()
    store_marks = marks.take(4)

    def stores(slot, block):
        return (
            pltpu.make_async_copy(
                inner_stage.at[slot], inner_out.at[block], store_marks.at[slot]
            ),
            pltpu.make_async_copy(
                second_stage.at[slot], second_grad.at[block], store_marks.at[2 + slot]
            ),
        )

    fetch(0).start()

    def blocks(turn, carry):
        step = 3 - turn
        for slot in range(2):
            index = 2 * turn + slot
            block = step + 4 * (1 - slot)
            fetch(index).wait()

            @pl.when(index < 7)
            def _():
                fetch(index + 1).start()

            second = second_mat[...].reshape(width, 2 * half)
            inner, grad = unit_values(matmul(row_block[slot], second), f32(inner_grads[block]))

            @pl.when(turn > 0)
            def _():
                for copy in stores(slot, block + 1):
                    copy.wait()

            inner_stage[slot] = inner
            second_stage[slot] = grad
            for copy in stores(slot, block):
                copy.start()
            part = matmul(
                jnp.concatenate([inner_first[block], inner], axis=1),
                down_mat[...].reshape(2 * half, width),
            )
            grad = matmul_nt(first_grad[block], first_mat[...]) + matmul_nt(grad, second)
            if slot == 0:
                upstream[step] = low(part)
                upstream[4 + step] = low(grad)
                for copy in sends(step):
                    copy.start()
            else:
                for copy in sends(step):
                    copy.wait_recv()
                part_sums[step] = low(part + f32(part_sums[step]))
                grad_sums[step] = low(grad + f32(grad_sums[step]))
        return carry

    lax.fori_loop(0, 1, blocks, 0)
    grad_far.start()
    part_far.start()
    lax.fori_loop(1, 2, blocks, 0)
    first_line.middle()
    lax.fori_loop(2, 4, blocks, 0)
    for slot in range(2):
        for copy in stores(slot, 4 * (1 - slot)):
            copy.wait()
    grad_far.add()
    part_far.add()
    first_line.finish()
    first_line.drain()
    grad_far.drain()
    part_far.drain()
    for step in range(4):
        for copy in sends(step):
            copy.wait_send()
    line.finish()
    to_two.wait_send()
    pl.when(place.z == 1)(pass_down.wait_send)
    pl.when(place.z == 2)(pass_up.wait_send)


def units_products(rows, upstream, near, second_pieces, first_all, down_weight, above, below):
    block_rows, width = rows.shape
    half = first_all.shape[1] // 2
    half_rows = down_weight.shape[1]
    second_rows = jax.ShapeDtypeStruct((4 * second_pieces.shape[1], 2 * half), LOW)
    hidden = lambda count: jax.ShapeDtypeStruct((8, block_rows, count * half), LOW)
    sums = jax.ShapeDtypeStruct((4, block_rows, width), LOW)
    blocks = jax.ShapeDtypeStruct((8, block_rows, width), LOW)
    return pl.pallas_call(
        units_kernel,
        out_shape=(
            blocks,
            blocks,
            jax.ShapeDtypeStruct(second_pieces.shape, LOW),
            hidden(1),
            hidden(2),
            jax.ShapeDtypeStruct(second_rows.shape, LOW),
            jax.ShapeDtypeStruct((half, width), LOW),
            sums,
            sums,
        ),
        in_specs=[ANYWHERE] * 8,
        out_specs=(ANYWHERE,) * 5 + (WHOLE,) * 4,
        scratch_shapes=[
            pltpu.SemaphoreType.DMA((140,)),
            pltpu.VMEM(first_all.shape, LOW),
            pltpu.VMEM((4,) + second_pieces.shape, LOW),
            pltpu.VMEM((2, 4, half_rows, width), LOW),
            pltpu.VMEM((8, block_rows, width), LOW),
            pltpu.VMEM((2, block_rows, width), LOW),
            pltpu.VMEM((2, 8, block_rows, 256), LOW),
            pltpu.VMEM((8, block_rows, half), LOW),
            pltpu.VMEM((8, block_rows, 2 * half), LOW),
            pltpu.VMEM((8, block_rows, half), LOW),
            pltpu.VMEM((width, 2 * half), LOW),
            pltpu.VMEM((2, block_rows, half), LOW),
            pltpu.VMEM((2, block_rows, 2 * half), LOW),
        ]
        + LineScatter.scratch(*second_rows.shape, True)
        + FarScatter.scratch(block_rows, width) * 2,
        compiler_params=comm_params(1),
        cost_estimate=comm_cost(150),
    )(rows, upstream, near, second_pieces, first_all, down_weight, above, below)


def unit_grads_kernel(
    rows_all,
    upstream_ref,
    inner_ref,
    second_ref,
    down_first,
    part_sums,
    grad_sums,
    hidden_ref,
    upstream_own,
    norm_ref,
    layer_out,
    hidden_grad,
    branch,
    mlp_gain,
    down_out,
    second_part,
    marks_ref,
    upstream,
    inner,
    second_grad,
    row_slab,
    gain_rows,
    down_part,
    *buffers,
):
    place = Place()
    marks = Marks(marks_ref)
    greet(place, [place.x, place.y], True)
    grad_near = NearScatter(place, grad_sums, buffers[:1], marks)
    part_near = NearScatter(place, part_sums, buffers[1:2], marks)
    half_rows = down_out.shape[1]
    first_line = LineScatter(
        place, lambda z: down_first.at[z], down_out.at[0], buffers[2:3], marks
    )
    second_line = LineScatter(
        place,
        lambda z: down_part.at[pl.ds(pl.multiple_of(z * half_rows, 16), half_rows)],
        down_out.at[1],
        buffers[3:],
        marks,
        True,
    )
    loads = [
        pltpu.make_async_copy(upstream_ref, upstream, marks.take()),
        pltpu.make_async_copy(inner_ref, inner, marks.take()),
        pltpu.make_async_copy(second_ref, second_grad, marks.take()),
    ]
    slab_marks = marks.take(2)
    rows, width = hidden_ref.shape
    half = inner.shape[2]
    all_rows = 8 * rows
    tile = row_slab.shape[3]
    tiles = width // tile

    def slab(index):
        return rows_all.at[:, :, pl.ds(pl.multiple_of(index * tile, tile), tile)]

    def slab_work(index, values):
        second_part[pl.ds(pl.multiple_of(index * tile, tile), tile)] = low(
            matmul_tn(values.reshape(all_rows, tile), second_grad[...].reshape(all_rows, 2 * half))
        )

    first_line.start()
    grad_near.start()
    for copy in loads:
        copy.start()
    loads[0].wait()
    loads[1].wait()
    down_part[...] = low(
        matmul_tn(inner[...].reshape(all_rows, half), upstream[...].reshape(all_rows, width))
    )
    loads[2].wait()
    blocks_of(slab, row_slab, slab_marks, 0, tiles // 2, slab_work)
    first_line.middle()
    second_line.start()
    blocks_of(slab, row_slab, slab_marks, tiles // 2, tiles, slab_work)
    second_line.middle()
    part_near.start()
    gain_rows[...] = jnp.zeros_like(gain_rows)
    norm_row = norm_ref[...]

    def norm_work(rows, row_grad):
        values = hidden_ref[rows]
        scales = inv_rms(values)
        weighted = row_grad * norm_row
        inner_mean = jnp.mean(weighted * values, axis=-1, keepdims=True)
        grad = (
            f32(upstream_own[rows])
            + scales * weighted
            - values * (scales * scales * scales) * inner_mean
        )
        hidden_grad[rows] = grad
        branch[rows] = low(grad)
        parts = row_grad * values * scales
        gain_rows[...] += parts[:8] + parts[8:]

    def out_work(rows, row_part):
        layer_out[rows] = low(hidden_ref[rows] + row_part)

    grad_near.finish(norm_work)
    mlp_gain[...] = jnp.sum(gain_rows[...], axis=0, keepdims=True)
    part_near.finish(out_work)
    first_line.finish()
    second_line.finish()
    for part in (first_line, second_line, grad_near, part_near):
        part.drain()


def unit_grads(
    rows_all,
    upstream,
    inner,
    second_grad,
    down_first,
    part_sums,
    grad_sums,
    hidden,
    upstream_own,
    norm,
):
    _, rows, width = rows_all.shape
    half = inner.shape[2]
    half_rows = down_first.shape[1]
    return pl.pallas_call(
        unit_grads_kernel,
        out_shape=(
            jax.ShapeDtypeStruct((rows, width), LOW),
            jax.ShapeDtypeStruct((rows, width), jnp.float32),
            jax.ShapeDtypeStruct((rows, width), LOW),
            jax.ShapeDtypeStruct((1, width), jnp.float32),
            jax.ShapeDtypeStruct((2, half_rows, width), LOW),
            jax.ShapeDtypeStruct((width, 2 * half), LOW),
        ),
        in_specs=[ANYWHERE] * 7 + [WHOLE] * 3,
        out_specs=(WHOLE,) * 6,
        scratch_shapes=[
            pltpu.SemaphoreType.DMA((64,)),
            pltpu.VMEM(upstream.shape, LOW),
            pltpu.VMEM(inner.shape, LOW),
            pltpu.VMEM(second_grad.shape, LOW),
            pltpu.VMEM((2, 8, rows, 256), LOW),
            pltpu.VMEM((8, width), jnp.float32),
            pltpu.VMEM((half, width), LOW),
        ]
        + NearScatter.scratch(rows, width) * 2
        + LineScatter.scratch(half_rows, width)
        + LineScatter.scratch(half_rows, width, True),
        compiler_params=comm_params(4),
        cost_estimate=comm_cost(65),
    )(
        rows_all,
        upstream,
        inner,
        second_grad,
        down_first,
        part_sums,
        grad_sums,
        hidden,
        upstream_own,
        norm,
    )


def turn_pairs(values, cosine, sine):
    return values * cosine + pltpu.roll(values, HEAD_SIZE // 2, 1) * sine


def softmax_of(query, key, allowed):
    scores = matmul_nt(query, key) * HEAD_SIZE ** (-0.5)
    masked = jnp.where(allowed, scores, MASKED)
    exponent = jnp.exp(masked - jnp.max(masked, axis=-1, keepdims=True))
    return exponent / jnp.sum(exponent, axis=-1, keepdims=True)


def lanes(values, head):
    return values[:, head * HEAD_SIZE : (head + 1) * HEAD_SIZE]


def roll_half(values):
    return pltpu.roll(values, HEAD_SIZE // 2, 1)


def attend_back_values(raw, kept, grad, allowed, cosine, sine, gains_ref, roll=roll_half):
    group_rows = raw.shape[0]
    heads = raw.shape[1] // HEAD_SIZE - 2
    key, value = lanes(kept, heads), lanes(kept, heads + 1)
    scale = HEAD_SIZE ** (-0.5)
    turned_grads = []
    key_grad = jnp.zeros((group_rows, HEAD_SIZE), jnp.float32)
    value_grad = jnp.zeros((group_rows, HEAD_SIZE), jnp.float32)
    for head in range(heads):
        query, upstream = lanes(kept, head), lanes(grad, head)
        probs = softmax_of(query, key, allowed)
        probs_grad = matmul_nt(upstream, value)
        scores_grad = low(
            probs * (probs_grad - jnp.sum(probs * probs_grad, axis=-1, keepdims=True))
        )
        turned_grads.append(matmul(scores_grad, key) * scale)
        key_grad = key_grad + matmul_tn(scores_grad, query)
        value_grad = value_grad + matmul_tn(low(probs), upstream)
    turned_grads.append(key_grad * scale)
    outs, gains = [], []
    for head in range(heads + 1):
        gain = gains_ref[min(head // heads, 1)][None, :]
        unnormed = lanes(raw, head)
        upstream = turned_grads[head] * cosine - roll(turned_grads[head]) * sine
        grad_raw, gain_part = norm_back(unnormed, inv_rms(unnormed), gain, upstream)
        outs.append(low(grad_raw))
        gains.append(gain_part[None, :])
    outs.append(low(value_grad))
    query_gain = sum(gains[1:heads], gains[0])
    return (jnp.concatenate(outs, axis=1), jnp.concatenate([query_gain, gains[heads]], axis=1))


def heads_back_kernel(
    branch_ref,
    out_ref,
    attended_ref,
    raw_ref,
    low_ref,
    cos_ref,
    sin_ref,
    segment_col,
    segment_row,
    id_col,
    id_row,
    gains_ref,
    rows_all,
    qkv_ref,
    second_part,
    first_rows,
    input_ref,
    hidden_ref,
    norm_ref,
    mlp_gain,
    grad_ref,
    qkv_columns,
    proj_out,
    first_columns,
    second_columns,
    gains_out,
    marks_ref,
    qkv_part,
    proj_sum,
    grad_sums,
    line_sum,
    qkv_sum,
    row_sum,
    gain_rows,
    gain_mine,
    gain_got,
    out_mat,
    qkv_mat,
    attended,
    branch,
    own_grad,
    heads_grad,
    raw_block,
    low_block,
    qkv_grad,
    row_slab,
    proj_part,
    *buffers,
):
    place = Place()
    marks = Marks(marks_ref)
    greet(place, [place.x, place.y, place.d, place.pair], True)
    rows, width = branch_ref.shape
    half_heads = heads_grad.shape[2]
    group_rows = 2 * rows
    second_line = LineScatter(place, lambda z: second_part.at[z], line_sum, buffers[0:1], marks)
    first_pieces = Exchange(
        place, lambda p, step: first_rows.at[p], lambda p, step: first_columns.at[p], marks
    )
    proj_plane = PlaneScatter(
        place,
        proj_part,
        proj_sum,
        buffers[1:2],
        marks,
        (place.p, place.px, place.py, place.pd),
    )
    tokens = PlaneScatter(place, grad_sums, row_sum, buffers[2:3], marks)
    qkv_rows, proj_rows = qkv_sum.shape[0], proj_out.shape[0]
    qkv_line = LineScatter(
        place,
        lambda z: qkv_part.at[pl.ds(pl.multiple_of(z * qkv_rows, 16), qkv_rows)],
        qkv_sum,
        buffers[3:4],
        marks,
        True,
    )
    proj_line = LineScatter(
        place,
        lambda z: proj_sum.at[pl.ds(pl.multiple_of(z * proj_rows, 16), proj_rows)],
        proj_out,
        buffers[4:],
        marks,
        True,
    )
    piece_rows, second_piece = qkv_rows // 4, line_sum.shape[0] // 4
    qkv_pieces = Exchange(
        place,
        lambda p, step: qkv_sum.at[pl.ds(pl.multiple_of(p * piece_rows, 16), piece_rows)],
        lambda p, step: qkv_columns.at[p],
        marks,
    )
    second_pieces = Exchange(
        place,
        lambda p, step: line_sum.at[pl.ds(pl.multiple_of(p * second_piece, 16), second_piece)],
        lambda p, step: second_columns.at[p],
        marks,
    )
    near_z = {"f": place.z + 1 - 2 * (place.z % 2)}
    rounds = [
        remote(gain_mine.at[index], gain_got.at[index], marks.take(), marks.take(), to)
        for index, to in enumerate((place.pair, place.x, place.y, near_z, place.two))
    ]
    heads = Exchange(
        place, lambda p, step: own_grad.at[p], lambda p, step: heads_grad.at[step], marks
    )
    to_pair = remote(branch_ref, branch.at[1], marks.take(), marks.take(), place.pair)
    loads = [
        pltpu.make_async_copy(out_ref, out_mat, marks.take()),
        pltpu.make_async_copy(attended_ref, attended, marks.take()),
        pltpu.make_async_copy(qkv_ref, qkv_mat, marks.take()),
    ]
    fetch_marks, slab_marks = marks.take(4), marks.take(2)
    send_marks, recv_marks = marks.take(4), marks.take(4)

    to_pair.start()
    second_line.start()
    for copy in loads:
        copy.start()
    branch[0] = branch_ref[...]
    for copy in loads:
        copy.wait()

    def own_half(core_step):
        grad = low(matmul_nt(branch[core_step], out_mat[...]))
        for p in range(4):
            own_grad[p, pl.ds(core_step * rows, rows)] = grad[
                :, p * half_heads : (p + 1) * half_heads
            ]

    own_half(0)
    to_pair.wait()
    own_half(1)
    heads.start()
    second_line.middle()

    def proj_work(z, carry):
        block = attended[z].reshape(group_rows, half_heads)
        grad = low(matmul_tn(block, branch[...].reshape(group_rows, width)))
        part = half_heads // 4
        for p in range(4):
            proj_part[p, pl.ds(pl.multiple_of(z * part, part), part)] = grad[
                p * part : (p + 1) * part
            ]
        return carry

    def fetches(step):
        return (
            pltpu.make_async_copy(raw_ref.at[:, step], raw_block, fetch_marks.at[0]),
            pltpu.make_async_copy(low_ref.at[:, step], low_block, fetch_marks.at[1]),
        )

    lax.fori_loop(0, 4, proj_work, 0)
    heads.wait()
    proj_plane.start()
    first_pieces.start()
    head_width = 2 * HEAD_SIZE
    head_gain = gain_mine.at[0, :, pl.ds(2 * width, head_width)]
    head_gain[...] = jnp.zeros((1, head_width), jnp.float32)

    def sends(step):
        return remote(
            out_mat.at[pl.ds(pl.multiple_of(step * rows, rows), rows)],
            grad_sums.at[step],
            send_marks.at[step],
            recv_marks.at[step],
            place.pair,
        )

    def bucket(step, carry):
        for copy in fetches(step):
            copy.start()
        for copy in fetches(step):
            copy.wait()
        allowed = (segment_col[step] == segment_row[step]) & (id_row[...] <= id_col[...])
        grads, gains = attend_back_values(
            raw_block[...].reshape(group_rows, -1),
            low_block[...].reshape(group_rows, -1),
            heads_grad[step],
            allowed,
            cos_ref[step],
            sin_ref[step],
            gains_ref,
        )
        head_gain[...] += gains
        qkv_grad[0, step] = grads[:rows]
        qkv_grad[1, step] = grads[rows:]
        out_mat[pl.ds(pl.multiple_of(step * rows, rows), rows)] = low(
            matmul_nt(grads[rows:], qkv_mat[...])
        )
        sends(step).start()
        return carry

    lax.fori_loop(0, 2, bucket, 0)
    proj_plane.middle()
    lax.fori_loop(2, 4, bucket, 0)

    tile = row_slab.shape[3]
    tiles = width // tile

    def slab(index):
        return pltpu.make_async_copy(
            rows_all.at[:, :, pl.ds(pl.multiple_of(index * tile, tile), tile)],
            row_slab.at[index % 2],
            slab_marks.at[index % 2],
        )

    slab(0).start()

    def own_work(step, carry):
        copy = sends(step)
        copy.wait_recv()
        grad = matmul_nt(qkv_grad[0, step], qkv_mat[...])
        grad_sums[step] = low(grad + f32(grad_sums[step]))
        return carry

    lax.fori_loop(0, 4, own_work, 0)
    tokens.start()

    def row_tile(index, carry):
        slab(index).wait()

        @pl.when(index < tiles - 1)
        def _():
            slab(index + 1).start()

        block = row_slab[index % 2].reshape(4 * group_rows, tile)
        out_rows = pl.ds(pl.multiple_of(index * tile, tile), tile)
        qkv_part[out_rows] = low(
            matmul_tn(block, qkv_grad[...].reshape(4 * group_rows, qkv_grad.shape[3]))
        )
        return carry

    lax.fori_loop(0, tiles, row_tile, 0)
    second_line.finish()
    qkv_line.start()
    proj_plane.finish()
    tokens.middle()
    second_pieces.start()
    qkv_line.middle()
    proj_line.start()
    tokens.finish()
    proj_line.middle()

    gain_rows[...] = jnp.zeros_like(gain_rows)
    norm_row = norm_ref[...]

    def norm_work(part):
        values = f32(input_ref[part])
        scales = inv_rms(values)
        upstream = row_sum[part]
        weighted = upstream * norm_row
        inner_mean = jnp.mean(weighted * values, axis=-1, keepdims=True)
        grad_ref[part] = (
            hidden_ref[part]
            + scales * weighted
            - values * (scales * scales * scales) * inner_mean
        )
        parts = upstream * values * scales
        gain_rows[...] += parts[:8] + parts[8:]

    each_rows(rows, 16, norm_work)
    gain_mine[0, :, pl.ds(0, width)] = jnp.sum(gain_rows[...], axis=0, keepdims=True)
    gain_mine[0, :, pl.ds(width, width)] = mlp_gain[...]
    for index, copy in enumerate(rounds):
        copy.start()
        copy.wait()
        summed = gain_mine[index] + gain_got[index]
        if index < 4:
            gain_mine[index + 1] = summed
        else:
            gains_out[...] = summed
    qkv_line.finish()
    qkv_pieces.start()
    proj_line.finish()
    for step in range(4):
        sends(step).wait_send()
    heads.finish()
    for part in (proj_plane, second_line, qkv_line, proj_line, tokens):
        part.drain()
    for part in (first_pieces, second_pieces, qkv_pieces):
        part.wait()
        part.finish()


def heads_backward(
    branch,
    out_all,
    attended,
    raw,
    kept,
    tables,
    rows_all,
    qkv_all,
    second_part,
    first_rows,
    layer_input,
    hidden_grad,
    norm,
    mlp_gain,
):
    rows, width = branch.shape
    head_part = raw.shape[3]
    query_part = head_part - 2 * HEAD_SIZE
    line_rows, units = second_part.shape[1:]
    qkv_rows = width // 4
    tile = 256
    gain_width = 2 * width + 2 * HEAD_SIZE
    pieces = jax.ShapeDtypeStruct((4, line_rows // 4, units), LOW)
    return pl.pallas_call(
        heads_back_kernel,
        out_shape=(
            jax.ShapeDtypeStruct((rows, width), jnp.float32),
            jax.ShapeDtypeStruct((4, qkv_rows // 4, head_part), LOW),
            jax.ShapeDtypeStruct((query_part // 4, width), LOW),
            pieces,
            pieces,
            jax.ShapeDtypeStruct((1, gain_width), jnp.float32),
        ),
        in_specs=[WHOLE]
        + [ANYWHERE] * 4
        + [WHOLE] * len(tables)
        + [ANYWHERE] * 4
        + [WHOLE] * 4,
        out_specs=(WHOLE, ANYWHERE, WHOLE, ANYWHERE, ANYWHERE, WHOLE),
        scratch_shapes=[
            pltpu.SemaphoreType.DMA((160,)),
            pltpu.VMEM((width, head_part), LOW),
            pltpu.VMEM((query_part, width), LOW),
            pltpu.VMEM((4, rows, width), LOW),
            pltpu.VMEM((line_rows, units), LOW),
            pltpu.VMEM((qkv_rows, head_part), LOW),
            pltpu.VMEM((rows, width), jnp.float32),
            pltpu.VMEM((8, width), jnp.float32),
            pltpu.VMEM((5, 1, gain_width), jnp.float32),
            pltpu.VMEM((5, 1, gain_width), jnp.float32),
            pltpu.VMEM(out_all.shape, LOW),
            pltpu.VMEM(qkv_all.shape, LOW),
            pltpu.VMEM(attended.shape, LOW),
            pltpu.VMEM((2, rows, width), LOW),
            pltpu.VMEM((4, 2 * rows, query_part), LOW),
            pltpu.VMEM((4, 2 * rows, query_part), LOW),
            pltpu.VMEM((2, rows, head_part), jnp.float32),
            pltpu.VMEM((2, rows, head_part), LOW),
            pltpu.VMEM((2, 4, rows, head_part), LOW),
            pltpu.VMEM((2, 8, rows, tile), LOW),
            pltpu.VMEM((4, query_part, width), LOW),
        ]
        + LineScatter.scratch(line_rows, units)
        + PlaneScatter.scratch(query_part, width)
        + PlaneScatter.scratch(rows, width)
        + LineScatter.scratch(qkv_rows, head_part, True)
        + LineScatter.scratch(query_part // 4, width, True),
        compiler_params=comm_params(3),
        cost_estimate=comm_cost(120),
    )(
        branch,
        out_all,
        attended,
        raw,
        kept,
        *tables,
        rows_all,
        qkv_all,
        second_part,
        first_rows,
        layer_input,
        hidden_grad,
        norm,
        mlp_gain,
    )


def row_ids_of(local_rows):
    core = lax.axis_index("tensor")
    local_ids = jnp.arange(local_rows, dtype=jnp.int32)
    return jnp.concatenate([core * local_rows + local_ids, (1 - core) * local_rows + local_ids])


def heads_of(weight):
    return weight.reshape(weight.shape[0], 4, -1).transpose(1, 0, 2)


def heads_back(pieces):
    return f32(pieces).transpose(1, 0, 2).reshape(pieces.shape[1], -1)


def units_of(weight, down_rows):
    split = weight.reshape(weight.shape[0], -1, 4, down_rows)
    return split.transpose(2, 0, 1, 3).reshape(4, weight.shape[0], -1)


def units_back(pieces, down_rows):
    rows = pieces.shape[1]
    return f32(pieces).reshape(4, rows, -1, down_rows).transpose(1, 2, 0, 3).reshape(rows, -1)


def shards(*arguments):
    if lax.axis_size("f") == 4:
        return line_of_four(*arguments)
    return any_line(*arguments)


def line_of_four(
    layer_input,
    attn_norm,
    head_norms,
    query_weight,
    key_matrix,
    value_matrix,
    output_weight,
    mlp_norm,
    gate_weight,
    up_weight,
    down_weight,
    grad_out,
    doc_lengths,
):
    local_rows, model_width = layer_input.shape
    weight_rows = gate_weight.shape[0]
    down_rows = down_weight.shape[0]
    half_rows = down_rows // 2
    half = 4 * half_rows
    qkv_pieces = jnp.concatenate(
        [heads_of(query_weight), heads_of(key_matrix), heads_of(value_matrix)], axis=2
    )
    head_part = qkv_pieces.shape[2]
    query_part = head_part - 2 * HEAD_SIZE
    input_float = f32(layer_input)

    def half_pieces(index):
        return jnp.concatenate(
            [
                weight.reshape(weight_rows, 4, 4, 2, half_rows)[:, :, :, index]
                .transpose(2, 0, 1, 3)
                .reshape(4, weight_rows, half)
                for weight in (gate_weight, up_weight)
            ],
            axis=2,
        )

    down_halves = down_weight.reshape(2, half_rows, model_width)
    row_ids = row_ids_of(local_rows)
    (
        normed_attn,
        _,
        first_all,
        above,
        below,
        grad_near,
        qkv_all,
        out_all,
        qkv_raw,
        qkv_low,
        cos_tab,
        sin_tab,
        segment_col,
        segment_row,
        attended,
        hidden_state,
        normed_mlp,
    ) = first_part(
        low(input_float * inv_rms(input_float) * attn_norm),
        qkv_pieces,
        output_weight,
        half_pieces(0),
        down_halves,
        doc_lengths,
        row_ids,
        head_norms,
        layer_input,
        mlp_norm,
        grad_out,
    )
    tables = (
        cos_tab,
        sin_tab,
        segment_col,
        segment_row,
        row_ids[:, None],
        row_ids[None, :],
        head_norms,
    )
    (
        rows_all,
        grad_all,
        _,
        inner_low,
        second_grad,
        first_rows,
        grad_down_first,
        part_sums,
        grad_sums,
    ) = (
        units_products(
            normed_mlp,
            grad_out,
            grad_near,
            half_pieces(1),
            first_all.reshape(model_width, 2 * half),
            down_halves,
            above,
            below,
        )
    )
    line_shape = (4, 4 * weight_rows, 2 * half)
    (
        layer_out,
        hidden_grad,
        branch_grad,
        mlp_gain_part,
        grad_down,
        grad_second,
    ) = unit_grads(
        rows_all,
        grad_all,
        inner_low,
        second_grad,
        grad_down_first.reshape(4, half_rows, model_width),
        part_sums,
        grad_sums,
        hidden_state,
        grad_out,
        mlp_norm[None],
    )
    grad_input, grad_qkv_columns, grad_out_proj, first_columns, second_columns, gains = (
        heads_backward(
            branch_grad,
            out_all.reshape(-1, model_width),
            attended,
            qkv_raw,
            qkv_low,
            tables,
            normed_attn,
            qkv_all.reshape(model_width, head_part),
            grad_second.reshape(line_shape),
            first_rows.reshape(4, weight_rows, 2 * half),
            layer_input,
            hidden_grad,
            attn_norm[None],
            mlp_gain_part,
        )
    )
    gains = gains.reshape(-1)

    def units_joined(offset):
        halves = [
            f32(columns[:, :, offset : offset + half]).reshape(4, weight_rows, 4, 1, half_rows)
            for columns in (first_columns, second_columns)
        ]
        joined = jnp.concatenate(halves, axis=3)
        return joined.transpose(1, 2, 0, 3, 4).reshape(weight_rows, -1)

    return (
        layer_out,
        grad_input,
        gains[:model_width],
        gains[2 * model_width :].reshape(2, HEAD_SIZE),
        heads_back(grad_qkv_columns[:, :, :query_part]),
        heads_back(grad_qkv_columns[:, :, query_part : query_part + HEAD_SIZE]),
        heads_back(grad_qkv_columns[:, :, query_part + HEAD_SIZE :]),
        f32(grad_out_proj),
        gains[model_width : 2 * model_width],
        units_joined(0),
        units_joined(half),
        f32(grad_down).reshape(down_weight.shape),
    )


def any_line(
    layer_input,
    attn_norm,
    head_norms,
    query_weight,
    key_matrix,
    value_matrix,
    output_weight,
    mlp_norm,
    gate_weight,
    up_weight,
    down_weight,
    grad_out,
    doc_lengths,
):
    line_extent = lax.axis_size("f")
    local_rows, model_width = layer_input.shape
    group_rows = 2 * local_rows
    all_rows = 8 * local_rows
    weight_rows = gate_weight.shape[0]
    down_rows = down_weight.shape[0]
    hidden_part = line_extent * down_rows
    qkv_pieces = jnp.concatenate(
        [heads_of(query_weight), heads_of(key_matrix), heads_of(value_matrix)], axis=2
    )
    head_part = qkv_pieces.shape[2]
    query_part = head_part - 2 * HEAD_SIZE
    heads = head_part // HEAD_SIZE - 2

    def exchanged(pieces):
        return natural_plane(plane_exchange(own_plane(pieces, 0)), 0)

    def line_rows(pieces):
        return line_gather(exchanged(pieces)).reshape(model_width, -1)

    def line_sums(partial):
        parts = low(partial).reshape(line_extent, 4 * weight_rows, -1)
        return exchanged(low(line_scatter(parts)).reshape(4, weight_rows, -1))

    qkv_all = line_rows(qkv_pieces)
    out_all = full_gather(output_weight)
    gate_all = line_rows(units_of(gate_weight, down_rows))
    up_all = line_rows(units_of(up_weight, down_rows))
    down_all = line_gather(down_weight).reshape(hidden_part, model_width)

    input_float = f32(layer_input)
    scale_attn = inv_rms(input_float)
    normed_attn = tokens_gather(low(input_float * scale_attn * attn_norm))
    row_ids = row_ids_of(local_rows)
    segments, positions = jax.vmap(lambda lengths: doc_layout(lengths, row_ids))(
        plane_lengths(doc_lengths)
    )
    qkv_raw = matmul(normed_attn, qkv_all).reshape(2, 4, local_rows, head_part)
    roll = lambda values: jnp.roll(values, HEAD_SIZE // 2, 1)
    buckets, attended_parts = [], []
    for step in range(4):
        cos_tab, sin_tab = rope_tables(positions[step], HEAD_SIZE)
        cosine = jnp.concatenate([cos_tab, cos_tab], axis=1)
        sine = jnp.concatenate([-sin_tab, sin_tab], axis=1)
        allowed = (segments[step][:, None] == segments[step][None, :]) & (
            row_ids[None, :] <= row_ids[:, None]
        )
        raw = qkv_raw[:, step].reshape(group_rows, head_part)
        turned = []
        for head in range(heads + 1):
            unnormed = lanes(raw, head)
            normed = unnormed * inv_rms(unnormed) * head_norms[min(head // heads, 1)]
            turned.append(low(normed * cosine + roll(normed) * sine))
        value = low(lanes(raw, heads + 1))
        attended_parts.append(
            jnp.concatenate(
                [
                    low(matmul(low(softmax_of(turned[head], turned[heads], allowed)), value))
                    for head in range(heads)
                ],
                axis=1,
            )
        )
        buckets.append((raw, jnp.concatenate(turned + [value], axis=1), allowed, cosine, sine))
    attended = natural_plane(plane_exchange(attended_parts), 0)
    attended = attended.transpose(1, 0, 2).reshape(group_rows, 4 * query_part)
    hidden_state = input_float + pair_scatter(low(matmul(attended, out_all)))

    scale_mlp = inv_rms(hidden_state)
    normed_mlp = tokens_gather(low(hidden_state * scale_mlp * mlp_norm))
    grad_all = tokens_gather(grad_out)
    gate_raw = matmul(normed_mlp, gate_all)
    up_raw = matmul(normed_mlp, up_all)
    activated = jax.nn.silu(gate_raw)
    inner_low = low(activated * up_raw)
    layer_out = low(hidden_state + tokens_scatter(low(matmul(inner_low, down_all))))
    inner_grad = matmul_nt(grad_all, down_all)
    sigmoid_gate = jax.nn.sigmoid(gate_raw)
    gate_grad = low(inner_grad * up_raw * sigmoid_gate * (1.0 + gate_raw * (1.0 - sigmoid_gate)))
    up_grad = low(inner_grad * activated)
    mlp_row_grad = tokens_scatter(
        low(matmul_nt(gate_grad, gate_all) + matmul_nt(up_grad, up_all))
    )
    grad_down = line_scatter(
        low(matmul_tn(inner_low, grad_all)).reshape(line_extent, down_rows, model_width)
    )

    hidden_norm_grad, mlp_gain_part = norm_back(hidden_state, scale_mlp, mlp_norm, mlp_row_grad)
    hidden_grad = f32(grad_out) + hidden_norm_grad
    branch_grad = pair_gather(low(hidden_grad))
    split = low(matmul_nt(branch_grad, out_all)).reshape(group_rows, 4, query_part)
    heads_grad = plane_exchange(own_plane(split.transpose(1, 0, 2), 0))
    grad_out_proj = line_scatter(full_scatter_plane(low(matmul_tn(attended, branch_grad))))
    back = [
        attend_back_values(raw, kept, heads_grad[step], allowed, cosine, sine, head_norms, roll)
        for step, (raw, kept, allowed, cosine, sine) in enumerate(buckets)
    ]
    qkv_grad = jnp.stack([grads for grads, _ in back]).reshape(4, 2, local_rows, head_part)
    qkv_grad = qkv_grad.transpose(1, 0, 2, 3).reshape(all_rows, head_part)
    attn_row_grad = tokens_scatter(low(matmul_nt(qkv_grad, qkv_all)))
    grad_qkv_columns = line_sums(matmul_tn(normed_attn, qkv_grad))
    input_norm_grad, attn_gain_part = norm_back(input_float, scale_attn, attn_norm, attn_row_grad)
    head_gains = sum(gains for _, gains in back)[0]
    gains = total_sum(
        jnp.concatenate([attn_gain_part, mlp_gain_part, head_gains]).reshape(-1, HEAD_SIZE)
    ).reshape(-1)
    return (
        layer_out,
        hidden_grad + input_norm_grad,
        gains[:model_width],
        gains[2 * model_width :].reshape(2, HEAD_SIZE),
        heads_back(grad_qkv_columns[:, :, :query_part]),
        heads_back(grad_qkv_columns[:, :, query_part : query_part + HEAD_SIZE]),
        heads_back(grad_qkv_columns[:, :, query_part + HEAD_SIZE :]),
        grad_out_proj,
        gains[model_width : 2 * model_width],
        units_back(line_sums(matmul_tn(normed_mlp, gate_grad)), down_rows),
        units_back(line_sums(matmul_tn(normed_mlp, up_grad)), down_rows),
        grad_down,
    )


def solution(mesh):
    dp, tensor = mesh.shape["dp"], mesh.shape["tensor"]
    fine = Mesh(mesh.devices.reshape(dp // 4, 2, 2, tensor), ("f", "ty", "tx", "tensor"))
    rows = ("f", "ty", "tx")
    tokens = P(rows + ("tensor",), None)
    grid = P(rows, "tensor")
    units = P(("tensor",) + rows, None)
    return jax.shard_map(
        shards,
        mesh=fine,
        in_specs=(
            tokens, P(), P(), grid, grid, grid, units, P(), grid, grid, units, tokens, P(rows, None),
        ),
        out_specs=(tokens, tokens, P(), P(), grid, grid, grid, units, P(), grid, grid, units),
        check_vma=False,
    )
```

```python
import jax
import jax.numpy as jnp
from jax import lax
from jax.experimental import pallas as pl
from jax.experimental.pallas import tpu as pltpu
from jax.sharding import Mesh, PartitionSpec as P

QUERY_HEADS = 16
KEY_VALUE_HEADS = 8
HEAD_SIZE = 128


EPS = 1e-06
ROPE_BASE = 1000000.0
MASKED = -1e30
LOW = jnp.bfloat16


def matmul(left_mat, right_mat):
    return jnp.dot(left_mat, right_mat, preferred_element_type=jnp.float32)


def matmul_tn(left_mat, right_mat):
    return lax.dot_general(
        left_mat, right_mat, (((0,), (0,)), ((), ())), preferred_element_type=jnp.float32
    )


def matmul_nt(left_mat, right_mat):
    return lax.dot_general(
        left_mat, right_mat, (((1,), (1,)), ((), ())), preferred_element_type=jnp.float32
    )


def inv_rms(values):
    return lax.rsqrt(jnp.mean(values * values, axis=-1, keepdims=True) + EPS)


def norm_back(values, scales, gain_row, upstream):
    weighted = upstream * gain_row
    inner_mean = jnp.mean(weighted * values, axis=-1, keepdims=True)
    value_grad = scales * weighted - values * (scales * scales * scales) * inner_mean
    lead_axes = tuple(range(upstream.ndim - 1))
    return (value_grad, jnp.sum(upstream * values * scales, axis=lead_axes))


def rope_tables(position, head_width):
    half_dim = head_width // 2
    inverse = ROPE_BASE ** (-(jnp.arange(half_dim, dtype=jnp.float32) * (2.0 / head_width)))
    angles = position.astype(jnp.float32)[:, None] * inverse[None, :]
    return (jnp.cos(angles), jnp.sin(angles))


def rotate(values, cos_tab, sin_tab, direction):
    half_dim = values.shape[-1] // 2
    first_half = values[..., :half_dim]
    second_half = values[..., half_dim:]
    cosine = cos_tab[:, None, :]
    sine_tab = direction * sin_tab[:, None, :]
    return jnp.concatenate(
        [
            first_half * cosine - second_half * sine_tab,
            second_half * cosine + first_half * sine_tab,
        ],
        axis=-1,
    )


def doc_layout(lengths_row, row_ids):
    doc_ends = jnp.cumsum(lengths_row, dtype=jnp.int32)
    document_segment = jnp.sum(
        (row_ids[:, None] >= doc_ends[None, :]).astype(jnp.int32), axis=1, dtype=jnp.int32
    )
    doc_starts = doc_ends - lengths_row
    member = document_segment[:, None] == jnp.arange(lengths_row.shape[0], dtype=jnp.int32)[None, :]
    start_of = jnp.sum(jnp.where(member, doc_starts[None, :], 0), axis=1, dtype=jnp.int32)
    return (document_segment, row_ids - start_of)


def f32(values):
    return values.astype(jnp.float32)


def low(values):
    return values.astype(LOW)


def swap(block, axis):
    return lax.ppermute(block, axis, [(0, 1), (1, 0)])


def plane_index():
    return 2 * lax.axis_index("ty") + lax.axis_index("tx")


def plane_gather(block):
    across_x = swap(block, "tx")
    across_y = swap(block, "ty")
    return [block, across_x, across_y, swap(across_y, "tx")]


def plane_scatter(parts):
    own, for_x, for_y, for_far = parts
    for_y = low(f32(for_y) + f32(swap(for_far, "tx")))
    return f32(own) + f32(swap(for_x, "tx")) + f32(swap(for_y, "ty"))


def plane_exchange(parts):
    own, for_x, for_y, for_far = parts
    return [own, swap(for_x, "tx"), swap(for_y, "ty"), swap(swap(for_far, "tx"), "ty")]


def plane_lengths(lengths):
    return jnp.concatenate(plane_gather(lengths))


def line_gather(block):
    return lax.all_gather(block, "f", axis=0)


def line_scatter(parts):
    return f32(lax.psum_scatter(parts, "f", scatter_dimension=0))


def natural_plane(blocks, axis):
    own = plane_index()
    shape = list(blocks[0].shape)
    shape.insert(axis, 4)
    whole = jnp.zeros(shape, blocks[0].dtype)
    for step in range(4):
        whole = lax.dynamic_update_index_in_dim(whole, blocks[step], own ^ step, axis)
    return whole


def own_plane(whole, axis):
    own = plane_index()
    return [
        lax.dynamic_index_in_dim(whole, own ^ step, axis, keepdims=False) for step in range(4)
    ]


def full_gather(rows_block):
    rows, width = rows_block.shape
    line = line_gather(rows_block)
    extent = line.shape[0]
    blocks = plane_gather(line.reshape(extent * rows, width))
    whole = natural_plane([block.reshape(extent, rows, width) for block in blocks], 1)
    return whole.reshape(extent * 4 * rows, width)


def full_scatter_plane(partial):
    extent = lax.axis_size("f")
    rows, width = partial.shape[0] // (4 * extent), partial.shape[1]
    parts = own_plane(partial.reshape(extent, 4, rows, width), 1)
    plane_sum = plane_scatter([part.reshape(extent * rows, width) for part in parts])
    return low(plane_sum).reshape(extent, rows, width)


def tokens_gather(block):
    near = plane_gather(block)
    return jnp.concatenate(near + [swap(piece, "tensor") for piece in near])


def tokens_scatter(partial):
    rows = partial.shape[0] // 8
    near = []
    for step in range(4):
        mine = partial[step * rows : (step + 1) * rows]
        other = swap(partial[(4 + step) * rows : (5 + step) * rows], "tensor")
        near.append(low(f32(mine) + f32(other)))
    return plane_scatter(near)


def pair_gather(block):
    return jnp.concatenate([block, swap(block, "tensor")])


def pair_scatter(partial):
    rows = partial.shape[0] // 2
    return f32(partial[:rows]) + f32(swap(partial[rows:], "tensor"))


def total_sum(values):
    return lax.psum(values, ("f", "ty", "tx", "tensor"))


class Place:
    def __init__(self):
        self.z = lax.axis_index("f")
        self.ty = lax.axis_index("ty")
        self.tx = lax.axis_index("tx")
        self.core = lax.axis_index("tensor")
        self.p = 2 * self.ty + self.tx
        self.px = 2 * self.ty + 1 - self.tx
        self.py = 2 * (1 - self.ty) + self.tx
        self.pd = 2 * (1 - self.ty) + 1 - self.tx
        self.x = {"tx": 1 - self.tx}
        self.y = {"ty": 1 - self.ty}
        self.d = {"tx": 1 - self.tx, "ty": 1 - self.ty}
        self.pair = {"tensor": 1 - self.core}
        self.up = {"f": self.z + 1}
        self.down = {"f": self.z - 1}
        self.two = {"f": (self.z + 2) % 4}

    def at(self, step):
        return (self.z + step) % 4


def remote(src, dst, send, recv, to):
    return pltpu.make_async_remote_copy(
        src_ref=src,
        dst_ref=dst,
        send_sem=send,
        recv_sem=recv,
        device_id=to,
        device_id_type=pl.DeviceIdType.MESH,
    )


def arrived(dst, recv, to):
    remote(dst, dst, recv, recv, to).wait_recv()


def greet(place, partners, line):
    barrier = pltpu.get_barrier_semaphore()
    for to in partners:
        pl.semaphore_signal(barrier, inc=1, device_id=to, device_id_type=pl.DeviceIdType.MESH)
    if not line:
        pl.semaphore_wait(barrier, len(partners))
        return

    @pl.when(place.z > 0)
    def _():
        pl.semaphore_signal(
            barrier, inc=1, device_id=place.down, device_id_type=pl.DeviceIdType.MESH
        )

    @pl.when(place.z < 3)
    def _():
        pl.semaphore_signal(barrier, inc=1, device_id=place.up, device_id_type=pl.DeviceIdType.MESH)

    pl.semaphore_signal(barrier, inc=1, device_id=place.two, device_id_type=pl.DeviceIdType.MESH)
    pl.semaphore_wait(barrier, len(partners) + 2 + (place.z + 1) // 2 % 2)


class LineGather:
    def __init__(self, place, own, slot, send, recv):
        self.place, self.own, self.slot, self.send, self.recv = place, own, slot, send, recv
        here = slot(place.z)
        self.to_down = remote(own, here, send.at[0], recv.at[1], place.down)
        self.to_up = remote(own, here, send.at[1], recv.at[3], place.up)
        self.to_two = remote(own, here, send.at[2], recv.at[2], place.two)
        two = slot(place.at(2))
        self.pass_down = remote(two, two, send.at[3], recv.at[3], place.down)
        self.pass_up = remote(two, two, send.at[3], recv.at[1], place.up)

    def start(self):
        z = self.place.z
        self.to_two.start()
        pl.when((z == 1) | (z == 3))(self.to_down.start)
        pl.when((z == 0) | (z == 2))(self.to_up.start)

    def step(self, turn):
        if turn == 2:
            return 2
        if turn == 1:
            return jnp.where(self.place.z == 3, 3, 1)
        return jnp.where(self.place.z == 3, 1, 3)

    def wait(self, turn):
        step = self.step(turn)
        slot = self.slot(self.place.at(step))
        arrived(slot, self.recv.at[step], self.place.two)
        if turn == 2:
            pl.when(self.place.z == 1)(self.pass_down.start)
            pl.when(self.place.z == 2)(self.pass_up.start)
            pl.when(self.place.z == 1)(self.to_up.start)
            pl.when(self.place.z == 2)(self.to_down.start)

    def finish(self):
        pl.when(self.place.z > 0)(self.to_down.wait_send)
        pl.when(self.place.z < 3)(self.to_up.wait_send)
        self.to_two.wait_send()
        pl.when(self.place.z == 1)(self.pass_down.wait_send)
        pl.when(self.place.z == 2)(self.pass_up.wait_send)


class PlaneGather:
    def __init__(self, place, own, slot, rows, send, recv):
        half = rows // 2
        whole, top, end = pl.ds(0, rows), pl.ds(0, half), pl.ds(half, half)
        self.place, self.recv = place, recv
        self.to_x = remote(own, slot(place.p, whole), send.at[0], recv.at[0], place.x)
        self.to_y = remote(own, slot(place.p, whole), send.at[1], recv.at[1], place.y)
        self.from_x, self.from_y = slot(place.px, whole), slot(place.py, whole)
        self.far_top, self.far_end = slot(place.pd, top), slot(place.pd, end)
        pass_x, pass_y = slot(place.py, top), slot(place.px, end)
        self.pass_x = remote(pass_x, pass_x, send.at[2], recv.at[2], place.x)
        self.pass_y = remote(pass_y, pass_y, send.at[3], recv.at[3], place.y)

    def start(self):
        self.to_x.start()
        self.to_y.start()

    def forward(self):
        arrived(self.from_y, self.recv.at[1], self.place.y)
        self.pass_x.start()
        arrived(self.from_x, self.recv.at[0], self.place.x)
        self.pass_y.start()

    def wait_far(self):
        arrived(self.far_top, self.recv.at[2], self.place.x)
        arrived(self.far_end, self.recv.at[3], self.place.y)

    def finish(self):
        self.to_x.wait_send()
        self.to_y.wait_send()
        self.pass_x.wait_send()
        self.pass_y.wait_send()


ANYWHERE = pl.BlockSpec(memory_space=pl.ANY)
WHOLE = pl.BlockSpec(memory_space=pltpu.VMEM)


class Marks:
    def __init__(self, ref):
        self.ref, self.used = ref, 0

    def take(self, count=1):
        first = self.used
        self.used += count
        return self.ref.at[first] if count == 1 else self.ref.at[pl.ds(first, count)]


def each_rows(rows, chunk, work):
    def body(index, carry):
        work(pl.ds(pl.multiple_of(index * chunk, chunk), chunk))
        return carry

    lax.fori_loop(0, rows // chunk, body, 0)


class TokensGather:
    def __init__(self, place, own, whole, marks):
        half = own.shape[0] // 2
        top, end = pl.ds(0, half), pl.ds(half, half)
        self.place, self.whole = place, whole
        self.copy = pltpu.make_async_copy(own, whole.at[0], marks.take())
        self.recv = [marks.take() for _ in range(8)]
        x, y, pair = place.x, place.y, place.pair
        self.to_x = remote(own, whole.at[1], marks.take(), self.recv[0], x)
        self.to_y = remote(own, whole.at[2], marks.take(), self.recv[1], y)
        self.pass_x = remote(
            whole.at[2, top], whole.at[3, top], marks.take(), self.recv[2], x
        )
        self.pass_y = remote(
            whole.at[1, end], whole.at[3, end], marks.take(), self.recv[3], y
        )
        self.to_pair = [
            remote(
                own if step == 0 else whole.at[step],
                whole.at[4 + step],
                marks.take(),
                self.recv[4 + step],
                pair,
            )
            for step in range(4)
        ]
        self.far = (whole.at[3, top], whole.at[3, end])

    def start(self):
        self.to_x.start()
        self.to_y.start()
        self.to_pair[0].start()
        self.copy.start()

    def forward(self):
        arrived(self.whole.at[2], self.recv[1], self.place.y)
        self.pass_x.start()
        arrived(self.whole.at[1], self.recv[0], self.place.x)
        self.pass_y.start()
        self.to_pair[2].start()
        self.to_pair[1].start()

    def start_near(self, near, marks):
        self.copy.start()
        self.to_pair[0].start()
        copies = [
            pltpu.make_async_copy(near.at[index], self.whole.at[1 + index], marks.take())
            for index in range(2)
        ]
        for copy in copies:
            copy.start()
        for copy in copies:
            copy.wait()
        self.pass_x.start()
        self.pass_y.start()
        self.to_pair[2].start()
        self.to_pair[1].start()

    def finish_near(self):
        for step in range(4):
            arrived(self.whole.at[4 + step], self.recv[4 + step], self.place.pair)
        for copy in [self.pass_x, self.pass_y] + self.to_pair:
            copy.wait_send()
        self.copy.wait()

    def last(self):
        arrived(self.far[0], self.recv[2], self.place.x)
        arrived(self.far[1], self.recv[3], self.place.y)
        self.to_pair[3].start()

    def finish(self):
        for step in range(4):
            arrived(self.whole.at[4 + step], self.recv[4 + step], self.place.pair)
        for copy in [self.to_x, self.to_y, self.pass_x, self.pass_y] + self.to_pair:
            copy.wait_send()
        self.copy.wait()


class Exchange:
    def __init__(self, place, piece, slot, marks):
        self.place = place
        there = ((place.px, place.x), (place.py, place.y), (place.pd, place.d))
        self.copy = pltpu.make_async_copy(piece(place.p, 0), slot(place.p, 0), marks.take())
        self.sends, self.slots = [], []
        for index, (p, to) in enumerate(there):
            recv = marks.take()
            self.sends.append(
                remote(piece(p, index + 1), slot(place.p, index + 1), marks.take(), recv, to)
            )
            self.slots.append((slot(p, index + 1), recv, to))

    def start(self):
        for copy in (self.sends[2], self.sends[0], self.sends[1], self.copy):
            copy.start()

    def wait(self):
        self.copy.wait()
        for slot, recv, to in self.slots:
            arrived(slot, recv, to)

    def finish(self):
        for copy in self.sends:
            copy.wait_send()


class LineScatter:
    @staticmethod
    def scratch(rows, width, here=False):
        return [pltpu.VMEM((4 if here else 5, rows, width), LOW)]

    def __init__(self, place, part, out, buffers, marks, here=False):
        self.place, self.out, self.here = place, out, here
        kept = buffers[0]
        self.rows = kept.shape[1]
        self.passed, self.above, self.below, self.two = (kept.at[index] for index in range(4))
        z = place.z
        if here:
            self.mid, self.own = part(place.at(2)), part(z)
        else:
            self.mid, self.own = kept.at[4], self.passed
            self.load_mid = pltpu.make_async_copy(part(place.at(2)), self.mid, marks.take())
            self.load_own = pltpu.make_async_copy(part(z), self.own, marks.take())
        self.recv = [marks.take() for _ in range(4)]
        self.pass_up = remote(part(3), self.passed, marks.take(), self.recv[0], place.up)
        self.pass_down = remote(part(0), self.passed, marks.take(), self.recv[0], place.down)
        self.to_down = remote(
            part(place.at(3)), self.above, marks.take(), self.recv[1], place.down
        )
        self.to_up = remote(part(place.at(1)), self.below, marks.take(), self.recv[2], place.up)
        self.to_two = remote(self.mid, self.two, marks.take(), self.recv[3], place.two)

    def start(self):
        z = self.place.z
        pl.when(z == 0)(self.pass_up.start)
        pl.when(z == 3)(self.pass_down.start)
        if not self.here:
            self.load_mid.start()
        pl.when((z == 1) | (z == 2))(self.to_down.start)
        pl.when((z == 1) | (z == 2))(self.to_up.start)

    def add(self, target, other):
        def work(rows):
            target[rows] = low(f32(target[rows]) + f32(other[rows]))

        each_rows(self.rows, 16, work)

    def middle(self):
        z = self.place.z
        if not self.here:
            self.load_mid.wait()
        pl.when(z == 0)(self.pass_up.wait_send)
        pl.when(z == 3)(self.pass_down.wait_send)

        @pl.when((z == 1) | (z == 2))
        def _():
            arrived(self.passed, self.recv[0], self.place.two)
            self.add(self.mid, self.passed)

        self.to_two.start()
        pl.when(z == 0)(self.to_up.start)
        pl.when(z == 3)(self.to_down.start)
        if not self.here:
            self.load_own.start()

    def finish(self):
        z = self.place.z
        if not self.here:
            self.load_own.wait()

        @pl.when(z < 3)
        def _():
            arrived(self.above, self.recv[1], self.place.two)
            self.add(self.own, self.above)

        @pl.when(z > 0)
        def _():
            arrived(self.below, self.recv[2], self.place.two)
            self.add(self.own, self.below)

        arrived(self.two, self.recv[3], self.place.two)
        out, own, two = self.out, self.own, self.two

        def work(rows):
            out[rows] = (f32(own[rows]) + f32(two[rows])).astype(out.dtype)

        each_rows(self.rows, 16, work)

    def drain(self):
        z = self.place.z
        pl.when(z > 0)(self.to_down.wait_send)
        pl.when(z < 3)(self.to_up.wait_send)
        self.to_two.wait_send()


def comm_params(number):
    return pltpu.CompilerParams(
        collective_id=number, has_side_effects=True, vmem_limit_bytes=62 * 1024 * 1024
    )


def comm_cost(micros):
    return pl.CostEstimate(flops=0, bytes_accessed=micros * 3_000_000, transcendentals=0)


def tables_of(lengths_row, id_col, id_row, inverse, count):
    zero = jnp.zeros((1, 1), jnp.int32)
    segment_col, segment_row = jnp.zeros_like(id_col), jnp.zeros_like(id_row)
    ends, starts, end = [], [], zero
    for index in range(count):
        starts.append(end)
        end = end + lengths_row[:, index : index + 1]
        ends.append(end)
        segment_col = segment_col + jnp.where(id_col >= end, 1, 0)
        segment_row = segment_row + jnp.where(id_row >= end, 1, 0)
    start_of = jnp.zeros_like(id_col)
    for index in range(count):
        start_of = start_of + jnp.where(segment_col == index, starts[index], 0)
    angles = f32(id_col - start_of) * inverse
    return segment_col, segment_row, jnp.cos(angles), jnp.sin(angles)


def units_split(half, half_rows, weights, out):
    for p in range(4):
        parts = []
        for weight in weights:
            for z in range(4):
                start = ((z * 4 + p) * 2 + half) * half_rows
                parts.append(f32(weight[:, start : start + half_rows]))
        out[p] = low(jnp.concatenate(parts, axis=1))


def units_joined(halves, outs, stage, marks):
    width = stage.shape[2]
    half_rows = width // 8
    copies = []
    for which, out in enumerate(outs):
        for z in range(4):
            slot = z % 2
            if len(copies) > 1:
                copies[-2].wait()
            start = (4 * which + z) * half_rows
            parts = [
                f32(columns[p][:, start : start + half_rows])
                for p in range(4)
                for columns in halves
            ]
            stage[slot] = jnp.concatenate(parts, axis=1)
            copies.append(
                pltpu.make_async_copy(
                    stage.at[slot], out.at[:, pl.ds(z * width, width)], marks.at[slot]
                )
            )
            copies[-1].start()
    for copy in copies[-2:]:
        copy.wait()


def first_kernel(
    documents,
    attn_norm,
    query_ref,
    key_ref,
    value_ref,
    gate_weight,
    up_weight,
    out_ref,
    down_ref,
    lengths_ref,
    id_col,
    id_row,
    inverse_ref,
    head_norms,
    input_ref,
    norm_ref,
    upstream_ref,
    rows_all,
    second_pieces,
    gate_rows,
    gate_all,
    above_ref,
    below_ref,
    upstream_near,
    qkv_hbm,
    out_hbm,
    raw_hbm,
    low_hbm,
    cos_hbm,
    sin_hbm,
    segment_col,
    segment_row,
    attended,
    hidden,
    normed,
    marks_ref,
    rows_ref,
    qkv_ref,
    halves,
    qkv_all,
    out_all,
    raw_out,
    low_out,
    cos_out,
    sin_out,
    lengths_all,
    row_block,
    heads_stage,
    pair_stage,
    pair_got,
):
    place = Place()
    marks = Marks(marks_ref)
    greet(place, [place.x, place.y, place.d, place.pair], True)
    rows, width = rows_ref.shape
    head_part = raw_out.shape[3]
    heads = head_part // HEAD_SIZE - 2
    lengths = Exchange(
        place, lambda p, step: lengths_ref, lambda p, step: lengths_all.at[step], marks
    )
    qkv_pieces = Exchange(
        place, lambda p, step: qkv_ref.at[p], lambda p, step: qkv_all.at[place.z, p], marks
    )
    gate_pieces = Exchange(
        place, lambda p, step: halves.at[0, p], lambda p, step: gate_rows.at[p], marks
    )
    tokens = TokensGather(place, rows_ref, rows_all, marks)
    upstream_recv = [marks.take(), marks.take()]
    upstream = [
        remote(upstream_ref, upstream_near.at[index], marks.take(), upstream_recv[index], to)
        for index, to in enumerate((place.x, place.y))
    ]
    qkv_line = LineGather(
        place, qkv_all.at[place.z], lambda z: qkv_all.at[z], marks.take(4), marks.take(4)
    )
    gate_line = LineGather(
        place, gate_rows, lambda z: gate_all.at[z], marks.take(4), marks.take(4)
    )
    out_line = LineGather(
        place, out_ref, lambda z: out_all.at[z, place.p], marks.take(4), marks.take(4)
    )
    own_copies = [
        pltpu.make_async_copy(out_ref, out_all.at[place.z, place.p], marks.take()),
    ]
    gate_copy = pltpu.make_async_copy(gate_rows, gate_all.at[place.z], marks.take())
    near_recv = [marks.take(), marks.take()]
    to_down = remote(down_ref, above_ref, marks.take(), near_recv[0], place.down)
    to_up = remote(down_ref, below_ref, marks.take(), near_recv[1], place.up)
    out_planes = []
    for turn in range(4):
        z = place.z if turn == 0 else place.at(out_line.step(turn))
        out_planes.append(
            PlaneGather(
                place,
                out_ref if turn == 0 else out_all.at[z, place.p],
                lambda p, part, z=z: out_all.at[z, p, part],
                out_ref.shape[0],
                marks.take(4),
                marks.take(4),
            )
        )
    heads_out = Exchange(
        place, lambda p, step: heads_stage.at[step], lambda p, step: attended.at[p], marks
    )
    to_pair = remote(pair_stage, pair_got, marks.take(), marks.take(), place.pair)
    fetch_marks = marks.take(2)
    qkv_copy = pltpu.make_async_copy(qkv_all, qkv_hbm, marks.take())
    out_copy = pltpu.make_async_copy(out_all, out_hbm, marks.take())
    bucket_copies = [
        pltpu.make_async_copy(raw_out, raw_hbm, marks.take()),
        pltpu.make_async_copy(low_out, low_hbm, marks.take()),
    ]
    table_copies = [
        pltpu.make_async_copy(cos_out, cos_hbm, marks.take()),
        pltpu.make_async_copy(sin_out, sin_hbm, marks.take()),
    ]

    second_copy = pltpu.make_async_copy(halves.at[1], second_pieces, marks.take())
    half_rows = down_ref.shape[1]

    lengths.start()
    for p in range(4):
        parts = []
        for weight in (query_ref, key_ref, value_ref):
            part = weight.shape[1] // 4
            parts.append(weight[:, p * part : (p + 1) * part])
        qkv_ref[p] = jnp.concatenate(parts, axis=1)
    qkv_pieces.start()
    attn_row = attn_norm[...]

    def rows_work(part):
        values = f32(input_ref[part])
        rows_ref[part] = low(values * inv_rms(values) * attn_row)

    each_rows(rows, 16, rows_work)
    tokens.start()
    units_split(0, half_rows, (gate_weight, up_weight), halves.at[0])
    gate_pieces.start()
    for copy in own_copies:
        copy.start()
    lengths.wait()
    qkv_pieces.wait()
    qkv_line.start()

    def table_work(step, carry):
        seg_col, seg_row, cosine, sine = tables_of(
            lengths_all[step][:1], id_col[...], id_row[...], inverse_ref[...], documents
        )
        segment_col[step] = seg_col
        segment_row[step] = seg_row
        cos_out[step] = cosine
        lane = lax.broadcasted_iota(jnp.int32, sine.shape, 1)
        sin_out[step] = jnp.where(lane < HEAD_SIZE // 2, -sine, sine)
        return carry

    lax.fori_loop(0, 2, table_work, 0)
    tokens.forward()
    out_planes[0].start()
    units_split(1, half_rows, (gate_weight, up_weight), halves.at[1])
    second_copy.start()
    lax.fori_loop(2, 4, table_work, 0)
    qkv_line.wait(2)
    out_line.start()
    tokens.last()
    out_planes[0].forward()
    qkv_line.wait(1)
    qkv_line.wait(3)
    out_line.wait(2)
    out_planes[2].start()
    gate_pieces.wait()
    gate_line.start()
    gate_copy.start()
    for copy in table_copies:
        copy.start()
    qkv_copy.start()
    tokens.finish()

    def fetches(step):
        return (
            pltpu.make_async_copy(rows_all.at[step], row_block.at[0], fetch_marks.at[0]),
            pltpu.make_async_copy(rows_all.at[4 + step], row_block.at[1], fetch_marks.at[1]),
        )

    def bucket(turn, carry):
        step = 3 - turn
        for copy in fetches(step):
            copy.start()
        for copy in fetches(step):
            copy.wait()
        raw = matmul(
            row_block[...].reshape(2 * rows, width), qkv_all[...].reshape(width, head_part)
        )
        raw_out[0, step] = raw[:rows]
        raw_out[1, step] = raw[rows:]
        allowed = (segment_col[step] == segment_row[step]) & (id_row[...] <= id_col[...])
        turned = []
        for head in range(heads + 1):
            gain = head_norms[min(head // heads, 1)][None, :]
            unnormed = lanes(raw, head)
            turned.append(
                low(
                    turn_pairs(
                        unnormed * inv_rms(unnormed) * gain, cos_out[step], sin_out[step]
                    )
                )
            )
        value = low(lanes(raw, heads + 1))
        outs = [
            low(matmul(low(softmax_of(turned[head], turned[heads], allowed)), value))
            for head in range(heads)
        ]
        kept = jnp.concatenate(turned + [value], axis=1)
        low_out[0, step] = kept[:rows]
        low_out[1, step] = kept[rows:]
        outs = jnp.concatenate(outs, axis=1)
        heads_stage[step, 0] = outs[:rows]
        heads_stage[step, 1] = outs[rows:]
        for index, at in enumerate((1, 2, 3)):
            pl.when(step == at)(heads_out.sends[index].start)
        pl.when(step == 0)(heads_out.copy.start)
        return carry

    lax.fori_loop(0, 1, bucket, 0)
    out_line.wait(1)
    out_line.wait(3)
    out_planes[1].start()
    out_planes[3].start()
    lax.fori_loop(1, 2, bucket, 0)
    out_planes[2].forward()
    for copy in upstream:
        copy.start()
    lax.fori_loop(2, 3, bucket, 0)
    out_planes[1].forward()
    out_planes[3].forward()
    lax.fori_loop(3, 4, bucket, 0)
    for copy in bucket_copies:
        copy.start()
    gate_line.wait(2)
    pl.when(place.z > 0)(to_down.start)
    pl.when(place.z < 3)(to_up.start)
    for plane in out_planes:
        plane.wait_far()
    for copy in own_copies:
        copy.wait()
    out_copy.start()
    heads_out.wait()

    def projected(core_step):
        block = jnp.concatenate([attended[p, core_step] for p in range(4)], axis=1)
        return matmul(block, out_all[...].reshape(block.shape[1], width))

    pair_stage[...] = low(projected(1))
    to_pair.start()
    hidden[...] = f32(input_ref[...]) + projected(0)
    to_pair.wait()
    norm_row = norm_ref[...]

    def norm_work(part):
        values = hidden[part] + f32(pair_got[part])
        hidden[part] = values
        normed[part] = low(values * inv_rms(values) * norm_row)

    each_rows(rows, 16, norm_work)
    gate_line.wait(1)
    gate_line.wait(3)
    for index, to in enumerate((place.x, place.y)):
        arrived(upstream_near.at[index], upstream_recv[index], to)
        upstream[index].wait_send()
    gate_copy.wait()
    second_copy.wait()
    for copy in [qkv_copy, out_copy] + bucket_copies + table_copies:
        copy.wait()
    parts = [lengths, qkv_pieces, gate_pieces, heads_out, qkv_line, gate_line, out_line]
    for part in parts + out_planes:
        part.finish()

    @pl.when(place.z < 3)
    def _():
        arrived(above_ref, near_recv[0], place.two)
        to_up.wait_send()

    @pl.when(place.z > 0)
    def _():
        arrived(below_ref, near_recv[1], place.two)
        to_down.wait_send()


def first_part(
    attn_norm,
    query_weight,
    key_matrix,
    value_matrix,
    gate_weight,
    up_weight,
    output_weight,
    down_weight,
    doc_lengths,
    row_ids,
    head_norms,
    layer_input,
    mlp_norm,
    grad_out,
):
    block_rows, width = layer_input.shape
    group_rows = 2 * block_rows
    weight_rows = query_weight.shape[0]
    head_part = (query_weight.shape[1] + key_matrix.shape[1] + value_matrix.shape[1]) // 4
    qkv_pieces = jax.ShapeDtypeStruct((4, weight_rows, head_part), LOW)
    gate_pieces = jax.ShapeDtypeStruct((4, weight_rows, gate_weight.shape[1] // 4), LOW)
    query_part = head_part - 2 * HEAD_SIZE
    documents = doc_lengths.shape[1]
    lengths = jnp.pad(doc_lengths, ((0, 7), (0, HEAD_SIZE - documents)))
    half = jnp.arange(HEAD_SIZE // 2, dtype=jnp.float32)
    inverse = ROPE_BASE ** (-(half * (2.0 / HEAD_SIZE)))
    low_like = lambda *shape: jax.ShapeDtypeStruct(shape, LOW)
    table = jax.ShapeDtypeStruct((4, group_rows, HEAD_SIZE), jnp.float32)
    return pl.pallas_call(
        lambda *refs: first_kernel(documents, *refs),
        out_shape=(
            low_like(8, block_rows, width),
            low_like(*gate_pieces.shape),
            low_like(*gate_pieces.shape),
            low_like(4, *gate_pieces.shape),
            low_like(*down_weight.shape),
            low_like(*down_weight.shape),
            low_like(2, block_rows, width),
            low_like(4, *qkv_pieces.shape),
            low_like(4, 4, *output_weight.shape),
            jax.ShapeDtypeStruct((2, 4, block_rows, head_part), jnp.float32),
            low_like(2, 4, block_rows, head_part),
            table,
            table,
            jax.ShapeDtypeStruct((4, group_rows, 1), jnp.int32),
            jax.ShapeDtypeStruct((4, 1, group_rows), jnp.int32),
            low_like(4, 2, block_rows, query_part),
            jax.ShapeDtypeStruct((block_rows, width), jnp.float32),
            low_like(block_rows, width),
        ),
        in_specs=[WHOLE] * 6 + [ANYWHERE] * 2 + [WHOLE] * 7 + [ANYWHERE],
        out_specs=(ANYWHERE,) * 13 + (WHOLE,) * 5,
        scratch_shapes=[
            pltpu.SemaphoreType.DMA((160,)),
            pltpu.VMEM((block_rows, width), LOW),
            pltpu.VMEM(qkv_pieces.shape, LOW),
            pltpu.VMEM((2,) + gate_pieces.shape, LOW),
            pltpu.VMEM((4,) + qkv_pieces.shape, LOW),
            pltpu.VMEM((4, 4) + output_weight.shape, LOW),
            pltpu.VMEM((2, 4, block_rows, head_part), jnp.float32),
            pltpu.VMEM((2, 4, block_rows, head_part), LOW),
            pltpu.VMEM(table.shape, jnp.float32),
            pltpu.VMEM(table.shape, jnp.float32),
            pltpu.VMEM((4,) + lengths.shape, jnp.int32),
            pltpu.VMEM((2, block_rows, width), LOW),
            pltpu.VMEM((4, 2, block_rows, query_part), LOW),
            pltpu.VMEM((block_rows, width), LOW),
            pltpu.VMEM((block_rows, width), LOW),
        ],
        compiler_params=comm_params(0),
        cost_estimate=comm_cost(130),
    )(
        attn_norm[None],
        query_weight,
        key_matrix,
        value_matrix,
        gate_weight,
        up_weight,
        output_weight,
        down_weight,
        lengths,
        row_ids[:, None],
        row_ids[None, :],
        jnp.concatenate([inverse, inverse])[None],
        head_norms,
        layer_input,
        mlp_norm[None],
        grad_out,
    )


class FarScatter:
    @staticmethod
    def scratch(rows, width):
        return [pltpu.VMEM((2, rows // 2, width), LOW)]

    def __init__(self, place, summed, buffers, marks):
        self.place, self.summed, self.landed = place, summed, buffers[0]
        self.half = summed.shape[1] // 2
        self.recv = [marks.take(), marks.take()]
        self.sends = [
            remote(
                summed.at[3, pl.ds(index * self.half, self.half)],
                self.landed.at[index],
                marks.take(),
                self.recv[index],
                to,
            )
            for index, to in enumerate((place.x, place.y))
        ]

    def start(self):
        for copy in self.sends:
            copy.start()

    def add(self):
        summed, landed = self.summed, self.landed
        for index, block, base, to in (
            (0, 2, 0, self.place.x),
            (1, 1, self.half, self.place.y),
        ):
            arrived(landed.at[index], self.recv[index], to)

            def work(rows):
                own_rows = pl.ds(pl.multiple_of(rows.start + base, 16), rows.size)
                summed[block, own_rows] = low(
                    f32(summed[block, own_rows]) + f32(landed[index, rows])
                )

            each_rows(self.half, 16, work)

    def drain(self):
        for copy in self.sends:
            copy.wait_send()


class NearScatter:
    @staticmethod
    def scratch(rows, width):
        return [pltpu.VMEM((3, rows, width), LOW)]

    def __init__(self, place, summed, buffers, marks):
        self.place, self.landed = place, buffers[0]
        self.load = pltpu.make_async_copy(summed.at[0], self.landed.at[2], marks.take())
        self.recv = [marks.take(), marks.take()]
        self.sends = [
            remote(summed.at[1 + index], self.landed.at[index], marks.take(), self.recv[index], to)
            for index, to in enumerate((place.x, place.y))
        ]

    def start(self):
        self.load.start()
        for copy in self.sends:
            copy.start()

    def finish(self, work):
        landed = self.landed
        self.load.wait()
        for index, to in enumerate((self.place.x, self.place.y)):
            arrived(self.landed.at[index], self.recv[index], to)

        def total(rows):
            work(
                rows,
                f32(landed[0, rows]) + f32(landed[1, rows]) + f32(landed[2, rows]),
            )

        each_rows(landed.shape[1], 16, total)

    def drain(self):
        for copy in self.sends:
            copy.wait_send()


class PlaneScatter:
    @staticmethod
    def scratch(rows, width):
        return [pltpu.VMEM((6, rows // 2, width), LOW)]

    def __init__(self, place, summed, out, buffers, marks, at=(0, 1, 2, 3)):
        self.place, self.summed, self.out, self.at = place, summed, out, at
        self.landed = buffers[0]
        self.rows = summed.shape[1]
        half = self.rows // 2
        top, end = pl.ds(0, half), pl.ds(half, half)
        x, y = place.x, place.y
        self.recv = [marks.take() for _ in range(6)]
        routes = (
            (summed.at[at[3], top], x),
            (summed.at[at[3], end], y),
            (summed.at[at[1], top], x),
            (summed.at[at[1], end], x),
            (summed.at[at[2], top], y),
            (summed.at[at[2], end], y),
        )
        self.sends = [
            remote(src, self.landed.at[index], marks.take(), self.recv[index], to)
            for index, (src, to) in enumerate(routes)
        ]

    def start(self):
        for index in (0, 1, 2, 5):
            self.sends[index].start()

    def landed_at(self, index, to):
        arrived(self.landed.at[index], self.recv[index], to)

    def middle(self):
        half = self.rows // 2
        summed, landed = self.summed, self.landed
        _, for_x, for_y, _ = self.at
        self.landed_at(0, self.place.x)

        def top_work(rows):
            summed[for_y, rows] = low(f32(summed[for_y, rows]) + f32(landed[0, rows]))

        each_rows(half, 16, top_work)
        self.sends[4].start()
        self.landed_at(1, self.place.y)

        def end_work(rows):
            end_rows = pl.ds(pl.multiple_of(rows.start + half, 16), rows.size)
            summed[for_x, end_rows] = low(f32(summed[for_x, end_rows]) + f32(landed[1, rows]))

        each_rows(half, 16, end_work)
        self.sends[3].start()

    def finish(self):
        half = self.rows // 2
        for index, to in ((2, self.place.x), (5, self.place.y), (4, self.place.y), (3, self.place.x)):
            self.landed_at(index, to)

        for base, first, second in ((0, 2, 4), (half, 3, 5)):

            def work(rows):
                own_rows = pl.ds(pl.multiple_of(rows.start + base, 16), rows.size)
                self.out[own_rows] = (
                    f32(self.summed[self.at[0], own_rows])
                    + f32(self.landed[first, rows])
                    + f32(self.landed[second, rows])
                ).astype(self.out.dtype)

            each_rows(half, 16, work)

    def drain(self):
        for copy in self.sends:
            copy.wait_send()


def blocks_of(source, block_ref, marks, first, last, work):
    def fetch(block):
        return pltpu.make_async_copy(
            source(block), block_ref.at[block % 2], marks.at[block % 2]
        )

    fetch(first).start()

    def body(block, carry):
        fetch(block).wait()

        @pl.when(block < last - 1)
        def _():
            fetch(block + 1).start()

        work(block, block_ref[block % 2])
        return carry

    lax.fori_loop(first, last, body, 0)


def unit_values(raws, inner_grad):
    units = inner_grad.shape[1]
    gate_raw, up_raw = raws[:, :units], raws[:, units:]
    sigmoid_gate = jax.nn.sigmoid(gate_raw)
    activated = gate_raw * sigmoid_gate
    gate_grad = inner_grad * up_raw * sigmoid_gate * (1.0 + gate_raw * (1.0 - sigmoid_gate))
    return low(activated * up_raw), jnp.concatenate(
        [low(gate_grad), low(inner_grad * activated)], axis=1
    )


def units_kernel(
    rows_ref,
    upstream_ref,
    near_ref,
    pieces_ref,
    first_ref,
    down_ref,
    above_ref,
    below_ref,
    rows_all,
    upstream_all,
    line_ref,
    inner_out,
    second_grad,
    first_sum,
    down_part,
    part_sums,
    grad_sums,
    marks_ref,
    first_mat,
    second_mat,
    down_mat,
    upstream,
    row_block,
    row_slab,
    inner_first,
    first_grad,
    inner_grads,
    first_part,
    inner_stage,
    second_stage,
    *buffers,
):
    place = Place()
    marks = Marks(marks_ref)
    greet(place, [place.x, place.y, place.d, place.pair], True)
    tokens = TokensGather(place, rows_ref, rows_all, marks)
    upstream_tokens = TokensGather(place, upstream_ref, upstream, marks)
    pieces = Exchange(
        place, lambda p, step: pieces_ref.at[p], lambda p, step: line_ref.at[p], marks
    )
    keep = pltpu.make_async_copy(upstream, upstream_all, marks.take())
    line = LineGather(place, line_ref, lambda z: second_mat.at[z], marks.take(4), marks.take(4))
    far_recv = marks.take(2)
    two = down_mat.at[:, place.at(2)]
    to_two = remote(down_ref, down_mat.at[:, place.z], marks.take(), far_recv.at[0], place.two)
    pass_mark = marks.take()
    pass_down = remote(two, two, pass_mark, far_recv.at[1], place.down)
    pass_up = remote(two, two, pass_mark, far_recv.at[1], place.up)
    copies = [
        pltpu.make_async_copy(first_ref, first_mat, marks.take()),
        pltpu.make_async_copy(down_ref, down_mat.at[:, place.z], marks.take()),
    ]
    line_copy = pltpu.make_async_copy(line_ref, second_mat.at[place.z], marks.take())
    above = pltpu.make_async_copy(above_ref, down_mat.at[:, place.at(1)], marks.take())
    below = pltpu.make_async_copy(below_ref, down_mat.at[:, place.at(3)], marks.take())
    line_rows = first_sum.shape[0]
    first_line = LineScatter(
        place,
        lambda z: first_part.at[pl.ds(pl.multiple_of(z * line_rows, 16), line_rows)],
        first_sum,
        buffers[:1],
        marks,
        True,
    )
    part_far = FarScatter(place, part_sums, buffers[1:2], marks)
    grad_far = FarScatter(place, grad_sums, buffers[2:], marks)
    fetch_marks, slab_marks = marks.take(2), marks.take(2)
    send_marks, recv_marks = marks.take(8), marks.take(8)
    width = rows_ref.shape[1]
    half = inner_first.shape[2]
    all_rows = 8 * rows_ref.shape[0]

    to_two.start()
    pieces.start()
    tokens.start()
    for copy in copies:
        copy.start()
    pl.when(place.z < 3)(above.start)
    pl.when(place.z > 0)(below.start)
    tokens.forward()
    upstream_tokens.start_near(near_ref, marks)
    pieces.wait()
    line_copy.start()
    arrived(two, far_recv.at[0], place.two)
    pl.when(place.z == 1)(pass_down.start)
    pl.when(place.z == 2)(pass_up.start)
    line.start()
    tokens.last()
    upstream_tokens.last()
    for copy in copies:
        copy.wait()
    line_copy.wait()
    pl.when(place.z < 3)(above.wait)
    pl.when(place.z > 0)(below.wait)

    @pl.when(place.z == 0)
    def _():
        arrived(down_mat.at[:, 3], far_recv.at[1], place.two)

    @pl.when(place.z == 3)
    def _():
        arrived(down_mat.at[:, 0], far_recv.at[1], place.two)

    tokens.finish()
    upstream_tokens.finish_near()
    keep.start()
    pieces.finish()

    def first_work(block, values):
        grads = matmul_nt(upstream[block], down_mat[...].reshape(2 * half, width))
        inner_grads[block] = low(grads[:, half:])
        inner, grad = unit_values(matmul(values, first_mat[...]), grads[:, :half])
        inner_first[block] = inner
        first_grad[block] = grad

    blocks_of(lambda block: rows_all.at[block], row_block, fetch_marks, 0, 8, first_work)
    line.wait(2)
    tile = row_slab.shape[3]
    tiles = width // tile

    def slab(index):
        return rows_all.at[:, :, pl.ds(pl.multiple_of(index * tile, tile), tile)]

    def slab_work(index, values):
        first_part[pl.ds(pl.multiple_of(index * tile, tile), tile)] = low(
            matmul_tn(values.reshape(all_rows, tile), first_grad[...].reshape(all_rows, 2 * half))
        )

    down_part[...] = low(
        matmul_tn(
            inner_first[...].reshape(all_rows, half), upstream[...].reshape(all_rows, width)
        )
    )
    blocks_of(slab, row_slab, slab_marks, 0, tiles, slab_work)
    line.wait(1)
    line.wait(3)
    first_line.start()

    def fetch(index):
        step, slot = 3 - index // 2, index % 2
        return pltpu.make_async_copy(
            rows_all.at[step + 4 * (1 - slot)], row_block.at[slot], fetch_marks.at[slot]
        )

    def sends(step):
        return (
            remote(
                upstream.at[step],
                part_sums.at[step],
                send_marks.at[step],
                recv_marks.at[step],
                place.pair,
            ),
            remote(
                upstream.at[4 + step],
                grad_sums.at[step],
                send_marks.at[4 + step],
                recv_marks.at[4 + step],
                place.pair,
            ),
        )

    keep.wait()
    store_marks = marks.take(4)

    def stores(slot, block):
        return (
            pltpu.make_async_copy(
                inner_stage.at[slot], inner_out.at[block], store_marks.at[slot]
            ),
            pltpu.make_async_copy(
                second_stage.at[slot], second_grad.at[block], store_marks.at[2 + slot]
            ),
        )

    fetch(0).start()

    def blocks(turn, carry):
        step = 3 - turn
        for slot in range(2):
            index = 2 * turn + slot
            block = step + 4 * (1 - slot)
            fetch(index).wait()

            @pl.when(index < 7)
            def _():
                fetch(index + 1).start()

            second = second_mat[...].reshape(width, 2 * half)
            inner, grad = unit_values(matmul(row_block[slot], second), f32(inner_grads[block]))

            @pl.when(turn > 0)
            def _():
                for copy in stores(slot, block + 1):
                    copy.wait()

            inner_stage[slot] = inner
            second_stage[slot] = grad
            for copy in stores(slot, block):
                copy.start()
            part = matmul(
                jnp.concatenate([inner_first[block], inner], axis=1),
                down_mat[...].reshape(2 * half, width),
            )
            grad = matmul_nt(first_grad[block], first_mat[...]) + matmul_nt(grad, second)
            if slot == 0:
                upstream[step] = low(part)
                upstream[4 + step] = low(grad)
                for copy in sends(step):
                    copy.start()
            else:
                for copy in sends(step):
                    copy.wait_recv()
                part_sums[step] = low(part + f32(part_sums[step]))
                grad_sums[step] = low(grad + f32(grad_sums[step]))
        return carry

    lax.fori_loop(0, 1, blocks, 0)
    grad_far.start()
    part_far.start()
    lax.fori_loop(1, 2, blocks, 0)
    first_line.middle()
    lax.fori_loop(2, 4, blocks, 0)
    for slot in range(2):
        for copy in stores(slot, 4 * (1 - slot)):
            copy.wait()
    grad_far.add()
    part_far.add()
    first_line.finish()
    first_line.drain()
    grad_far.drain()
    part_far.drain()
    for step in range(4):
        for copy in sends(step):
            copy.wait_send()
    line.finish()
    to_two.wait_send()
    pl.when(place.z == 1)(pass_down.wait_send)
    pl.when(place.z == 2)(pass_up.wait_send)


def units_products(rows, upstream, near, second_pieces, first_all, down_weight, above, below):
    block_rows, width = rows.shape
    half = first_all.shape[1] // 2
    half_rows = down_weight.shape[1]
    second_rows = jax.ShapeDtypeStruct((4 * second_pieces.shape[1], 2 * half), LOW)
    hidden = lambda count: jax.ShapeDtypeStruct((8, block_rows, count * half), LOW)
    sums = jax.ShapeDtypeStruct((4, block_rows, width), LOW)
    blocks = jax.ShapeDtypeStruct((8, block_rows, width), LOW)
    return pl.pallas_call(
        units_kernel,
        out_shape=(
            blocks,
            blocks,
            jax.ShapeDtypeStruct(second_pieces.shape, LOW),
            hidden(1),
            hidden(2),
            jax.ShapeDtypeStruct(second_rows.shape, LOW),
            jax.ShapeDtypeStruct((half, width), LOW),
            sums,
            sums,
        ),
        in_specs=[ANYWHERE] * 8,
        out_specs=(ANYWHERE,) * 5 + (WHOLE,) * 4,
        scratch_shapes=[
            pltpu.SemaphoreType.DMA((140,)),
            pltpu.VMEM(first_all.shape, LOW),
            pltpu.VMEM((4,) + second_pieces.shape, LOW),
            pltpu.VMEM((2, 4, half_rows, width), LOW),
            pltpu.VMEM((8, block_rows, width), LOW),
            pltpu.VMEM((2, block_rows, width), LOW),
            pltpu.VMEM((2, 8, block_rows, 256), LOW),
            pltpu.VMEM((8, block_rows, half), LOW),
            pltpu.VMEM((8, block_rows, 2 * half), LOW),
            pltpu.VMEM((8, block_rows, half), LOW),
            pltpu.VMEM((width, 2 * half), LOW),
            pltpu.VMEM((2, block_rows, half), LOW),
            pltpu.VMEM((2, block_rows, 2 * half), LOW),
        ]
        + LineScatter.scratch(*second_rows.shape, True)
        + FarScatter.scratch(block_rows, width) * 2,
        compiler_params=comm_params(1),
        cost_estimate=comm_cost(150),
    )(rows, upstream, near, second_pieces, first_all, down_weight, above, below)


def unit_grads_kernel(
    rows_all,
    upstream_ref,
    inner_ref,
    second_ref,
    down_first,
    part_sums,
    grad_sums,
    hidden_ref,
    upstream_own,
    norm_ref,
    layer_out,
    hidden_grad,
    branch,
    mlp_gain,
    down_out,
    second_part,
    marks_ref,
    upstream,
    inner,
    second_grad,
    row_slab,
    gain_rows,
    down_part,
    *buffers,
):
    place = Place()
    marks = Marks(marks_ref)
    greet(place, [place.x, place.y], True)
    grad_near = NearScatter(place, grad_sums, buffers[:1], marks)
    part_near = NearScatter(place, part_sums, buffers[1:2], marks)
    half_rows = down_out.shape[1]
    first_line = LineScatter(
        place, lambda z: down_first.at[z], down_out.at[0], buffers[2:3], marks
    )
    second_line = LineScatter(
        place,
        lambda z: down_part.at[pl.ds(pl.multiple_of(z * half_rows, 16), half_rows)],
        down_out.at[1],
        buffers[3:],
        marks,
        True,
    )
    loads = [
        pltpu.make_async_copy(upstream_ref, upstream, marks.take()),
        pltpu.make_async_copy(inner_ref, inner, marks.take()),
        pltpu.make_async_copy(second_ref, second_grad, marks.take()),
    ]
    slab_marks = marks.take(2)
    rows, width = hidden_ref.shape
    half = inner.shape[2]
    all_rows = 8 * rows
    tile = row_slab.shape[3]
    tiles = width // tile

    def slab(index):
        return rows_all.at[:, :, pl.ds(pl.multiple_of(index * tile, tile), tile)]

    def slab_work(index, values):
        second_part[pl.ds(pl.multiple_of(index * tile, tile), tile)] = low(
            matmul_tn(values.reshape(all_rows, tile), second_grad[...].reshape(all_rows, 2 * half))
        )

    first_line.start()
    grad_near.start()
    for copy in loads:
        copy.start()
    loads[0].wait()
    loads[1].wait()
    down_part[...] = low(
        matmul_tn(inner[...].reshape(all_rows, half), upstream[...].reshape(all_rows, width))
    )
    loads[2].wait()
    blocks_of(slab, row_slab, slab_marks, 0, tiles // 2, slab_work)
    first_line.middle()
    second_line.start()
    blocks_of(slab, row_slab, slab_marks, tiles // 2, tiles, slab_work)
    second_line.middle()
    part_near.start()
    gain_rows[...] = jnp.zeros_like(gain_rows)
    norm_row = norm_ref[...]

    def norm_work(rows, row_grad):
        values = hidden_ref[rows]
        scales = inv_rms(values)
        weighted = row_grad * norm_row
        inner_mean = jnp.mean(weighted * values, axis=-1, keepdims=True)
        grad = (
            f32(upstream_own[rows])
            + scales * weighted
            - values * (scales * scales * scales) * inner_mean
        )
        hidden_grad[rows] = grad
        branch[rows] = low(grad)
        parts = row_grad * values * scales
        gain_rows[...] += parts[:8] + parts[8:]

    def out_work(rows, row_part):
        layer_out[rows] = low(hidden_ref[rows] + row_part)

    grad_near.finish(norm_work)
    mlp_gain[...] = jnp.sum(gain_rows[...], axis=0, keepdims=True)
    part_near.finish(out_work)
    first_line.finish()
    second_line.finish()
    for part in (first_line, second_line, grad_near, part_near):
        part.drain()


def unit_grads(
    rows_all,
    upstream,
    inner,
    second_grad,
    down_first,
    part_sums,
    grad_sums,
    hidden,
    upstream_own,
    norm,
):
    _, rows, width = rows_all.shape
    half = inner.shape[2]
    half_rows = down_first.shape[1]
    return pl.pallas_call(
        unit_grads_kernel,
        out_shape=(
            jax.ShapeDtypeStruct((rows, width), LOW),
            jax.ShapeDtypeStruct((rows, width), jnp.float32),
            jax.ShapeDtypeStruct((rows, width), LOW),
            jax.ShapeDtypeStruct((1, width), jnp.float32),
            jax.ShapeDtypeStruct((2, half_rows, width), jnp.float32),
            jax.ShapeDtypeStruct((width, 2 * half), LOW),
        ),
        in_specs=[ANYWHERE] * 7 + [WHOLE] * 3,
        out_specs=(WHOLE,) * 6,
        scratch_shapes=[
            pltpu.SemaphoreType.DMA((64,)),
            pltpu.VMEM(upstream.shape, LOW),
            pltpu.VMEM(inner.shape, LOW),
            pltpu.VMEM(second_grad.shape, LOW),
            pltpu.VMEM((2, 8, rows, 256), LOW),
            pltpu.VMEM((8, width), jnp.float32),
            pltpu.VMEM((half, width), LOW),
        ]
        + NearScatter.scratch(rows, width) * 2
        + LineScatter.scratch(half_rows, width)
        + LineScatter.scratch(half_rows, width, True),
        compiler_params=comm_params(4),
        cost_estimate=comm_cost(65),
    )(
        rows_all,
        upstream,
        inner,
        second_grad,
        down_first,
        part_sums,
        grad_sums,
        hidden,
        upstream_own,
        norm,
    )


def turn_pairs(values, cosine, sine):
    return values * cosine + pltpu.roll(values, HEAD_SIZE // 2, 1) * sine


def softmax_of(query, key, allowed):
    scores = matmul_nt(query, key) * HEAD_SIZE ** (-0.5)
    masked = jnp.where(allowed, scores, MASKED)
    exponent = jnp.exp(masked - jnp.max(masked, axis=-1, keepdims=True))
    return exponent / jnp.sum(exponent, axis=-1, keepdims=True)


def lanes(values, head):
    return values[:, head * HEAD_SIZE : (head + 1) * HEAD_SIZE]


def roll_half(values):
    return pltpu.roll(values, HEAD_SIZE // 2, 1)


def attend_back_values(raw, kept, grad, allowed, cosine, sine, gains_ref, roll=roll_half):
    group_rows = raw.shape[0]
    heads = raw.shape[1] // HEAD_SIZE - 2
    key, value = lanes(kept, heads), lanes(kept, heads + 1)
    scale = HEAD_SIZE ** (-0.5)
    turned_grads = []
    key_grad = jnp.zeros((group_rows, HEAD_SIZE), jnp.float32)
    value_grad = jnp.zeros((group_rows, HEAD_SIZE), jnp.float32)
    for head in range(heads):
        query, upstream = lanes(kept, head), lanes(grad, head)
        probs = softmax_of(query, key, allowed)
        probs_grad = matmul_nt(upstream, value)
        scores_grad = low(
            probs * (probs_grad - jnp.sum(probs * probs_grad, axis=-1, keepdims=True))
        )
        turned_grads.append(matmul(scores_grad, key) * scale)
        key_grad = key_grad + matmul_tn(scores_grad, query)
        value_grad = value_grad + matmul_tn(low(probs), upstream)
    turned_grads.append(key_grad * scale)
    outs, gains = [], []
    for head in range(heads + 1):
        gain = gains_ref[min(head // heads, 1)][None, :]
        unnormed = lanes(raw, head)
        upstream = turned_grads[head] * cosine - roll(turned_grads[head]) * sine
        grad_raw, gain_part = norm_back(unnormed, inv_rms(unnormed), gain, upstream)
        outs.append(low(grad_raw))
        gains.append(gain_part[None, :])
    outs.append(low(value_grad))
    query_gain = sum(gains[1:heads], gains[0])
    return (jnp.concatenate(outs, axis=1), jnp.concatenate([query_gain, gains[heads]], axis=1))


def heads_back_kernel(
    branch_ref,
    out_ref,
    attended_ref,
    raw_ref,
    low_ref,
    cos_ref,
    sin_ref,
    segment_col,
    segment_row,
    id_col,
    id_row,
    gains_ref,
    rows_all,
    qkv_ref,
    second_part,
    first_rows,
    input_ref,
    hidden_ref,
    norm_ref,
    mlp_gain,
    grad_ref,
    query_out,
    key_out,
    value_out,
    proj_out,
    gate_out,
    up_out,
    attn_gain_out,
    mlp_gain_out,
    head_gain_out,
    marks_ref,
    qkv_columns,
    first_columns,
    second_columns,
    joined_stage,
    qkv_part,
    proj_sum,
    grad_sums,
    line_sum,
    qkv_sum,
    gain_rows,
    gain_mine,
    gain_got,
    out_mat,
    qkv_mat,
    attended,
    branch,
    own_grad,
    heads_grad,
    raw_block,
    low_block,
    qkv_grad,
    row_slab,
    proj_part,
    *buffers,
):
    place = Place()
    marks = Marks(marks_ref)
    greet(place, [place.x, place.y, place.d, place.pair], True)
    rows, width = branch_ref.shape
    half_heads = heads_grad.shape[2]
    group_rows = 2 * rows
    second_line = LineScatter(place, lambda z: second_part.at[z], line_sum, buffers[0:1], marks)
    first_pieces = Exchange(
        place, lambda p, step: first_rows.at[p], lambda p, step: first_columns.at[p], marks
    )
    proj_plane = PlaneScatter(
        place,
        proj_part,
        proj_sum,
        buffers[1:2],
        marks,
        (place.p, place.px, place.py, place.pd),
    )
    tokens = PlaneScatter(place, grad_sums, grad_ref, buffers[2:3], marks)
    qkv_rows, proj_rows = qkv_sum.shape[0], proj_out.shape[0]
    qkv_line = LineScatter(
        place,
        lambda z: qkv_part.at[pl.ds(pl.multiple_of(z * qkv_rows, 16), qkv_rows)],
        qkv_sum,
        buffers[3:4],
        marks,
        True,
    )
    proj_line = LineScatter(
        place,
        lambda z: proj_sum.at[pl.ds(pl.multiple_of(z * proj_rows, 16), proj_rows)],
        proj_out,
        buffers[4:],
        marks,
        True,
    )
    piece_rows, second_piece = qkv_rows // 4, line_sum.shape[0] // 4
    qkv_pieces = Exchange(
        place,
        lambda p, step: qkv_sum.at[pl.ds(pl.multiple_of(p * piece_rows, 16), piece_rows)],
        lambda p, step: qkv_columns.at[p],
        marks,
    )
    second_pieces = Exchange(
        place,
        lambda p, step: line_sum.at[pl.ds(pl.multiple_of(p * second_piece, 16), second_piece)],
        lambda p, step: second_columns.at[p],
        marks,
    )
    near_z = {"f": place.z + 1 - 2 * (place.z % 2)}
    rounds = [
        remote(gain_mine.at[index], gain_got.at[index], marks.take(), marks.take(), to)
        for index, to in enumerate((place.pair, place.x, place.y, near_z, place.two))
    ]
    heads = Exchange(
        place, lambda p, step: own_grad.at[p], lambda p, step: heads_grad.at[step], marks
    )
    to_pair = remote(branch_ref, branch.at[1], marks.take(), marks.take(), place.pair)
    loads = [
        pltpu.make_async_copy(branch_ref, branch.at[0], marks.take()),
        pltpu.make_async_copy(out_ref, out_mat, marks.take()),
        pltpu.make_async_copy(attended_ref, attended, marks.take()),
        pltpu.make_async_copy(qkv_ref, qkv_mat, marks.take()),
    ]
    fetch_marks, slab_marks = marks.take(4), marks.take(2)
    send_marks, recv_marks = marks.take(4), marks.take(4)

    to_pair.start()
    second_line.start()
    for copy in loads:
        copy.start()
    for copy in loads:
        copy.wait()

    def own_half(core_step):
        grad = low(matmul_nt(branch[core_step], out_mat[...]))
        for p in range(4):
            own_grad[p, pl.ds(core_step * rows, rows)] = grad[
                :, p * half_heads : (p + 1) * half_heads
            ]

    own_half(0)
    to_pair.wait()
    own_half(1)
    heads.start()
    second_line.middle()

    def proj_work(z, carry):
        block = attended[z].reshape(group_rows, half_heads)
        grad = low(matmul_tn(block, branch[...].reshape(group_rows, width)))
        part = half_heads // 4
        for p in range(4):
            proj_part[p, pl.ds(pl.multiple_of(z * part, part), part)] = grad[
                p * part : (p + 1) * part
            ]
        return carry

    def fetches(step):
        return (
            pltpu.make_async_copy(raw_ref.at[:, step], raw_block, fetch_marks.at[0]),
            pltpu.make_async_copy(low_ref.at[:, step], low_block, fetch_marks.at[1]),
        )

    lax.fori_loop(0, 4, proj_work, 0)
    heads.wait()
    proj_plane.start()
    first_pieces.start()
    head_width = 2 * HEAD_SIZE
    head_gain = gain_mine.at[0, :, pl.ds(2 * width, head_width)]
    head_gain[...] = jnp.zeros((1, head_width), jnp.float32)

    def sends(step):
        return remote(
            out_mat.at[pl.ds(pl.multiple_of(step * rows, rows), rows)],
            grad_sums.at[step],
            send_marks.at[step],
            recv_marks.at[step],
            place.pair,
        )

    def bucket(step, carry):
        for copy in fetches(step):
            copy.start()
        for copy in fetches(step):
            copy.wait()
        allowed = (segment_col[step] == segment_row[step]) & (id_row[...] <= id_col[...])
        grads, gains = attend_back_values(
            raw_block[...].reshape(group_rows, -1),
            low_block[...].reshape(group_rows, -1),
            heads_grad[step],
            allowed,
            cos_ref[step],
            sin_ref[step],
            gains_ref,
        )
        head_gain[...] += gains
        qkv_grad[0, step] = grads[:rows]
        qkv_grad[1, step] = grads[rows:]
        out_mat[pl.ds(pl.multiple_of(step * rows, rows), rows)] = low(
            matmul_nt(grads[rows:], qkv_mat[...])
        )
        sends(step).start()
        return carry

    lax.fori_loop(0, 2, bucket, 0)
    proj_plane.middle()
    lax.fori_loop(2, 4, bucket, 0)

    tile = row_slab.shape[3]
    tiles = width // tile

    def slab(index):
        return pltpu.make_async_copy(
            rows_all.at[:, :, pl.ds(pl.multiple_of(index * tile, tile), tile)],
            row_slab.at[index % 2],
            slab_marks.at[index % 2],
        )

    slab(0).start()

    def own_work(step, carry):
        copy = sends(step)
        copy.wait_recv()
        grad = matmul_nt(qkv_grad[0, step], qkv_mat[...])
        grad_sums[step] = low(grad + f32(grad_sums[step]))
        return carry

    lax.fori_loop(0, 4, own_work, 0)
    tokens.start()

    def row_tile(index, carry):
        slab(index).wait()

        @pl.when(index < tiles - 1)
        def _():
            slab(index + 1).start()

        block = row_slab[index % 2].reshape(4 * group_rows, tile)
        out_rows = pl.ds(pl.multiple_of(index * tile, tile), tile)
        qkv_part[out_rows] = low(
            matmul_tn(block, qkv_grad[...].reshape(4 * group_rows, qkv_grad.shape[3]))
        )
        return carry

    lax.fori_loop(0, tiles, row_tile, 0)
    second_line.finish()
    qkv_line.start()
    proj_plane.finish()
    tokens.middle()
    second_pieces.start()
    qkv_line.middle()
    proj_line.start()
    tokens.finish()
    proj_line.middle()

    gain_rows[...] = jnp.zeros_like(gain_rows)
    norm_row = norm_ref[...]

    def norm_work(part):
        values = f32(input_ref[part])
        scales = inv_rms(values)
        upstream = grad_ref[part]
        weighted = upstream * norm_row
        inner_mean = jnp.mean(weighted * values, axis=-1, keepdims=True)
        grad_ref[part] = (
            hidden_ref[part]
            + scales * weighted
            - values * (scales * scales * scales) * inner_mean
        )
        parts = upstream * values * scales
        gain_rows[...] += parts[:8] + parts[8:]

    each_rows(rows, 16, norm_work)
    gain_mine[0, :, pl.ds(0, width)] = jnp.sum(gain_rows[...], axis=0, keepdims=True)
    gain_mine[0, :, pl.ds(width, width)] = mlp_gain[...]
    for index, copy in enumerate(rounds):
        copy.start()
        copy.wait()
        summed = gain_mine[index] + gain_got[index]
        if index < 4:
            gain_mine[index + 1] = summed
        else:
            attn_gain_out[...] = summed[:, :width]
            mlp_gain_out[...] = summed[:, width : 2 * width]
            head_gain_out[...] = summed[:, 2 * width :]
    qkv_line.finish()
    qkv_pieces.start()
    proj_line.finish()
    for step in range(4):
        sends(step).wait_send()
    heads.finish()
    for part in (proj_plane, second_line, qkv_line, proj_line, tokens):
        part.drain()
    for part in (first_pieces, second_pieces):
        part.wait()
        part.finish()
    units_joined(
        (first_columns, second_columns), (gate_out, up_out), joined_stage, marks.take(2)
    )
    qkv_pieces.wait()
    qkv_pieces.finish()
    for p in range(4):
        start = 0
        for out in (query_out, key_out, value_out):
            part = out.shape[1] // 4
            out[:, p * part : (p + 1) * part] = f32(qkv_columns[p][:, start : start + part])
            start += part


def heads_backward(
    branch,
    out_all,
    attended,
    raw,
    kept,
    tables,
    rows_all,
    qkv_all,
    second_part,
    first_rows,
    layer_input,
    hidden_grad,
    norm,
    mlp_gain,
):
    rows, width = branch.shape
    head_part = raw.shape[3]
    query_part = head_part - 2 * HEAD_SIZE
    line_rows, units = second_part.shape[1:]
    qkv_rows = width // 4
    tile = 256
    gain_width = 2 * width + 2 * HEAD_SIZE
    weight_rows = line_rows // 4
    pieces = pltpu.VMEM((4, weight_rows, units), LOW)
    wide = lambda *shape: jax.ShapeDtypeStruct(shape, jnp.float32)
    return pl.pallas_call(
        heads_back_kernel,
        out_shape=(
            wide(rows, width),
            wide(weight_rows, 4 * query_part),
            wide(weight_rows, 4 * HEAD_SIZE),
            wide(weight_rows, 4 * HEAD_SIZE),
            wide(query_part // 4, width),
            wide(weight_rows, 4 * units),
            wide(weight_rows, 4 * units),
            wide(1, width),
            wide(1, width),
            wide(1, 2 * HEAD_SIZE),
        ),
        in_specs=[ANYWHERE] * 5
        + [WHOLE] * len(tables)
        + [ANYWHERE] * 4
        + [WHOLE] * 4,
        out_specs=(WHOLE,) * 5 + (ANYWHERE,) * 2 + (WHOLE,) * 3,
        scratch_shapes=[
            pltpu.SemaphoreType.DMA((160,)),
            pltpu.VMEM((4, weight_rows, head_part), LOW),
            pieces,
            pieces,
            pltpu.VMEM((2, weight_rows, units), jnp.float32),
            pltpu.VMEM((width, head_part), LOW),
            pltpu.VMEM((query_part, width), LOW),
            pltpu.VMEM((4, rows, width), LOW),
            pltpu.VMEM((line_rows, units), LOW),
            pltpu.VMEM((qkv_rows, head_part), LOW),
            pltpu.VMEM((8, width), jnp.float32),
            pltpu.VMEM((5, 1, gain_width), jnp.float32),
            pltpu.VMEM((5, 1, gain_width), jnp.float32),
            pltpu.VMEM(out_all.shape, LOW),
            pltpu.VMEM(qkv_all.shape, LOW),
            pltpu.VMEM(attended.shape, LOW),
            pltpu.VMEM((2, rows, width), LOW),
            pltpu.VMEM((4, 2 * rows, query_part), LOW),
            pltpu.VMEM((4, 2 * rows, query_part), LOW),
            pltpu.VMEM((2, rows, head_part), jnp.float32),
            pltpu.VMEM((2, rows, head_part), LOW),
            pltpu.VMEM((2, 4, rows, head_part), LOW),
            pltpu.VMEM((2, 8, rows, tile), LOW),
            pltpu.VMEM((4, query_part, width), LOW),
        ]
        + LineScatter.scratch(line_rows, units)
        + PlaneScatter.scratch(query_part, width)
        + PlaneScatter.scratch(rows, width)
        + LineScatter.scratch(qkv_rows, head_part, True)
        + LineScatter.scratch(query_part // 4, width, True),
        compiler_params=comm_params(3),
        cost_estimate=comm_cost(120),
    )(
        branch,
        out_all,
        attended,
        raw,
        kept,
        *tables,
        rows_all,
        qkv_all,
        second_part,
        first_rows,
        layer_input,
        hidden_grad,
        norm,
        mlp_gain,
    )


def row_ids_of(local_rows):
    core = lax.axis_index("tensor")
    local_ids = jnp.arange(local_rows, dtype=jnp.int32)
    return jnp.concatenate([core * local_rows + local_ids, (1 - core) * local_rows + local_ids])


def heads_of(weight):
    return weight.reshape(weight.shape[0], 4, -1).transpose(1, 0, 2)


def heads_back(pieces):
    return f32(pieces).transpose(1, 0, 2).reshape(pieces.shape[1], -1)


def units_of(weight, down_rows):
    split = weight.reshape(weight.shape[0], -1, 4, down_rows)
    return split.transpose(2, 0, 1, 3).reshape(4, weight.shape[0], -1)


def units_back(pieces, down_rows):
    rows = pieces.shape[1]
    return f32(pieces).reshape(4, rows, -1, down_rows).transpose(1, 2, 0, 3).reshape(rows, -1)


def shards(*arguments):
    if lax.axis_size("f") == 4:
        return line_of_four(*arguments)
    return any_line(*arguments)


def line_of_four(
    layer_input,
    attn_norm,
    head_norms,
    query_weight,
    key_matrix,
    value_matrix,
    output_weight,
    mlp_norm,
    gate_weight,
    up_weight,
    down_weight,
    grad_out,
    doc_lengths,
):
    local_rows, model_width = layer_input.shape
    weight_rows = gate_weight.shape[0]
    down_rows = down_weight.shape[0]
    half_rows = down_rows // 2
    half = 4 * half_rows
    head_part = (query_weight.shape[1] + key_matrix.shape[1] + value_matrix.shape[1]) // 4
    down_halves = down_weight.reshape(2, half_rows, model_width)
    row_ids = row_ids_of(local_rows)
    (
        normed_attn,
        second_pieces,
        _,
        first_all,
        above,
        below,
        grad_near,
        qkv_all,
        out_all,
        qkv_raw,
        qkv_low,
        cos_tab,
        sin_tab,
        segment_col,
        segment_row,
        attended,
        hidden_state,
        normed_mlp,
    ) = first_part(
        attn_norm,
        query_weight,
        key_matrix,
        value_matrix,
        gate_weight,
        up_weight,
        output_weight,
        down_halves,
        doc_lengths,
        row_ids,
        head_norms,
        layer_input,
        mlp_norm,
        grad_out,
    )
    tables = (
        cos_tab,
        sin_tab,
        segment_col,
        segment_row,
        row_ids[:, None],
        row_ids[None, :],
        head_norms,
    )
    (
        rows_all,
        grad_all,
        _,
        inner_low,
        second_grad,
        first_rows,
        grad_down_first,
        part_sums,
        grad_sums,
    ) = (
        units_products(
            normed_mlp,
            grad_out,
            grad_near,
            second_pieces,
            first_all.reshape(model_width, 2 * half),
            down_halves,
            above,
            below,
        )
    )
    line_shape = (4, 4 * weight_rows, 2 * half)
    (
        layer_out,
        hidden_grad,
        branch_grad,
        mlp_gain_part,
        grad_down,
        grad_second,
    ) = unit_grads(
        rows_all,
        grad_all,
        inner_low,
        second_grad,
        grad_down_first.reshape(4, half_rows, model_width),
        part_sums,
        grad_sums,
        hidden_state,
        grad_out,
        mlp_norm[None],
    )
    (
        grad_input,
        grad_query,
        grad_key,
        grad_value,
        grad_out_proj,
        grad_gate,
        grad_up,
        attn_gain,
        mlp_gain,
        head_gains,
    ) = (
        heads_backward(
            branch_grad,
            out_all.reshape(-1, model_width),
            attended,
            qkv_raw,
            qkv_low,
            tables,
            normed_attn,
            qkv_all.reshape(model_width, head_part),
            grad_second.reshape(line_shape),
            first_rows.reshape(4, weight_rows, 2 * half),
            layer_input,
            hidden_grad,
            attn_norm[None],
            mlp_gain_part,
        )
    )
    return (
        layer_out,
        grad_input,
        attn_gain.reshape(-1),
        head_gains.reshape(2, HEAD_SIZE),
        grad_query,
        grad_key,
        grad_value,
        grad_out_proj,
        mlp_gain.reshape(-1),
        grad_gate,
        grad_up,
        grad_down.reshape(down_weight.shape),
    )


def any_line(
    layer_input,
    attn_norm,
    head_norms,
    query_weight,
    key_matrix,
    value_matrix,
    output_weight,
    mlp_norm,
    gate_weight,
    up_weight,
    down_weight,
    grad_out,
    doc_lengths,
):
    line_extent = lax.axis_size("f")
    local_rows, model_width = layer_input.shape
    group_rows = 2 * local_rows
    all_rows = 8 * local_rows
    weight_rows = gate_weight.shape[0]
    down_rows = down_weight.shape[0]
    hidden_part = line_extent * down_rows
    qkv_pieces = jnp.concatenate(
        [heads_of(query_weight), heads_of(key_matrix), heads_of(value_matrix)], axis=2
    )
    head_part = qkv_pieces.shape[2]
    query_part = head_part - 2 * HEAD_SIZE
    heads = head_part // HEAD_SIZE - 2

    def exchanged(pieces):
        return natural_plane(plane_exchange(own_plane(pieces, 0)), 0)

    def line_rows(pieces):
        return line_gather(exchanged(pieces)).reshape(model_width, -1)

    def line_sums(partial):
        parts = low(partial).reshape(line_extent, 4 * weight_rows, -1)
        return exchanged(low(line_scatter(parts)).reshape(4, weight_rows, -1))

    qkv_all = line_rows(qkv_pieces)
    out_all = full_gather(output_weight)
    gate_all = line_rows(units_of(gate_weight, down_rows))
    up_all = line_rows(units_of(up_weight, down_rows))
    down_all = line_gather(down_weight).reshape(hidden_part, model_width)

    input_float = f32(layer_input)
    scale_attn = inv_rms(input_float)
    normed_attn = tokens_gather(low(input_float * scale_attn * attn_norm))
    row_ids = row_ids_of(local_rows)
    segments, positions = jax.vmap(lambda lengths: doc_layout(lengths, row_ids))(
        plane_lengths(doc_lengths)
    )
    qkv_raw = matmul(normed_attn, qkv_all).reshape(2, 4, local_rows, head_part)
    roll = lambda values: jnp.roll(values, HEAD_SIZE // 2, 1)
    buckets, attended_parts = [], []
    for step in range(4):
        cos_tab, sin_tab = rope_tables(positions[step], HEAD_SIZE)
        cosine = jnp.concatenate([cos_tab, cos_tab], axis=1)
        sine = jnp.concatenate([-sin_tab, sin_tab], axis=1)
        allowed = (segments[step][:, None] == segments[step][None, :]) & (
            row_ids[None, :] <= row_ids[:, None]
        )
        raw = qkv_raw[:, step].reshape(group_rows, head_part)
        turned = []
        for head in range(heads + 1):
            unnormed = lanes(raw, head)
            normed = unnormed * inv_rms(unnormed) * head_norms[min(head // heads, 1)]
            turned.append(low(normed * cosine + roll(normed) * sine))
        value = low(lanes(raw, heads + 1))
        attended_parts.append(
            jnp.concatenate(
                [
                    low(matmul(low(softmax_of(turned[head], turned[heads], allowed)), value))
                    for head in range(heads)
                ],
                axis=1,
            )
        )
        buckets.append((raw, jnp.concatenate(turned + [value], axis=1), allowed, cosine, sine))
    attended = natural_plane(plane_exchange(attended_parts), 0)
    attended = attended.transpose(1, 0, 2).reshape(group_rows, 4 * query_part)
    hidden_state = input_float + pair_scatter(low(matmul(attended, out_all)))

    scale_mlp = inv_rms(hidden_state)
    normed_mlp = tokens_gather(low(hidden_state * scale_mlp * mlp_norm))
    grad_all = tokens_gather(grad_out)
    gate_raw = matmul(normed_mlp, gate_all)
    up_raw = matmul(normed_mlp, up_all)
    activated = jax.nn.silu(gate_raw)
    inner_low = low(activated * up_raw)
    layer_out = low(hidden_state + tokens_scatter(low(matmul(inner_low, down_all))))
    inner_grad = matmul_nt(grad_all, down_all)
    sigmoid_gate = jax.nn.sigmoid(gate_raw)
    gate_grad = low(inner_grad * up_raw * sigmoid_gate * (1.0 + gate_raw * (1.0 - sigmoid_gate)))
    up_grad = low(inner_grad * activated)
    mlp_row_grad = tokens_scatter(
        low(matmul_nt(gate_grad, gate_all) + matmul_nt(up_grad, up_all))
    )
    grad_down = line_scatter(
        low(matmul_tn(inner_low, grad_all)).reshape(line_extent, down_rows, model_width)
    )

    hidden_norm_grad, mlp_gain_part = norm_back(hidden_state, scale_mlp, mlp_norm, mlp_row_grad)
    hidden_grad = f32(grad_out) + hidden_norm_grad
    branch_grad = pair_gather(low(hidden_grad))
    split = low(matmul_nt(branch_grad, out_all)).reshape(group_rows, 4, query_part)
    heads_grad = plane_exchange(own_plane(split.transpose(1, 0, 2), 0))
    grad_out_proj = line_scatter(full_scatter_plane(low(matmul_tn(attended, branch_grad))))
    back = [
        attend_back_values(raw, kept, heads_grad[step], allowed, cosine, sine, head_norms, roll)
        for step, (raw, kept, allowed, cosine, sine) in enumerate(buckets)
    ]
    qkv_grad = jnp.stack([grads for grads, _ in back]).reshape(4, 2, local_rows, head_part)
    qkv_grad = qkv_grad.transpose(1, 0, 2, 3).reshape(all_rows, head_part)
    attn_row_grad = tokens_scatter(low(matmul_nt(qkv_grad, qkv_all)))
    grad_qkv_columns = line_sums(matmul_tn(normed_attn, qkv_grad))
    input_norm_grad, attn_gain_part = norm_back(input_float, scale_attn, attn_norm, attn_row_grad)
    head_gains = sum(gains for _, gains in back)[0]
    gains = total_sum(
        jnp.concatenate([attn_gain_part, mlp_gain_part, head_gains]).reshape(-1, HEAD_SIZE)
    ).reshape(-1)
    return (
        layer_out,
        hidden_grad + input_norm_grad,
        gains[:model_width],
        gains[2 * model_width :].reshape(2, HEAD_SIZE),
        heads_back(grad_qkv_columns[:, :, :query_part]),
        heads_back(grad_qkv_columns[:, :, query_part : query_part + HEAD_SIZE]),
        heads_back(grad_qkv_columns[:, :, query_part + HEAD_SIZE :]),
        grad_out_proj,
        gains[model_width : 2 * model_width],
        units_back(line_sums(matmul_tn(normed_mlp, gate_grad)), down_rows),
        units_back(line_sums(matmul_tn(normed_mlp, up_grad)), down_rows),
        grad_down,
    )


def solution(mesh):
    dp, tensor = mesh.shape["dp"], mesh.shape["tensor"]
    fine = Mesh(mesh.devices.reshape(dp // 4, 2, 2, tensor), ("f", "ty", "tx", "tensor"))
    rows = ("f", "ty", "tx")
    tokens = P(rows + ("tensor",), None)
    grid = P(rows, "tensor")
    units = P(("tensor",) + rows, None)
    return jax.shard_map(
        shards,
        mesh=fine,
        in_specs=(
            tokens, P(), P(), grid, grid, grid, units, P(), grid, grid, units, tokens, P(rows, None),
        ),
        out_specs=(tokens, tokens, P(), P(), grid, grid, grid, units, P(), grid, grid, units),
        check_vma=False,
    )
```

```python
import jax
import jax.numpy as jnp
from jax import lax
from jax.experimental import pallas as pl
from jax.experimental.pallas import tpu as pltpu
from jax.sharding import Mesh, PartitionSpec as P

QUERY_HEADS = 16
KEY_VALUE_HEADS = 8
HEAD_SIZE = 128


EPS = 1e-06
ROPE_BASE = 1000000.0
MASKED = -1e30
LOW = jnp.bfloat16


def matmul(left_mat, right_mat):
    return jnp.dot(left_mat, right_mat, preferred_element_type=jnp.float32)


def matmul_tn(left_mat, right_mat):
    return lax.dot_general(
        left_mat, right_mat, (((0,), (0,)), ((), ())), preferred_element_type=jnp.float32
    )


def matmul_nt(left_mat, right_mat):
    return lax.dot_general(
        left_mat, right_mat, (((1,), (1,)), ((), ())), preferred_element_type=jnp.float32
    )


def inv_rms(values):
    return lax.rsqrt(jnp.mean(values * values, axis=-1, keepdims=True) + EPS)


def norm_back(values, scales, gain_row, upstream):
    weighted = upstream * gain_row
    inner_mean = jnp.mean(weighted * values, axis=-1, keepdims=True)
    value_grad = scales * weighted - values * (scales * scales * scales) * inner_mean
    lead_axes = tuple(range(upstream.ndim - 1))
    return (value_grad, jnp.sum(upstream * values * scales, axis=lead_axes))


def rope_tables(position, head_width):
    half_dim = head_width // 2
    inverse = ROPE_BASE ** (-(jnp.arange(half_dim, dtype=jnp.float32) * (2.0 / head_width)))
    angles = position.astype(jnp.float32)[:, None] * inverse[None, :]
    return (jnp.cos(angles), jnp.sin(angles))


def rotate(values, cos_tab, sin_tab, direction):
    half_dim = values.shape[-1] // 2
    first_half = values[..., :half_dim]
    second_half = values[..., half_dim:]
    cosine = cos_tab[:, None, :]
    sine_tab = direction * sin_tab[:, None, :]
    return jnp.concatenate(
        [
            first_half * cosine - second_half * sine_tab,
            second_half * cosine + first_half * sine_tab,
        ],
        axis=-1,
    )


def doc_layout(lengths_row, row_ids):
    doc_ends = jnp.cumsum(lengths_row, dtype=jnp.int32)
    document_segment = jnp.sum(
        (row_ids[:, None] >= doc_ends[None, :]).astype(jnp.int32), axis=1, dtype=jnp.int32
    )
    doc_starts = doc_ends - lengths_row
    member = document_segment[:, None] == jnp.arange(lengths_row.shape[0], dtype=jnp.int32)[None, :]
    start_of = jnp.sum(jnp.where(member, doc_starts[None, :], 0), axis=1, dtype=jnp.int32)
    return (document_segment, row_ids - start_of)


def f32(values):
    return values.astype(jnp.float32)


def low(values):
    return values.astype(LOW)


def swap(block, axis):
    return lax.ppermute(block, axis, [(0, 1), (1, 0)])


def plane_index():
    return 2 * lax.axis_index("ty") + lax.axis_index("tx")


def plane_gather(block):
    across_x = swap(block, "tx")
    across_y = swap(block, "ty")
    return [block, across_x, across_y, swap(across_y, "tx")]


def plane_scatter(parts):
    own, for_x, for_y, for_far = parts
    for_y = low(f32(for_y) + f32(swap(for_far, "tx")))
    return f32(own) + f32(swap(for_x, "tx")) + f32(swap(for_y, "ty"))


def plane_exchange(parts):
    own, for_x, for_y, for_far = parts
    return [own, swap(for_x, "tx"), swap(for_y, "ty"), swap(swap(for_far, "tx"), "ty")]


def plane_lengths(lengths):
    return jnp.concatenate(plane_gather(lengths))


def line_gather(block):
    return lax.all_gather(block, "f", axis=0)


def line_scatter(parts):
    return f32(lax.psum_scatter(parts, "f", scatter_dimension=0))


def natural_plane(blocks, axis):
    own = plane_index()
    shape = list(blocks[0].shape)
    shape.insert(axis, 4)
    whole = jnp.zeros(shape, blocks[0].dtype)
    for step in range(4):
        whole = lax.dynamic_update_index_in_dim(whole, blocks[step], own ^ step, axis)
    return whole


def own_plane(whole, axis):
    own = plane_index()
    return [
        lax.dynamic_index_in_dim(whole, own ^ step, axis, keepdims=False) for step in range(4)
    ]


def full_gather(rows_block):
    rows, width = rows_block.shape
    line = line_gather(rows_block)
    extent = line.shape[0]
    blocks = plane_gather(line.reshape(extent * rows, width))
    whole = natural_plane([block.reshape(extent, rows, width) for block in blocks], 1)
    return whole.reshape(extent * 4 * rows, width)


def full_scatter_plane(partial):
    extent = lax.axis_size("f")
    rows, width = partial.shape[0] // (4 * extent), partial.shape[1]
    parts = own_plane(partial.reshape(extent, 4, rows, width), 1)
    plane_sum = plane_scatter([part.reshape(extent * rows, width) for part in parts])
    return low(plane_sum).reshape(extent, rows, width)


def tokens_gather(block):
    near = plane_gather(block)
    return jnp.concatenate(near + [swap(piece, "tensor") for piece in near])


def tokens_scatter(partial):
    rows = partial.shape[0] // 8
    near = []
    for step in range(4):
        mine = partial[step * rows : (step + 1) * rows]
        other = swap(partial[(4 + step) * rows : (5 + step) * rows], "tensor")
        near.append(low(f32(mine) + f32(other)))
    return plane_scatter(near)


def pair_gather(block):
    return jnp.concatenate([block, swap(block, "tensor")])


def pair_scatter(partial):
    rows = partial.shape[0] // 2
    return f32(partial[:rows]) + f32(swap(partial[rows:], "tensor"))


def total_sum(values):
    return lax.psum(values, ("f", "ty", "tx", "tensor"))


class Place:
    def __init__(self):
        self.z = lax.axis_index("f")
        self.ty = lax.axis_index("ty")
        self.tx = lax.axis_index("tx")
        self.core = lax.axis_index("tensor")
        self.p = 2 * self.ty + self.tx
        self.px = 2 * self.ty + 1 - self.tx
        self.py = 2 * (1 - self.ty) + self.tx
        self.pd = 2 * (1 - self.ty) + 1 - self.tx
        self.x = {"tx": 1 - self.tx}
        self.y = {"ty": 1 - self.ty}
        self.d = {"tx": 1 - self.tx, "ty": 1 - self.ty}
        self.pair = {"tensor": 1 - self.core}
        self.up = {"f": self.z + 1}
        self.down = {"f": self.z - 1}
        self.two = {"f": (self.z + 2) % 4}

    def at(self, step):
        return (self.z + step) % 4


def remote(src, dst, send, recv, to):
    return pltpu.make_async_remote_copy(
        src_ref=src,
        dst_ref=dst,
        send_sem=send,
        recv_sem=recv,
        device_id=to,
        device_id_type=pl.DeviceIdType.MESH,
    )


def arrived(dst, recv, to):
    remote(dst, dst, recv, recv, to).wait_recv()


def greet(place, partners, line):
    barrier = pltpu.get_barrier_semaphore()
    for to in partners:
        pl.semaphore_signal(barrier, inc=1, device_id=to, device_id_type=pl.DeviceIdType.MESH)
    if not line:
        pl.semaphore_wait(barrier, len(partners))
        return

    @pl.when(place.z > 0)
    def _():
        pl.semaphore_signal(
            barrier, inc=1, device_id=place.down, device_id_type=pl.DeviceIdType.MESH
        )

    @pl.when(place.z < 3)
    def _():
        pl.semaphore_signal(barrier, inc=1, device_id=place.up, device_id_type=pl.DeviceIdType.MESH)

    pl.semaphore_signal(barrier, inc=1, device_id=place.two, device_id_type=pl.DeviceIdType.MESH)
    pl.semaphore_wait(barrier, len(partners) + 2 + (place.z + 1) // 2 % 2)


class LineGather:
    def __init__(self, place, own, slot, send, recv):
        self.place, self.own, self.slot, self.send, self.recv = place, own, slot, send, recv
        here = slot(place.z)
        self.to_down = remote(own, here, send.at[0], recv.at[1], place.down)
        self.to_up = remote(own, here, send.at[1], recv.at[3], place.up)
        self.to_two = remote(own, here, send.at[2], recv.at[2], place.two)
        two = slot(place.at(2))
        self.pass_down = remote(two, two, send.at[3], recv.at[3], place.down)
        self.pass_up = remote(two, two, send.at[3], recv.at[1], place.up)

    def start(self):
        z = self.place.z
        self.to_two.start()
        pl.when((z == 1) | (z == 3))(self.to_down.start)
        pl.when((z == 0) | (z == 2))(self.to_up.start)

    def step(self, turn):
        if turn == 2:
            return 2
        if turn == 1:
            return jnp.where(self.place.z == 3, 3, 1)
        return jnp.where(self.place.z == 3, 1, 3)

    def wait(self, turn):
        step = self.step(turn)
        slot = self.slot(self.place.at(step))
        arrived(slot, self.recv.at[step], self.place.two)
        if turn == 2:
            pl.when(self.place.z == 1)(self.pass_down.start)
            pl.when(self.place.z == 2)(self.pass_up.start)
            pl.when(self.place.z == 1)(self.to_up.start)
            pl.when(self.place.z == 2)(self.to_down.start)

    def finish(self):
        pl.when(self.place.z > 0)(self.to_down.wait_send)
        pl.when(self.place.z < 3)(self.to_up.wait_send)
        self.to_two.wait_send()
        pl.when(self.place.z == 1)(self.pass_down.wait_send)
        pl.when(self.place.z == 2)(self.pass_up.wait_send)


class PlaneGather:
    def __init__(self, place, own, slot, rows, send, recv):
        half = rows // 2
        whole, top, end = pl.ds(0, rows), pl.ds(0, half), pl.ds(half, half)
        self.place, self.recv = place, recv
        self.to_x = remote(own, slot(place.p, whole), send.at[0], recv.at[0], place.x)
        self.to_y = remote(own, slot(place.p, whole), send.at[1], recv.at[1], place.y)
        self.from_x, self.from_y = slot(place.px, whole), slot(place.py, whole)
        self.far_top, self.far_end = slot(place.pd, top), slot(place.pd, end)
        pass_x, pass_y = slot(place.py, top), slot(place.px, end)
        self.pass_x = remote(pass_x, pass_x, send.at[2], recv.at[2], place.x)
        self.pass_y = remote(pass_y, pass_y, send.at[3], recv.at[3], place.y)

    def start(self):
        self.to_x.start()
        self.to_y.start()

    def forward(self):
        arrived(self.from_y, self.recv.at[1], self.place.y)
        self.pass_x.start()
        arrived(self.from_x, self.recv.at[0], self.place.x)
        self.pass_y.start()

    def wait_far(self):
        arrived(self.far_top, self.recv.at[2], self.place.x)
        arrived(self.far_end, self.recv.at[3], self.place.y)

    def finish(self):
        self.to_x.wait_send()
        self.to_y.wait_send()
        self.pass_x.wait_send()
        self.pass_y.wait_send()


ANYWHERE = pl.BlockSpec(memory_space=pl.ANY)
WHOLE = pl.BlockSpec(memory_space=pltpu.VMEM)


class Marks:
    def __init__(self, ref):
        self.ref, self.used = ref, 0

    def take(self, count=1):
        first = self.used
        self.used += count
        return self.ref.at[first] if count == 1 else self.ref.at[pl.ds(first, count)]


def each_rows(rows, chunk, work):
    def body(index, carry):
        work(pl.ds(pl.multiple_of(index * chunk, chunk), chunk))
        return carry

    lax.fori_loop(0, rows // chunk, body, 0)


class TokensGather:
    def __init__(self, place, own, whole, marks):
        half = own.shape[0] // 2
        top, end = pl.ds(0, half), pl.ds(half, half)
        self.place, self.whole = place, whole
        self.copy = pltpu.make_async_copy(own, whole.at[0], marks.take())
        self.recv = [marks.take() for _ in range(8)]
        x, y, pair = place.x, place.y, place.pair
        self.to_x = remote(own, whole.at[1], marks.take(), self.recv[0], x)
        self.to_y = remote(own, whole.at[2], marks.take(), self.recv[1], y)
        self.pass_x = remote(
            whole.at[2, top], whole.at[3, top], marks.take(), self.recv[2], x
        )
        self.pass_y = remote(
            whole.at[1, end], whole.at[3, end], marks.take(), self.recv[3], y
        )
        self.to_pair = [
            remote(
                own if step == 0 else whole.at[step],
                whole.at[4 + step],
                marks.take(),
                self.recv[4 + step],
                pair,
            )
            for step in range(4)
        ]
        self.far = (whole.at[3, top], whole.at[3, end])

    def start(self):
        self.to_x.start()
        self.to_y.start()
        self.to_pair[0].start()
        self.copy.start()

    def forward(self):
        arrived(self.whole.at[2], self.recv[1], self.place.y)
        self.pass_x.start()
        arrived(self.whole.at[1], self.recv[0], self.place.x)
        self.pass_y.start()
        self.to_pair[2].start()
        self.to_pair[1].start()

    def start_near(self, near, marks):
        self.copy.start()
        self.to_pair[0].start()
        copies = [
            pltpu.make_async_copy(near.at[index], self.whole.at[1 + index], marks.take())
            for index in range(2)
        ]
        for copy in copies:
            copy.start()
        for copy in copies:
            copy.wait()
        self.pass_x.start()
        self.pass_y.start()
        self.to_pair[2].start()
        self.to_pair[1].start()

    def finish_near(self):
        for step in range(4):
            arrived(self.whole.at[4 + step], self.recv[4 + step], self.place.pair)
        for copy in [self.pass_x, self.pass_y] + self.to_pair:
            copy.wait_send()
        self.copy.wait()

    def last(self):
        arrived(self.far[0], self.recv[2], self.place.x)
        arrived(self.far[1], self.recv[3], self.place.y)
        self.to_pair[3].start()

    def finish(self):
        for step in range(4):
            arrived(self.whole.at[4 + step], self.recv[4 + step], self.place.pair)
        for copy in [self.to_x, self.to_y, self.pass_x, self.pass_y] + self.to_pair:
            copy.wait_send()
        self.copy.wait()


class Exchange:
    def __init__(self, place, piece, slot, marks):
        self.place = place
        there = ((place.px, place.x), (place.py, place.y), (place.pd, place.d))
        self.copy = pltpu.make_async_copy(piece(place.p, 0), slot(place.p, 0), marks.take())
        self.sends, self.slots = [], []
        for index, (p, to) in enumerate(there):
            recv = marks.take()
            self.sends.append(
                remote(piece(p, index + 1), slot(place.p, index + 1), marks.take(), recv, to)
            )
            self.slots.append((slot(p, index + 1), recv, to))

    def start(self):
        for copy in (self.sends[2], self.sends[0], self.sends[1], self.copy):
            copy.start()

    def wait(self):
        self.copy.wait()
        for slot, recv, to in self.slots:
            arrived(slot, recv, to)

    def finish(self):
        for copy in self.sends:
            copy.wait_send()


class LineScatter:
    @staticmethod
    def scratch(rows, width, here=False):
        return [pltpu.VMEM((4 if here else 5, rows, width), LOW)]

    def __init__(self, place, part, out, buffers, marks, here=False):
        self.place, self.out, self.here = place, out, here
        kept = buffers[0]
        self.rows = kept.shape[1]
        self.passed, self.above, self.below, self.two = (kept.at[index] for index in range(4))
        z = place.z
        if here:
            self.mid, self.own = part(place.at(2)), part(z)
        else:
            self.mid, self.own = kept.at[4], self.passed
            self.load_mid = pltpu.make_async_copy(part(place.at(2)), self.mid, marks.take())
            self.load_own = pltpu.make_async_copy(part(z), self.own, marks.take())
        self.recv = [marks.take() for _ in range(4)]
        self.pass_up = remote(part(3), self.passed, marks.take(), self.recv[0], place.up)
        self.pass_down = remote(part(0), self.passed, marks.take(), self.recv[0], place.down)
        self.to_down = remote(
            part(place.at(3)), self.above, marks.take(), self.recv[1], place.down
        )
        self.to_up = remote(part(place.at(1)), self.below, marks.take(), self.recv[2], place.up)
        self.to_two = remote(self.mid, self.two, marks.take(), self.recv[3], place.two)

    def start(self):
        z = self.place.z
        pl.when(z == 0)(self.pass_up.start)
        pl.when(z == 3)(self.pass_down.start)
        if not self.here:
            self.load_mid.start()
        pl.when((z == 1) | (z == 2))(self.to_down.start)
        pl.when((z == 1) | (z == 2))(self.to_up.start)

    def add(self, target, other):
        def work(rows):
            target[rows] = low(f32(target[rows]) + f32(other[rows]))

        each_rows(self.rows, 16, work)

    def middle(self):
        z = self.place.z
        if not self.here:
            self.load_mid.wait()
        pl.when(z == 0)(self.pass_up.wait_send)
        pl.when(z == 3)(self.pass_down.wait_send)

        @pl.when((z == 1) | (z == 2))
        def _():
            arrived(self.passed, self.recv[0], self.place.two)
            self.add(self.mid, self.passed)

        self.to_two.start()
        pl.when(z == 0)(self.to_up.start)
        pl.when(z == 3)(self.to_down.start)
        if not self.here:
            self.load_own.start()

    def finish(self):
        z = self.place.z
        if not self.here:
            self.load_own.wait()

        @pl.when(z < 3)
        def _():
            arrived(self.above, self.recv[1], self.place.two)
            self.add(self.own, self.above)

        @pl.when(z > 0)
        def _():
            arrived(self.below, self.recv[2], self.place.two)
            self.add(self.own, self.below)

        arrived(self.two, self.recv[3], self.place.two)
        out, own, two = self.out, self.own, self.two

        def work(rows):
            out[rows] = (f32(own[rows]) + f32(two[rows])).astype(out.dtype)

        each_rows(self.rows, 16, work)

    def drain(self):
        z = self.place.z
        pl.when(z > 0)(self.to_down.wait_send)
        pl.when(z < 3)(self.to_up.wait_send)
        self.to_two.wait_send()


def comm_params(number):
    return pltpu.CompilerParams(
        collective_id=number, has_side_effects=True, vmem_limit_bytes=62 * 1024 * 1024
    )


def comm_cost(micros):
    return pl.CostEstimate(flops=0, bytes_accessed=micros * 3_000_000, transcendentals=0)


def tables_of(lengths_row, id_col, id_row, inverse, count):
    zero = jnp.zeros((1, 1), jnp.int32)
    segment_col, segment_row = jnp.zeros_like(id_col), jnp.zeros_like(id_row)
    ends, starts, end = [], [], zero
    for index in range(count):
        starts.append(end)
        end = end + lengths_row[:, index : index + 1]
        ends.append(end)
        segment_col = segment_col + jnp.where(id_col >= end, 1, 0)
        segment_row = segment_row + jnp.where(id_row >= end, 1, 0)
    start_of = jnp.zeros_like(id_col)
    for index in range(count):
        start_of = start_of + jnp.where(segment_col == index, starts[index], 0)
    angles = f32(id_col - start_of) * inverse
    return segment_col, segment_row, jnp.cos(angles), jnp.sin(angles)


def units_split(half, half_rows, weights, out):
    for p in range(4):
        parts = []
        for weight in weights:
            for z in range(4):
                start = ((z * 4 + p) * 2 + half) * half_rows
                parts.append(f32(weight[:, start : start + half_rows]))
        out[p] = low(jnp.concatenate(parts, axis=1))


def units_joined(halves, outs, stage, marks):
    width = stage.shape[2]
    half_rows = width // 8
    copies = []
    for which, out in enumerate(outs):
        for z in range(4):
            slot = z % 2
            if len(copies) > 1:
                copies[-2].wait()
            start = (4 * which + z) * half_rows
            parts = [
                f32(columns[p][:, start : start + half_rows])
                for p in range(4)
                for columns in halves
            ]
            stage[slot] = jnp.concatenate(parts, axis=1)
            copies.append(
                pltpu.make_async_copy(
                    stage.at[slot], out.at[:, pl.ds(z * width, width)], marks.at[slot]
                )
            )
            copies[-1].start()
    for copy in copies[-2:]:
        copy.wait()


def first_kernel(
    documents,
    attn_norm,
    query_ref,
    key_ref,
    value_ref,
    gate_weight,
    up_weight,
    out_ref,
    down_ref,
    lengths_ref,
    id_col,
    id_row,
    inverse_ref,
    head_norms,
    input_ref,
    norm_ref,
    upstream_ref,
    rows_all,
    second_pieces,
    gate_rows,
    gate_all,
    above_ref,
    below_ref,
    upstream_near,
    qkv_hbm,
    out_hbm,
    raw_hbm,
    low_hbm,
    cos_hbm,
    sin_hbm,
    segment_col,
    segment_row,
    attended,
    hidden,
    normed,
    marks_ref,
    rows_ref,
    qkv_ref,
    halves,
    qkv_all,
    out_all,
    raw_out,
    low_out,
    cos_out,
    sin_out,
    lengths_all,
    row_block,
    heads_stage,
    pair_stage,
    pair_got,
):
    place = Place()
    marks = Marks(marks_ref)
    greet(place, [place.x, place.y, place.d, place.pair], True)
    rows, width = rows_ref.shape
    head_part = raw_out.shape[3]
    heads = head_part // HEAD_SIZE - 2
    lengths = Exchange(
        place, lambda p, step: lengths_ref, lambda p, step: lengths_all.at[step], marks
    )
    qkv_pieces = Exchange(
        place, lambda p, step: qkv_ref.at[p], lambda p, step: qkv_all.at[place.z, p], marks
    )
    gate_pieces = Exchange(
        place, lambda p, step: halves.at[0, p], lambda p, step: gate_rows.at[p], marks
    )
    tokens = TokensGather(place, rows_ref, rows_all, marks)
    upstream_recv = [marks.take(), marks.take()]
    upstream = [
        remote(upstream_ref, upstream_near.at[index], marks.take(), upstream_recv[index], to)
        for index, to in enumerate((place.x, place.y))
    ]
    qkv_line = LineGather(
        place, qkv_all.at[place.z], lambda z: qkv_all.at[z], marks.take(4), marks.take(4)
    )
    gate_line = LineGather(
        place, gate_rows, lambda z: gate_all.at[z], marks.take(4), marks.take(4)
    )
    out_line = LineGather(
        place, out_ref, lambda z: out_all.at[z, place.p], marks.take(4), marks.take(4)
    )
    own_copies = [
        pltpu.make_async_copy(out_ref, out_all.at[place.z, place.p], marks.take()),
    ]
    gate_copy = pltpu.make_async_copy(gate_rows, gate_all.at[place.z], marks.take())
    near_recv = [marks.take(), marks.take()]
    to_down = remote(down_ref, above_ref, marks.take(), near_recv[0], place.down)
    to_up = remote(down_ref, below_ref, marks.take(), near_recv[1], place.up)
    out_planes = []
    for turn in range(4):
        z = place.z if turn == 0 else place.at(out_line.step(turn))
        out_planes.append(
            PlaneGather(
                place,
                out_ref if turn == 0 else out_all.at[z, place.p],
                lambda p, part, z=z: out_all.at[z, p, part],
                out_ref.shape[0],
                marks.take(4),
                marks.take(4),
            )
        )
    heads_out = Exchange(
        place, lambda p, step: heads_stage.at[step], lambda p, step: attended.at[p], marks
    )
    to_pair = remote(pair_stage, pair_got, marks.take(), marks.take(), place.pair)
    fetch_marks = marks.take(2)
    qkv_copy = pltpu.make_async_copy(qkv_all, qkv_hbm, marks.take())
    out_copy = pltpu.make_async_copy(out_all, out_hbm, marks.take())
    bucket_copies = [
        pltpu.make_async_copy(raw_out, raw_hbm, marks.take()),
        pltpu.make_async_copy(low_out, low_hbm, marks.take()),
    ]
    table_copies = [
        pltpu.make_async_copy(cos_out, cos_hbm, marks.take()),
        pltpu.make_async_copy(sin_out, sin_hbm, marks.take()),
    ]

    second_copy = pltpu.make_async_copy(halves.at[1], second_pieces, marks.take())
    half_rows = down_ref.shape[1]

    lengths.start()
    for p in range(4):
        parts = []
        for weight in (query_ref, key_ref, value_ref):
            part = weight.shape[1] // 4
            parts.append(weight[:, p * part : (p + 1) * part])
        qkv_ref[p] = jnp.concatenate(parts, axis=1)
    qkv_pieces.start()
    attn_row = attn_norm[...]

    def rows_work(part):
        values = f32(input_ref[part])
        rows_ref[part] = low(values * inv_rms(values) * attn_row)

    each_rows(rows, 16, rows_work)
    tokens.start()
    units_split(0, half_rows, (gate_weight, up_weight), halves.at[0])
    gate_pieces.start()
    for copy in own_copies:
        copy.start()
    lengths.wait()
    qkv_pieces.wait()
    qkv_line.start()

    def table_work(step, carry):
        seg_col, seg_row, cosine, sine = tables_of(
            lengths_all[step][:1], id_col[...], id_row[...], inverse_ref[...], documents
        )
        segment_col[step] = seg_col
        segment_row[step] = seg_row
        cos_out[step] = cosine
        lane = lax.broadcasted_iota(jnp.int32, sine.shape, 1)
        sin_out[step] = jnp.where(lane < HEAD_SIZE // 2, -sine, sine)
        return carry

    lax.fori_loop(0, 2, table_work, 0)
    tokens.forward()
    out_planes[0].start()
    units_split(1, half_rows, (gate_weight, up_weight), halves.at[1])
    second_copy.start()
    lax.fori_loop(2, 4, table_work, 0)
    qkv_line.wait(2)
    out_line.start()
    tokens.last()
    out_planes[0].forward()
    qkv_line.wait(1)
    qkv_line.wait(3)
    out_line.wait(2)
    out_planes[2].start()
    gate_pieces.wait()
    gate_line.start()
    gate_copy.start()
    for copy in table_copies:
        copy.start()
    qkv_copy.start()
    tokens.finish()

    def fetches(step):
        return (
            pltpu.make_async_copy(rows_all.at[step], row_block.at[0], fetch_marks.at[0]),
            pltpu.make_async_copy(rows_all.at[4 + step], row_block.at[1], fetch_marks.at[1]),
        )

    def bucket(turn, carry):
        step = 3 - turn
        for copy in fetches(step):
            copy.start()
        for copy in fetches(step):
            copy.wait()
        raw = matmul(
            row_block[...].reshape(2 * rows, width), qkv_all[...].reshape(width, head_part)
        )
        raw_out[0, step] = raw[:rows]
        raw_out[1, step] = raw[rows:]
        allowed = (segment_col[step] == segment_row[step]) & (id_row[...] <= id_col[...])
        turned = []
        for head in range(heads + 1):
            gain = head_norms[min(head // heads, 1)][None, :]
            unnormed = lanes(raw, head)
            turned.append(
                low(
                    turn_pairs(
                        unnormed * inv_rms(unnormed) * gain, cos_out[step], sin_out[step]
                    )
                )
            )
        value = low(lanes(raw, heads + 1))
        outs = [
            low(matmul(low(softmax_of(turned[head], turned[heads], allowed)), value))
            for head in range(heads)
        ]
        kept = jnp.concatenate(turned + [value], axis=1)
        low_out[0, step] = kept[:rows]
        low_out[1, step] = kept[rows:]
        outs = jnp.concatenate(outs, axis=1)
        heads_stage[step, 0] = outs[:rows]
        heads_stage[step, 1] = outs[rows:]
        for index, at in enumerate((1, 2, 3)):
            pl.when(step == at)(heads_out.sends[index].start)
        pl.when(step == 0)(heads_out.copy.start)
        return carry

    lax.fori_loop(0, 1, bucket, 0)
    out_line.wait(1)
    out_line.wait(3)
    out_planes[1].start()
    out_planes[3].start()
    lax.fori_loop(1, 2, bucket, 0)
    out_planes[2].forward()
    for copy in upstream:
        copy.start()
    lax.fori_loop(2, 3, bucket, 0)
    out_planes[1].forward()
    out_planes[3].forward()
    lax.fori_loop(3, 4, bucket, 0)
    for copy in bucket_copies:
        copy.start()
    gate_line.wait(2)
    pl.when(place.z > 0)(to_down.start)
    pl.when(place.z < 3)(to_up.start)
    for plane in out_planes:
        plane.wait_far()
    for copy in own_copies:
        copy.wait()
    out_copy.start()
    heads_out.wait()

    def projected(core_step):
        block = jnp.concatenate([attended[p, core_step] for p in range(4)], axis=1)
        return matmul(block, out_all[...].reshape(block.shape[1], width))

    pair_stage[...] = low(projected(1))
    to_pair.start()
    hidden[...] = f32(input_ref[...]) + projected(0)
    to_pair.wait()
    norm_row = norm_ref[...]

    def norm_work(part):
        values = hidden[part] + f32(pair_got[part])
        hidden[part] = values
        normed[part] = low(values * inv_rms(values) * norm_row)

    each_rows(rows, 16, norm_work)
    gate_line.wait(1)
    gate_line.wait(3)
    for index, to in enumerate((place.x, place.y)):
        arrived(upstream_near.at[index], upstream_recv[index], to)
        upstream[index].wait_send()
    gate_copy.wait()
    second_copy.wait()
    for copy in [qkv_copy, out_copy] + bucket_copies + table_copies:
        copy.wait()
    parts = [lengths, qkv_pieces, gate_pieces, heads_out, qkv_line, gate_line, out_line]
    for part in parts + out_planes:
        part.finish()

    @pl.when(place.z < 3)
    def _():
        arrived(above_ref, near_recv[0], place.two)
        to_up.wait_send()

    @pl.when(place.z > 0)
    def _():
        arrived(below_ref, near_recv[1], place.two)
        to_down.wait_send()


def first_part(
    attn_norm,
    query_weight,
    key_matrix,
    value_matrix,
    gate_weight,
    up_weight,
    output_weight,
    down_weight,
    doc_lengths,
    row_ids,
    head_norms,
    layer_input,
    mlp_norm,
    grad_out,
):
    block_rows, width = layer_input.shape
    group_rows = 2 * block_rows
    weight_rows = query_weight.shape[0]
    head_part = (query_weight.shape[1] + key_matrix.shape[1] + value_matrix.shape[1]) // 4
    qkv_pieces = jax.ShapeDtypeStruct((4, weight_rows, head_part), LOW)
    gate_pieces = jax.ShapeDtypeStruct((4, weight_rows, gate_weight.shape[1] // 4), LOW)
    query_part = head_part - 2 * HEAD_SIZE
    documents = doc_lengths.shape[1]
    lengths = jnp.pad(doc_lengths, ((0, 7), (0, HEAD_SIZE - documents)))
    half = jnp.arange(HEAD_SIZE // 2, dtype=jnp.float32)
    inverse = ROPE_BASE ** (-(half * (2.0 / HEAD_SIZE)))
    low_like = lambda *shape: jax.ShapeDtypeStruct(shape, LOW)
    table = jax.ShapeDtypeStruct((4, group_rows, HEAD_SIZE), jnp.float32)
    return pl.pallas_call(
        lambda *refs: first_kernel(documents, *refs),
        out_shape=(
            low_like(8, block_rows, width),
            low_like(*gate_pieces.shape),
            low_like(*gate_pieces.shape),
            low_like(4, *gate_pieces.shape),
            low_like(*down_weight.shape),
            low_like(*down_weight.shape),
            low_like(2, block_rows, width),
            low_like(4, *qkv_pieces.shape),
            low_like(4, 4, *output_weight.shape),
            jax.ShapeDtypeStruct((2, 4, block_rows, head_part), jnp.float32),
            low_like(2, 4, block_rows, head_part),
            table,
            table,
            jax.ShapeDtypeStruct((4, group_rows, 1), jnp.int32),
            jax.ShapeDtypeStruct((4, 1, group_rows), jnp.int32),
            low_like(4, 2, block_rows, query_part),
            jax.ShapeDtypeStruct((block_rows, width), jnp.float32),
            low_like(block_rows, width),
        ),
        in_specs=[WHOLE] * 6 + [ANYWHERE] * 2 + [WHOLE] * 7 + [ANYWHERE],
        out_specs=(ANYWHERE,) * 13 + (WHOLE,) * 5,
        scratch_shapes=[
            pltpu.SemaphoreType.DMA((160,)),
            pltpu.VMEM((block_rows, width), LOW),
            pltpu.VMEM(qkv_pieces.shape, LOW),
            pltpu.VMEM((2,) + gate_pieces.shape, LOW),
            pltpu.VMEM((4,) + qkv_pieces.shape, LOW),
            pltpu.VMEM((4, 4) + output_weight.shape, LOW),
            pltpu.VMEM((2, 4, block_rows, head_part), jnp.float32),
            pltpu.VMEM((2, 4, block_rows, head_part), LOW),
            pltpu.VMEM(table.shape, jnp.float32),
            pltpu.VMEM(table.shape, jnp.float32),
            pltpu.VMEM((4,) + lengths.shape, jnp.int32),
            pltpu.VMEM((2, block_rows, width), LOW),
            pltpu.VMEM((4, 2, block_rows, query_part), LOW),
            pltpu.VMEM((block_rows, width), LOW),
            pltpu.VMEM((block_rows, width), LOW),
        ],
        compiler_params=comm_params(0),
        cost_estimate=comm_cost(130),
    )(
        attn_norm[None],
        query_weight,
        key_matrix,
        value_matrix,
        gate_weight,
        up_weight,
        output_weight,
        down_weight,
        lengths,
        row_ids[:, None],
        row_ids[None, :],
        jnp.concatenate([inverse, inverse])[None],
        head_norms,
        layer_input,
        mlp_norm[None],
        grad_out,
    )


class FarScatter:
    @staticmethod
    def scratch(rows, width):
        return [pltpu.VMEM((2, rows // 2, width), LOW)]

    def __init__(self, place, summed, buffers, marks):
        self.place, self.summed, self.landed = place, summed, buffers[0]
        self.half = summed.shape[1] // 2
        self.recv = [marks.take(), marks.take()]
        self.sends = [
            remote(
                summed.at[3, pl.ds(index * self.half, self.half)],
                self.landed.at[index],
                marks.take(),
                self.recv[index],
                to,
            )
            for index, to in enumerate((place.x, place.y))
        ]

    def start(self):
        for copy in self.sends:
            copy.start()

    def add(self):
        summed, landed = self.summed, self.landed
        for index, block, base, to in (
            (0, 2, 0, self.place.x),
            (1, 1, self.half, self.place.y),
        ):
            arrived(landed.at[index], self.recv[index], to)

            def work(rows):
                own_rows = pl.ds(pl.multiple_of(rows.start + base, 16), rows.size)
                summed[block, own_rows] = low(
                    f32(summed[block, own_rows]) + f32(landed[index, rows])
                )

            each_rows(self.half, 16, work)

    def drain(self):
        for copy in self.sends:
            copy.wait_send()


class NearScatter:
    @staticmethod
    def scratch(rows, width):
        return [pltpu.VMEM((3, rows, width), LOW)]

    def __init__(self, place, summed, buffers, marks):
        self.place, self.landed = place, buffers[0]
        self.load = pltpu.make_async_copy(summed.at[0], self.landed.at[2], marks.take())
        self.recv = [marks.take(), marks.take()]
        self.sends = [
            remote(summed.at[1 + index], self.landed.at[index], marks.take(), self.recv[index], to)
            for index, to in enumerate((place.x, place.y))
        ]

    def start(self):
        self.load.start()
        for copy in self.sends:
            copy.start()

    def finish(self, work):
        landed = self.landed
        self.load.wait()
        for index, to in enumerate((self.place.x, self.place.y)):
            arrived(self.landed.at[index], self.recv[index], to)

        def total(rows):
            work(
                rows,
                f32(landed[0, rows]) + f32(landed[1, rows]) + f32(landed[2, rows]),
            )

        each_rows(landed.shape[1], 16, total)

    def drain(self):
        for copy in self.sends:
            copy.wait_send()


class PlaneScatter:
    @staticmethod
    def scratch(rows, width):
        return [pltpu.VMEM((6, rows // 2, width), LOW)]

    def __init__(self, place, summed, out, buffers, marks, at=(0, 1, 2, 3)):
        self.place, self.summed, self.out, self.at = place, summed, out, at
        self.landed = buffers[0]
        self.rows = summed.shape[1]
        half = self.rows // 2
        top, end = pl.ds(0, half), pl.ds(half, half)
        x, y = place.x, place.y
        self.recv = [marks.take() for _ in range(6)]
        routes = (
            (summed.at[at[3], top], x),
            (summed.at[at[3], end], y),
            (summed.at[at[1], top], x),
            (summed.at[at[1], end], x),
            (summed.at[at[2], top], y),
            (summed.at[at[2], end], y),
        )
        self.sends = [
            remote(src, self.landed.at[index], marks.take(), self.recv[index], to)
            for index, (src, to) in enumerate(routes)
        ]

    def start(self):
        for index in (0, 1, 2, 5):
            self.sends[index].start()

    def landed_at(self, index, to):
        arrived(self.landed.at[index], self.recv[index], to)

    def middle(self):
        half = self.rows // 2
        summed, landed = self.summed, self.landed
        _, for_x, for_y, _ = self.at
        self.landed_at(0, self.place.x)

        def top_work(rows):
            summed[for_y, rows] = low(f32(summed[for_y, rows]) + f32(landed[0, rows]))

        each_rows(half, 16, top_work)
        self.sends[4].start()
        self.landed_at(1, self.place.y)

        def end_work(rows):
            end_rows = pl.ds(pl.multiple_of(rows.start + half, 16), rows.size)
            summed[for_x, end_rows] = low(f32(summed[for_x, end_rows]) + f32(landed[1, rows]))

        each_rows(half, 16, end_work)
        self.sends[3].start()

    def finish(self):
        half = self.rows // 2
        for index, to in ((2, self.place.x), (5, self.place.y), (4, self.place.y), (3, self.place.x)):
            self.landed_at(index, to)

        for base, first, second in ((0, 2, 4), (half, 3, 5)):

            def work(rows):
                own_rows = pl.ds(pl.multiple_of(rows.start + base, 16), rows.size)
                self.out[own_rows] = (
                    f32(self.summed[self.at[0], own_rows])
                    + f32(self.landed[first, rows])
                    + f32(self.landed[second, rows])
                ).astype(self.out.dtype)

            each_rows(half, 16, work)

    def drain(self):
        for copy in self.sends:
            copy.wait_send()


def blocks_of(source, block_ref, marks, first, last, work):
    def fetch(block):
        return pltpu.make_async_copy(
            source(block), block_ref.at[block % 2], marks.at[block % 2]
        )

    fetch(first).start()

    def body(block, carry):
        fetch(block).wait()

        @pl.when(block < last - 1)
        def _():
            fetch(block + 1).start()

        work(block, block_ref[block % 2])
        return carry

    lax.fori_loop(first, last, body, 0)


def unit_values(raws, inner_grad):
    units = inner_grad.shape[1]
    gate_raw, up_raw = raws[:, :units], raws[:, units:]
    sigmoid_gate = jax.nn.sigmoid(gate_raw)
    activated = gate_raw * sigmoid_gate
    gate_grad = inner_grad * up_raw * sigmoid_gate * (1.0 + gate_raw * (1.0 - sigmoid_gate))
    return low(activated * up_raw), jnp.concatenate(
        [low(gate_grad), low(inner_grad * activated)], axis=1
    )


def units_kernel(
    rows_ref,
    upstream_ref,
    near_ref,
    pieces_ref,
    first_ref,
    down_ref,
    above_ref,
    below_ref,
    rows_all,
    upstream_all,
    line_ref,
    inner_out,
    second_grad,
    first_sum,
    down_part,
    part_sums,
    grad_sums,
    marks_ref,
    first_mat,
    second_mat,
    down_mat,
    upstream,
    row_block,
    row_slab,
    inner_first,
    first_grad,
    inner_grads,
    first_part,
    inner_stage,
    second_stage,
    *buffers,
):
    place = Place()
    marks = Marks(marks_ref)
    greet(place, [place.x, place.y, place.d, place.pair], True)
    tokens = TokensGather(place, rows_ref, rows_all, marks)
    upstream_tokens = TokensGather(place, upstream_ref, upstream, marks)
    pieces = Exchange(
        place, lambda p, step: pieces_ref.at[p], lambda p, step: line_ref.at[p], marks
    )
    keep = pltpu.make_async_copy(upstream, upstream_all, marks.take())
    line = LineGather(place, line_ref, lambda z: second_mat.at[z], marks.take(4), marks.take(4))
    far_recv = marks.take(2)
    two = down_mat.at[:, place.at(2)]
    to_two = remote(down_ref, down_mat.at[:, place.z], marks.take(), far_recv.at[0], place.two)
    pass_mark = marks.take()
    pass_down = remote(two, two, pass_mark, far_recv.at[1], place.down)
    pass_up = remote(two, two, pass_mark, far_recv.at[1], place.up)
    copies = [
        pltpu.make_async_copy(first_ref, first_mat, marks.take()),
        pltpu.make_async_copy(down_ref, down_mat.at[:, place.z], marks.take()),
    ]
    line_copy = pltpu.make_async_copy(line_ref, second_mat.at[place.z], marks.take())
    above = pltpu.make_async_copy(above_ref, down_mat.at[:, place.at(1)], marks.take())
    below = pltpu.make_async_copy(below_ref, down_mat.at[:, place.at(3)], marks.take())
    line_rows = first_sum.shape[0]
    first_line = LineScatter(
        place,
        lambda z: first_part.at[pl.ds(pl.multiple_of(z * line_rows, 16), line_rows)],
        first_sum,
        buffers[:1],
        marks,
        True,
    )
    part_far = FarScatter(place, part_sums, buffers[1:2], marks)
    grad_far = FarScatter(place, grad_sums, buffers[2:], marks)
    fetch_marks, slab_marks = marks.take(2), marks.take(2)
    send_marks, recv_marks = marks.take(8), marks.take(8)
    width = rows_ref.shape[1]
    half = inner_first.shape[2]
    all_rows = 8 * rows_ref.shape[0]

    to_two.start()
    pieces.start()
    tokens.start()
    for copy in copies:
        copy.start()
    pl.when(place.z < 3)(above.start)
    pl.when(place.z > 0)(below.start)
    tokens.forward()
    upstream_tokens.start_near(near_ref, marks)
    pieces.wait()
    line_copy.start()
    arrived(two, far_recv.at[0], place.two)
    pl.when(place.z == 1)(pass_down.start)
    pl.when(place.z == 2)(pass_up.start)
    line.start()
    tokens.last()
    upstream_tokens.last()
    for copy in copies:
        copy.wait()
    line_copy.wait()
    pl.when(place.z < 3)(above.wait)
    pl.when(place.z > 0)(below.wait)

    @pl.when(place.z == 0)
    def _():
        arrived(down_mat.at[:, 3], far_recv.at[1], place.two)

    @pl.when(place.z == 3)
    def _():
        arrived(down_mat.at[:, 0], far_recv.at[1], place.two)

    tokens.finish()
    upstream_tokens.finish_near()
    keep.start()
    pieces.finish()

    def first_work(block, values):
        grads = matmul_nt(upstream[block], down_mat[...].reshape(2 * half, width))
        inner_grads[block] = low(grads[:, half:])
        inner, grad = unit_values(matmul(values, first_mat[...]), grads[:, :half])
        inner_first[block] = inner
        first_grad[block] = grad

    blocks_of(lambda block: rows_all.at[block], row_block, fetch_marks, 0, 8, first_work)
    line.wait(2)
    tile = row_slab.shape[3]
    tiles = width // tile

    def slab(index):
        return rows_all.at[:, :, pl.ds(pl.multiple_of(index * tile, tile), tile)]

    def slab_work(index, values):
        first_part[pl.ds(pl.multiple_of(index * tile, tile), tile)] = low(
            matmul_tn(values.reshape(all_rows, tile), first_grad[...].reshape(all_rows, 2 * half))
        )

    down_part[...] = low(
        matmul_tn(
            inner_first[...].reshape(all_rows, half), upstream[...].reshape(all_rows, width)
        )
    )
    blocks_of(slab, row_slab, slab_marks, 0, tiles, slab_work)
    first_line.start()
    line.wait(1)
    line.wait(3)

    def fetch(index):
        step, slot = 3 - index // 2, index % 2
        return pltpu.make_async_copy(
            rows_all.at[step + 4 * (1 - slot)], row_block.at[slot], fetch_marks.at[slot]
        )

    def sends(step):
        return (
            remote(
                upstream.at[step],
                part_sums.at[step],
                send_marks.at[step],
                recv_marks.at[step],
                place.pair,
            ),
            remote(
                upstream.at[4 + step],
                grad_sums.at[step],
                send_marks.at[4 + step],
                recv_marks.at[4 + step],
                place.pair,
            ),
        )

    keep.wait()
    store_marks = marks.take(4)

    def stores(slot, block):
        return (
            pltpu.make_async_copy(
                inner_stage.at[slot], inner_out.at[block], store_marks.at[slot]
            ),
            pltpu.make_async_copy(
                second_stage.at[slot], second_grad.at[block], store_marks.at[2 + slot]
            ),
        )

    fetch(0).start()

    def blocks(turn, carry):
        step = 3 - turn
        for slot in range(2):
            index = 2 * turn + slot
            block = step + 4 * (1 - slot)
            fetch(index).wait()

            @pl.when(index < 7)
            def _():
                fetch(index + 1).start()

            second = second_mat[...].reshape(width, 2 * half)
            inner, grad = unit_values(matmul(row_block[slot], second), f32(inner_grads[block]))

            @pl.when(turn > 0)
            def _():
                for copy in stores(slot, block + 1):
                    copy.wait()

            inner_stage[slot] = inner
            second_stage[slot] = grad
            for copy in stores(slot, block):
                copy.start()
            part = matmul(
                jnp.concatenate([inner_first[block], inner], axis=1),
                down_mat[...].reshape(2 * half, width),
            )
            grad = matmul_nt(first_grad[block], first_mat[...]) + matmul_nt(grad, second)
            if slot == 0:
                upstream[step] = low(part)
                upstream[4 + step] = low(grad)
                for copy in sends(step):
                    copy.start()
            else:
                for copy in sends(step):
                    copy.wait_recv()
                part_sums[step] = low(part + f32(part_sums[step]))
                grad_sums[step] = low(grad + f32(grad_sums[step]))
        return carry

    lax.fori_loop(0, 1, blocks, 0)
    grad_far.start()
    part_far.start()
    first_line.middle()
    lax.fori_loop(1, 4, blocks, 0)
    for slot in range(2):
        for copy in stores(slot, 4 * (1 - slot)):
            copy.wait()
    grad_far.add()
    part_far.add()
    first_line.finish()
    first_line.drain()
    grad_far.drain()
    part_far.drain()
    for step in range(4):
        for copy in sends(step):
            copy.wait_send()
    line.finish()
    to_two.wait_send()
    pl.when(place.z == 1)(pass_down.wait_send)
    pl.when(place.z == 2)(pass_up.wait_send)


def units_products(rows, upstream, near, second_pieces, first_all, down_weight, above, below):
    block_rows, width = rows.shape
    half = first_all.shape[1] // 2
    half_rows = down_weight.shape[1]
    second_rows = jax.ShapeDtypeStruct((4 * second_pieces.shape[1], 2 * half), LOW)
    hidden = lambda count: jax.ShapeDtypeStruct((8, block_rows, count * half), LOW)
    sums = jax.ShapeDtypeStruct((4, block_rows, width), LOW)
    blocks = jax.ShapeDtypeStruct((8, block_rows, width), LOW)
    return pl.pallas_call(
        units_kernel,
        out_shape=(
            blocks,
            blocks,
            jax.ShapeDtypeStruct(second_pieces.shape, LOW),
            hidden(1),
            hidden(2),
            jax.ShapeDtypeStruct(second_rows.shape, LOW),
            jax.ShapeDtypeStruct((half, width), LOW),
            sums,
            sums,
        ),
        in_specs=[ANYWHERE] * 8,
        out_specs=(ANYWHERE,) * 5 + (WHOLE,) * 4,
        scratch_shapes=[
            pltpu.SemaphoreType.DMA((140,)),
            pltpu.VMEM(first_all.shape, LOW),
            pltpu.VMEM((4,) + second_pieces.shape, LOW),
            pltpu.VMEM((2, 4, half_rows, width), LOW),
            pltpu.VMEM((8, block_rows, width), LOW),
            pltpu.VMEM((2, block_rows, width), LOW),
            pltpu.VMEM((2, 8, block_rows, 256), LOW),
            pltpu.VMEM((8, block_rows, half), LOW),
            pltpu.VMEM((8, block_rows, 2 * half), LOW),
            pltpu.VMEM((8, block_rows, half), LOW),
            pltpu.VMEM((width, 2 * half), LOW),
            pltpu.VMEM((2, block_rows, half), LOW),
            pltpu.VMEM((2, block_rows, 2 * half), LOW),
        ]
        + LineScatter.scratch(*second_rows.shape, True)
        + FarScatter.scratch(block_rows, width) * 2,
        compiler_params=comm_params(1),
        cost_estimate=comm_cost(150),
    )(rows, upstream, near, second_pieces, first_all, down_weight, above, below)


def unit_grads_kernel(
    rows_all,
    upstream_ref,
    inner_ref,
    second_ref,
    down_first,
    part_sums,
    grad_sums,
    hidden_ref,
    upstream_own,
    norm_ref,
    layer_out,
    hidden_grad,
    branch,
    mlp_gain,
    down_out,
    second_part,
    marks_ref,
    upstream,
    inner,
    second_grad,
    row_slab,
    gain_rows,
    down_part,
    *buffers,
):
    place = Place()
    marks = Marks(marks_ref)
    greet(place, [place.x, place.y], True)
    grad_near = NearScatter(place, grad_sums, buffers[:1], marks)
    part_near = NearScatter(place, part_sums, buffers[1:2], marks)
    half_rows = down_out.shape[1]
    first_line = LineScatter(
        place, lambda z: down_first.at[z], down_out.at[0], buffers[2:3], marks
    )
    second_line = LineScatter(
        place,
        lambda z: down_part.at[pl.ds(pl.multiple_of(z * half_rows, 16), half_rows)],
        down_out.at[1],
        buffers[3:],
        marks,
        True,
    )
    loads = [
        pltpu.make_async_copy(upstream_ref, upstream, marks.take()),
        pltpu.make_async_copy(inner_ref, inner, marks.take()),
        pltpu.make_async_copy(second_ref, second_grad, marks.take()),
    ]
    slab_marks = marks.take(2)
    rows, width = hidden_ref.shape
    half = inner.shape[2]
    all_rows = 8 * rows
    tile = row_slab.shape[3]
    tiles = width // tile

    def slab(index):
        return rows_all.at[:, :, pl.ds(pl.multiple_of(index * tile, tile), tile)]

    def slab_work(index, values):
        second_part[pl.ds(pl.multiple_of(index * tile, tile), tile)] = low(
            matmul_tn(values.reshape(all_rows, tile), second_grad[...].reshape(all_rows, 2 * half))
        )

    first_line.start()
    grad_near.start()
    for copy in loads:
        copy.start()
    loads[0].wait()
    loads[1].wait()
    down_part[...] = low(
        matmul_tn(inner[...].reshape(all_rows, half), upstream[...].reshape(all_rows, width))
    )
    first_line.middle()
    second_line.start()
    loads[2].wait()
    blocks_of(slab, row_slab, slab_marks, 0, tiles, slab_work)
    second_line.middle()
    part_near.start()
    gain_rows[...] = jnp.zeros_like(gain_rows)
    norm_row = norm_ref[...]

    def norm_work(rows, row_grad):
        values = hidden_ref[rows]
        scales = inv_rms(values)
        weighted = row_grad * norm_row
        inner_mean = jnp.mean(weighted * values, axis=-1, keepdims=True)
        grad = (
            f32(upstream_own[rows])
            + scales * weighted
            - values * (scales * scales * scales) * inner_mean
        )
        hidden_grad[rows] = grad
        branch[rows] = low(grad)
        parts = row_grad * values * scales
        gain_rows[...] += parts[:8] + parts[8:]

    def out_work(rows, row_part):
        layer_out[rows] = low(hidden_ref[rows] + row_part)

    grad_near.finish(norm_work)
    mlp_gain[...] = jnp.sum(gain_rows[...], axis=0, keepdims=True)
    part_near.finish(out_work)
    first_line.finish()
    second_line.finish()
    for part in (first_line, second_line, grad_near, part_near):
        part.drain()


def unit_grads(
    rows_all,
    upstream,
    inner,
    second_grad,
    down_first,
    part_sums,
    grad_sums,
    hidden,
    upstream_own,
    norm,
):
    _, rows, width = rows_all.shape
    half = inner.shape[2]
    half_rows = down_first.shape[1]
    return pl.pallas_call(
        unit_grads_kernel,
        out_shape=(
            jax.ShapeDtypeStruct((rows, width), LOW),
            jax.ShapeDtypeStruct((rows, width), jnp.float32),
            jax.ShapeDtypeStruct((rows, width), LOW),
            jax.ShapeDtypeStruct((1, width), jnp.float32),
            jax.ShapeDtypeStruct((2, half_rows, width), jnp.float32),
            jax.ShapeDtypeStruct((width, 2 * half), LOW),
        ),
        in_specs=[ANYWHERE] * 7 + [WHOLE] * 3,
        out_specs=(WHOLE,) * 6,
        scratch_shapes=[
            pltpu.SemaphoreType.DMA((64,)),
            pltpu.VMEM(upstream.shape, LOW),
            pltpu.VMEM(inner.shape, LOW),
            pltpu.VMEM(second_grad.shape, LOW),
            pltpu.VMEM((2, 8, rows, 256), LOW),
            pltpu.VMEM((8, width), jnp.float32),
            pltpu.VMEM((half, width), LOW),
        ]
        + NearScatter.scratch(rows, width) * 2
        + LineScatter.scratch(half_rows, width)
        + LineScatter.scratch(half_rows, width, True),
        compiler_params=comm_params(4),
        cost_estimate=comm_cost(65),
    )(
        rows_all,
        upstream,
        inner,
        second_grad,
        down_first,
        part_sums,
        grad_sums,
        hidden,
        upstream_own,
        norm,
    )


def turn_pairs(values, cosine, sine):
    return values * cosine + pltpu.roll(values, HEAD_SIZE // 2, 1) * sine


def softmax_of(query, key, allowed):
    scores = matmul_nt(query, key) * HEAD_SIZE ** (-0.5)
    masked = jnp.where(allowed, scores, MASKED)
    exponent = jnp.exp(masked - jnp.max(masked, axis=-1, keepdims=True))
    return exponent / jnp.sum(exponent, axis=-1, keepdims=True)


def lanes(values, head):
    return values[:, head * HEAD_SIZE : (head + 1) * HEAD_SIZE]


def roll_half(values):
    return pltpu.roll(values, HEAD_SIZE // 2, 1)


def attend_back_values(raw, kept, grad, allowed, cosine, sine, gains_ref, roll=roll_half):
    group_rows = raw.shape[0]
    heads = raw.shape[1] // HEAD_SIZE - 2
    key, value = lanes(kept, heads), lanes(kept, heads + 1)
    scale = HEAD_SIZE ** (-0.5)
    turned_grads = []
    key_grad = jnp.zeros((group_rows, HEAD_SIZE), jnp.float32)
    value_grad = jnp.zeros((group_rows, HEAD_SIZE), jnp.float32)
    for head in range(heads):
        query, upstream = lanes(kept, head), lanes(grad, head)
        probs = softmax_of(query, key, allowed)
        probs_grad = matmul_nt(upstream, value)
        scores_grad = low(
            probs * (probs_grad - jnp.sum(probs * probs_grad, axis=-1, keepdims=True))
        )
        turned_grads.append(matmul(scores_grad, key) * scale)
        key_grad = key_grad + matmul_tn(scores_grad, query)
        value_grad = value_grad + matmul_tn(low(probs), upstream)
    turned_grads.append(key_grad * scale)
    outs, gains = [], []
    for head in range(heads + 1):
        gain = gains_ref[min(head // heads, 1)][None, :]
        unnormed = lanes(raw, head)
        upstream = turned_grads[head] * cosine - roll(turned_grads[head]) * sine
        grad_raw, gain_part = norm_back(unnormed, inv_rms(unnormed), gain, upstream)
        outs.append(low(grad_raw))
        gains.append(gain_part[None, :])
    outs.append(low(value_grad))
    query_gain = sum(gains[1:heads], gains[0])
    return (jnp.concatenate(outs, axis=1), jnp.concatenate([query_gain, gains[heads]], axis=1))


def heads_back_kernel(
    branch_ref,
    out_ref,
    attended_ref,
    raw_ref,
    low_ref,
    cos_ref,
    sin_ref,
    segment_col,
    segment_row,
    id_col,
    id_row,
    gains_ref,
    rows_all,
    qkv_ref,
    second_part,
    first_rows,
    input_ref,
    hidden_ref,
    norm_ref,
    mlp_gain,
    grad_ref,
    query_out,
    key_out,
    value_out,
    proj_out,
    gate_out,
    up_out,
    attn_gain_out,
    mlp_gain_out,
    head_gain_out,
    marks_ref,
    qkv_columns,
    first_columns,
    second_columns,
    joined_stage,
    qkv_part,
    proj_sum,
    grad_sums,
    line_sum,
    qkv_sum,
    gain_rows,
    gain_mine,
    gain_got,
    out_mat,
    qkv_mat,
    attended,
    branch,
    own_grad,
    heads_grad,
    raw_block,
    low_block,
    qkv_grad,
    row_slab,
    proj_part,
    *buffers,
):
    place = Place()
    marks = Marks(marks_ref)
    greet(place, [place.x, place.y, place.d, place.pair], True)
    rows, width = branch_ref.shape
    half_heads = heads_grad.shape[2]
    group_rows = 2 * rows
    second_line = LineScatter(place, lambda z: second_part.at[z], line_sum, buffers[0:1], marks)
    first_pieces = Exchange(
        place, lambda p, step: first_rows.at[p], lambda p, step: first_columns.at[p], marks
    )
    proj_plane = PlaneScatter(
        place,
        proj_part,
        proj_sum,
        buffers[1:2],
        marks,
        (place.p, place.px, place.py, place.pd),
    )
    tokens = PlaneScatter(place, grad_sums, grad_ref, buffers[2:3], marks)
    qkv_rows, proj_rows = qkv_sum.shape[0], proj_out.shape[0]
    qkv_line = LineScatter(
        place,
        lambda z: qkv_part.at[pl.ds(pl.multiple_of(z * qkv_rows, 16), qkv_rows)],
        qkv_sum,
        buffers[3:4],
        marks,
        True,
    )
    proj_line = LineScatter(
        place,
        lambda z: proj_sum.at[pl.ds(pl.multiple_of(z * proj_rows, 16), proj_rows)],
        proj_out,
        buffers[4:],
        marks,
        True,
    )
    piece_rows, second_piece = qkv_rows // 4, line_sum.shape[0] // 4
    qkv_pieces = Exchange(
        place,
        lambda p, step: qkv_sum.at[pl.ds(pl.multiple_of(p * piece_rows, 16), piece_rows)],
        lambda p, step: qkv_columns.at[p],
        marks,
    )
    second_pieces = Exchange(
        place,
        lambda p, step: line_sum.at[pl.ds(pl.multiple_of(p * second_piece, 16), second_piece)],
        lambda p, step: second_columns.at[p],
        marks,
    )
    near_z = {"f": place.z + 1 - 2 * (place.z % 2)}
    rounds = [
        remote(gain_mine.at[index], gain_got.at[index], marks.take(), marks.take(), to)
        for index, to in enumerate((place.pair, place.x, place.y, near_z, place.two))
    ]
    heads = Exchange(
        place, lambda p, step: own_grad.at[p], lambda p, step: heads_grad.at[step], marks
    )
    to_pair = remote(branch_ref, branch.at[1], marks.take(), marks.take(), place.pair)
    loads = [
        pltpu.make_async_copy(branch_ref, branch.at[0], marks.take()),
        pltpu.make_async_copy(out_ref, out_mat, marks.take()),
        pltpu.make_async_copy(attended_ref, attended, marks.take()),
        pltpu.make_async_copy(qkv_ref, qkv_mat, marks.take()),
    ]
    fetch_marks, slab_marks = marks.take(4), marks.take(2)
    send_marks, recv_marks = marks.take(4), marks.take(4)

    to_pair.start()
    second_line.start()
    for copy in loads:
        copy.start()
    for copy in loads:
        copy.wait()

    def own_half(core_step):
        grad = low(matmul_nt(branch[core_step], out_mat[...]))
        for p in range(4):
            own_grad[p, pl.ds(core_step * rows, rows)] = grad[
                :, p * half_heads : (p + 1) * half_heads
            ]

    own_half(0)
    to_pair.wait()
    own_half(1)
    heads.start()
    second_line.middle()

    def proj_work(z, carry):
        block = attended[z].reshape(group_rows, half_heads)
        grad = low(matmul_tn(block, branch[...].reshape(group_rows, width)))
        part = half_heads // 4
        for p in range(4):
            proj_part[p, pl.ds(pl.multiple_of(z * part, part), part)] = grad[
                p * part : (p + 1) * part
            ]
        return carry

    def fetches(step):
        return (
            pltpu.make_async_copy(raw_ref.at[:, step], raw_block, fetch_marks.at[0]),
            pltpu.make_async_copy(low_ref.at[:, step], low_block, fetch_marks.at[1]),
        )

    lax.fori_loop(0, 4, proj_work, 0)
    heads.wait()
    proj_plane.start()
    first_pieces.start()
    head_width = 2 * HEAD_SIZE
    head_gain = gain_mine.at[0, :, pl.ds(2 * width, head_width)]
    head_gain[...] = jnp.zeros((1, head_width), jnp.float32)

    def sends(step):
        return remote(
            out_mat.at[pl.ds(pl.multiple_of(step * rows, rows), rows)],
            grad_sums.at[step],
            send_marks.at[step],
            recv_marks.at[step],
            place.pair,
        )

    def bucket(step, carry):
        for copy in fetches(step):
            copy.start()
        for copy in fetches(step):
            copy.wait()
        allowed = (segment_col[step] == segment_row[step]) & (id_row[...] <= id_col[...])
        grads, gains = attend_back_values(
            raw_block[...].reshape(group_rows, -1),
            low_block[...].reshape(group_rows, -1),
            heads_grad[step],
            allowed,
            cos_ref[step],
            sin_ref[step],
            gains_ref,
        )
        head_gain[...] += gains
        qkv_grad[0, step] = grads[:rows]
        qkv_grad[1, step] = grads[rows:]
        out_mat[pl.ds(pl.multiple_of(step * rows, rows), rows)] = low(
            matmul_nt(grads[rows:], qkv_mat[...])
        )
        sends(step).start()
        return carry

    lax.fori_loop(0, 2, bucket, 0)
    proj_plane.middle()
    lax.fori_loop(2, 4, bucket, 0)

    tile = row_slab.shape[3]
    tiles = width // tile

    def slab(index):
        return pltpu.make_async_copy(
            rows_all.at[:, :, pl.ds(pl.multiple_of(index * tile, tile), tile)],
            row_slab.at[index % 2],
            slab_marks.at[index % 2],
        )

    slab(0).start()

    def own_work(step, carry):
        copy = sends(step)
        copy.wait_recv()
        grad = matmul_nt(qkv_grad[0, step], qkv_mat[...])
        grad_sums[step] = low(grad + f32(grad_sums[step]))
        return carry

    lax.fori_loop(0, 4, own_work, 0)
    tokens.start()

    def row_tile(index, carry):
        slab(index).wait()

        @pl.when(index < tiles - 1)
        def _():
            slab(index + 1).start()

        block = row_slab[index % 2].reshape(4 * group_rows, tile)
        out_rows = pl.ds(pl.multiple_of(index * tile, tile), tile)
        qkv_part[out_rows] = low(
            matmul_tn(block, qkv_grad[...].reshape(4 * group_rows, qkv_grad.shape[3]))
        )
        return carry

    lax.fori_loop(0, tiles, row_tile, 0)
    qkv_line.start()
    second_line.finish()
    proj_plane.finish()
    proj_line.start()
    tokens.middle()
    second_pieces.start()
    qkv_line.middle()
    proj_line.middle()
    tokens.finish()

    gain_rows[...] = jnp.zeros_like(gain_rows)
    norm_row = norm_ref[...]

    def norm_work(part):
        values = f32(input_ref[part])
        scales = inv_rms(values)
        upstream = grad_ref[part]
        weighted = upstream * norm_row
        inner_mean = jnp.mean(weighted * values, axis=-1, keepdims=True)
        grad_ref[part] = (
            hidden_ref[part]
            + scales * weighted
            - values * (scales * scales * scales) * inner_mean
        )
        parts = upstream * values * scales
        gain_rows[...] += parts[:8] + parts[8:]

    each_rows(rows, 16, norm_work)
    gain_mine[0, :, pl.ds(0, width)] = jnp.sum(gain_rows[...], axis=0, keepdims=True)
    gain_mine[0, :, pl.ds(width, width)] = mlp_gain[...]
    for index, copy in enumerate(rounds):
        copy.start()
        copy.wait()
        summed = gain_mine[index] + gain_got[index]
        if index < 4:
            gain_mine[index + 1] = summed
        else:
            attn_gain_out[...] = summed[:, :width]
            mlp_gain_out[...] = summed[:, width : 2 * width]
            head_gain_out[...] = summed[:, 2 * width :]
    qkv_line.finish()
    qkv_pieces.start()
    proj_line.finish()
    for step in range(4):
        sends(step).wait_send()
    heads.finish()
    for part in (proj_plane, second_line, qkv_line, proj_line, tokens):
        part.drain()
    for part in (first_pieces, second_pieces):
        part.wait()
        part.finish()
    units_joined(
        (first_columns, second_columns), (gate_out, up_out), joined_stage, marks.take(2)
    )
    qkv_pieces.wait()
    qkv_pieces.finish()
    for p in range(4):
        start = 0
        for out in (query_out, key_out, value_out):
            part = out.shape[1] // 4
            out[:, p * part : (p + 1) * part] = f32(qkv_columns[p][:, start : start + part])
            start += part


def heads_backward(
    branch,
    out_all,
    attended,
    raw,
    kept,
    tables,
    rows_all,
    qkv_all,
    second_part,
    first_rows,
    layer_input,
    hidden_grad,
    norm,
    mlp_gain,
):
    rows, width = branch.shape
    head_part = raw.shape[3]
    query_part = head_part - 2 * HEAD_SIZE
    line_rows, units = second_part.shape[1:]
    qkv_rows = width // 4
    tile = 256
    gain_width = 2 * width + 2 * HEAD_SIZE
    weight_rows = line_rows // 4
    pieces = pltpu.VMEM((4, weight_rows, units), LOW)
    wide = lambda *shape: jax.ShapeDtypeStruct(shape, jnp.float32)
    return pl.pallas_call(
        heads_back_kernel,
        out_shape=(
            wide(rows, width),
            wide(weight_rows, 4 * query_part),
            wide(weight_rows, 4 * HEAD_SIZE),
            wide(weight_rows, 4 * HEAD_SIZE),
            wide(query_part // 4, width),
            wide(weight_rows, 4 * units),
            wide(weight_rows, 4 * units),
            wide(1, width),
            wide(1, width),
            wide(1, 2 * HEAD_SIZE),
        ),
        in_specs=[ANYWHERE] * 5
        + [WHOLE] * len(tables)
        + [ANYWHERE] * 4
        + [WHOLE] * 4,
        out_specs=(WHOLE,) * 5 + (ANYWHERE,) * 2 + (WHOLE,) * 3,
        scratch_shapes=[
            pltpu.SemaphoreType.DMA((160,)),
            pltpu.VMEM((4, weight_rows, head_part), LOW),
            pieces,
            pieces,
            pltpu.VMEM((2, weight_rows, units), jnp.float32),
            pltpu.VMEM((width, head_part), LOW),
            pltpu.VMEM((query_part, width), LOW),
            pltpu.VMEM((4, rows, width), LOW),
            pltpu.VMEM((line_rows, units), LOW),
            pltpu.VMEM((qkv_rows, head_part), LOW),
            pltpu.VMEM((8, width), jnp.float32),
            pltpu.VMEM((5, 1, gain_width), jnp.float32),
            pltpu.VMEM((5, 1, gain_width), jnp.float32),
            pltpu.VMEM(out_all.shape, LOW),
            pltpu.VMEM(qkv_all.shape, LOW),
            pltpu.VMEM(attended.shape, LOW),
            pltpu.VMEM((2, rows, width), LOW),
            pltpu.VMEM((4, 2 * rows, query_part), LOW),
            pltpu.VMEM((4, 2 * rows, query_part), LOW),
            pltpu.VMEM((2, rows, head_part), jnp.float32),
            pltpu.VMEM((2, rows, head_part), LOW),
            pltpu.VMEM((2, 4, rows, head_part), LOW),
            pltpu.VMEM((2, 8, rows, tile), LOW),
            pltpu.VMEM((4, query_part, width), LOW),
        ]
        + LineScatter.scratch(line_rows, units)
        + PlaneScatter.scratch(query_part, width)
        + PlaneScatter.scratch(rows, width)
        + LineScatter.scratch(qkv_rows, head_part, True)
        + LineScatter.scratch(query_part // 4, width, True),
        compiler_params=comm_params(3),
        cost_estimate=comm_cost(120),
    )(
        branch,
        out_all,
        attended,
        raw,
        kept,
        *tables,
        rows_all,
        qkv_all,
        second_part,
        first_rows,
        layer_input,
        hidden_grad,
        norm,
        mlp_gain,
    )


def row_ids_of(local_rows):
    core = lax.axis_index("tensor")
    local_ids = jnp.arange(local_rows, dtype=jnp.int32)
    return jnp.concatenate([core * local_rows + local_ids, (1 - core) * local_rows + local_ids])


def heads_of(weight):
    return weight.reshape(weight.shape[0], 4, -1).transpose(1, 0, 2)


def heads_back(pieces):
    return f32(pieces).transpose(1, 0, 2).reshape(pieces.shape[1], -1)


def units_of(weight, down_rows):
    split = weight.reshape(weight.shape[0], -1, 4, down_rows)
    return split.transpose(2, 0, 1, 3).reshape(4, weight.shape[0], -1)


def units_back(pieces, down_rows):
    rows = pieces.shape[1]
    return f32(pieces).reshape(4, rows, -1, down_rows).transpose(1, 2, 0, 3).reshape(rows, -1)


def shards(*arguments):
    if lax.axis_size("f") == 4:
        return line_of_four(*arguments)
    return any_line(*arguments)


def line_of_four(
    layer_input,
    attn_norm,
    head_norms,
    query_weight,
    key_matrix,
    value_matrix,
    output_weight,
    mlp_norm,
    gate_weight,
    up_weight,
    down_weight,
    grad_out,
    doc_lengths,
):
    local_rows, model_width = layer_input.shape
    weight_rows = gate_weight.shape[0]
    down_rows = down_weight.shape[0]
    half_rows = down_rows // 2
    half = 4 * half_rows
    head_part = (query_weight.shape[1] + key_matrix.shape[1] + value_matrix.shape[1]) // 4
    down_halves = down_weight.reshape(2, half_rows, model_width)
    row_ids = row_ids_of(local_rows)
    (
        normed_attn,
        second_pieces,
        _,
        first_all,
        above,
        below,
        grad_near,
        qkv_all,
        out_all,
        qkv_raw,
        qkv_low,
        cos_tab,
        sin_tab,
        segment_col,
        segment_row,
        attended,
        hidden_state,
        normed_mlp,
    ) = first_part(
        attn_norm,
        query_weight,
        key_matrix,
        value_matrix,
        gate_weight,
        up_weight,
        output_weight,
        down_halves,
        doc_lengths,
        row_ids,
        head_norms,
        layer_input,
        mlp_norm,
        grad_out,
    )
    tables = (
        cos_tab,
        sin_tab,
        segment_col,
        segment_row,
        row_ids[:, None],
        row_ids[None, :],
        head_norms,
    )
    (
        rows_all,
        grad_all,
        _,
        inner_low,
        second_grad,
        first_rows,
        grad_down_first,
        part_sums,
        grad_sums,
    ) = (
        units_products(
            normed_mlp,
            grad_out,
            grad_near,
            second_pieces,
            first_all.reshape(model_width, 2 * half),
            down_halves,
            above,
            below,
        )
    )
    line_shape = (4, 4 * weight_rows, 2 * half)
    (
        layer_out,
        hidden_grad,
        branch_grad,
        mlp_gain_part,
        grad_down,
        grad_second,
    ) = unit_grads(
        rows_all,
        grad_all,
        inner_low,
        second_grad,
        grad_down_first.reshape(4, half_rows, model_width),
        part_sums,
        grad_sums,
        hidden_state,
        grad_out,
        mlp_norm[None],
    )
    (
        grad_input,
        grad_query,
        grad_key,
        grad_value,
        grad_out_proj,
        grad_gate,
        grad_up,
        attn_gain,
        mlp_gain,
        head_gains,
    ) = (
        heads_backward(
            branch_grad,
            out_all.reshape(-1, model_width),
            attended,
            qkv_raw,
            qkv_low,
            tables,
            normed_attn,
            qkv_all.reshape(model_width, head_part),
            grad_second.reshape(line_shape),
            first_rows.reshape(4, weight_rows, 2 * half),
            layer_input,
            hidden_grad,
            attn_norm[None],
            mlp_gain_part,
        )
    )
    return (
        layer_out,
        grad_input,
        attn_gain.reshape(-1),
        head_gains.reshape(2, HEAD_SIZE),
        grad_query,
        grad_key,
        grad_value,
        grad_out_proj,
        mlp_gain.reshape(-1),
        grad_gate,
        grad_up,
        grad_down.reshape(down_weight.shape),
    )


def any_line(
    layer_input,
    attn_norm,
    head_norms,
    query_weight,
    key_matrix,
    value_matrix,
    output_weight,
    mlp_norm,
    gate_weight,
    up_weight,
    down_weight,
    grad_out,
    doc_lengths,
):
    line_extent = lax.axis_size("f")
    local_rows, model_width = layer_input.shape
    group_rows = 2 * local_rows
    all_rows = 8 * local_rows
    weight_rows = gate_weight.shape[0]
    down_rows = down_weight.shape[0]
    hidden_part = line_extent * down_rows
    qkv_pieces = jnp.concatenate(
        [heads_of(query_weight), heads_of(key_matrix), heads_of(value_matrix)], axis=2
    )
    head_part = qkv_pieces.shape[2]
    query_part = head_part - 2 * HEAD_SIZE
    heads = head_part // HEAD_SIZE - 2

    def exchanged(pieces):
        return natural_plane(plane_exchange(own_plane(pieces, 0)), 0)

    def line_rows(pieces):
        return line_gather(exchanged(pieces)).reshape(model_width, -1)

    def line_sums(partial):
        parts = low(partial).reshape(line_extent, 4 * weight_rows, -1)
        return exchanged(low(line_scatter(parts)).reshape(4, weight_rows, -1))

    qkv_all = line_rows(qkv_pieces)
    out_all = full_gather(output_weight)
    gate_all = line_rows(units_of(gate_weight, down_rows))
    up_all = line_rows(units_of(up_weight, down_rows))
    down_all = line_gather(down_weight).reshape(hidden_part, model_width)

    input_float = f32(layer_input)
    scale_attn = inv_rms(input_float)
    normed_attn = tokens_gather(low(input_float * scale_attn * attn_norm))
    row_ids = row_ids_of(local_rows)
    segments, positions = jax.vmap(lambda lengths: doc_layout(lengths, row_ids))(
        plane_lengths(doc_lengths)
    )
    qkv_raw = matmul(normed_attn, qkv_all).reshape(2, 4, local_rows, head_part)
    roll = lambda values: jnp.roll(values, HEAD_SIZE // 2, 1)
    buckets, attended_parts = [], []
    for step in range(4):
        cos_tab, sin_tab = rope_tables(positions[step], HEAD_SIZE)
        cosine = jnp.concatenate([cos_tab, cos_tab], axis=1)
        sine = jnp.concatenate([-sin_tab, sin_tab], axis=1)
        allowed = (segments[step][:, None] == segments[step][None, :]) & (
            row_ids[None, :] <= row_ids[:, None]
        )
        raw = qkv_raw[:, step].reshape(group_rows, head_part)
        turned = []
        for head in range(heads + 1):
            unnormed = lanes(raw, head)
            normed = unnormed * inv_rms(unnormed) * head_norms[min(head // heads, 1)]
            turned.append(low(normed * cosine + roll(normed) * sine))
        value = low(lanes(raw, heads + 1))
        attended_parts.append(
            jnp.concatenate(
                [
                    low(matmul(low(softmax_of(turned[head], turned[heads], allowed)), value))
                    for head in range(heads)
                ],
                axis=1,
            )
        )
        buckets.append((raw, jnp.concatenate(turned + [value], axis=1), allowed, cosine, sine))
    attended = natural_plane(plane_exchange(attended_parts), 0)
    attended = attended.transpose(1, 0, 2).reshape(group_rows, 4 * query_part)
    hidden_state = input_float + pair_scatter(low(matmul(attended, out_all)))

    scale_mlp = inv_rms(hidden_state)
    normed_mlp = tokens_gather(low(hidden_state * scale_mlp * mlp_norm))
    grad_all = tokens_gather(grad_out)
    gate_raw = matmul(normed_mlp, gate_all)
    up_raw = matmul(normed_mlp, up_all)
    activated = jax.nn.silu(gate_raw)
    inner_low = low(activated * up_raw)
    layer_out = low(hidden_state + tokens_scatter(low(matmul(inner_low, down_all))))
    inner_grad = matmul_nt(grad_all, down_all)
    sigmoid_gate = jax.nn.sigmoid(gate_raw)
    gate_grad = low(inner_grad * up_raw * sigmoid_gate * (1.0 + gate_raw * (1.0 - sigmoid_gate)))
    up_grad = low(inner_grad * activated)
    mlp_row_grad = tokens_scatter(
        low(matmul_nt(gate_grad, gate_all) + matmul_nt(up_grad, up_all))
    )
    grad_down = line_scatter(
        low(matmul_tn(inner_low, grad_all)).reshape(line_extent, down_rows, model_width)
    )

    hidden_norm_grad, mlp_gain_part = norm_back(hidden_state, scale_mlp, mlp_norm, mlp_row_grad)
    hidden_grad = f32(grad_out) + hidden_norm_grad
    branch_grad = pair_gather(low(hidden_grad))
    split = low(matmul_nt(branch_grad, out_all)).reshape(group_rows, 4, query_part)
    heads_grad = plane_exchange(own_plane(split.transpose(1, 0, 2), 0))
    grad_out_proj = line_scatter(full_scatter_plane(low(matmul_tn(attended, branch_grad))))
    back = [
        attend_back_values(raw, kept, heads_grad[step], allowed, cosine, sine, head_norms, roll)
        for step, (raw, kept, allowed, cosine, sine) in enumerate(buckets)
    ]
    qkv_grad = jnp.stack([grads for grads, _ in back]).reshape(4, 2, local_rows, head_part)
    qkv_grad = qkv_grad.transpose(1, 0, 2, 3).reshape(all_rows, head_part)
    attn_row_grad = tokens_scatter(low(matmul_nt(qkv_grad, qkv_all)))
    grad_qkv_columns = line_sums(matmul_tn(normed_attn, qkv_grad))
    input_norm_grad, attn_gain_part = norm_back(input_float, scale_attn, attn_norm, attn_row_grad)
    head_gains = sum(gains for _, gains in back)[0]
    gains = total_sum(
        jnp.concatenate([attn_gain_part, mlp_gain_part, head_gains]).reshape(-1, HEAD_SIZE)
    ).reshape(-1)
    return (
        layer_out,
        hidden_grad + input_norm_grad,
        gains[:model_width],
        gains[2 * model_width :].reshape(2, HEAD_SIZE),
        heads_back(grad_qkv_columns[:, :, :query_part]),
        heads_back(grad_qkv_columns[:, :, query_part : query_part + HEAD_SIZE]),
        heads_back(grad_qkv_columns[:, :, query_part + HEAD_SIZE :]),
        grad_out_proj,
        gains[model_width : 2 * model_width],
        units_back(line_sums(matmul_tn(normed_mlp, gate_grad)), down_rows),
        units_back(line_sums(matmul_tn(normed_mlp, up_grad)), down_rows),
        grad_down,
    )


def solution(mesh):
    dp, tensor = mesh.shape["dp"], mesh.shape["tensor"]
    fine = Mesh(mesh.devices.reshape(dp // 4, 2, 2, tensor), ("f", "ty", "tx", "tensor"))
    rows = ("f", "ty", "tx")
    tokens = P(rows + ("tensor",), None)
    grid = P(rows, "tensor")
    units = P(("tensor",) + rows, None)
    return jax.shard_map(
        shards,
        mesh=fine,
        in_specs=(
            tokens, P(), P(), grid, grid, grid, units, P(), grid, grid, units, tokens, P(rows, None),
        ),
        out_specs=(tokens, tokens, P(), P(), grid, grid, grid, units, P(), grid, grid, units),
        check_vma=False,
    )
```

```python
import jax
import jax.numpy as jnp
from jax import lax
from jax.experimental import pallas as pl
from jax.experimental.pallas import tpu as pltpu
from jax.sharding import Mesh, PartitionSpec as P

QUERY_HEADS = 16
KEY_VALUE_HEADS = 8
HEAD_SIZE = 128


EPS = 1e-06
ROPE_BASE = 1000000.0
MASKED = -1e30
LOW = jnp.bfloat16


def matmul(left_mat, right_mat):
    return jnp.dot(left_mat, right_mat, preferred_element_type=jnp.float32)


def matmul_tn(left_mat, right_mat):
    return lax.dot_general(
        left_mat, right_mat, (((0,), (0,)), ((), ())), preferred_element_type=jnp.float32
    )


def matmul_nt(left_mat, right_mat):
    return lax.dot_general(
        left_mat, right_mat, (((1,), (1,)), ((), ())), preferred_element_type=jnp.float32
    )


def inv_rms(values):
    return lax.rsqrt(jnp.mean(values * values, axis=-1, keepdims=True) + EPS)


def norm_back(values, scales, gain_row, upstream):
    weighted = upstream * gain_row
    inner_mean = jnp.mean(weighted * values, axis=-1, keepdims=True)
    value_grad = scales * weighted - values * (scales * scales * scales) * inner_mean
    lead_axes = tuple(range(upstream.ndim - 1))
    return (value_grad, jnp.sum(upstream * values * scales, axis=lead_axes))


def rope_tables(position, head_width):
    half_dim = head_width // 2
    inverse = ROPE_BASE ** (-(jnp.arange(half_dim, dtype=jnp.float32) * (2.0 / head_width)))
    angles = position.astype(jnp.float32)[:, None] * inverse[None, :]
    return (jnp.cos(angles), jnp.sin(angles))


def rotate(values, cos_tab, sin_tab, direction):
    half_dim = values.shape[-1] // 2
    first_half = values[..., :half_dim]
    second_half = values[..., half_dim:]
    cosine = cos_tab[:, None, :]
    sine_tab = direction * sin_tab[:, None, :]
    return jnp.concatenate(
        [
            first_half * cosine - second_half * sine_tab,
            second_half * cosine + first_half * sine_tab,
        ],
        axis=-1,
    )


def doc_layout(lengths_row, row_ids):
    doc_ends = jnp.cumsum(lengths_row, dtype=jnp.int32)
    document_segment = jnp.sum(
        (row_ids[:, None] >= doc_ends[None, :]).astype(jnp.int32), axis=1, dtype=jnp.int32
    )
    doc_starts = doc_ends - lengths_row
    member = document_segment[:, None] == jnp.arange(lengths_row.shape[0], dtype=jnp.int32)[None, :]
    start_of = jnp.sum(jnp.where(member, doc_starts[None, :], 0), axis=1, dtype=jnp.int32)
    return (document_segment, row_ids - start_of)


def f32(values):
    return values.astype(jnp.float32)


def low(values):
    return values.astype(LOW)


def swap(block, axis):
    return lax.ppermute(block, axis, [(0, 1), (1, 0)])


def plane_index():
    return 2 * lax.axis_index("ty") + lax.axis_index("tx")


def plane_gather(block):
    across_x = swap(block, "tx")
    across_y = swap(block, "ty")
    return [block, across_x, across_y, swap(across_y, "tx")]


def plane_scatter(parts):
    own, for_x, for_y, for_far = parts
    for_y = low(f32(for_y) + f32(swap(for_far, "tx")))
    return f32(own) + f32(swap(for_x, "tx")) + f32(swap(for_y, "ty"))


def plane_exchange(parts):
    own, for_x, for_y, for_far = parts
    return [own, swap(for_x, "tx"), swap(for_y, "ty"), swap(swap(for_far, "tx"), "ty")]


def plane_lengths(lengths):
    return jnp.concatenate(plane_gather(lengths))


def line_gather(block):
    return lax.all_gather(block, "f", axis=0)


def line_scatter(parts):
    return f32(lax.psum_scatter(parts, "f", scatter_dimension=0))


def natural_plane(blocks, axis):
    own = plane_index()
    shape = list(blocks[0].shape)
    shape.insert(axis, 4)
    whole = jnp.zeros(shape, blocks[0].dtype)
    for step in range(4):
        whole = lax.dynamic_update_index_in_dim(whole, blocks[step], own ^ step, axis)
    return whole


def own_plane(whole, axis):
    own = plane_index()
    return [
        lax.dynamic_index_in_dim(whole, own ^ step, axis, keepdims=False) for step in range(4)
    ]


def full_gather(rows_block):
    rows, width = rows_block.shape
    line = line_gather(rows_block)
    extent = line.shape[0]
    blocks = plane_gather(line.reshape(extent * rows, width))
    whole = natural_plane([block.reshape(extent, rows, width) for block in blocks], 1)
    return whole.reshape(extent * 4 * rows, width)


def full_scatter_plane(partial):
    extent = lax.axis_size("f")
    rows, width = partial.shape[0] // (4 * extent), partial.shape[1]
    parts = own_plane(partial.reshape(extent, 4, rows, width), 1)
    plane_sum = plane_scatter([part.reshape(extent * rows, width) for part in parts])
    return low(plane_sum).reshape(extent, rows, width)


def tokens_gather(block):
    near = plane_gather(block)
    return jnp.concatenate(near + [swap(piece, "tensor") for piece in near])


def tokens_scatter(partial):
    rows = partial.shape[0] // 8
    near = []
    for step in range(4):
        mine = partial[step * rows : (step + 1) * rows]
        other = swap(partial[(4 + step) * rows : (5 + step) * rows], "tensor")
        near.append(low(f32(mine) + f32(other)))
    return plane_scatter(near)


def pair_gather(block):
    return jnp.concatenate([block, swap(block, "tensor")])


def pair_scatter(partial):
    rows = partial.shape[0] // 2
    return f32(partial[:rows]) + f32(swap(partial[rows:], "tensor"))


def total_sum(values):
    return lax.psum(values, ("f", "ty", "tx", "tensor"))


class Place:
    def __init__(self):
        self.z = lax.axis_index("f")
        self.ty = lax.axis_index("ty")
        self.tx = lax.axis_index("tx")
        self.core = lax.axis_index("tensor")
        self.p = 2 * self.ty + self.tx
        self.px = 2 * self.ty + 1 - self.tx
        self.py = 2 * (1 - self.ty) + self.tx
        self.pd = 2 * (1 - self.ty) + 1 - self.tx
        self.x = {"tx": 1 - self.tx}
        self.y = {"ty": 1 - self.ty}
        self.d = {"tx": 1 - self.tx, "ty": 1 - self.ty}
        self.pair = {"tensor": 1 - self.core}
        self.up = {"f": self.z + 1}
        self.down = {"f": self.z - 1}
        self.two = {"f": (self.z + 2) % 4}

    def at(self, step):
        return (self.z + step) % 4


def remote(src, dst, send, recv, to):
    return pltpu.make_async_remote_copy(
        src_ref=src,
        dst_ref=dst,
        send_sem=send,
        recv_sem=recv,
        device_id=to,
        device_id_type=pl.DeviceIdType.MESH,
    )


def arrived(dst, recv, to):
    remote(dst, dst, recv, recv, to).wait_recv()


def greet(place, partners, line):
    barrier = pltpu.get_barrier_semaphore()
    for to in partners:
        pl.semaphore_signal(barrier, inc=1, device_id=to, device_id_type=pl.DeviceIdType.MESH)
    if not line:
        pl.semaphore_wait(barrier, len(partners))
        return

    @pl.when(place.z > 0)
    def _():
        pl.semaphore_signal(
            barrier, inc=1, device_id=place.down, device_id_type=pl.DeviceIdType.MESH
        )

    @pl.when(place.z < 3)
    def _():
        pl.semaphore_signal(barrier, inc=1, device_id=place.up, device_id_type=pl.DeviceIdType.MESH)

    pl.semaphore_signal(barrier, inc=1, device_id=place.two, device_id_type=pl.DeviceIdType.MESH)
    pl.semaphore_wait(barrier, len(partners) + 2 + (place.z + 1) // 2 % 2)


class LineGather:
    def __init__(self, place, own, slot, send, recv):
        self.place, self.own, self.slot, self.send, self.recv = place, own, slot, send, recv
        here = slot(place.z)
        self.to_down = remote(own, here, send.at[0], recv.at[1], place.down)
        self.to_up = remote(own, here, send.at[1], recv.at[3], place.up)
        self.to_two = remote(own, here, send.at[2], recv.at[2], place.two)
        two = slot(place.at(2))
        self.pass_down = remote(two, two, send.at[3], recv.at[3], place.down)
        self.pass_up = remote(two, two, send.at[3], recv.at[1], place.up)

    def start(self):
        z = self.place.z
        self.to_two.start()
        pl.when((z == 1) | (z == 3))(self.to_down.start)
        pl.when((z == 0) | (z == 2))(self.to_up.start)

    def step(self, turn):
        if turn == 2:
            return 2
        if turn == 1:
            return jnp.where(self.place.z == 3, 3, 1)
        return jnp.where(self.place.z == 3, 1, 3)

    def wait(self, turn):
        step = self.step(turn)
        slot = self.slot(self.place.at(step))
        arrived(slot, self.recv.at[step], self.place.two)
        if turn == 2:
            pl.when(self.place.z == 1)(self.pass_down.start)
            pl.when(self.place.z == 2)(self.pass_up.start)
            pl.when(self.place.z == 1)(self.to_up.start)
            pl.when(self.place.z == 2)(self.to_down.start)

    def finish(self):
        pl.when(self.place.z > 0)(self.to_down.wait_send)
        pl.when(self.place.z < 3)(self.to_up.wait_send)
        self.to_two.wait_send()
        pl.when(self.place.z == 1)(self.pass_down.wait_send)
        pl.when(self.place.z == 2)(self.pass_up.wait_send)


class PlaneGather:
    def __init__(self, place, own, slot, rows, send, recv):
        half = rows // 2
        whole, top, end = pl.ds(0, rows), pl.ds(0, half), pl.ds(half, half)
        self.place, self.recv = place, recv
        self.to_x = remote(own, slot(place.p, whole), send.at[0], recv.at[0], place.x)
        self.to_y = remote(own, slot(place.p, whole), send.at[1], recv.at[1], place.y)
        self.from_x, self.from_y = slot(place.px, whole), slot(place.py, whole)
        self.far_top, self.far_end = slot(place.pd, top), slot(place.pd, end)
        pass_x, pass_y = slot(place.py, top), slot(place.px, end)
        self.pass_x = remote(pass_x, pass_x, send.at[2], recv.at[2], place.x)
        self.pass_y = remote(pass_y, pass_y, send.at[3], recv.at[3], place.y)

    def start(self):
        self.to_x.start()
        self.to_y.start()

    def forward(self):
        arrived(self.from_y, self.recv.at[1], self.place.y)
        self.pass_x.start()
        arrived(self.from_x, self.recv.at[0], self.place.x)
        self.pass_y.start()

    def wait_far(self):
        arrived(self.far_top, self.recv.at[2], self.place.x)
        arrived(self.far_end, self.recv.at[3], self.place.y)

    def finish(self):
        self.to_x.wait_send()
        self.to_y.wait_send()
        self.pass_x.wait_send()
        self.pass_y.wait_send()


ANYWHERE = pl.BlockSpec(memory_space=pl.ANY)
WHOLE = pl.BlockSpec(memory_space=pltpu.VMEM)


class Marks:
    def __init__(self, ref):
        self.ref, self.used = ref, 0

    def take(self, count=1):
        first = self.used
        self.used += count
        return self.ref.at[first] if count == 1 else self.ref.at[pl.ds(first, count)]


def each_rows(rows, chunk, work):
    def body(index, carry):
        work(pl.ds(pl.multiple_of(index * chunk, chunk), chunk))
        return carry

    lax.fori_loop(0, rows // chunk, body, 0)


class TokensGather:
    def __init__(self, place, own, whole, marks):
        half = own.shape[0] // 2
        top, end = pl.ds(0, half), pl.ds(half, half)
        self.place, self.whole = place, whole
        self.copy = pltpu.make_async_copy(own, whole.at[0], marks.take())
        self.recv = [marks.take() for _ in range(8)]
        x, y, pair = place.x, place.y, place.pair
        self.to_x = remote(own, whole.at[1], marks.take(), self.recv[0], x)
        self.to_y = remote(own, whole.at[2], marks.take(), self.recv[1], y)
        self.pass_x = remote(
            whole.at[2, top], whole.at[3, top], marks.take(), self.recv[2], x
        )
        self.pass_y = remote(
            whole.at[1, end], whole.at[3, end], marks.take(), self.recv[3], y
        )
        self.to_pair = [
            remote(
                own if step == 0 else whole.at[step],
                whole.at[4 + step],
                marks.take(),
                self.recv[4 + step],
                pair,
            )
            for step in range(4)
        ]
        self.far = (whole.at[3, top], whole.at[3, end])

    def start(self):
        self.to_x.start()
        self.to_y.start()
        self.to_pair[0].start()
        self.copy.start()

    def forward(self):
        arrived(self.whole.at[2], self.recv[1], self.place.y)
        self.pass_x.start()
        arrived(self.whole.at[1], self.recv[0], self.place.x)
        self.pass_y.start()
        self.to_pair[2].start()
        self.to_pair[1].start()

    def start_near(self, near, marks):
        self.copy.start()
        self.to_pair[0].start()
        copies = [
            pltpu.make_async_copy(near.at[index], self.whole.at[1 + index], marks.take())
            for index in range(2)
        ]
        for copy in copies:
            copy.start()
        for copy in copies:
            copy.wait()
        self.pass_x.start()
        self.pass_y.start()
        self.to_pair[2].start()
        self.to_pair[1].start()

    def finish_near(self):
        for step in range(4):
            arrived(self.whole.at[4 + step], self.recv[4 + step], self.place.pair)
        for copy in [self.pass_x, self.pass_y] + self.to_pair:
            copy.wait_send()
        self.copy.wait()

    def last(self):
        arrived(self.far[0], self.recv[2], self.place.x)
        arrived(self.far[1], self.recv[3], self.place.y)
        self.to_pair[3].start()

    def finish(self):
        for step in range(4):
            arrived(self.whole.at[4 + step], self.recv[4 + step], self.place.pair)
        for copy in [self.to_x, self.to_y, self.pass_x, self.pass_y] + self.to_pair:
            copy.wait_send()
        self.copy.wait()


class Exchange:
    def __init__(self, place, piece, slot, marks):
        self.place = place
        there = ((place.px, place.x), (place.py, place.y), (place.pd, place.d))
        self.copy = pltpu.make_async_copy(piece(place.p, 0), slot(place.p, 0), marks.take())
        self.sends, self.slots = [], []
        for index, (p, to) in enumerate(there):
            recv = marks.take()
            self.sends.append(
                remote(piece(p, index + 1), slot(place.p, index + 1), marks.take(), recv, to)
            )
            self.slots.append((slot(p, index + 1), recv, to))

    def start(self):
        for copy in (self.sends[2], self.sends[0], self.sends[1], self.copy):
            copy.start()

    def wait(self):
        self.copy.wait()
        for slot, recv, to in self.slots:
            arrived(slot, recv, to)

    def finish(self):
        for copy in self.sends:
            copy.wait_send()


class LineScatter:
    @staticmethod
    def scratch(rows, width, here=False):
        return [pltpu.VMEM((4 if here else 5, rows, width), LOW)]

    def __init__(self, place, part, out, buffers, marks, here=False):
        self.place, self.out, self.here = place, out, here
        kept = buffers[0]
        self.rows = kept.shape[1]
        self.passed, self.above, self.below, self.two = (kept.at[index] for index in range(4))
        z = place.z
        if here:
            self.mid, self.own = part(place.at(2)), part(z)
        else:
            self.mid, self.own = kept.at[4], self.passed
            self.load_mid = pltpu.make_async_copy(part(place.at(2)), self.mid, marks.take())
            self.load_own = pltpu.make_async_copy(part(z), self.own, marks.take())
        self.recv = [marks.take() for _ in range(4)]
        self.pass_up = remote(part(3), self.passed, marks.take(), self.recv[0], place.up)
        self.pass_down = remote(part(0), self.passed, marks.take(), self.recv[0], place.down)
        self.to_down = remote(
            part(place.at(3)), self.above, marks.take(), self.recv[1], place.down
        )
        self.to_up = remote(part(place.at(1)), self.below, marks.take(), self.recv[2], place.up)
        self.to_two = remote(self.mid, self.two, marks.take(), self.recv[3], place.two)

    def start(self):
        z = self.place.z
        pl.when(z == 0)(self.pass_up.start)
        pl.when(z == 3)(self.pass_down.start)
        if not self.here:
            self.load_mid.start()
        pl.when((z == 1) | (z == 2))(self.to_down.start)
        pl.when((z == 1) | (z == 2))(self.to_up.start)

    def add(self, target, other):
        def work(rows):
            target[rows] = low(f32(target[rows]) + f32(other[rows]))

        each_rows(self.rows, 16, work)

    def middle(self):
        z = self.place.z
        if not self.here:
            self.load_mid.wait()
        pl.when(z == 0)(self.pass_up.wait_send)
        pl.when(z == 3)(self.pass_down.wait_send)

        @pl.when((z == 1) | (z == 2))
        def _():
            arrived(self.passed, self.recv[0], self.place.two)
            self.add(self.mid, self.passed)

        self.to_two.start()
        pl.when(z == 0)(self.to_up.start)
        pl.when(z == 3)(self.to_down.start)
        if not self.here:
            self.load_own.start()

    def finish(self):
        z = self.place.z
        if not self.here:
            self.load_own.wait()

        @pl.when(z < 3)
        def _():
            arrived(self.above, self.recv[1], self.place.two)
            self.add(self.own, self.above)

        @pl.when(z > 0)
        def _():
            arrived(self.below, self.recv[2], self.place.two)
            self.add(self.own, self.below)

        arrived(self.two, self.recv[3], self.place.two)
        out, own, two = self.out, self.own, self.two

        def work(rows):
            out[rows] = (f32(own[rows]) + f32(two[rows])).astype(out.dtype)

        each_rows(self.rows, 16, work)

    def drain(self):
        z = self.place.z
        pl.when(z > 0)(self.to_down.wait_send)
        pl.when(z < 3)(self.to_up.wait_send)
        self.to_two.wait_send()


def comm_params(number):
    return pltpu.CompilerParams(
        collective_id=number, has_side_effects=True, vmem_limit_bytes=62 * 1024 * 1024
    )


def comm_cost(micros):
    return pl.CostEstimate(flops=0, bytes_accessed=micros * 3_000_000, transcendentals=0)


def tables_of(lengths_row, id_col, id_row, inverse, count):
    zero = jnp.zeros((1, 1), jnp.int32)
    segment_col, segment_row = jnp.zeros_like(id_col), jnp.zeros_like(id_row)
    ends, starts, end = [], [], zero
    for index in range(count):
        starts.append(end)
        end = end + lengths_row[:, index : index + 1]
        ends.append(end)
        segment_col = segment_col + jnp.where(id_col >= end, 1, 0)
        segment_row = segment_row + jnp.where(id_row >= end, 1, 0)
    start_of = jnp.zeros_like(id_col)
    for index in range(count):
        start_of = start_of + jnp.where(segment_col == index, starts[index], 0)
    angles = f32(id_col - start_of) * inverse
    return segment_col, segment_row, jnp.cos(angles), jnp.sin(angles)


def units_split(half, half_rows, weights, out):
    for p in range(4):
        parts = []
        for weight in weights:
            for z in range(4):
                start = ((z * 4 + p) * 2 + half) * half_rows
                parts.append(f32(weight[:, start : start + half_rows]))
        out[p] = low(jnp.concatenate(parts, axis=1))


def units_joined(halves, outs, stage, marks):
    width = stage.shape[2]
    half_rows = width // 8
    copies = []
    for which, out in enumerate(outs):
        for z in range(4):
            slot = z % 2
            if len(copies) > 1:
                copies[-2].wait()
            start = (4 * which + z) * half_rows
            parts = [
                f32(columns[p][:, start : start + half_rows])
                for p in range(4)
                for columns in halves
            ]
            stage[slot] = jnp.concatenate(parts, axis=1)
            copies.append(
                pltpu.make_async_copy(
                    stage.at[slot], out.at[:, pl.ds(z * width, width)], marks.at[slot]
                )
            )
            copies[-1].start()
    for copy in copies[-2:]:
        copy.wait()


def first_kernel(
    documents,
    attn_norm,
    query_ref,
    key_ref,
    value_ref,
    gate_weight,
    up_weight,
    out_ref,
    down_ref,
    lengths_ref,
    id_col,
    id_row,
    inverse_ref,
    head_norms,
    input_ref,
    norm_ref,
    upstream_ref,
    rows_all,
    second_pieces,
    gate_rows,
    gate_all,
    above_ref,
    below_ref,
    upstream_near,
    qkv_hbm,
    out_hbm,
    raw_hbm,
    low_hbm,
    cos_hbm,
    sin_hbm,
    segment_col,
    segment_row,
    attended,
    hidden,
    normed,
    marks_ref,
    rows_ref,
    qkv_ref,
    halves,
    qkv_all,
    out_all,
    raw_out,
    low_out,
    cos_out,
    sin_out,
    lengths_all,
    row_block,
    heads_stage,
    pair_stage,
    pair_got,
):
    place = Place()
    marks = Marks(marks_ref)
    greet(place, [place.x, place.y, place.d, place.pair], True)
    rows, width = rows_ref.shape
    head_part = raw_out.shape[3]
    heads = head_part // HEAD_SIZE - 2
    lengths = Exchange(
        place, lambda p, step: lengths_ref, lambda p, step: lengths_all.at[step], marks
    )
    qkv_pieces = Exchange(
        place, lambda p, step: qkv_ref.at[p], lambda p, step: qkv_all.at[place.z, p], marks
    )
    gate_pieces = Exchange(
        place, lambda p, step: halves.at[0, p], lambda p, step: gate_rows.at[p], marks
    )
    tokens = TokensGather(place, rows_ref, rows_all, marks)
    upstream_recv = [marks.take(), marks.take()]
    upstream = [
        remote(upstream_ref, upstream_near.at[index], marks.take(), upstream_recv[index], to)
        for index, to in enumerate((place.x, place.y))
    ]
    qkv_line = LineGather(
        place, qkv_all.at[place.z], lambda z: qkv_all.at[z], marks.take(4), marks.take(4)
    )
    gate_line = LineGather(
        place, gate_rows, lambda z: gate_all.at[z], marks.take(4), marks.take(4)
    )
    out_line = LineGather(
        place, out_ref, lambda z: out_all.at[z, place.p], marks.take(4), marks.take(4)
    )
    own_copies = [
        pltpu.make_async_copy(out_ref, out_all.at[place.z, place.p], marks.take()),
    ]
    gate_copy = pltpu.make_async_copy(gate_rows, gate_all.at[place.z], marks.take())
    near_recv = [marks.take(), marks.take()]
    to_down = remote(down_ref, above_ref, marks.take(), near_recv[0], place.down)
    to_up = remote(down_ref, below_ref, marks.take(), near_recv[1], place.up)
    out_planes = []
    for turn in range(4):
        z = place.z if turn == 0 else place.at(out_line.step(turn))
        out_planes.append(
            PlaneGather(
                place,
                out_ref if turn == 0 else out_all.at[z, place.p],
                lambda p, part, z=z: out_all.at[z, p, part],
                out_ref.shape[0],
                marks.take(4),
                marks.take(4),
            )
        )
    heads_out = Exchange(
        place, lambda p, step: heads_stage.at[step], lambda p, step: attended.at[p], marks
    )
    to_pair = remote(pair_stage, pair_got, marks.take(), marks.take(), place.pair)
    fetch_marks = marks.take(2)
    qkv_copy = pltpu.make_async_copy(qkv_all, qkv_hbm, marks.take())
    out_copy = pltpu.make_async_copy(out_all, out_hbm, marks.take())
    bucket_copies = [
        pltpu.make_async_copy(raw_out, raw_hbm, marks.take()),
        pltpu.make_async_copy(low_out, low_hbm, marks.take()),
    ]
    table_copies = [
        pltpu.make_async_copy(cos_out, cos_hbm, marks.take()),
        pltpu.make_async_copy(sin_out, sin_hbm, marks.take()),
    ]

    second_copy = pltpu.make_async_copy(halves.at[1], second_pieces, marks.take())
    half_rows = down_ref.shape[1]

    lengths.start()
    for p in range(4):
        parts = []
        for weight in (query_ref, key_ref, value_ref):
            part = weight.shape[1] // 4
            parts.append(weight[:, p * part : (p + 1) * part])
        qkv_ref[p] = jnp.concatenate(parts, axis=1)
    qkv_pieces.start()
    attn_row = attn_norm[...]

    def rows_work(part):
        values = f32(input_ref[part])
        rows_ref[part] = low(values * inv_rms(values) * attn_row)

    each_rows(rows, 16, rows_work)
    tokens.start()
    units_split(0, half_rows, (gate_weight, up_weight), halves.at[0])
    gate_pieces.start()
    for copy in own_copies:
        copy.start()
    lengths.wait()
    qkv_pieces.wait()
    qkv_line.start()

    def table_work(step, carry):
        seg_col, seg_row, cosine, sine = tables_of(
            lengths_all[step][:1], id_col[...], id_row[...], inverse_ref[...], documents
        )
        segment_col[step] = seg_col
        segment_row[step] = seg_row
        cos_out[step] = cosine
        lane = lax.broadcasted_iota(jnp.int32, sine.shape, 1)
        sin_out[step] = jnp.where(lane < HEAD_SIZE // 2, -sine, sine)
        return carry

    lax.fori_loop(0, 2, table_work, 0)
    tokens.forward()
    out_planes[0].start()
    units_split(1, half_rows, (gate_weight, up_weight), halves.at[1])
    second_copy.start()
    lax.fori_loop(2, 4, table_work, 0)
    qkv_line.wait(2)
    out_line.start()
    tokens.last()
    out_planes[0].forward()
    qkv_line.wait(1)
    qkv_line.wait(3)
    out_line.wait(2)
    out_planes[2].start()
    gate_pieces.wait()
    for copy in table_copies:
        copy.start()
    qkv_copy.start()
    tokens.finish()

    def fetches(step):
        return (
            pltpu.make_async_copy(rows_all.at[step], row_block.at[0], fetch_marks.at[0]),
            pltpu.make_async_copy(rows_all.at[4 + step], row_block.at[1], fetch_marks.at[1]),
        )

    def bucket(turn, carry):
        step = 3 - turn
        for copy in fetches(step):
            copy.start()
        for copy in fetches(step):
            copy.wait()
        raw = matmul(
            row_block[...].reshape(2 * rows, width), qkv_all[...].reshape(width, head_part)
        )
        raw_out[0, step] = raw[:rows]
        raw_out[1, step] = raw[rows:]
        allowed = (segment_col[step] == segment_row[step]) & (id_row[...] <= id_col[...])
        turned = []
        for head in range(heads + 1):
            gain = head_norms[min(head // heads, 1)][None, :]
            unnormed = lanes(raw, head)
            turned.append(
                low(
                    turn_pairs(
                        unnormed * inv_rms(unnormed) * gain, cos_out[step], sin_out[step]
                    )
                )
            )
        value = low(lanes(raw, heads + 1))
        outs = [
            low(matmul(low(softmax_of(turned[head], turned[heads], allowed)), value))
            for head in range(heads)
        ]
        kept = jnp.concatenate(turned + [value], axis=1)
        low_out[0, step] = kept[:rows]
        low_out[1, step] = kept[rows:]
        outs = jnp.concatenate(outs, axis=1)
        heads_stage[step, 0] = outs[:rows]
        heads_stage[step, 1] = outs[rows:]
        for index, at in enumerate((1, 2, 3)):
            pl.when(step == at)(heads_out.sends[index].start)
        pl.when(step == 0)(heads_out.copy.start)
        return carry

    out_line.wait(1)
    out_line.wait(3)
    gate_line.start()
    gate_copy.start()
    lax.fori_loop(0, 1, bucket, 0)
    out_planes[1].start()
    out_planes[3].start()
    lax.fori_loop(1, 2, bucket, 0)
    out_planes[2].forward()
    for copy in upstream:
        copy.start()
    lax.fori_loop(2, 3, bucket, 0)
    out_planes[1].forward()
    out_planes[3].forward()
    lax.fori_loop(3, 4, bucket, 0)
    for copy in bucket_copies:
        copy.start()
    gate_line.wait(2)
    pl.when(place.z > 0)(to_down.start)
    pl.when(place.z < 3)(to_up.start)
    for plane in out_planes:
        plane.wait_far()
    for copy in own_copies:
        copy.wait()
    out_copy.start()
    heads_out.wait()

    def projected(core_step):
        block = jnp.concatenate([attended[p, core_step] for p in range(4)], axis=1)
        return matmul(block, out_all[...].reshape(block.shape[1], width))

    pair_stage[...] = low(projected(1))
    to_pair.start()
    hidden[...] = f32(input_ref[...]) + projected(0)
    to_pair.wait()
    norm_row = norm_ref[...]

    def norm_work(part):
        values = hidden[part] + f32(pair_got[part])
        hidden[part] = values
        normed[part] = low(values * inv_rms(values) * norm_row)

    each_rows(rows, 16, norm_work)
    gate_line.wait(1)
    gate_line.wait(3)
    for index, to in enumerate((place.x, place.y)):
        arrived(upstream_near.at[index], upstream_recv[index], to)
        upstream[index].wait_send()
    gate_copy.wait()
    second_copy.wait()
    for copy in [qkv_copy, out_copy] + bucket_copies + table_copies:
        copy.wait()
    parts = [lengths, qkv_pieces, gate_pieces, heads_out, qkv_line, gate_line, out_line]
    for part in parts + out_planes:
        part.finish()

    @pl.when(place.z < 3)
    def _():
        arrived(above_ref, near_recv[0], place.two)
        to_up.wait_send()

    @pl.when(place.z > 0)
    def _():
        arrived(below_ref, near_recv[1], place.two)
        to_down.wait_send()


def first_part(
    attn_norm,
    query_weight,
    key_matrix,
    value_matrix,
    gate_weight,
    up_weight,
    output_weight,
    down_weight,
    doc_lengths,
    row_ids,
    head_norms,
    layer_input,
    mlp_norm,
    grad_out,
):
    block_rows, width = layer_input.shape
    group_rows = 2 * block_rows
    weight_rows = query_weight.shape[0]
    head_part = (query_weight.shape[1] + key_matrix.shape[1] + value_matrix.shape[1]) // 4
    qkv_pieces = jax.ShapeDtypeStruct((4, weight_rows, head_part), LOW)
    gate_pieces = jax.ShapeDtypeStruct((4, weight_rows, gate_weight.shape[1] // 4), LOW)
    query_part = head_part - 2 * HEAD_SIZE
    documents = doc_lengths.shape[1]
    lengths = jnp.pad(doc_lengths, ((0, 7), (0, HEAD_SIZE - documents)))
    half = jnp.arange(HEAD_SIZE // 2, dtype=jnp.float32)
    inverse = ROPE_BASE ** (-(half * (2.0 / HEAD_SIZE)))
    low_like = lambda *shape: jax.ShapeDtypeStruct(shape, LOW)
    table = jax.ShapeDtypeStruct((4, group_rows, HEAD_SIZE), jnp.float32)
    return pl.pallas_call(
        lambda *refs: first_kernel(documents, *refs),
        out_shape=(
            low_like(8, block_rows, width),
            low_like(*gate_pieces.shape),
            low_like(*gate_pieces.shape),
            low_like(4, *gate_pieces.shape),
            low_like(*down_weight.shape),
            low_like(*down_weight.shape),
            low_like(2, block_rows, width),
            low_like(4, *qkv_pieces.shape),
            low_like(4, 4, *output_weight.shape),
            jax.ShapeDtypeStruct((2, 4, block_rows, head_part), jnp.float32),
            low_like(2, 4, block_rows, head_part),
            table,
            table,
            jax.ShapeDtypeStruct((4, group_rows, 1), jnp.int32),
            jax.ShapeDtypeStruct((4, 1, group_rows), jnp.int32),
            low_like(4, 2, block_rows, query_part),
            jax.ShapeDtypeStruct((block_rows, width), jnp.float32),
            low_like(block_rows, width),
        ),
        in_specs=[WHOLE] * 6 + [ANYWHERE] * 2 + [WHOLE] * 7 + [ANYWHERE],
        out_specs=(ANYWHERE,) * 13 + (WHOLE,) * 5,
        scratch_shapes=[
            pltpu.SemaphoreType.DMA((160,)),
            pltpu.VMEM((block_rows, width), LOW),
            pltpu.VMEM(qkv_pieces.shape, LOW),
            pltpu.VMEM((2,) + gate_pieces.shape, LOW),
            pltpu.VMEM((4,) + qkv_pieces.shape, LOW),
            pltpu.VMEM((4, 4) + output_weight.shape, LOW),
            pltpu.VMEM((2, 4, block_rows, head_part), jnp.float32),
            pltpu.VMEM((2, 4, block_rows, head_part), LOW),
            pltpu.VMEM(table.shape, jnp.float32),
            pltpu.VMEM(table.shape, jnp.float32),
            pltpu.VMEM((4,) + lengths.shape, jnp.int32),
            pltpu.VMEM((2, block_rows, width), LOW),
            pltpu.VMEM((4, 2, block_rows, query_part), LOW),
            pltpu.VMEM((block_rows, width), LOW),
            pltpu.VMEM((block_rows, width), LOW),
        ],
        compiler_params=comm_params(0),
        cost_estimate=comm_cost(130),
    )(
        attn_norm[None],
        query_weight,
        key_matrix,
        value_matrix,
        gate_weight,
        up_weight,
        output_weight,
        down_weight,
        lengths,
        row_ids[:, None],
        row_ids[None, :],
        jnp.concatenate([inverse, inverse])[None],
        head_norms,
        layer_input,
        mlp_norm[None],
        grad_out,
    )


class FarScatter:
    @staticmethod
    def scratch(rows, width):
        return [pltpu.VMEM((2, rows // 2, width), LOW)]

    def __init__(self, place, summed, buffers, marks):
        self.place, self.summed, self.landed = place, summed, buffers[0]
        self.half = summed.shape[1] // 2
        self.recv = [marks.take(), marks.take()]
        self.sends = [
            remote(
                summed.at[3, pl.ds(index * self.half, self.half)],
                self.landed.at[index],
                marks.take(),
                self.recv[index],
                to,
            )
            for index, to in enumerate((place.x, place.y))
        ]

    def start(self):
        for copy in self.sends:
            copy.start()

    def add(self):
        summed, landed = self.summed, self.landed
        for index, block, base, to in (
            (0, 2, 0, self.place.x),
            (1, 1, self.half, self.place.y),
        ):
            arrived(landed.at[index], self.recv[index], to)

            def work(rows):
                own_rows = pl.ds(pl.multiple_of(rows.start + base, 16), rows.size)
                summed[block, own_rows] = low(
                    f32(summed[block, own_rows]) + f32(landed[index, rows])
                )

            each_rows(self.half, 16, work)

    def drain(self):
        for copy in self.sends:
            copy.wait_send()


class NearScatter:
    @staticmethod
    def scratch(rows, width):
        return [pltpu.VMEM((3, rows, width), LOW)]

    def __init__(self, place, summed, buffers, marks):
        self.place, self.landed = place, buffers[0]
        self.load = pltpu.make_async_copy(summed.at[0], self.landed.at[2], marks.take())
        self.recv = [marks.take(), marks.take()]
        self.sends = [
            remote(summed.at[1 + index], self.landed.at[index], marks.take(), self.recv[index], to)
            for index, to in enumerate((place.x, place.y))
        ]

    def start(self):
        self.load.start()
        for copy in self.sends:
            copy.start()

    def finish(self, work):
        landed = self.landed
        self.load.wait()
        for index, to in enumerate((self.place.x, self.place.y)):
            arrived(self.landed.at[index], self.recv[index], to)

        def total(rows):
            work(
                rows,
                f32(landed[0, rows]) + f32(landed[1, rows]) + f32(landed[2, rows]),
            )

        each_rows(landed.shape[1], 16, total)

    def drain(self):
        for copy in self.sends:
            copy.wait_send()


class PlaneScatter:
    @staticmethod
    def scratch(rows, width):
        return [pltpu.VMEM((6, rows // 2, width), LOW)]

    def __init__(self, place, summed, out, buffers, marks, at=(0, 1, 2, 3)):
        self.place, self.summed, self.out, self.at = place, summed, out, at
        self.landed = buffers[0]
        self.rows = summed.shape[1]
        half = self.rows // 2
        top, end = pl.ds(0, half), pl.ds(half, half)
        x, y = place.x, place.y
        self.recv = [marks.take() for _ in range(6)]
        routes = (
            (summed.at[at[3], top], x),
            (summed.at[at[3], end], y),
            (summed.at[at[1], top], x),
            (summed.at[at[1], end], x),
            (summed.at[at[2], top], y),
            (summed.at[at[2], end], y),
        )
        self.sends = [
            remote(src, self.landed.at[index], marks.take(), self.recv[index], to)
            for index, (src, to) in enumerate(routes)
        ]

    def start(self):
        for index in (0, 1, 2, 5):
            self.sends[index].start()

    def landed_at(self, index, to):
        arrived(self.landed.at[index], self.recv[index], to)

    def middle(self):
        half = self.rows // 2
        summed, landed = self.summed, self.landed
        _, for_x, for_y, _ = self.at
        self.landed_at(0, self.place.x)

        def top_work(rows):
            summed[for_y, rows] = low(f32(summed[for_y, rows]) + f32(landed[0, rows]))

        each_rows(half, 16, top_work)
        self.sends[4].start()
        self.landed_at(1, self.place.y)

        def end_work(rows):
            end_rows = pl.ds(pl.multiple_of(rows.start + half, 16), rows.size)
            summed[for_x, end_rows] = low(f32(summed[for_x, end_rows]) + f32(landed[1, rows]))

        each_rows(half, 16, end_work)
        self.sends[3].start()

    def finish(self):
        half = self.rows // 2
        for index, to in ((2, self.place.x), (5, self.place.y), (4, self.place.y), (3, self.place.x)):
            self.landed_at(index, to)

        for base, first, second in ((0, 2, 4), (half, 3, 5)):

            def work(rows):
                own_rows = pl.ds(pl.multiple_of(rows.start + base, 16), rows.size)
                self.out[own_rows] = (
                    f32(self.summed[self.at[0], own_rows])
                    + f32(self.landed[first, rows])
                    + f32(self.landed[second, rows])
                ).astype(self.out.dtype)

            each_rows(half, 16, work)

    def drain(self):
        for copy in self.sends:
            copy.wait_send()


def blocks_of(source, block_ref, marks, first, last, work):
    def fetch(block):
        return pltpu.make_async_copy(
            source(block), block_ref.at[block % 2], marks.at[block % 2]
        )

    fetch(first).start()

    def body(block, carry):
        fetch(block).wait()

        @pl.when(block < last - 1)
        def _():
            fetch(block + 1).start()

        work(block, block_ref[block % 2])
        return carry

    lax.fori_loop(first, last, body, 0)


def unit_values(raws, inner_grad):
    units = inner_grad.shape[1]
    gate_raw, up_raw = raws[:, :units], raws[:, units:]
    sigmoid_gate = jax.nn.sigmoid(gate_raw)
    activated = gate_raw * sigmoid_gate
    gate_grad = inner_grad * up_raw * sigmoid_gate * (1.0 + gate_raw * (1.0 - sigmoid_gate))
    return low(activated * up_raw), jnp.concatenate(
        [low(gate_grad), low(inner_grad * activated)], axis=1
    )


def units_kernel(
    rows_ref,
    upstream_ref,
    near_ref,
    pieces_ref,
    first_ref,
    down_ref,
    above_ref,
    below_ref,
    rows_all,
    upstream_all,
    line_ref,
    inner_out,
    second_grad,
    first_sum,
    down_part,
    part_sums,
    grad_sums,
    marks_ref,
    first_mat,
    second_mat,
    down_mat,
    upstream,
    row_block,
    row_slab,
    inner_first,
    first_grad,
    inner_grads,
    first_part,
    inner_stage,
    second_stage,
    *buffers,
):
    place = Place()
    marks = Marks(marks_ref)
    greet(place, [place.x, place.y, place.d, place.pair], True)
    tokens = TokensGather(place, rows_ref, rows_all, marks)
    upstream_tokens = TokensGather(place, upstream_ref, upstream, marks)
    pieces = Exchange(
        place, lambda p, step: pieces_ref.at[p], lambda p, step: line_ref.at[p], marks
    )
    keep = pltpu.make_async_copy(upstream, upstream_all, marks.take())
    line = LineGather(place, line_ref, lambda z: second_mat.at[z], marks.take(4), marks.take(4))
    far_recv = marks.take(2)
    two = down_mat.at[:, place.at(2)]
    to_two = remote(down_ref, down_mat.at[:, place.z], marks.take(), far_recv.at[0], place.two)
    pass_mark = marks.take()
    pass_down = remote(two, two, pass_mark, far_recv.at[1], place.down)
    pass_up = remote(two, two, pass_mark, far_recv.at[1], place.up)
    copies = [
        pltpu.make_async_copy(first_ref, first_mat, marks.take()),
        pltpu.make_async_copy(down_ref, down_mat.at[:, place.z], marks.take()),
    ]
    line_copy = pltpu.make_async_copy(line_ref, second_mat.at[place.z], marks.take())
    above = pltpu.make_async_copy(above_ref, down_mat.at[:, place.at(1)], marks.take())
    below = pltpu.make_async_copy(below_ref, down_mat.at[:, place.at(3)], marks.take())
    line_rows = first_sum.shape[0]
    first_line = LineScatter(
        place,
        lambda z: first_part.at[pl.ds(pl.multiple_of(z * line_rows, 16), line_rows)],
        first_sum,
        buffers[:1],
        marks,
        True,
    )
    part_far = FarScatter(place, part_sums, buffers[1:2], marks)
    grad_far = FarScatter(place, grad_sums, buffers[2:], marks)
    fetch_marks, slab_marks = marks.take(2), marks.take(2)
    send_marks, recv_marks = marks.take(8), marks.take(8)
    width = rows_ref.shape[1]
    half = inner_first.shape[2]
    all_rows = 8 * rows_ref.shape[0]

    to_two.start()
    pieces.start()
    tokens.start()
    for copy in copies:
        copy.start()
    pl.when(place.z < 3)(above.start)
    pl.when(place.z > 0)(below.start)
    tokens.forward()
    upstream_tokens.start_near(near_ref, marks)
    pieces.wait()
    line_copy.start()
    arrived(two, far_recv.at[0], place.two)
    pl.when(place.z == 1)(pass_down.start)
    pl.when(place.z == 2)(pass_up.start)
    line.start()
    tokens.last()
    upstream_tokens.last()
    for copy in copies:
        copy.wait()
    line_copy.wait()
    pl.when(place.z < 3)(above.wait)
    pl.when(place.z > 0)(below.wait)

    @pl.when(place.z == 0)
    def _():
        arrived(down_mat.at[:, 3], far_recv.at[1], place.two)

    @pl.when(place.z == 3)
    def _():
        arrived(down_mat.at[:, 0], far_recv.at[1], place.two)

    tokens.finish()
    upstream_tokens.finish_near()
    keep.start()
    pieces.finish()

    def first_work(block, values):
        grads = matmul_nt(upstream[block], down_mat[...].reshape(2 * half, width))
        inner_grads[block] = low(grads[:, half:])
        inner, grad = unit_values(matmul(values, first_mat[...]), grads[:, :half])
        inner_first[block] = inner
        first_grad[block] = grad

    blocks_of(lambda block: rows_all.at[block], row_block, fetch_marks, 0, 8, first_work)
    tile = row_slab.shape[3]
    tiles = width // tile

    def slab(index):
        return rows_all.at[:, :, pl.ds(pl.multiple_of(index * tile, tile), tile)]

    def slab_work(index, values):
        first_part[pl.ds(pl.multiple_of(index * tile, tile), tile)] = low(
            matmul_tn(values.reshape(all_rows, tile), first_grad[...].reshape(all_rows, 2 * half))
        )

    down_part[...] = low(
        matmul_tn(
            inner_first[...].reshape(all_rows, half), upstream[...].reshape(all_rows, width)
        )
    )
    line.wait(2)
    blocks_of(slab, row_slab, slab_marks, 0, tiles, slab_work)
    first_line.start()
    line.wait(1)
    line.wait(3)

    def fetch(index):
        step, slot = 3 - index // 2, index % 2
        return pltpu.make_async_copy(
            rows_all.at[step + 4 * (1 - slot)], row_block.at[slot], fetch_marks.at[slot]
        )

    def sends(step):
        return (
            remote(
                upstream.at[step],
                part_sums.at[step],
                send_marks.at[step],
                recv_marks.at[step],
                place.pair,
            ),
            remote(
                upstream.at[4 + step],
                grad_sums.at[step],
                send_marks.at[4 + step],
                recv_marks.at[4 + step],
                place.pair,
            ),
        )

    keep.wait()
    store_marks = marks.take(4)

    def stores(slot, block):
        return (
            pltpu.make_async_copy(
                inner_stage.at[slot], inner_out.at[block], store_marks.at[slot]
            ),
            pltpu.make_async_copy(
                second_stage.at[slot], second_grad.at[block], store_marks.at[2 + slot]
            ),
        )

    fetch(0).start()

    def blocks(turn, carry):
        step = 3 - turn
        for slot in range(2):
            index = 2 * turn + slot
            block = step + 4 * (1 - slot)
            fetch(index).wait()

            @pl.when(index < 7)
            def _():
                fetch(index + 1).start()

            second = second_mat[...].reshape(width, 2 * half)
            inner, grad = unit_values(matmul(row_block[slot], second), f32(inner_grads[block]))

            @pl.when(turn > 0)
            def _():
                for copy in stores(slot, block + 1):
                    copy.wait()

            inner_stage[slot] = inner
            second_stage[slot] = grad
            for copy in stores(slot, block):
                copy.start()
            part = matmul(
                jnp.concatenate([inner_first[block], inner], axis=1),
                down_mat[...].reshape(2 * half, width),
            )
            grad = matmul_nt(first_grad[block], first_mat[...]) + matmul_nt(grad, second)
            if slot == 0:
                upstream[step] = low(part)
                upstream[4 + step] = low(grad)
                for copy in sends(step):
                    copy.start()
            else:
                for copy in sends(step):
                    copy.wait_recv()
                part_sums[step] = low(part + f32(part_sums[step]))
                grad_sums[step] = low(grad + f32(grad_sums[step]))
        return carry

    lax.fori_loop(0, 1, blocks, 0)
    grad_far.start()
    part_far.start()
    first_line.middle()
    lax.fori_loop(1, 4, blocks, 0)
    for slot in range(2):
        for copy in stores(slot, 4 * (1 - slot)):
            copy.wait()
    grad_far.add()
    part_far.add()
    first_line.finish()
    first_line.drain()
    grad_far.drain()
    part_far.drain()
    for step in range(4):
        for copy in sends(step):
            copy.wait_send()
    line.finish()
    to_two.wait_send()
    pl.when(place.z == 1)(pass_down.wait_send)
    pl.when(place.z == 2)(pass_up.wait_send)


def units_products(rows, upstream, near, second_pieces, first_all, down_weight, above, below):
    block_rows, width = rows.shape
    half = first_all.shape[1] // 2
    half_rows = down_weight.shape[1]
    second_rows = jax.ShapeDtypeStruct((4 * second_pieces.shape[1], 2 * half), LOW)
    hidden = lambda count: jax.ShapeDtypeStruct((8, block_rows, count * half), LOW)
    sums = jax.ShapeDtypeStruct((4, block_rows, width), LOW)
    blocks = jax.ShapeDtypeStruct((8, block_rows, width), LOW)
    return pl.pallas_call(
        units_kernel,
        out_shape=(
            blocks,
            blocks,
            jax.ShapeDtypeStruct(second_pieces.shape, LOW),
            hidden(1),
            hidden(2),
            jax.ShapeDtypeStruct(second_rows.shape, LOW),
            jax.ShapeDtypeStruct((half, width), LOW),
            sums,
            sums,
        ),
        in_specs=[ANYWHERE] * 8,
        out_specs=(ANYWHERE,) * 5 + (WHOLE,) * 4,
        scratch_shapes=[
            pltpu.SemaphoreType.DMA((140,)),
            pltpu.VMEM(first_all.shape, LOW),
            pltpu.VMEM((4,) + second_pieces.shape, LOW),
            pltpu.VMEM((2, 4, half_rows, width), LOW),
            pltpu.VMEM((8, block_rows, width), LOW),
            pltpu.VMEM((2, block_rows, width), LOW),
            pltpu.VMEM((2, 8, block_rows, 256), LOW),
            pltpu.VMEM((8, block_rows, half), LOW),
            pltpu.VMEM((8, block_rows, 2 * half), LOW),
            pltpu.VMEM((8, block_rows, half), LOW),
            pltpu.VMEM((width, 2 * half), LOW),
            pltpu.VMEM((2, block_rows, half), LOW),
            pltpu.VMEM((2, block_rows, 2 * half), LOW),
        ]
        + LineScatter.scratch(*second_rows.shape, True)
        + FarScatter.scratch(block_rows, width) * 2,
        compiler_params=comm_params(1),
        cost_estimate=comm_cost(150),
    )(rows, upstream, near, second_pieces, first_all, down_weight, above, below)


def unit_grads_kernel(
    rows_all,
    upstream_ref,
    inner_ref,
    second_ref,
    down_first,
    part_sums,
    grad_sums,
    hidden_ref,
    upstream_own,
    norm_ref,
    layer_out,
    hidden_grad,
    branch,
    mlp_gain,
    down_out,
    second_part,
    marks_ref,
    upstream,
    inner,
    second_grad,
    row_slab,
    gain_rows,
    down_part,
    *buffers,
):
    place = Place()
    marks = Marks(marks_ref)
    greet(place, [place.x, place.y], True)
    grad_near = NearScatter(place, grad_sums, buffers[:1], marks)
    part_near = NearScatter(place, part_sums, buffers[1:2], marks)
    half_rows = down_out.shape[1]
    first_line = LineScatter(
        place, lambda z: down_first.at[z], down_out.at[0], buffers[2:3], marks
    )
    second_line = LineScatter(
        place,
        lambda z: down_part.at[pl.ds(pl.multiple_of(z * half_rows, 16), half_rows)],
        down_out.at[1],
        buffers[3:],
        marks,
        True,
    )
    loads = [
        pltpu.make_async_copy(upstream_ref, upstream, marks.take()),
        pltpu.make_async_copy(inner_ref, inner, marks.take()),
        pltpu.make_async_copy(second_ref, second_grad, marks.take()),
    ]
    slab_marks = marks.take(2)
    rows, width = hidden_ref.shape
    half = inner.shape[2]
    all_rows = 8 * rows
    tile = row_slab.shape[3]
    tiles = width // tile

    def slab(index):
        return rows_all.at[:, :, pl.ds(pl.multiple_of(index * tile, tile), tile)]

    def slab_work(index, values):
        second_part[pl.ds(pl.multiple_of(index * tile, tile), tile)] = low(
            matmul_tn(values.reshape(all_rows, tile), second_grad[...].reshape(all_rows, 2 * half))
        )

    first_line.start()
    grad_near.start()
    for copy in loads:
        copy.start()
    loads[0].wait()
    loads[1].wait()
    down_part[...] = low(
        matmul_tn(inner[...].reshape(all_rows, half), upstream[...].reshape(all_rows, width))
    )
    first_line.middle()
    second_line.start()
    loads[2].wait()
    blocks_of(slab, row_slab, slab_marks, 0, tiles, slab_work)
    second_line.middle()
    part_near.start()
    gain_rows[...] = jnp.zeros_like(gain_rows)
    norm_row = norm_ref[...]

    def norm_work(rows, row_grad):
        values = hidden_ref[rows]
        scales = inv_rms(values)
        weighted = row_grad * norm_row
        inner_mean = jnp.mean(weighted * values, axis=-1, keepdims=True)
        grad = (
            f32(upstream_own[rows])
            + scales * weighted
            - values * (scales * scales * scales) * inner_mean
        )
        hidden_grad[rows] = grad
        branch[rows] = low(grad)
        parts = row_grad * values * scales
        gain_rows[...] += parts[:8] + parts[8:]

    def out_work(rows, row_part):
        layer_out[rows] = low(hidden_ref[rows] + row_part)

    grad_near.finish(norm_work)
    mlp_gain[...] = jnp.sum(gain_rows[...], axis=0, keepdims=True)
    part_near.finish(out_work)
    first_line.finish()
    second_line.finish()
    for part in (first_line, second_line, grad_near, part_near):
        part.drain()


def unit_grads(
    rows_all,
    upstream,
    inner,
    second_grad,
    down_first,
    part_sums,
    grad_sums,
    hidden,
    upstream_own,
    norm,
):
    _, rows, width = rows_all.shape
    half = inner.shape[2]
    half_rows = down_first.shape[1]
    return pl.pallas_call(
        unit_grads_kernel,
        out_shape=(
            jax.ShapeDtypeStruct((rows, width), LOW),
            jax.ShapeDtypeStruct((rows, width), jnp.float32),
            jax.ShapeDtypeStruct((rows, width), LOW),
            jax.ShapeDtypeStruct((1, width), jnp.float32),
            jax.ShapeDtypeStruct((2, half_rows, width), jnp.float32),
            jax.ShapeDtypeStruct((width, 2 * half), LOW),
        ),
        in_specs=[ANYWHERE] * 7 + [WHOLE] * 3,
        out_specs=(WHOLE,) * 6,
        scratch_shapes=[
            pltpu.SemaphoreType.DMA((64,)),
            pltpu.VMEM(upstream.shape, LOW),
            pltpu.VMEM(inner.shape, LOW),
            pltpu.VMEM(second_grad.shape, LOW),
            pltpu.VMEM((2, 8, rows, 256), LOW),
            pltpu.VMEM((8, width), jnp.float32),
            pltpu.VMEM((half, width), LOW),
        ]
        + NearScatter.scratch(rows, width) * 2
        + LineScatter.scratch(half_rows, width)
        + LineScatter.scratch(half_rows, width, True),
        compiler_params=comm_params(4),
        cost_estimate=comm_cost(65),
    )(
        rows_all,
        upstream,
        inner,
        second_grad,
        down_first,
        part_sums,
        grad_sums,
        hidden,
        upstream_own,
        norm,
    )


def turn_pairs(values, cosine, sine):
    return values * cosine + pltpu.roll(values, HEAD_SIZE // 2, 1) * sine


def softmax_of(query, key, allowed):
    scores = matmul_nt(query, key) * HEAD_SIZE ** (-0.5)
    masked = jnp.where(allowed, scores, MASKED)
    exponent = jnp.exp(masked - jnp.max(masked, axis=-1, keepdims=True))
    return exponent / jnp.sum(exponent, axis=-1, keepdims=True)


def lanes(values, head):
    return values[:, head * HEAD_SIZE : (head + 1) * HEAD_SIZE]


def roll_half(values):
    return pltpu.roll(values, HEAD_SIZE // 2, 1)


def attend_back_values(raw, kept, grad, allowed, cosine, sine, gains_ref, roll=roll_half):
    group_rows = raw.shape[0]
    heads = raw.shape[1] // HEAD_SIZE - 2
    key, value = lanes(kept, heads), lanes(kept, heads + 1)
    scale = HEAD_SIZE ** (-0.5)
    turned_grads = []
    key_grad = jnp.zeros((group_rows, HEAD_SIZE), jnp.float32)
    value_grad = jnp.zeros((group_rows, HEAD_SIZE), jnp.float32)
    for head in range(heads):
        query, upstream = lanes(kept, head), lanes(grad, head)
        probs = softmax_of(query, key, allowed)
        probs_grad = matmul_nt(upstream, value)
        scores_grad = low(
            probs * (probs_grad - jnp.sum(probs * probs_grad, axis=-1, keepdims=True))
        )
        turned_grads.append(matmul(scores_grad, key) * scale)
        key_grad = key_grad + matmul_tn(scores_grad, query)
        value_grad = value_grad + matmul_tn(low(probs), upstream)
    turned_grads.append(key_grad * scale)
    outs, gains = [], []
    for head in range(heads + 1):
        gain = gains_ref[min(head // heads, 1)][None, :]
        unnormed = lanes(raw, head)
        upstream = turned_grads[head] * cosine - roll(turned_grads[head]) * sine
        grad_raw, gain_part = norm_back(unnormed, inv_rms(unnormed), gain, upstream)
        outs.append(low(grad_raw))
        gains.append(gain_part[None, :])
    outs.append(low(value_grad))
    query_gain = sum(gains[1:heads], gains[0])
    return (jnp.concatenate(outs, axis=1), jnp.concatenate([query_gain, gains[heads]], axis=1))


def heads_back_kernel(
    branch_ref,
    out_ref,
    attended_ref,
    raw_ref,
    low_ref,
    cos_ref,
    sin_ref,
    segment_col,
    segment_row,
    id_col,
    id_row,
    gains_ref,
    rows_all,
    qkv_ref,
    second_part,
    first_rows,
    input_ref,
    hidden_ref,
    norm_ref,
    mlp_gain,
    grad_ref,
    query_out,
    key_out,
    value_out,
    proj_out,
    gate_out,
    up_out,
    attn_gain_out,
    mlp_gain_out,
    head_gain_out,
    marks_ref,
    qkv_columns,
    first_columns,
    second_columns,
    joined_stage,
    qkv_part,
    proj_sum,
    grad_sums,
    line_sum,
    qkv_sum,
    gain_rows,
    gain_mine,
    gain_got,
    out_mat,
    qkv_mat,
    attended,
    branch,
    own_grad,
    heads_grad,
    raw_block,
    low_block,
    qkv_grad,
    row_slab,
    proj_part,
    *buffers,
):
    place = Place()
    marks = Marks(marks_ref)
    greet(place, [place.x, place.y, place.d, place.pair], True)
    rows, width = branch_ref.shape
    half_heads = heads_grad.shape[2]
    group_rows = 2 * rows
    second_line = LineScatter(place, lambda z: second_part.at[z], line_sum, buffers[0:1], marks)
    first_pieces = Exchange(
        place, lambda p, step: first_rows.at[p], lambda p, step: first_columns.at[p], marks
    )
    proj_plane = PlaneScatter(
        place,
        proj_part,
        proj_sum,
        buffers[1:2],
        marks,
        (place.p, place.px, place.py, place.pd),
    )
    tokens = PlaneScatter(place, grad_sums, grad_ref, buffers[2:3], marks)
    qkv_rows, proj_rows = qkv_sum.shape[0], proj_out.shape[0]
    qkv_line = LineScatter(
        place,
        lambda z: qkv_part.at[pl.ds(pl.multiple_of(z * qkv_rows, 16), qkv_rows)],
        qkv_sum,
        buffers[3:4],
        marks,
        True,
    )
    proj_line = LineScatter(
        place,
        lambda z: proj_sum.at[pl.ds(pl.multiple_of(z * proj_rows, 16), proj_rows)],
        proj_out,
        buffers[4:],
        marks,
        True,
    )
    piece_rows, second_piece = qkv_rows // 4, line_sum.shape[0] // 4
    qkv_pieces = Exchange(
        place,
        lambda p, step: qkv_sum.at[pl.ds(pl.multiple_of(p * piece_rows, 16), piece_rows)],
        lambda p, step: qkv_columns.at[p],
        marks,
    )
    second_pieces = Exchange(
        place,
        lambda p, step: line_sum.at[pl.ds(pl.multiple_of(p * second_piece, 16), second_piece)],
        lambda p, step: second_columns.at[p],
        marks,
    )
    near_z = {"f": place.z + 1 - 2 * (place.z % 2)}
    rounds = [
        remote(gain_mine.at[index], gain_got.at[index], marks.take(), marks.take(), to)
        for index, to in enumerate((place.pair, place.x, place.y, near_z, place.two))
    ]
    heads = Exchange(
        place, lambda p, step: own_grad.at[p], lambda p, step: heads_grad.at[step], marks
    )
    to_pair = remote(branch_ref, branch.at[1], marks.take(), marks.take(), place.pair)
    loads = [
        pltpu.make_async_copy(branch_ref, branch.at[0], marks.take()),
        pltpu.make_async_copy(out_ref, out_mat, marks.take()),
        pltpu.make_async_copy(attended_ref, attended, marks.take()),
        pltpu.make_async_copy(qkv_ref, qkv_mat, marks.take()),
    ]
    fetch_marks, slab_marks = marks.take(4), marks.take(2)
    send_marks, recv_marks = marks.take(4), marks.take(4)

    to_pair.start()
    second_line.start()
    for copy in loads:
        copy.start()
    for copy in loads:
        copy.wait()

    def own_half(core_step):
        grad = low(matmul_nt(branch[core_step], out_mat[...]))
        for p in range(4):
            own_grad[p, pl.ds(core_step * rows, rows)] = grad[
                :, p * half_heads : (p + 1) * half_heads
            ]

    own_half(0)
    to_pair.wait()
    own_half(1)
    heads.start()
    second_line.middle()

    def proj_work(z, carry):
        block = attended[z].reshape(group_rows, half_heads)
        grad = low(matmul_tn(block, branch[...].reshape(group_rows, width)))
        part = half_heads // 4
        for p in range(4):
            proj_part[p, pl.ds(pl.multiple_of(z * part, part), part)] = grad[
                p * part : (p + 1) * part
            ]
        return carry

    def fetches(step):
        return (
            pltpu.make_async_copy(raw_ref.at[:, step], raw_block, fetch_marks.at[0]),
            pltpu.make_async_copy(low_ref.at[:, step], low_block, fetch_marks.at[1]),
        )

    lax.fori_loop(0, 4, proj_work, 0)
    heads.wait()
    proj_plane.start()
    first_pieces.start()
    head_width = 2 * HEAD_SIZE
    head_gain = gain_mine.at[0, :, pl.ds(2 * width, head_width)]
    head_gain[...] = jnp.zeros((1, head_width), jnp.float32)

    def sends(step):
        return remote(
            out_mat.at[pl.ds(pl.multiple_of(step * rows, rows), rows)],
            grad_sums.at[step],
            send_marks.at[step],
            recv_marks.at[step],
            place.pair,
        )

    def bucket(step, carry):
        for copy in fetches(step):
            copy.start()
        for copy in fetches(step):
            copy.wait()
        allowed = (segment_col[step] == segment_row[step]) & (id_row[...] <= id_col[...])
        grads, gains = attend_back_values(
            raw_block[...].reshape(group_rows, -1),
            low_block[...].reshape(group_rows, -1),
            heads_grad[step],
            allowed,
            cos_ref[step],
            sin_ref[step],
            gains_ref,
        )
        head_gain[...] += gains
        qkv_grad[0, step] = grads[:rows]
        qkv_grad[1, step] = grads[rows:]
        out_mat[pl.ds(pl.multiple_of(step * rows, rows), rows)] = low(
            matmul_nt(grads[rows:], qkv_mat[...])
        )
        sends(step).start()
        return carry

    lax.fori_loop(0, 2, bucket, 0)
    proj_plane.middle()
    lax.fori_loop(2, 4, bucket, 0)

    tile = row_slab.shape[3]
    tiles = width // tile

    def slab(index):
        return pltpu.make_async_copy(
            rows_all.at[:, :, pl.ds(pl.multiple_of(index * tile, tile), tile)],
            row_slab.at[index % 2],
            slab_marks.at[index % 2],
        )

    slab(0).start()

    def own_work(step, carry):
        copy = sends(step)
        copy.wait_recv()
        grad = matmul_nt(qkv_grad[0, step], qkv_mat[...])
        grad_sums[step] = low(grad + f32(grad_sums[step]))
        return carry

    def row_tile(index, carry):
        slab(index).wait()

        @pl.when(index < tiles - 1)
        def _():
            slab(index + 1).start()

        block = row_slab[index % 2].reshape(4 * group_rows, tile)
        out_rows = pl.ds(pl.multiple_of(index * tile, tile), tile)
        qkv_part[out_rows] = low(
            matmul_tn(block, qkv_grad[...].reshape(4 * group_rows, qkv_grad.shape[3]))
        )
        return carry

    lax.fori_loop(0, tiles, row_tile, 0)
    qkv_line.start()
    lax.fori_loop(0, 4, own_work, 0)
    tokens.start()
    second_line.finish()
    proj_plane.finish()
    proj_line.start()
    tokens.middle()
    second_pieces.start()
    qkv_line.middle()
    proj_line.middle()
    tokens.finish()

    gain_rows[...] = jnp.zeros_like(gain_rows)
    norm_row = norm_ref[...]

    def norm_work(part):
        values = f32(input_ref[part])
        scales = inv_rms(values)
        upstream = grad_ref[part]
        weighted = upstream * norm_row
        inner_mean = jnp.mean(weighted * values, axis=-1, keepdims=True)
        grad_ref[part] = (
            hidden_ref[part]
            + scales * weighted
            - values * (scales * scales * scales) * inner_mean
        )
        parts = upstream * values * scales
        gain_rows[...] += parts[:8] + parts[8:]

    each_rows(rows, 16, norm_work)
    gain_mine[0, :, pl.ds(0, width)] = jnp.sum(gain_rows[...], axis=0, keepdims=True)
    gain_mine[0, :, pl.ds(width, width)] = mlp_gain[...]
    for index, copy in enumerate(rounds):
        copy.start()
        copy.wait()
        summed = gain_mine[index] + gain_got[index]
        if index < 4:
            gain_mine[index + 1] = summed
        else:
            attn_gain_out[...] = summed[:, :width]
            mlp_gain_out[...] = summed[:, width : 2 * width]
            head_gain_out[...] = summed[:, 2 * width :]
    qkv_line.finish()
    qkv_pieces.start()
    proj_line.finish()
    for step in range(4):
        sends(step).wait_send()
    heads.finish()
    for part in (proj_plane, second_line, qkv_line, proj_line, tokens):
        part.drain()
    for part in (first_pieces, second_pieces):
        part.wait()
        part.finish()
    units_joined(
        (first_columns, second_columns), (gate_out, up_out), joined_stage, marks.take(2)
    )
    qkv_pieces.wait()
    qkv_pieces.finish()
    for p in range(4):
        start = 0
        for out in (query_out, key_out, value_out):
            part = out.shape[1] // 4
            out[:, p * part : (p + 1) * part] = f32(qkv_columns[p][:, start : start + part])
            start += part


def heads_backward(
    branch,
    out_all,
    attended,
    raw,
    kept,
    tables,
    rows_all,
    qkv_all,
    second_part,
    first_rows,
    layer_input,
    hidden_grad,
    norm,
    mlp_gain,
):
    rows, width = branch.shape
    head_part = raw.shape[3]
    query_part = head_part - 2 * HEAD_SIZE
    line_rows, units = second_part.shape[1:]
    qkv_rows = width // 4
    tile = 256
    gain_width = 2 * width + 2 * HEAD_SIZE
    weight_rows = line_rows // 4
    pieces = pltpu.VMEM((4, weight_rows, units), LOW)
    wide = lambda *shape: jax.ShapeDtypeStruct(shape, jnp.float32)
    return pl.pallas_call(
        heads_back_kernel,
        out_shape=(
            wide(rows, width),
            wide(weight_rows, 4 * query_part),
            wide(weight_rows, 4 * HEAD_SIZE),
            wide(weight_rows, 4 * HEAD_SIZE),
            wide(query_part // 4, width),
            wide(weight_rows, 4 * units),
            wide(weight_rows, 4 * units),
            wide(1, width),
            wide(1, width),
            wide(1, 2 * HEAD_SIZE),
        ),
        in_specs=[ANYWHERE] * 5
        + [WHOLE] * len(tables)
        + [ANYWHERE] * 4
        + [WHOLE] * 4,
        out_specs=(WHOLE,) * 5 + (ANYWHERE,) * 2 + (WHOLE,) * 3,
        scratch_shapes=[
            pltpu.SemaphoreType.DMA((160,)),
            pltpu.VMEM((4, weight_rows, head_part), LOW),
            pieces,
            pieces,
            pltpu.VMEM((2, weight_rows, units), jnp.float32),
            pltpu.VMEM((width, head_part), LOW),
            pltpu.VMEM((query_part, width), LOW),
            pltpu.VMEM((4, rows, width), LOW),
            pltpu.VMEM((line_rows, units), LOW),
            pltpu.VMEM((qkv_rows, head_part), LOW),
            pltpu.VMEM((8, width), jnp.float32),
            pltpu.VMEM((5, 1, gain_width), jnp.float32),
            pltpu.VMEM((5, 1, gain_width), jnp.float32),
            pltpu.VMEM(out_all.shape, LOW),
            pltpu.VMEM(qkv_all.shape, LOW),
            pltpu.VMEM(attended.shape, LOW),
            pltpu.VMEM((2, rows, width), LOW),
            pltpu.VMEM((4, 2 * rows, query_part), LOW),
            pltpu.VMEM((4, 2 * rows, query_part), LOW),
            pltpu.VMEM((2, rows, head_part), jnp.float32),
            pltpu.VMEM((2, rows, head_part), LOW),
            pltpu.VMEM((2, 4, rows, head_part), LOW),
            pltpu.VMEM((2, 8, rows, tile), LOW),
            pltpu.VMEM((4, query_part, width), LOW),
        ]
        + LineScatter.scratch(line_rows, units)
        + PlaneScatter.scratch(query_part, width)
        + PlaneScatter.scratch(rows, width)
        + LineScatter.scratch(qkv_rows, head_part, True)
        + LineScatter.scratch(query_part // 4, width, True),
        compiler_params=comm_params(3),
        cost_estimate=comm_cost(120),
    )(
        branch,
        out_all,
        attended,
        raw,
        kept,
        *tables,
        rows_all,
        qkv_all,
        second_part,
        first_rows,
        layer_input,
        hidden_grad,
        norm,
        mlp_gain,
    )


def row_ids_of(local_rows):
    core = lax.axis_index("tensor")
    local_ids = jnp.arange(local_rows, dtype=jnp.int32)
    return jnp.concatenate([core * local_rows + local_ids, (1 - core) * local_rows + local_ids])


def heads_of(weight):
    return weight.reshape(weight.shape[0], 4, -1).transpose(1, 0, 2)


def heads_back(pieces):
    return f32(pieces).transpose(1, 0, 2).reshape(pieces.shape[1], -1)


def units_of(weight, down_rows):
    split = weight.reshape(weight.shape[0], -1, 4, down_rows)
    return split.transpose(2, 0, 1, 3).reshape(4, weight.shape[0], -1)


def units_back(pieces, down_rows):
    rows = pieces.shape[1]
    return f32(pieces).reshape(4, rows, -1, down_rows).transpose(1, 2, 0, 3).reshape(rows, -1)


def shards(*arguments):
    if lax.axis_size("f") == 4:
        return line_of_four(*arguments)
    return any_line(*arguments)


def line_of_four(
    layer_input,
    attn_norm,
    head_norms,
    query_weight,
    key_matrix,
    value_matrix,
    output_weight,
    mlp_norm,
    gate_weight,
    up_weight,
    down_weight,
    grad_out,
    doc_lengths,
):
    local_rows, model_width = layer_input.shape
    weight_rows = gate_weight.shape[0]
    down_rows = down_weight.shape[0]
    half_rows = down_rows // 2
    half = 4 * half_rows
    head_part = (query_weight.shape[1] + key_matrix.shape[1] + value_matrix.shape[1]) // 4
    down_halves = down_weight.reshape(2, half_rows, model_width)
    row_ids = row_ids_of(local_rows)
    (
        normed_attn,
        second_pieces,
        _,
        first_all,
        above,
        below,
        grad_near,
        qkv_all,
        out_all,
        qkv_raw,
        qkv_low,
        cos_tab,
        sin_tab,
        segment_col,
        segment_row,
        attended,
        hidden_state,
        normed_mlp,
    ) = first_part(
        attn_norm,
        query_weight,
        key_matrix,
        value_matrix,
        gate_weight,
        up_weight,
        output_weight,
        down_halves,
        doc_lengths,
        row_ids,
        head_norms,
        layer_input,
        mlp_norm,
        grad_out,
    )
    tables = (
        cos_tab,
        sin_tab,
        segment_col,
        segment_row,
        row_ids[:, None],
        row_ids[None, :],
        head_norms,
    )
    (
        rows_all,
        grad_all,
        _,
        inner_low,
        second_grad,
        first_rows,
        grad_down_first,
        part_sums,
        grad_sums,
    ) = (
        units_products(
            normed_mlp,
            grad_out,
            grad_near,
            second_pieces,
            first_all.reshape(model_width, 2 * half),
            down_halves,
            above,
            below,
        )
    )
    line_shape = (4, 4 * weight_rows, 2 * half)
    (
        layer_out,
        hidden_grad,
        branch_grad,
        mlp_gain_part,
        grad_down,
        grad_second,
    ) = unit_grads(
        rows_all,
        grad_all,
        inner_low,
        second_grad,
        grad_down_first.reshape(4, half_rows, model_width),
        part_sums,
        grad_sums,
        hidden_state,
        grad_out,
        mlp_norm[None],
    )
    (
        grad_input,
        grad_query,
        grad_key,
        grad_value,
        grad_out_proj,
        grad_gate,
        grad_up,
        attn_gain,
        mlp_gain,
        head_gains,
    ) = (
        heads_backward(
            branch_grad,
            out_all.reshape(-1, model_width),
            attended,
            qkv_raw,
            qkv_low,
            tables,
            normed_attn,
            qkv_all.reshape(model_width, head_part),
            grad_second.reshape(line_shape),
            first_rows.reshape(4, weight_rows, 2 * half),
            layer_input,
            hidden_grad,
            attn_norm[None],
            mlp_gain_part,
        )
    )
    return (
        layer_out,
        grad_input,
        attn_gain.reshape(-1),
        head_gains.reshape(2, HEAD_SIZE),
        grad_query,
        grad_key,
        grad_value,
        grad_out_proj,
        mlp_gain.reshape(-1),
        grad_gate,
        grad_up,
        grad_down.reshape(down_weight.shape),
    )


def any_line(
    layer_input,
    attn_norm,
    head_norms,
    query_weight,
    key_matrix,
    value_matrix,
    output_weight,
    mlp_norm,
    gate_weight,
    up_weight,
    down_weight,
    grad_out,
    doc_lengths,
):
    line_extent = lax.axis_size("f")
    local_rows, model_width = layer_input.shape
    group_rows = 2 * local_rows
    all_rows = 8 * local_rows
    weight_rows = gate_weight.shape[0]
    down_rows = down_weight.shape[0]
    hidden_part = line_extent * down_rows
    qkv_pieces = jnp.concatenate(
        [heads_of(query_weight), heads_of(key_matrix), heads_of(value_matrix)], axis=2
    )
    head_part = qkv_pieces.shape[2]
    query_part = head_part - 2 * HEAD_SIZE
    heads = head_part // HEAD_SIZE - 2

    def exchanged(pieces):
        return natural_plane(plane_exchange(own_plane(pieces, 0)), 0)

    def line_rows(pieces):
        return line_gather(exchanged(pieces)).reshape(model_width, -1)

    def line_sums(partial):
        parts = low(partial).reshape(line_extent, 4 * weight_rows, -1)
        return exchanged(low(line_scatter(parts)).reshape(4, weight_rows, -1))

    qkv_all = line_rows(qkv_pieces)
    out_all = full_gather(output_weight)
    gate_all = line_rows(units_of(gate_weight, down_rows))
    up_all = line_rows(units_of(up_weight, down_rows))
    down_all = line_gather(down_weight).reshape(hidden_part, model_width)

    input_float = f32(layer_input)
    scale_attn = inv_rms(input_float)
    normed_attn = tokens_gather(low(input_float * scale_attn * attn_norm))
    row_ids = row_ids_of(local_rows)
    segments, positions = jax.vmap(lambda lengths: doc_layout(lengths, row_ids))(
        plane_lengths(doc_lengths)
    )
    qkv_raw = matmul(normed_attn, qkv_all).reshape(2, 4, local_rows, head_part)
    roll = lambda values: jnp.roll(values, HEAD_SIZE // 2, 1)
    buckets, attended_parts = [], []
    for step in range(4):
        cos_tab, sin_tab = rope_tables(positions[step], HEAD_SIZE)
        cosine = jnp.concatenate([cos_tab, cos_tab], axis=1)
        sine = jnp.concatenate([-sin_tab, sin_tab], axis=1)
        allowed = (segments[step][:, None] == segments[step][None, :]) & (
            row_ids[None, :] <= row_ids[:, None]
        )
        raw = qkv_raw[:, step].reshape(group_rows, head_part)
        turned = []
        for head in range(heads + 1):
            unnormed = lanes(raw, head)
            normed = unnormed * inv_rms(unnormed) * head_norms[min(head // heads, 1)]
            turned.append(low(normed * cosine + roll(normed) * sine))
        value = low(lanes(raw, heads + 1))
        attended_parts.append(
            jnp.concatenate(
                [
                    low(matmul(low(softmax_of(turned[head], turned[heads], allowed)), value))
                    for head in range(heads)
                ],
                axis=1,
            )
        )
        buckets.append((raw, jnp.concatenate(turned + [value], axis=1), allowed, cosine, sine))
    attended = natural_plane(plane_exchange(attended_parts), 0)
    attended = attended.transpose(1, 0, 2).reshape(group_rows, 4 * query_part)
    hidden_state = input_float + pair_scatter(low(matmul(attended, out_all)))

    scale_mlp = inv_rms(hidden_state)
    normed_mlp = tokens_gather(low(hidden_state * scale_mlp * mlp_norm))
    grad_all = tokens_gather(grad_out)
    gate_raw = matmul(normed_mlp, gate_all)
    up_raw = matmul(normed_mlp, up_all)
    activated = jax.nn.silu(gate_raw)
    inner_low = low(activated * up_raw)
    layer_out = low(hidden_state + tokens_scatter(low(matmul(inner_low, down_all))))
    inner_grad = matmul_nt(grad_all, down_all)
    sigmoid_gate = jax.nn.sigmoid(gate_raw)
    gate_grad = low(inner_grad * up_raw * sigmoid_gate * (1.0 + gate_raw * (1.0 - sigmoid_gate)))
    up_grad = low(inner_grad * activated)
    mlp_row_grad = tokens_scatter(
        low(matmul_nt(gate_grad, gate_all) + matmul_nt(up_grad, up_all))
    )
    grad_down = line_scatter(
        low(matmul_tn(inner_low, grad_all)).reshape(line_extent, down_rows, model_width)
    )

    hidden_norm_grad, mlp_gain_part = norm_back(hidden_state, scale_mlp, mlp_norm, mlp_row_grad)
    hidden_grad = f32(grad_out) + hidden_norm_grad
    branch_grad = pair_gather(low(hidden_grad))
    split = low(matmul_nt(branch_grad, out_all)).reshape(group_rows, 4, query_part)
    heads_grad = plane_exchange(own_plane(split.transpose(1, 0, 2), 0))
    grad_out_proj = line_scatter(full_scatter_plane(low(matmul_tn(attended, branch_grad))))
    back = [
        attend_back_values(raw, kept, heads_grad[step], allowed, cosine, sine, head_norms, roll)
        for step, (raw, kept, allowed, cosine, sine) in enumerate(buckets)
    ]
    qkv_grad = jnp.stack([grads for grads, _ in back]).reshape(4, 2, local_rows, head_part)
    qkv_grad = qkv_grad.transpose(1, 0, 2, 3).reshape(all_rows, head_part)
    attn_row_grad = tokens_scatter(low(matmul_nt(qkv_grad, qkv_all)))
    grad_qkv_columns = line_sums(matmul_tn(normed_attn, qkv_grad))
    input_norm_grad, attn_gain_part = norm_back(input_float, scale_attn, attn_norm, attn_row_grad)
    head_gains = sum(gains for _, gains in back)[0]
    gains = total_sum(
        jnp.concatenate([attn_gain_part, mlp_gain_part, head_gains]).reshape(-1, HEAD_SIZE)
    ).reshape(-1)
    return (
        layer_out,
        hidden_grad + input_norm_grad,
        gains[:model_width],
        gains[2 * model_width :].reshape(2, HEAD_SIZE),
        heads_back(grad_qkv_columns[:, :, :query_part]),
        heads_back(grad_qkv_columns[:, :, query_part : query_part + HEAD_SIZE]),
        heads_back(grad_qkv_columns[:, :, query_part + HEAD_SIZE :]),
        grad_out_proj,
        gains[model_width : 2 * model_width],
        units_back(line_sums(matmul_tn(normed_mlp, gate_grad)), down_rows),
        units_back(line_sums(matmul_tn(normed_mlp, up_grad)), down_rows),
        grad_down,
    )


def solution(mesh):
    dp, tensor = mesh.shape["dp"], mesh.shape["tensor"]
    fine = Mesh(mesh.devices.reshape(dp // 4, 2, 2, tensor), ("f", "ty", "tx", "tensor"))
    rows = ("f", "ty", "tx")
    tokens = P(rows + ("tensor",), None)
    grid = P(rows, "tensor")
    units = P(("tensor",) + rows, None)
    return jax.shard_map(
        shards,
        mesh=fine,
        in_specs=(
            tokens, P(), P(), grid, grid, grid, units, P(), grid, grid, units, tokens, P(rows, None),
        ),
        out_specs=(tokens, tokens, P(), P(), grid, grid, grid, units, P(), grid, grid, units),
        check_vma=False,
    )
```
